32 devices in a mesh: batch: 4 (over x, core), group: 8 (over z, y).
Axes of the slice: x: 2, y: 2, z: 4, core: 2. Of those that a mesh axis runs over, the one named last changes fastest.
Arguments:
- block_input: bfloat16 [2048, 50176], P('group', 'batch'), may hold values from -6 to 6
- reduce_weight: bfloat16 [2048, 1024], P('group'), may hold values from -0.1875 to 0.1875
- reduce_gain: float32 [1024], P('group'), may hold values from 0.5 to 1.5
- reduce_bias: float32 [1024], P('group'), may hold values from -3 to 3
- group_weight: bfloat16 [32, 3, 3, 32, 32], P('group'), may hold values from -0.375 to 0.375
- group_gain: float32 [1024], P('group'), may hold values from 0.5 to 1.5
- group_bias: float32 [1024], P('group'), may hold values from -3 to 3
- expand_weight: bfloat16 [2048, 1024], P('group'), may hold values from -0.25 to 0.25
- expand_gain: float32 [2048], P('group'), may hold values from 0.5 to 1.5
- expand_bias: float32 [2048], P('group'), may hold values from -3 to 3
- out_grad: bfloat16 [2048, 50176], P('group', 'batch'), may hold values from -6 to 6
Outputs:
- block_output: bfloat16 [2048, 50176], P('group', 'batch')
- input_grad: float32 [2048, 50176], P('group', 'batch')
- reduce_weight_grad: float32 [2048, 1024], P('group')
- group_weight_grad: float32 [32, 3, 3, 32, 32], P('group')
- expand_weight_grad: float32 [2048, 1024], P('group')
- reduce_gain_grad: float32 [1024], P('group')
- reduce_bias_grad: float32 [1024], P('group')
- group_gain_grad: float32 [1024], P('group')
- group_bias_grad: float32 [1024], P('group')
- expand_gain_grad: float32 [2048], P('group')
- expand_bias_grad: float32 [2048], P('group')
The draws below stay inside these ranges and needn't reach their ends.
All inputs are finite; a program needn't handle non-finite values.
Results may differ from the reference program's by a relative error of at most 0.013.
Values may be sent and summed in bfloat16 or wider, within the bound.
A program may use at most 512 MiB of HBM per device.

```python
import jax
import jax.numpy as jnp
from jax import lax

C = 2048
GROUPS = 32
GW = 32
SIDE = 14
MID = 1024
PIXELS = 50176


def with_spikes(values, own_key, source, target, blocks, factor):
    def block_of(axis_at):
        return (jnp.arange(values.shape[axis_at]) // (values.shape[axis_at] // blocks)).reshape((-1,) + (1,) * (values.ndim - 1 - axis_at))

    near = jax.random.permutation(own_key, blocks)[block_of(target)]
    other_side = (block_of(target) + blocks // 2) % blocks
    return jnp.where((block_of(source) == near) | (block_of(source) == other_side), factor * values, values)


def block_levels(rng, dims, pieces, low, top_value):
    factor_of, own = 1.0, jax.random.fold_in(rng, 6)
    for dim, parts in pieces:
        steps = jnp.exp(jax.random.uniform(jax.random.fold_in(own, dim), (parts,), jnp.float32, low / len(pieces), top_value / len(pieces)))
        factor_of = factor_of * jnp.repeat(steps, dims[dim] // parts).reshape([-1 if axis == dim else 1 for axis in range(len(dims))])
    return factor_of


def centred(rng, extent, width, bound, pieces=(), held_as=jnp.bfloat16):
    gain = block_levels(rng, extent, pieces, -0.22, 0.18) if pieces else 1.0
    array = jax.random.normal(rng, extent, jnp.float32) * width * gain
    return jnp.minimum(jnp.maximum(array, -bound), bound).astype(held_as)


def gaussian_with(stream_key, extent, scale, bound, pieces, heavy, dtype=jnp.bfloat16):
    array = scale * jax.random.normal(stream_key, extent, jnp.float32)
    if pieces:
        array = array * block_levels(stream_key, extent, pieces, -0.22, 0.18)
    return jnp.clip(with_spikes(array, jax.random.fold_in(stream_key, 3), *heavy), -bound, bound).astype(dtype)


def setup_inputs(seed: int = 0) -> dict:
    arg_keys = jax.random.split(jax.random.key(seed), 12)
    block_input = centred(arg_keys[0], (C, PIXELS), 1.0, 6.0, ((0, 8), (1, 4)))
    reduce_weight = gaussian_with(arg_keys[1], (C, MID), C ** -0.5, 0.1875, ((0, 8),), (0, 1, 8, 2.0))
    reduce_gain = jnp.clip(1.0 + 0.1 * jax.random.normal(arg_keys[2], (MID,), jnp.float32), 0.5, 1.5)
    reduce_bias = centred(arg_keys[3], (MID,), 0.5, 3.0, ((0, 8),), jnp.float32)
    group_weight = centred(arg_keys[4], (GROUPS, 3, 3, GW, GW), (9 * GW) ** -0.5, 0.375, ((0, 8),))
    group_gain = jnp.clip(1.0 + 0.1 * jax.random.normal(arg_keys[5], (MID,), jnp.float32), 0.5, 1.5)
    group_bias = centred(arg_keys[6], (MID,), 0.5, 3.0, ((0, 8),), jnp.float32)
    expand_weight = gaussian_with(arg_keys[7], (C, MID), MID ** -0.5, 0.25, ((0, 8),), (1, 0, 8, 2.0))
    expand_gain = jnp.clip(1.0 + 0.1 * jax.random.normal(arg_keys[8], (C,), jnp.float32), 0.5, 1.5)
    expand_bias = centred(arg_keys[9], (C,), 0.5, 3.0, ((0, 8),), jnp.float32)
    out_grad = centred(arg_keys[10], (C, PIXELS), 1.0, 6.0, ((0, 8), (1, 4)))
    return {"block_input": block_input, "reduce_weight": reduce_weight, "reduce_gain": reduce_gain, "reduce_bias": reduce_bias, "group_weight": group_weight, "group_gain": group_gain, "group_bias": group_bias, "expand_weight": expand_weight, "expand_gain": expand_gain, "expand_bias": expand_bias, "out_grad": out_grad}


EPS = 1e-05

@jax.custom_vjp
def low(v):
    return lax.optimization_barrier(v.astype(jnp.bfloat16)).astype(jnp.float32)

@jax.custom_vjp
def low_back(v):
    return v

def low_keep(v):
    return (low(v), None)

def low_pass(kept, grad):
    return (grad,)

def back_keep(v):
    return (v, None)

def back_low(kept, grad):
    return (low(grad),)
low.defvjp(low_keep, low_pass)
low_back.defvjp(back_keep, back_low)

def batch_norm(values, norm_gain, norm_bias):
    center = lax.optimization_barrier(jnp.mean(values, axis=0))
    spread = lax.optimization_barrier(jnp.mean(values * values, axis=0)) - center * center
    return (values - center) * lax.rsqrt(spread + EPS) * norm_gain + norm_bias

def group_conv(feature, kernel):
    pixels = feature.shape[0]
    lattice = feature.reshape(pixels // (SIDE * SIDE), SIDE, SIDE, GROUPS, GW)
    padded = jnp.pad(lattice, ((0, 0), (1, 1), (1, 1), (0, 0), (0, 0)))
    running = jnp.zeros(lattice.shape, jnp.float32)
    for row_off in range(3):
        for col_off in range(3):
            window = padded[:, row_off:row_off + SIDE, col_off:col_off + SIDE]
            running = running + jnp.einsum('nhwgi,gio->nhwgo', window, kernel[:, row_off, col_off], precision=lax.Precision.HIGHEST)
    return running.reshape(pixels, GROUPS * GW)

def forward(block_input, reduce_weight, reduce_gain, reduce_bias, group_weight, group_gain, group_bias, expand_weight, expand_gain, expand_bias):
    rows_input = block_input.T
    reduced = low_back(jnp.dot(rows_input, reduce_weight, precision=lax.Precision.HIGHEST))
    entered = low(jax.nn.silu(batch_norm(reduced, reduce_gain, reduce_bias)))
    grouped = low_back(group_conv(entered, group_weight))
    activated = low(jax.nn.silu(batch_norm(grouped, group_gain, group_bias)))
    expanded = low_back(jnp.dot(activated, expand_weight.T, precision=lax.Precision.HIGHEST))
    return jax.nn.silu(batch_norm(expanded, expand_gain, expand_bias) + rows_input).T

def reference(block_input, reduce_weight, reduce_gain, reduce_bias, group_weight, group_gain, group_bias, expand_weight, expand_gain, expand_bias, out_grad):
    floats = tuple((member.astype(jnp.float32) for member in (block_input, reduce_weight, reduce_gain, reduce_bias, group_weight, group_gain, group_bias, expand_weight, expand_gain, expand_bias)))
    result, pullback = jax.vjp(forward, *floats)
    gradients = pullback(out_grad.astype(jnp.float32))
    return (result.astype(jnp.bfloat16), gradients[0], gradients[1], gradients[4], gradients[7], gradients[2], gradients[3], gradients[5], gradients[6], gradients[8], gradients[9])
```

```python
import functools

import jax
import jax.numpy as jnp
from jax import lax
from jax.experimental import pallas as pl
from jax.experimental.pallas import tpu as pltpu
from jax.sharding import PartitionSpec as P

GW = 32
SIDE = 14
EPS = 1e-05
BLK = 256
HALF = 128
PAD = 16
F32 = jnp.float32
BF16 = jnp.bfloat16
MESH = pl.DeviceIdType.MESH
VMEM_LIMIT = 60 * 1024 * 1024


def silu_slope(values):
    sigma = jax.nn.sigmoid(values)
    return sigma * (1.0 + values * (1.0 - sigma))


def row_chunk(pixels):
    return 224 if pixels % 224 == 0 else pixels


def over_rows(pixels, body):
    size = row_chunk(pixels)
    if size == pixels:
        body(0, size)
    else:

        @pl.loop(0, pixels // size)
        def _(step):
            body(pl.multiple_of(step * size, 16), size)


def coefficients(sums, params, count):
    center = sums[0:1] / count
    spread = sums[1:2] / count - center * center
    inverse = lax.rsqrt(spread + EPS)
    return center, inverse, params[0:1], params[1:2]


def standardize(values, coef):
    standard = (values - coef[0]) * coef[1]
    return standard, standard * coef[2] + coef[3]


def add_stats(ref, first, second):
    ref[0, 0:1] += jnp.sum(first, 0, keepdims=True)
    ref[0, 1:2] += jnp.sum(second, 0, keepdims=True)


def dot(a, b, dims=((1,), (0,))):
    return lax.dot_general(a, b, (dims, ((), ())), preferred_element_type=F32)


def call(kernel, grid, in_specs, out_specs, out_shape, scratch, flops):
    return pl.pallas_call(
        kernel,
        grid=grid,
        in_specs=in_specs,
        out_specs=out_specs,
        out_shape=out_shape,
        scratch_shapes=scratch,
        compiler_params=pltpu.CompilerParams(vmem_limit_bytes=VMEM_LIMIT),
        cost_estimate=pl.CostEstimate(flops=flops, bytes_accessed=20_000_000, transcendentals=0),
    )


def shape(dims, dtype=F32):
    return jax.ShapeDtypeStruct(dims, dtype)


def block(*dims):
    return pl.BlockSpec((1,) + dims, lambda j: (j,) + (0,) * len(dims))


def whole(*dims):
    return pl.BlockSpec(dims, lambda j: (0,) * len(dims))


def reduce_kernel(x_ref, w_ref, out_ref, sum_ref):
    sum_ref[...] = jnp.zeros_like(sum_ref)

    def body(start, size):
        rows = pl.ds(start, size)
        total = dot(x_ref[0, rows], w_ref[0])
        for source in range(1, x_ref.shape[0]):
            total += dot(x_ref[source, rows], w_ref[source])
        out_ref[0, rows] = total
        add_stats(sum_ref, total, total * total)

    over_rows(x_ref.shape[1], body)


def reduce_product(x, weight):
    blocks, pixels, _ = x.shape
    mids = weight.shape[2] // BLK
    return call(
        reduce_kernel,
        (mids,),
        [whole(blocks, pixels, BLK), pl.BlockSpec((blocks, BLK, BLK), lambda j: (0, 0, j))],
        [block(pixels, BLK), block(2, BLK)],
        [shape((mids, pixels, BLK)), shape((mids, 2, BLK))],
        [],
        2 * pixels * blocks * BLK * mids * BLK,
    )(x, weight)


def spread_weight(compact_ref, dense_ref):
    cols = lax.broadcasted_iota(jnp.int32, (GW, BLK), 1)
    rows = lax.broadcasted_iota(jnp.int32, (GW, BLK), 0)
    tile = jnp.where(cols % GW == rows, 1.0, 0.0).astype(BF16)
    own = lax.broadcasted_iota(jnp.int32, (BLK, BLK), 0) // GW == lax.broadcasted_iota(jnp.int32, (BLK, BLK), 1) // GW

    @pl.loop(0, 9)
    def _(tap):
        dense_ref[tap] = jnp.where(own, dot(compact_ref[0, tap], tile), 0.0).astype(BF16)


def twice(mask):
    return jnp.concatenate([mask, mask], 1)


def fill(stack_ref, mask_ref, rows_start, size, values):
    rows = pl.ds(rows_start, size)
    target = pl.ds(rows_start + PAD, size)
    for half in range(2):
        part = values[:, half * HALF : (half + 1) * HALF]
        stack_ref[1, half, target] = part
        stack_ref[0, half, target] = part * mask_ref[1, rows]
        stack_ref[2, half, target] = part * mask_ref[0, rows]


def clear_edges(stack_ref, pixels):
    edge = jnp.zeros(stack_ref.shape[:2] + (PAD, HALF), F32)
    stack_ref[:, :, 0:PAD] = edge
    stack_ref[:, :, PAD + pixels : PAD + pixels + PAD] = edge


def window(stack_ref, start, size, row_off, col_off):
    rows = pl.ds(start + (PAD + row_off * SIDE + col_off), size)
    return jnp.concatenate([stack_ref[col_off + 1, half, rows] for half in range(2)], 1).astype(BF16)


def conv_rows(stack_ref, mask_ref, dense_ref, start, size):
    rows = pl.ds(start, size)
    total = None
    for row_off in (-1, 0, 1):
        part = None
        for col_off in (-1, 0, 1):
            term = dot(
                window(stack_ref, start, size, row_off, col_off), dense_ref[(row_off + 1) * 3 + col_off + 1]
            )
            part = term if part is None else part + term
        if row_off:
            part = part * twice(mask_ref[2 if row_off < 0 else 3, rows])
        total = part if total is None else total + part
    return total


def conv_kernel(count, red_ref, sums_ref, prm_ref, weight_ref, mask_ref, out_ref, stat_ref, stack_ref, dense_ref):
    pixels = red_ref.shape[1]
    spread_weight(weight_ref, dense_ref)
    clear_edges(stack_ref, pixels)
    coef = coefficients(sums_ref[0], prm_ref[0], count)

    def enter(start, size):
        _, norm = standardize(red_ref[0, pl.ds(start, size)], coef)
        fill(stack_ref, mask_ref, start, size, (norm * jax.nn.sigmoid(norm)).astype(BF16).astype(F32))

    over_rows(pixels, enter)
    stat_ref[...] = jnp.zeros_like(stat_ref)

    def body(start, size):
        total = conv_rows(stack_ref, mask_ref, dense_ref, start, size)
        out_ref[0, pl.ds(start, size)] = total
        add_stats(stat_ref, total, total * total)

    over_rows(pixels, body)


def conv(reduced, sums, params, weight, masks, count):
    mids, pixels, _ = reduced.shape
    return call(
        functools.partial(conv_kernel, count),
        (mids,),
        [
            block(pixels, BLK),
            block(2, BLK),
            block(2, BLK),
            block(9, BLK, GW),
            whole(4, pixels, HALF),
        ],
        [block(pixels, BLK), block(2, BLK)],
        [shape((mids, pixels, BLK)), shape((mids, 2, BLK))],
        [pltpu.VMEM((3, 2, pixels + 2 * PAD, HALF), F32), pltpu.VMEM((9, BLK, BLK), BF16)],
        2 * 9 * pixels * mids * BLK * BLK,
    )(reduced, sums, params, weight, masks)


def conv_back_kernel(
    count,
    red_ref,
    sums_ref,
    prm_ref,
    grp_ref,
    gsums_ref,
    gprm_ref,
    up_ref,
    upsums_ref,
    weight_ref,
    mask_ref,
    out_ref,
    stat_ref,
    wgrad_ref,
    stack_ref,
    dense_ref,
    back_ref,
):
    pixels = red_ref.shape[1]
    spread_weight(weight_ref, dense_ref)
    clear_edges(stack_ref, pixels)
    coef = coefficients(sums_ref[0], prm_ref[0], count)
    gcoef = coefficients(gsums_ref[0], gprm_ref[0], count)
    scale = gcoef[2] * gcoef[1]
    up_mean = upsums_ref[0, 0:1] / count
    up_lean = upsums_ref[0, 1:2] / count

    def back(start, size):
        rows = pl.ds(start, size)
        standard, _ = standardize(grp_ref[0, rows], gcoef)
        values = (scale * (up_ref[0, rows] - up_mean - standard * up_lean)).astype(BF16)
        back_ref[1, rows] = values
        values = values.astype(F32)
        back_ref[0, rows] = (values * twice(mask_ref[2, rows])).astype(BF16)
        back_ref[2, rows] = (values * twice(mask_ref[3, rows])).astype(BF16)
        fill(stack_ref, mask_ref, start, size, values)

    over_rows(pixels, back)
    stat_ref[...] = jnp.zeros_like(stat_ref)

    def body(start, size):
        rows = pl.ds(start, size)
        standard, norm = standardize(red_ref[0, rows], coef)
        up = conv_rows(stack_ref, mask_ref, dense_ref, start, size) * silu_slope(norm)
        out_ref[0, rows] = up
        add_stats(stat_ref, up, up * standard)

    over_rows(pixels, body)

    def enter(start, size):
        _, norm = standardize(red_ref[0, pl.ds(start, size)], coef)
        fill(stack_ref, mask_ref, start, size, (norm * jax.nn.sigmoid(norm)).astype(BF16).astype(F32))

    over_rows(pixels, enter)
    own = lax.broadcasted_iota(jnp.int32, (BLK, BLK), 0) // GW == lax.broadcasted_iota(jnp.int32, (BLK, BLK), 1) // GW
    for row_off in (-1, 0, 1):
        for col_off in (-1, 0, 1):
            full = dot(
                back_ref[row_off + 1], window(stack_ref, 0, pixels, row_off, col_off), ((0,), (0,))
            )
            full = jnp.where(own, full, 0.0)
            kept = full[:, 0:GW]
            for group in range(1, BLK // GW):
                kept += full[:, group * GW : (group + 1) * GW]
            wgrad_ref[0, (row_off + 1) * 3 + col_off + 1] = kept


def conv_back(reduced, sums, params, grouped, gsums, gparams, up, upsums, weight, masks, count):
    mids, pixels, _ = reduced.shape
    return call(
        functools.partial(conv_back_kernel, count),
        (mids,),
        [
            block(pixels, BLK),
            block(2, BLK),
            block(2, BLK),
            block(pixels, BLK),
            block(2, BLK),
            block(2, BLK),
            block(pixels, BLK),
            block(2, BLK),
            block(9, BLK, GW),
            whole(4, pixels, HALF),
        ],
        [block(pixels, BLK), block(2, BLK), block(9, BLK, GW)],
        [shape((mids, pixels, BLK)), shape((mids, 2, BLK)), shape((mids, 9, BLK, GW))],
        [
            pltpu.VMEM((3, 2, pixels + 2 * PAD, HALF), F32),
            pltpu.VMEM((9, BLK, BLK), BF16),
            pltpu.VMEM((3, pixels, BLK), BF16),
        ],
        4 * 9 * pixels * mids * BLK * BLK,
    )(reduced, sums, params, grouped, gsums, gparams, up, upsums, weight, masks)


def expand_kernel(count, grp_ref, gsums_ref, gprm_ref, w_ref, out_ref, sum_ref, act_ref):
    mids, pixels, _ = grp_ref.shape

    @pl.when(pl.program_id(0) == 0)
    def _():
        for mid in range(mids):
            coef = coefficients(gsums_ref[mid], gprm_ref[mid], count)

            def body(start, size):
                rows = pl.ds(start, size)
                _, norm = standardize(grp_ref[mid, rows], coef)
                act_ref[rows, mid * BLK : (mid + 1) * BLK] = (norm * jax.nn.sigmoid(norm)).astype(BF16)

            over_rows(pixels, body)

    sum_ref[...] = jnp.zeros_like(sum_ref)

    def product(start, size):
        rows = pl.ds(start, size)
        total = dot(act_ref[rows], w_ref[0], ((1,), (1,)))
        out_ref[0, rows] = total
        add_stats(sum_ref, total, total * total)

    over_rows(pixels, product)


def expand_product(grouped, gsums, gparams, weight, count):
    mids, pixels, _ = grouped.shape
    blocks = weight.shape[0]
    return call(
        functools.partial(expand_kernel, count),
        (blocks,),
        [
            whole(mids, pixels, BLK),
            whole(mids, 2, BLK),
            whole(mids, 2, BLK),
            block(BLK, mids * BLK),
        ],
        [block(pixels, BLK), block(2, BLK), whole(pixels, mids * BLK)],
        [shape((blocks, pixels, BLK)), shape((blocks, 2, BLK)), shape((pixels, mids * BLK), BF16)],
        [],
        2 * pixels * blocks * BLK * mids * BLK,
    )(grouped, gsums, gparams, weight)


def output_kernel(count, exp_ref, sums_ref, prm_ref, x_ref, grad_ref, out_ref, up_ref, stat_ref):
    coef = coefficients(sums_ref[0], prm_ref[0], count)
    stat_ref[...] = jnp.zeros_like(stat_ref)

    def body(start, size):
        rows = pl.ds(start, size)
        standard, norm = standardize(exp_ref[0, rows], coef)
        summed = norm + x_ref[0, rows].astype(F32)
        sigma = jax.nn.sigmoid(summed)
        out_ref[0, rows] = (summed * sigma).astype(BF16)
        up = grad_ref[0, rows].astype(F32) * (sigma * (1.0 + summed * (1.0 - sigma)))
        up_ref[0, rows] = up
        add_stats(stat_ref, up, up * standard)

    over_rows(exp_ref.shape[1], body)


def output(expanded, sums, params, x, grad, count):
    blocks, pixels, _ = expanded.shape
    return call(
        functools.partial(output_kernel, count),
        (blocks,),
        [block(pixels, BLK), block(2, BLK), block(2, BLK), block(pixels, BLK), block(pixels, BLK)],
        [block(pixels, BLK), block(pixels, BLK), block(2, BLK)],
        [shape((blocks, pixels, BLK), BF16), shape((blocks, pixels, BLK)), shape((blocks, 2, BLK))],
        [],
        20 * pixels * blocks * BLK,
    )(expanded, sums, params, x, grad)


def expand_back_kernel(
    count,
    exp_ref,
    sums_ref,
    prm_ref,
    up_ref,
    upsums_ref,
    w_ref,
    grp_ref,
    gsums_ref,
    gprm_ref,
    back_ref,
    out_ref,
    stat_ref,
    keep_ref,
):
    blocks, pixels, _ = keep_ref.shape
    step = pl.program_id(0)

    @pl.when(step < blocks)
    def _():
        coef = coefficients(sums_ref[0], prm_ref[0], count)
        scale = coef[2] * coef[1]
        up_mean = upsums_ref[0, 0:1] / count
        up_lean = upsums_ref[0, 1:2] / count

        def back(start, size):
            rows = pl.ds(start, size)
            standard, _ = standardize(exp_ref[0, rows], coef)
            values = (scale * (up_ref[0, rows] - up_mean - standard * up_lean)).astype(BF16)
            back_ref[0, rows] = values
            keep_ref[step, rows] = values

        over_rows(pixels, back)

    @pl.when(step >= blocks)
    def _():
        coef = coefficients(gsums_ref[0], gprm_ref[0], count)
        stat_ref[...] = jnp.zeros_like(stat_ref)

        def body(start, size):
            rows = pl.ds(start, size)
            total = dot(keep_ref[0, rows], w_ref[0])
            for source in range(1, blocks):
                total += dot(keep_ref[source, rows], w_ref[source])
            standard, norm = standardize(grp_ref[0, rows], coef)
            up = total * silu_slope(norm)
            out_ref[0, rows] = up
            add_stats(stat_ref, up, up * standard)

        over_rows(pixels, body)


def expand_back(expanded, sums, params, up, upsums, weight, grouped, gsums, gparams, count):
    blocks, pixels, _ = expanded.shape
    mids = grouped.shape[0]

    def first(*dims):
        return pl.BlockSpec((1,) + dims, lambda j: (jnp.minimum(j, blocks - 1),) + (0,) * len(dims))

    def second(*dims):
        return pl.BlockSpec((1,) + dims, lambda j: (jnp.maximum(j - blocks, 0),) + (0,) * len(dims))

    return call(
        functools.partial(expand_back_kernel, count),
        (blocks + mids,),
        [
            first(pixels, BLK),
            first(2, BLK),
            first(2, BLK),
            first(pixels, BLK),
            first(2, BLK),
            pl.BlockSpec((blocks, BLK, BLK), lambda j: (0, 0, jnp.maximum(j - blocks, 0))),
            second(pixels, BLK),
            second(2, BLK),
            second(2, BLK),
        ],
        [first(pixels, BLK), second(pixels, BLK), second(2, BLK)],
        [shape((blocks, pixels, BLK), BF16), shape((mids, pixels, BLK)), shape((mids, 2, BLK))],
        [pltpu.VMEM((blocks, pixels, BLK), BF16)],
        2 * pixels * blocks * BLK * mids * BLK,
    )(expanded, sums, params, up, upsums, weight, grouped, gsums, gparams)


def weight_grad_kernel(left_ref, right_ref, out_ref):
    for first in range(0, right_ref.shape[1], BLK):
        columns = slice(first, first + BLK)
        out_ref[0, :, columns] = dot(left_ref[0], right_ref[:, columns], ((0,), (0,))).astype(BF16)


def weight_grad(left, right):
    blocks, pixels, _ = left.shape
    width = right.shape[1]
    return call(
        weight_grad_kernel,
        (blocks,),
        [block(pixels, BLK), whole(pixels, width)],
        [block(BLK, width)],
        [shape((blocks, BLK, width), BF16)],
        [],
        2 * pixels * blocks * BLK * width,
    )(left, right)[0]


def reduce_back_kernel(count, red_ref, sums_ref, prm_ref, rup_ref, rupsums_ref, x_ref, up_ref, w_ref, grad_ref, wgrad_ref, back_ref):
    mids, pixels, _ = red_ref.shape

    @pl.when(pl.program_id(0) == 0)
    def _():
        for mid in range(mids):
            coef = coefficients(sums_ref[mid], prm_ref[mid], count)
            scale = coef[2] * coef[1]
            up_mean = rupsums_ref[mid, 0:1] / count
            up_lean = rupsums_ref[mid, 1:2] / count

            def body(start, size):
                rows = pl.ds(start, size)
                standard, _ = standardize(red_ref[mid, rows], coef)
                values = scale * (rup_ref[mid, rows] - up_mean - standard * up_lean)
                back_ref[rows, mid * BLK : (mid + 1) * BLK] = values.astype(BF16)

            over_rows(pixels, body)

    def product(start, size):
        rows = pl.ds(start, size)
        total = dot(back_ref[rows], w_ref[0], ((1,), (1,)))
        grad_ref[0, rows] = (up_ref[0, rows] + total).astype(BF16)

    over_rows(pixels, product)
    for mid in range(mids):
        columns = slice(mid * BLK, (mid + 1) * BLK)
        wgrad_ref[0, :, columns] = dot(x_ref[0], back_ref[:, columns], ((0,), (0,))).astype(BF16)


def reduce_back(reduced, sums, params, rup, rupsums, x, up, weight, count):
    mids, pixels, _ = reduced.shape
    blocks = x.shape[0]
    return call(
        functools.partial(reduce_back_kernel, count),
        (blocks,),
        [
            whole(mids, pixels, BLK),
            whole(mids, 2, BLK),
            whole(mids, 2, BLK),
            whole(mids, pixels, BLK),
            whole(mids, 2, BLK),
            block(pixels, BLK),
            block(pixels, BLK),
            block(BLK, mids * BLK),
        ],
        [block(pixels, BLK), block(BLK, mids * BLK)],
        [shape((blocks, pixels, BLK), BF16), shape((blocks, BLK, mids * BLK), BF16)],
        [pltpu.VMEM((pixels, mids * BLK), BF16)],
        4 * pixels * blocks * BLK * mids * BLK,
    )(reduced, sums, params, rup, rupsums, x, up, weight)


def exchange_kernel(batches, members, x_ref, out_ref, first_ref, second_ref, mid_ref, send1, recv1, send2, recv2):
    row, me = lax.axis_index("batch"), lax.axis_index("group")
    across = [(lax.rem(row + step, batches), me) for step in range(1, batches)]
    along = [(row, lax.rem(me + step, members)) for step in range(1, members)]
    barrier = pltpu.get_barrier_semaphore()
    for device in across + along:
        pl.semaphore_signal(barrier, inc=1, device_id=device, device_id_type=MESH)
    pl.semaphore_wait(barrier, len(across) + len(along))

    def spread(source, target, send, recv, devices):
        copies = []
        for step, device in enumerate(devices):
            copy = pltpu.make_async_remote_copy(
                src_ref=source,
                dst_ref=target.at[step],
                send_sem=send.at[step],
                recv_sem=recv.at[step],
                device_id=device,
                device_id_type=MESH,
            )
            copy.start()
            copies.append(copy)
        for copy in copies:
            copy.wait()

    spread(x_ref, first_ref, send1, recv1, across)
    total = x_ref[...]
    for step in range(batches - 1):
        total += first_ref[step]
    mid_ref[...] = total
    spread(mid_ref, second_ref, send2, recv2, along)
    for step in range(members - 1):
        total += second_ref[step]
    out_ref[...] = total


def exchange(values, batches, members, collective_id):
    return pl.pallas_call(
        functools.partial(exchange_kernel, batches, members),
        in_specs=[pl.BlockSpec(memory_space=pltpu.VMEM)],
        out_specs=pl.BlockSpec(memory_space=pltpu.VMEM),
        out_shape=shape(values.shape),
        scratch_shapes=[
            pltpu.VMEM((batches - 1,) + values.shape, F32),
            pltpu.VMEM((members - 1,) + values.shape, F32),
            pltpu.VMEM(values.shape, F32),
            pltpu.SemaphoreType.DMA((batches - 1,)),
            pltpu.SemaphoreType.DMA((batches - 1,)),
            pltpu.SemaphoreType.DMA((members - 1,)),
            pltpu.SemaphoreType.DMA((members - 1,)),
        ],
        compiler_params=pltpu.CompilerParams(collective_id=collective_id, has_side_effects=True),
    )(values)


def local(
    block_input,
    reduce_weight,
    reduce_gain,
    reduce_bias,
    group_weight,
    group_gain,
    group_bias,
    expand_weight,
    expand_gain,
    expand_bias,
    out_grad,
):
    batches, members = lax.axis_size("batch"), lax.axis_size("group")
    channels, row_pixels = block_input.shape
    pixels = row_pixels // members
    count = row_pixels * batches
    mid_total = reduce_weight.shape[1]
    mids = mid_total // BLK
    blocks = channels * members // BLK
    me = lax.axis_index("group")

    def to_pixels(values):
        moved = lax.all_to_all(values.T.reshape(members, pixels, channels), "group", 0, 0)
        if channels == BLK:
            return moved
        share = BLK // channels
        moved = moved.reshape(blocks, share, pixels, channels).transpose(0, 2, 1, 3)
        return moved.reshape(blocks, pixels, BLK)

    def to_channels(values):
        if channels != BLK:
            share = BLK // channels
            values = values.reshape(blocks, pixels, share, channels).transpose(0, 2, 1, 3)
            values = values.reshape(members, pixels, channels)
        moved = lax.all_to_all(values, "group", 0, 0)
        return moved.reshape(row_pixels, channels).T

    def gather(values):
        return lax.all_gather(values, "group", axis=0, tiled=True)

    local_mid = reduce_gain.shape[0]
    pack = jnp.concatenate([reduce_gain, reduce_bias, group_gain, group_bias, expand_gain, expand_bias])
    packs = gather(pack[None])
    vectors, offset = [], 0
    for length in (local_mid, local_mid, local_mid, local_mid, channels, channels):
        vectors.append(packs[:, offset : offset + length].reshape(-1, BLK))
        offset += length
    reduce_params = jnp.stack(vectors[0:2], 1)
    group_params = jnp.stack(vectors[2:4], 1)
    expand_params = jnp.stack(vectors[4:6], 1)
    reduce_full = gather(reduce_weight).reshape(blocks, BLK, mid_total)
    expand_full = gather(expand_weight).reshape(blocks, BLK, mid_total)
    taps = gather(group_weight.reshape(group_weight.shape[0], 9, GW, GW))
    taps = taps.reshape(mids, BLK // GW, 9, GW, GW)
    forward_taps = taps.transpose(0, 2, 1, 3, 4).reshape(mids, 9, BLK, GW)
    backward_taps = taps[:, :, ::-1].transpose(0, 2, 1, 4, 3).reshape(mids, 9, BLK, GW)
    place = jnp.arange(pixels, dtype=jnp.int32)
    tall, wide = (place // SIDE) % SIDE, place % SIDE
    masks = jnp.stack([wide != 0, wide != SIDE - 1, tall != 0, tall != SIDE - 1])
    masks = jnp.broadcast_to(masks[:, :, None].astype(F32), (4, pixels, HALF))

    x = to_pixels(block_input)
    grad = to_pixels(out_grad)

    reduced, reduce_sums = reduce_product(x, reduce_full)
    reduce_sums = exchange(reduce_sums, batches, members, 1)
    grouped, group_sums = conv(reduced, reduce_sums, reduce_params, forward_taps, masks, count)
    group_sums = exchange(group_sums, batches, members, 1)
    expanded, expand_sums, act = expand_product(grouped, group_sums, group_params, expand_full, count)
    expand_sums = exchange(expand_sums, batches, members, 2)
    out, upstream, expand_stats = output(expanded, expand_sums, expand_params, x, grad, count)
    expand_stats = exchange(expand_stats, batches, members, 2)
    back, group_up, group_stats = expand_back(
        expanded, expand_sums, expand_params, upstream, expand_stats, expand_full, grouped, group_sums, group_params, count
    )
    expand_part = weight_grad(back, act)
    group_stats = exchange(group_stats, batches, members, 1)
    reduce_up, reduce_stats, taps_part = conv_back(
        reduced,
        reduce_sums,
        reduce_params,
        grouped,
        group_sums,
        group_params,
        group_up,
        group_stats,
        backward_taps,
        masks,
        count,
    )
    reduce_stats = exchange(reduce_stats, batches, members, 1)
    inner, reduce_part = reduce_back(
        reduced, reduce_sums, reduce_params, reduce_up, reduce_stats, x, upstream, reduce_full, count
    )
    block_output = to_channels(out)
    input_grad = to_channels(inner).astype(F32)

    def shared_sum(part):
        rows = channels // batches
        part = part.reshape(members, batches, rows, mid_total).transpose(1, 0, 2, 3)
        part = lax.all_to_all(part, "batch", 0, 0).astype(F32).sum(0).astype(BF16)
        part = lax.all_to_all(part, "group", 0, 0).astype(F32).sum(0)
        return lax.all_gather(part, "batch", axis=0, tiled=True)

    expand_weight_grad = shared_sum(expand_part)
    reduce_weight_grad = shared_sum(reduce_part)
    taps_part = taps_part.reshape(mids, 9, BLK // GW, GW, GW).transpose(0, 2, 1, 4, 3)
    taps_part = taps_part.reshape(members, -1, 9, GW, GW)
    group_weight_grad = lax.all_to_all(taps_part.astype(BF16), "group", 0, 0).astype(F32).sum(0)
    group_weight_grad = lax.psum(group_weight_grad, "batch").reshape(group_weight.shape)

    def own(stats, which, length):
        return lax.dynamic_slice_in_dim(stats[:, which].reshape(-1), me * length, length, 0)

    return (
        block_output,
        input_grad,
        reduce_weight_grad,
        group_weight_grad,
        expand_weight_grad,
        own(reduce_stats, 1, local_mid),
        own(reduce_stats, 0, local_mid),
        own(group_stats, 1, local_mid),
        own(group_stats, 0, local_mid),
        own(expand_stats, 1, channels),
        own(expand_stats, 0, channels),
    )


def solution(mesh):
    in_specs = (
        P("group", "batch"),
        P("group", None),
        P("group"),
        P("group"),
        P("group", None, None, None, None),
        P("group"),
        P("group"),
        P("group", None),
        P("group"),
        P("group"),
        P("group", "batch"),
    )
    out_specs = (
        P("group", "batch"),
        P("group", "batch"),
        P("group", None),
        P("group", None, None, None, None),
        P("group", None),
        P("group"),
        P("group"),
        P("group"),
        P("group"),
        P("group"),
        P("group"),
    )
    return jax.shard_map(local, mesh=mesh, in_specs=in_specs, out_specs=out_specs, check_vma=False)
```

```python
import functools

import jax
import jax.numpy as jnp
from jax import lax
from jax.experimental import pallas as pl
from jax.experimental.pallas import tpu as pltpu
from jax.sharding import PartitionSpec as P

GW = 32
SIDE = 14
EPS = 1e-05
BLK = 256
HALF = 128
PAD = 16
F32 = jnp.float32
BF16 = jnp.bfloat16
MESH = pl.DeviceIdType.MESH
VMEM_LIMIT = 60 * 1024 * 1024


def silu_slope(values):
    sigma = jax.nn.sigmoid(values)
    return sigma * (1.0 + values * (1.0 - sigma))


def row_chunk(pixels):
    for size in (224, 208, 192, 176, 160, 144, 128, 112):
        if pixels % size == 0:
            return size
    return pixels


def over_rows(pixels, body):
    size = row_chunk(pixels)
    if size == pixels:
        body(0, size)
    else:

        @pl.loop(0, pixels // size)
        def _(step):
            body(pl.multiple_of(step * size, 16), size)


def coefficients(sums, params, count):
    center = sums[0:1] / count
    spread = sums[1:2] / count - center * center
    inverse = lax.rsqrt(spread + EPS)
    return center, inverse, params[0:1], params[1:2]


def standardize(values, coef):
    standard = (values - coef[0]) * coef[1]
    return standard, standard * coef[2] + coef[3]


def add_stats(ref, slot, first, second):
    ref[slot, 0:1] += jnp.sum(first, 0, keepdims=True)
    ref[slot, 1:2] += jnp.sum(second, 0, keepdims=True)


def clear_stats(ref):
    @pl.when(pl.program_id(0) == 0)
    def _():
        ref[...] = jnp.zeros_like(ref)


def dot(a, b, dims=((1,), (0,))):
    return lax.dot_general(a, b, (dims, ((), ())), preferred_element_type=F32)


def devices(batches, members):
    row, me = lax.axis_index("batch"), lax.axis_index("group")
    across = [(lax.rem(row + step, batches), me) for step in range(1, batches)]
    along = [(row, lax.rem(me + step, members)) for step in range(1, members)]
    return row, me, across, along


def greet(others):
    barrier = pltpu.get_barrier_semaphore()
    for device in others:
        pl.semaphore_signal(barrier, inc=1, device_id=device, device_id_type=MESH)
    pl.semaphore_wait(barrier, len(others))


def remote(source, target, send, recv, device):
    return pltpu.make_async_remote_copy(
        src_ref=source, dst_ref=target, send_sem=send, recv_sem=recv, device_id=device, device_id_type=MESH
    )


def spread(source, target, send, recv, others):
    copies = [
        remote(source, target.at[step], send.at[step], recv.at[step], device) for step, device in enumerate(others)
    ]
    for copy in copies:
        copy.start()
    for copy in copies:
        copy.wait()


def total_stats(ref, across, along, first_ref, second_ref, mid_ref, send1, recv1, send2, recv2):
    mid_ref[0] = ref[...]
    spread(mid_ref.at[0], first_ref, send1, recv1, across)
    total = mid_ref[0]
    for step in range(len(across)):
        total += first_ref[step]
    mid_ref[1] = total
    spread(mid_ref.at[1], second_ref, send2, recv2, along)
    for step in range(len(along)):
        total += second_ref[step]
    ref[...] = total


def stats_scratch(dims, batches, members):
    return [
        pltpu.VMEM((batches - 1,) + dims, F32),
        pltpu.VMEM((members - 1,) + dims, F32),
        pltpu.VMEM((2,) + dims, F32),
        pltpu.SemaphoreType.DMA((batches - 1,)),
        pltpu.SemaphoreType.DMA((batches - 1,)),
        pltpu.SemaphoreType.DMA((members - 1,)),
        pltpu.SemaphoreType.DMA((members - 1,)),
    ]


class Comm:
    def __init__(self, batches, members, collective_id, source=None, rows=None, into=None):
        self.batches, self.members, self.collective_id = batches, members, collective_id
        self.source, self.rows, self.into = source, rows, into


def piece_copies(source, target, rows, me, along, send, recv):
    rows = pl.ds(*rows)
    copies = [
        remote(source.at[device[1], rows], target.at[me, rows], send.at[step], recv.at[step], device)
        for step, device in enumerate(along)
    ]
    return copies + [pltpu.make_async_copy(source.at[me, rows], target.at[me, rows], send.at[len(along)])]


def call(kernel, grid, in_specs, out_specs, out_shape, scratch, flops, comm=None):
    if comm is None:
        return functools.partial(
            plain_call, kernel, grid, in_specs, out_specs, out_shape, scratch, flops, pltpu.CompilerParams(vmem_limit_bytes=VMEM_LIMIT)
        )
    n_in, n_out, n_scratch = len(in_specs), len(out_specs), len(scratch)
    stats = out_shape[-1].shape
    batches, members = comm.batches, comm.members

    def wrapped(*refs):
        refs = list(refs)
        ins = refs[:n_in]
        del refs[:n_in]
        source = refs.pop(0) if comm.rows else None
        if comm.into is not None:
            refs.pop(0)
        outs = refs[:n_out]
        del refs[:n_out]
        target = refs.pop(0) if comm.rows else None
        own = refs[:n_scratch]
        del refs[:n_scratch]
        stats_refs = refs[:7]
        del refs[:7]
        row, me, across, along = devices(batches, members)

        def copies():
            return piece_copies(source, target, comm.rows, me, along, *refs)

        @pl.when(pl.program_id(0) == 0)
        def _():
            greet(across + along)
            if comm.rows:
                for copy in copies():
                    copy.start()

        kernel(*ins, *outs, *own)

        @pl.when(pl.program_id(0) == pl.num_programs(0) - 1)
        def _():
            total_stats(outs[-1], across, along, *stats_refs)
            if comm.rows:
                for copy in copies():
                    copy.wait()

    scratch = list(scratch) + stats_scratch(stats, batches, members)
    in_specs, out_specs, out_shape = list(in_specs), list(out_specs), list(out_shape)
    extra, aliases = [], {}
    if comm.rows:
        extra = [comm.source]
        if comm.into is not None:
            extra.append(comm.into)
            aliases = {len(in_specs) + 1: len(out_specs)}
        in_specs += [pl.BlockSpec(memory_space=pl.ANY)] * len(extra)
        out_specs.append(pl.BlockSpec(memory_space=pl.ANY))
        out_shape.append(shape(comm.source.shape, comm.source.dtype))
        scratch += [pltpu.SemaphoreType.DMA((members,)), pltpu.SemaphoreType.DMA((members - 1,))]
    params = pltpu.CompilerParams(
        vmem_limit_bytes=VMEM_LIMIT, collective_id=comm.collective_id, has_side_effects=True
    )
    inner = functools.partial(
        plain_call, wrapped, grid, in_specs, out_specs, out_shape, scratch, flops, params, aliases=aliases
    )
    return lambda *args: inner(*args, *extra)


def plain_call(kernel, grid, in_specs, out_specs, out_shape, scratch, flops, params, *args, aliases={}):
    return pl.pallas_call(
        kernel,
        grid=grid,
        in_specs=in_specs,
        out_specs=out_specs,
        out_shape=out_shape,
        scratch_shapes=scratch,
        input_output_aliases=aliases,
        compiler_params=params,
        cost_estimate=pl.CostEstimate(flops=flops, bytes_accessed=20_000_000, transcendentals=0),
    )(*args)


def shape(dims, dtype=F32):
    return jax.ShapeDtypeStruct(dims, dtype)


def block(*dims):
    return pl.BlockSpec((1,) + dims, lambda j: (j,) + (0,) * len(dims))


def whole(*dims):
    return pl.BlockSpec(dims, lambda j: (0,) * len(dims))


def reduce_kernel(x_ref, w_ref, out_ref, sum_ref):
    clear_stats(sum_ref)
    slot = pl.program_id(0)

    def body(start, size):
        rows = pl.ds(start, size)
        total = dot(x_ref[0, rows], w_ref[0])
        for source in range(1, x_ref.shape[0]):
            total += dot(x_ref[source, rows], w_ref[source])
        out_ref[0, rows] = total
        add_stats(sum_ref, slot, total, total * total)

    over_rows(x_ref.shape[1], body)


def reduce_product(x, weight, comm):
    blocks, pixels, _ = x.shape
    mids = weight.shape[2] // BLK
    return call(
        reduce_kernel,
        (mids,),
        [whole(blocks, pixels, BLK), pl.BlockSpec((blocks, BLK, BLK), lambda j: (0, 0, j))],
        [block(pixels, BLK), whole(mids, 2, BLK)],
        [shape((mids, pixels, BLK)), shape((mids, 2, BLK))],
        [],
        2 * pixels * blocks * BLK * mids * BLK,
        comm,
    )(x, weight)


def same_group():
    return lax.broadcasted_iota(jnp.int32, (BLK, BLK), 0) // GW == lax.broadcasted_iota(jnp.int32, (BLK, BLK), 1) // GW


def spread_weight(compact_ref, dense_ref):
    own = same_group()
    for tap in range(9):
        rows = pl.ds(tap * GW, GW)
        compact = jnp.concatenate([compact_ref[0, rows], compact_ref[1, rows]], 1).astype(F32)
        tiled = jnp.concatenate([compact] * (BLK // GW), 0)
        dense_ref[tap] = jnp.where(own, tiled, 0.0).astype(BF16)


def twice(mask):
    return jnp.concatenate([mask, mask], 1)


def fill(stack_ref, mask_ref, rows_start, size, values):
    rows = pl.ds(rows_start, size)
    target = pl.ds(rows_start + PAD, size)
    for half in range(2):
        part = values[:, half * HALF : (half + 1) * HALF]
        stack_ref[1, half, target] = part
        stack_ref[0, half, target] = part * mask_ref[1, rows]
        stack_ref[2, half, target] = part * mask_ref[0, rows]


def clear_edges(stack_ref, pixels):
    edge = jnp.zeros(stack_ref.shape[:2] + (PAD, HALF), F32)
    stack_ref[:, :, 0:PAD] = edge
    stack_ref[:, :, PAD + pixels : PAD + pixels + PAD] = edge


def window(stack_ref, start, size, row_off, col_off):
    rows = pl.ds(start + (PAD + row_off * SIDE + col_off), size)
    return jnp.concatenate([stack_ref[col_off + 1, half, rows] for half in range(2)], 1).astype(BF16)


def conv_rows(stack_ref, mask_ref, dense_ref, start, size, flipped=False):
    rows = pl.ds(start, size)
    total = None
    for row_off in (-1, 0, 1):
        part = None
        for col_off in (-1, 0, 1):
            values = window(stack_ref, start, size, row_off, col_off)
            tap = (row_off + 1) * 3 + col_off + 1
            term = dot(values, dense_ref[8 - tap], ((1,), (1,))) if flipped else dot(values, dense_ref[tap])
            part = term if part is None else part + term
        if row_off:
            part = part * twice(mask_ref[2 if row_off < 0 else 3, rows])
        total = part if total is None else total + part
    return total


def conv_kernel(count, red_ref, sums_ref, prm_ref, weight_ref, mask_ref, out_ref, stat_ref, stack_ref, dense_ref):
    pixels = red_ref.shape[1]
    spread_weight(weight_ref, dense_ref)
    clear_edges(stack_ref, pixels)
    coef = coefficients(sums_ref[0], prm_ref[0], count)

    def enter(start, size):
        _, norm = standardize(red_ref[0, pl.ds(start, size)], coef)
        fill(stack_ref, mask_ref, start, size, (norm * jax.nn.sigmoid(norm)).astype(BF16).astype(F32))

    over_rows(pixels, enter)
    clear_stats(stat_ref)
    slot = pl.program_id(0)

    def body(start, size):
        total = conv_rows(stack_ref, mask_ref, dense_ref, start, size)
        out_ref[0, pl.ds(start, size)] = total
        add_stats(stat_ref, slot, total, total * total)

    over_rows(pixels, body)


def conv(reduced, sums, params, weight, masks, count, comm):
    mids, pixels, _ = reduced.shape
    return call(
        functools.partial(conv_kernel, count),
        (mids,),
        [
            block(pixels, BLK),
            block(2, BLK),
            block(2, BLK),
            pl.BlockSpec((2,) + weight.shape[1:], lambda j: (j, 0, 0)),
            whole(4, pixels, HALF),
        ],
        [block(pixels, BLK), whole(mids, 2, BLK)],
        [shape((mids, pixels, BLK)), shape((mids, 2, BLK))],
        [pltpu.VMEM((3, 2, pixels + 2 * PAD, HALF), F32), pltpu.VMEM((9, BLK, BLK), BF16)],
        2 * 9 * pixels * mids * BLK * BLK,
        comm,
    )(reduced, sums, params, weight, masks)


def conv_back_kernel(
    count,
    red_ref,
    sums_ref,
    prm_ref,
    grp_ref,
    gsums_ref,
    gprm_ref,
    up_ref,
    upsums_ref,
    weight_ref,
    mask_ref,
    out_ref,
    wgrad_ref,
    stat_ref,
    stack_ref,
    dense_ref,
    back_ref,
):
    pixels = red_ref.shape[1]
    spread_weight(weight_ref, dense_ref)
    clear_edges(stack_ref, pixels)
    coef = coefficients(sums_ref[0], prm_ref[0], count)
    gcoef = coefficients(gsums_ref[0], gprm_ref[0], count)
    scale = gcoef[2] * gcoef[1]
    up_mean = upsums_ref[0, 0:1] / count
    up_lean = upsums_ref[0, 1:2] / count

    def back(start, size):
        rows = pl.ds(start, size)
        standard, _ = standardize(grp_ref[0, rows], gcoef)
        values = (scale * (up_ref[0, rows] - up_mean - standard * up_lean)).astype(BF16)
        back_ref[1, rows] = values
        values = values.astype(F32)
        back_ref[0, rows] = (values * twice(mask_ref[2, rows])).astype(BF16)
        back_ref[2, rows] = (values * twice(mask_ref[3, rows])).astype(BF16)
        fill(stack_ref, mask_ref, start, size, values)

    over_rows(pixels, back)
    clear_stats(stat_ref)
    slot = pl.program_id(0)

    def body(start, size):
        rows = pl.ds(start, size)
        standard, norm = standardize(red_ref[0, rows], coef)
        up = conv_rows(stack_ref, mask_ref, dense_ref, start, size, True) * silu_slope(norm)
        out_ref[0, rows] = up
        add_stats(stat_ref, slot, up, up * standard)

    over_rows(pixels, body)

    def enter(start, size):
        _, norm = standardize(red_ref[0, pl.ds(start, size)], coef)
        fill(stack_ref, mask_ref, start, size, (norm * jax.nn.sigmoid(norm)).astype(BF16).astype(F32))

    over_rows(pixels, enter)
    own = same_group()
    for tap in range(9):
        full = dot(back_ref[tap // 3], window(stack_ref, 0, pixels, tap // 3 - 1, tap % 3 - 1), ((0,), (0,)))
        full = jnp.where(own, full, 0.0)
        kept = full[0:GW]
        for group in range(1, BLK // GW):
            kept += full[group * GW : (group + 1) * GW]
        for half in range(2):
            wgrad_ref[half, tap * GW : (tap + 1) * GW] = kept[:, half * HALF : (half + 1) * HALF].astype(BF16)
    for half in range(2):
        wgrad_ref[half, 9 * GW :] = jnp.zeros((wgrad_ref.shape[1] - 9 * GW, HALF), BF16)


def conv_back(reduced, sums, params, grouped, gsums, gparams, up, upsums, weight, masks, count, comm):
    mids, pixels, _ = reduced.shape
    return call(
        functools.partial(conv_back_kernel, count),
        (mids,),
        [
            block(pixels, BLK),
            block(2, BLK),
            block(2, BLK),
            block(pixels, BLK),
            block(2, BLK),
            block(2, BLK),
            block(pixels, BLK),
            block(2, BLK),
            pl.BlockSpec((2,) + weight.shape[1:], lambda j: (j, 0, 0)),
            whole(4, pixels, HALF),
        ],
        [block(pixels, BLK), pl.BlockSpec((2,) + weight.shape[1:], lambda j: (j, 0, 0)), whole(mids, 2, BLK)],
        [shape((mids, pixels, BLK)), shape(weight.shape, BF16), shape((mids, 2, BLK))],
        [
            pltpu.VMEM((3, 2, pixels + 2 * PAD, HALF), F32),
            pltpu.VMEM((9, BLK, BLK), BF16),
            pltpu.VMEM((3, pixels, BLK), BF16),
        ],
        4 * 9 * pixels * mids * BLK * BLK,
        comm,
    )(reduced, sums, params, grouped, gsums, gparams, up, upsums, weight, masks)


def expand_kernel(count, grp_ref, gsums_ref, gprm_ref, w_ref, out_ref, act_ref, sum_ref):
    mids, pixels, _ = grp_ref.shape

    @pl.when(pl.program_id(0) == 0)
    def _():
        for mid in range(mids):
            coef = coefficients(gsums_ref[mid], gprm_ref[mid], count)

            def body(start, size):
                rows = pl.ds(start, size)
                _, norm = standardize(grp_ref[mid, rows], coef)
                act_ref[rows, mid * BLK : (mid + 1) * BLK] = (norm * jax.nn.sigmoid(norm)).astype(BF16)

            over_rows(pixels, body)

    clear_stats(sum_ref)
    slot = pl.program_id(0)

    def product(start, size):
        rows = pl.ds(start, size)
        total = dot(act_ref[rows], w_ref[0], ((1,), (1,)))
        out_ref[0, rows] = total
        add_stats(sum_ref, slot, total, total * total)

    over_rows(pixels, product)


def expand_product(grouped, gsums, gparams, weight, count, comm):
    mids, pixels, _ = grouped.shape
    blocks = weight.shape[0]
    return call(
        functools.partial(expand_kernel, count),
        (blocks,),
        [
            whole(mids, pixels, BLK),
            whole(mids, 2, BLK),
            whole(mids, 2, BLK),
            block(BLK, mids * BLK),
        ],
        [block(pixels, BLK), whole(pixels, mids * BLK), whole(blocks, 2, BLK)],
        [shape((blocks, pixels, BLK)), shape((pixels, mids * BLK), BF16), shape((blocks, 2, BLK))],
        [],
        2 * pixels * blocks * BLK * mids * BLK,
        comm,
    )(grouped, gsums, gparams, weight)


def output_kernel(count, exp_ref, sums_ref, prm_ref, x_ref, grad_ref, out_ref, up_ref, stat_ref):
    coef = coefficients(sums_ref[0], prm_ref[0], count)
    clear_stats(stat_ref)
    slot = pl.program_id(0)

    def body(start, size):
        rows = pl.ds(start, size)
        standard, norm = standardize(exp_ref[0, rows], coef)
        summed = norm + x_ref[0, rows].astype(F32)
        sigma = jax.nn.sigmoid(summed)
        out_ref[0, rows] = (summed * sigma).astype(BF16)
        up = grad_ref[0, rows].astype(F32) * (sigma * (1.0 + summed * (1.0 - sigma)))
        up_ref[0, rows] = up
        add_stats(stat_ref, slot, up, up * standard)

    over_rows(exp_ref.shape[1], body)


def output(expanded, sums, params, x, grad, count, comm):
    blocks, pixels, _ = expanded.shape
    return call(
        functools.partial(output_kernel, count),
        (blocks,),
        [block(pixels, BLK), block(2, BLK), block(2, BLK), block(pixels, BLK), block(pixels, BLK)],
        [block(pixels, BLK), block(pixels, BLK), whole(blocks, 2, BLK)],
        [shape((blocks, pixels, BLK), BF16), shape((blocks, pixels, BLK)), shape((blocks, 2, BLK))],
        [],
        20 * pixels * blocks * BLK,
        comm,
    )(expanded, sums, params, x, grad)


def expand_back_kernel(
    count,
    exp_ref,
    sums_ref,
    prm_ref,
    up_ref,
    upsums_ref,
    w_ref,
    grp_ref,
    gsums_ref,
    gprm_ref,
    back_ref,
    out_ref,
    stat_ref,
    keep_ref,
):
    blocks, pixels, _ = keep_ref.shape
    step = pl.program_id(0)
    clear_stats(stat_ref)

    @pl.when(step < blocks)
    def _():
        coef = coefficients(sums_ref[0], prm_ref[0], count)
        scale = coef[2] * coef[1]
        up_mean = upsums_ref[0, 0:1] / count
        up_lean = upsums_ref[0, 1:2] / count

        def back(start, size):
            rows = pl.ds(start, size)
            standard, _ = standardize(exp_ref[0, rows], coef)
            values = (scale * (up_ref[0, rows] - up_mean - standard * up_lean)).astype(BF16)
            back_ref[0, rows] = values
            keep_ref[step, rows] = values

        over_rows(pixels, back)

    @pl.when(step >= blocks)
    def _():
        coef = coefficients(gsums_ref[0], gprm_ref[0], count)

        def body(start, size):
            rows = pl.ds(start, size)
            total = dot(keep_ref[0, rows], w_ref[0])
            for source in range(1, blocks):
                total += dot(keep_ref[source, rows], w_ref[source])
            standard, norm = standardize(grp_ref[0, rows], coef)
            up = total * silu_slope(norm)
            out_ref[0, rows] = up
            add_stats(stat_ref, step - blocks, up, up * standard)

        over_rows(pixels, body)


def expand_back(expanded, sums, params, up, upsums, weight, grouped, gsums, gparams, count, comm):
    blocks, pixels, _ = expanded.shape
    mids = grouped.shape[0]

    def first(*dims):
        return pl.BlockSpec((1,) + dims, lambda j: (jnp.minimum(j, blocks - 1),) + (0,) * len(dims))

    def second(*dims):
        return pl.BlockSpec((1,) + dims, lambda j: (jnp.maximum(j - blocks, 0),) + (0,) * len(dims))

    return call(
        functools.partial(expand_back_kernel, count),
        (blocks + mids,),
        [
            first(pixels, BLK),
            first(2, BLK),
            first(2, BLK),
            first(pixels, BLK),
            first(2, BLK),
            pl.BlockSpec((blocks, BLK, BLK), lambda j: (0, 0, jnp.maximum(j - blocks, 0))),
            second(pixels, BLK),
            second(2, BLK),
            second(2, BLK),
        ],
        [first(pixels, BLK), second(pixels, BLK), whole(mids, 2, BLK)],
        [shape((blocks, pixels, BLK), BF16), shape((mids, pixels, BLK)), shape((mids, 2, BLK))],
        [pltpu.VMEM((blocks, pixels, BLK), BF16)],
        2 * pixels * blocks * BLK * mids * BLK,
        comm,
    )(expanded, sums, params, up, upsums, weight, grouped, gsums, gparams)


def weight_grad_kernel(left_ref, right_ref, out_ref):
    weight_grad_block(left_ref[0], right_ref, out_ref, 0)


def weight_grad(left, right):
    blocks, pixels, _ = left.shape
    width = right.shape[1]
    return call(
        weight_grad_kernel,
        (blocks,),
        [block(pixels, BLK), whole(pixels, width)],
        [block(BLK, width)],
        [shape((blocks, BLK, width), BF16)],
        [],
        2 * pixels * blocks * BLK * width,
    )(left, right)[0]


def first_back(count, red_ref, sums_ref, prm_ref, rup_ref, rupsums_ref, back_ref):
    mids, pixels, _ = red_ref.shape
    for mid in range(mids):
        coef = coefficients(sums_ref[mid], prm_ref[mid], count)
        scale = coef[2] * coef[1]
        up_mean = rupsums_ref[mid, 0:1] / count
        up_lean = rupsums_ref[mid, 1:2] / count

        def body(start, size):
            rows = pl.ds(start, size)
            standard, _ = standardize(red_ref[mid, rows], coef)
            values = scale * (rup_ref[mid, rows] - up_mean - standard * up_lean)
            back_ref[rows, mid * BLK : (mid + 1) * BLK] = values.astype(BF16)

        over_rows(pixels, body)


def weight_grad_block(left, right_ref, out_ref, slot):
    for first in range(0, right_ref.shape[1], BLK):
        columns = slice(first, first + BLK)
        out_ref[slot, :, columns] = dot(left, right_ref[:, columns], ((0,), (0,))).astype(BF16)


def reduce_back_kernel(count, red_ref, sums_ref, prm_ref, rup_ref, rupsums_ref, x_ref, up_ref, w_ref, grad_ref, wgrad_ref, back_ref):
    @pl.when(pl.program_id(0) == 0)
    def _():
        first_back(count, red_ref, sums_ref, prm_ref, rup_ref, rupsums_ref, back_ref)

    def product(start, size):
        rows = pl.ds(start, size)
        total = dot(back_ref[rows], w_ref[0], ((1,), (1,)))
        grad_ref[0, rows] = (up_ref[0, rows] + total).astype(BF16)

    over_rows(x_ref.shape[1], product)
    weight_grad_block(x_ref[0], back_ref, wgrad_ref, 0)


def reduce_back(reduced, sums, params, rup, rupsums, x, up, weight, count):
    mids, pixels, _ = reduced.shape
    blocks = x.shape[0]
    return call(
        functools.partial(reduce_back_kernel, count),
        (blocks,),
        [
            whole(mids, pixels, BLK),
            whole(mids, 2, BLK),
            whole(mids, 2, BLK),
            whole(mids, pixels, BLK),
            whole(mids, 2, BLK),
            block(pixels, BLK),
            block(pixels, BLK),
            block(BLK, mids * BLK),
        ],
        [block(pixels, BLK), block(BLK, mids * BLK)],
        [shape((blocks, pixels, BLK), BF16), shape((blocks, BLK, mids * BLK), BF16)],
        [pltpu.VMEM((pixels, mids * BLK), BF16)],
        4 * pixels * blocks * BLK * mids * BLK,
    )(reduced, sums, params, rup, rupsums, x, up, weight)


def exchange_kernel(batches, members, x_ref, out_ref, *scratch):
    row, me, across, along = devices(batches, members)
    greet(across + along)
    out_ref[...] = x_ref[...]
    total_stats(out_ref, across, along, *scratch)


def exchange(values, batches, members, collective_id):
    return pl.pallas_call(
        functools.partial(exchange_kernel, batches, members),
        in_specs=[pl.BlockSpec(memory_space=pltpu.VMEM)],
        out_specs=pl.BlockSpec(memory_space=pltpu.VMEM),
        out_shape=shape(values.shape),
        scratch_shapes=stats_scratch(values.shape, batches, members),
        compiler_params=pltpu.CompilerParams(collective_id=collective_id, has_side_effects=True),
    )(values)


def turn(source_ref, target_ref, slot, chunk):
    first = (49 * chunk) // 4

    @pl.loop(0, 13)
    def _(tile):
        columns = pl.ds(pl.multiple_of((first + tile) * HALF, HALF), HALF)
        rows = pl.ds(pl.multiple_of(tile * HALF, HALF), HALF)
        target_ref[slot, rows] = source_ref[:, columns].T


def turned(target_ref, slot, chunk, pixels):
    return target_ref.at[slot, pl.ds(pl.multiple_of(32 * (chunk % 4), 16), pixels)]


def opening_kernel(batches, members, *refs):
    x_ref, grad_ref, wr_ref, we_ref, wg_ref, prm_ref = refs[:6]
    xp_ref, gradt_ref, wr_out, we_out, wg_out, prm_out = refs[6:12]
    xin, xturn, gin, gturn, load, own, xsend, xrecv, gsend, psend, precv, wsend, wrecv, fsend, frecv = refs[12:]
    row, me, across, along = devices(batches, members)
    pixels = xp_ref.shape[1]
    load_x = pltpu.make_async_copy(x_ref, xin, load.at[0])
    load_grad = pltpu.make_async_copy(grad_ref, gin, load.at[1])
    load_x.start()
    load_grad.start()
    weights = [(wr_ref, wr_out), (wg_ref, wg_out), (we_ref, we_out)]
    local_copies = [pltpu.make_async_copy(prm_ref, prm_out.at[me], own.at[3])]
    parts = []
    for index, (source, target) in enumerate(weights):
        size = source.shape[0] // batches
        part = pl.ds(pl.multiple_of(row * size, 16), size)
        parts.append(part)
        local_copies.append(pltpu.make_async_copy(source.at[part], target.at[me, part], own.at[index]))
    for copy in local_copies:
        copy.start()
    greet(across + along)
    copies = []
    for step, device in enumerate(along):
        copies.append(remote(prm_ref, prm_out.at[me], psend.at[step], precv.at[step], device))
    first = []
    for index, (source, target) in enumerate(weights):
        for step, device in enumerate(along):
            first.append(
                remote(
                    source.at[parts[index]],
                    target.at[me, parts[index]],
                    wsend.at[index, step],
                    wrecv.at[index, step],
                    device,
                )
            )
    for copy in copies + first:
        copy.start()
    load_x.wait()
    for step, device in enumerate(along):
        turn(xin, xturn, step, device[1])
        copy = remote(turned(xturn, step, device[1], pixels), xp_ref.at[me], xsend.at[step], xrecv.at[step], device)
        copy.start()
        copies.append(copy)
    last = members - 1
    turn(xin, xturn, last, me)
    copy = pltpu.make_async_copy(turned(xturn, last, me, pixels), xp_ref.at[me], xsend.at[last])
    copy.start()
    copies.append(copy)
    load_grad.wait()
    for member in range(members):
        turn(gin, gturn, member, member)
        copy = pltpu.make_async_copy(turned(gturn, member, member, pixels), gradt_ref.at[member], gsend.at[member])
        copy.start()
        copies.append(copy)
    for copy in local_copies:
        copy.wait()
    for index, (source, target) in enumerate(weights):
        for copy in first[index * len(along) : (index + 1) * len(along)]:
            copy.wait()
        for step, device in enumerate(across):
            held = target.at[:, parts[index]]
            copy = remote(held, held, fsend.at[index, step], frecv.at[index, step], device)
            copy.start()
            copies.append(copy)
    for copy in copies:
        copy.wait()


def opening(block_input, out_grad, reduce_weight, expand_weight, taps, params, batches, members):
    channels, row_pixels = block_input.shape
    pixels = row_pixels // members
    dma = pltpu.SemaphoreType.DMA
    other, across = members - 1, batches - 1
    padded = 13 * HALF
    return pl.pallas_call(
        functools.partial(opening_kernel, batches, members),
        in_specs=[pl.BlockSpec(memory_space=pl.ANY)] * 6,
        out_specs=[pl.BlockSpec(memory_space=pl.ANY)] * 6,
        out_shape=[
            shape((members, pixels, channels), BF16),
            shape((members, pixels, channels), BF16),
            shape((members,) + reduce_weight.shape, BF16),
            shape((members,) + expand_weight.shape, BF16),
            shape((members,) + taps.shape, BF16),
            shape((members,) + params.shape),
        ],
        scratch_shapes=[
            pltpu.VMEM((channels, row_pixels), BF16),
            pltpu.VMEM((members, padded, channels), BF16),
            pltpu.VMEM((channels, row_pixels), BF16),
            pltpu.VMEM((members, padded, channels), BF16),
            dma((2,)),
            dma((4,)),
            dma((members,)),
            dma((other,)),
            dma((members,)),
            dma((other,)),
            dma((other,)),
            dma((3, other)),
            dma((3, other)),
            dma((3, across)),
            dma((3, across)),
        ],
        compiler_params=pltpu.CompilerParams(vmem_limit_bytes=VMEM_LIMIT, collective_id=0, has_side_effects=True),
    )(block_input, out_grad, reduce_weight, expand_weight, taps, params)


class Reduce:
    def __init__(self, part, out, row, me, across, along, refs):
        self.part, self.out, self.row, self.me, self.across, self.along = part, out, row, me, across, along
        self.first, self.held, self.second, self.total = refs[:4]
        self.s1, self.r1, self.s2, self.r2, self.s3, self.r3 = refs[4:]
        self.size = self.total.shape[0]

    def rows(self, row):
        return pl.ds(pl.multiple_of(row * self.size, 16), self.size)

    def over_batch(self):
        return [
            remote(
                self.part.at[:, self.rows(device[0])], self.first.at[step], self.s1.at[step], self.r1.at[step], device
            )
            for step, device in enumerate(self.across)
        ]

    def add_batch(self):
        @pl.loop(0, self.held.shape[0])
        def _(member):
            total = self.part[member, self.rows(self.row)].astype(F32)
            for step in range(len(self.across)):
                total += self.first[step, member].astype(F32)
            self.held[member] = total.astype(BF16)

    def over_group(self):
        return [
            remote(self.held.at[device[1]], self.second.at[step], self.s2.at[step], self.r2.at[step], device)
            for step, device in enumerate(self.along)
        ]

    def add_group(self):
        total = self.held[self.me].astype(F32)
        for step in range(len(self.along)):
            total += self.second[step].astype(F32)
        self.total[...] = total

    def share(self):
        rows = self.rows(self.row)
        copies = [
            remote(self.total, self.out.at[rows], self.s3.at[step], self.r3.at[step], device)
            for step, device in enumerate(self.across)
        ]
        return copies + [pltpu.make_async_copy(self.total, self.out.at[rows], self.s3.at[len(self.across)])]


def reduce_scratch(dims, batches, members):
    rows, columns = dims[1] // batches, dims[2]
    dma = pltpu.SemaphoreType.DMA
    return [
        pltpu.VMEM((batches - 1, members, rows, columns), BF16),
        pltpu.VMEM((members, rows, columns), BF16),
        pltpu.VMEM((members - 1, rows, columns), BF16),
        pltpu.VMEM((rows, columns), F32),
        dma((batches - 1,)),
        dma((batches - 1,)),
        dma((members - 1,)),
        dma((members - 1,)),
        dma((batches,)),
        dma((batches - 1,)),
    ]


def each(copies, what):
    for copy in copies:
        getattr(copy, what)()


def closing_kernel(count, batches, members, rows, *refs):
    red_ref, sums_ref, prm_ref, rup_ref, rupsums_ref, x_ref, up_ref, w_ref, epart_ref, tpart_ref, src_ref, _ = refs[:12]
    recv_ref, rout_ref, eout_ref, tout_ref, dst_ref = refs[12:17]
    back_ref, grad_ref, wpart_ref, gsend, grecv, psend, precv = refs[17:24]
    row, me, across, along = devices(batches, members)
    step = pl.program_id(0)
    last = members - 1
    expand_sum = Reduce(epart_ref, eout_ref, row, me, across, along, refs[24:34])
    taps_sum = Reduce(tpart_ref, tout_ref, row, me, across, along, refs[34:44])
    reduce_sum = Reduce(wpart_ref, rout_ref, row, me, across, along, refs[44:54])
    other = lax.rem(me + 1 + step, members)

    def pieces():
        return piece_copies(src_ref, dst_ref, rows, me, along, psend, precv)

    @pl.when(step == 0)
    def _():
        greet(across + along)
        each(pieces(), "start")
        each(expand_sum.over_batch(), "start")
        each(taps_sum.over_batch(), "start")
        first_back(count, red_ref, sums_ref, prm_ref, rup_ref, rupsums_ref, back_ref)

    def product(start, size):
        part = pl.ds(start, size)
        total = dot(back_ref[part], w_ref[0], ((1,), (1,)))
        grad_ref[step, part] = (up_ref[0, part] + total).astype(BF16)

    over_rows(x_ref.shape[1], product)

    @pl.when(step < last)
    def _():
        remote(grad_ref.at[step], recv_ref.at[me], gsend.at[step], grecv.at[step], (row, other)).start()

    weight_grad_block(x_ref[0], back_ref, wpart_ref, other)

    @pl.when(step == last)
    def _():
        own = pltpu.make_async_copy(grad_ref.at[last], recv_ref.at[me], gsend.at[last])
        own.start()
        each(reduce_sum.over_batch(), "start")
        for part in (expand_sum, taps_sum, reduce_sum):
            each(part.over_batch(), "wait")
            part.add_batch()
            each(part.over_group(), "start")
        own.wait()
        each(pieces(), "wait")
        for past, device in enumerate(along):
            remote(grad_ref.at[past], recv_ref.at[me], gsend.at[past], grecv.at[past], device).wait()
        for part in (expand_sum, taps_sum, reduce_sum):
            each(part.over_group(), "wait")
            part.add_group()
            each(part.share(), "start")
        for part in (expand_sum, taps_sum, reduce_sum):
            each(part.share(), "wait")


def closing(reduced, sums, params, rup, rupsums, x, up, weight, epart, tpart, source, into, rows, count, batches, members):
    mids, pixels, _ = reduced.shape
    blocks = x.shape[0]
    once = pl.Buffered(1)

    def keep(*dims):
        return pl.BlockSpec(dims, lambda j: (0,) * len(dims), pipeline_mode=once)

    def turn_block(*dims):
        def index(j):
            return (lax.rem(lax.axis_index("group") + 1 + j, members),) + (0,) * len(dims)

        return pl.BlockSpec((1,) + dims, index)

    anywhere = pl.BlockSpec(memory_space=pl.ANY)
    dma = pltpu.SemaphoreType.DMA
    wdims = (blocks, BLK, mids * BLK)
    scratch = [
        pltpu.VMEM((pixels, mids * BLK), BF16),
        pltpu.VMEM((blocks, pixels, BLK), BF16),
        pltpu.VMEM(wdims, BF16),
        dma((members,)),
        dma((members - 1,)),
        dma((members,)),
        dma((members - 1,)),
    ]
    for dims in (wdims, tpart.shape, wdims):
        scratch += reduce_scratch(dims, batches, members)
    return pl.pallas_call(
        functools.partial(closing_kernel, count, batches, members, rows),
        grid=(blocks,),
        in_specs=[
            keep(mids, pixels, BLK),
            keep(mids, 2, BLK),
            keep(mids, 2, BLK),
            keep(mids, pixels, BLK),
            keep(mids, 2, BLK),
            turn_block(pixels, BLK),
            turn_block(pixels, BLK),
            turn_block(BLK, mids * BLK),
            keep(*wdims),
            keep(*tpart.shape),
            anywhere,
            anywhere,
        ],
        out_specs=[anywhere] * 5,
        out_shape=[
            shape((members, pixels, BLK), BF16),
            shape(wdims[1:]),
            shape(wdims[1:]),
            shape(tpart.shape[1:]),
            shape(source.shape, BF16),
        ],
        scratch_shapes=scratch,
        input_output_aliases={11: 4},
        compiler_params=pltpu.CompilerParams(vmem_limit_bytes=VMEM_LIMIT, collective_id=7, has_side_effects=True),
    )(reduced, sums, params, rup, rupsums, x, up, weight, epart, tpart, source, into)


def turn_out_kernel(in_ref, out_ref):
    for first in range(0, in_ref.shape[0], HALF):
        out_ref[:, first : first + HALF] = in_ref[first : first + HALF].astype(out_ref.dtype).T


def turn_out(values, dtype):
    rows, channels = values.shape
    size = next(part for part in (1792, 896, HALF) if rows % part == 0)
    return call(
        turn_out_kernel,
        (rows // size,),
        [pl.BlockSpec((size, channels), lambda j: (j, 0))],
        [pl.BlockSpec((channels, size), lambda j: (0, j))],
        [shape((channels, rows), dtype)],
        [],
        rows * channels,
    )(values)[0]


def pixel_masks(pixels):
    place = jnp.arange(pixels, dtype=jnp.int32)
    tall, wide = (place // SIDE) % SIDE, place % SIDE
    masks = jnp.stack([wide != 0, wide != SIDE - 1, tall != 0, tall != SIDE - 1])
    return jnp.broadcast_to(masks[:, :, None].astype(F32), (4, pixels, HALF))


def own_part(stats, which, length):
    return lax.dynamic_slice_in_dim(stats[:, which].reshape(-1), lax.axis_index("group") * length, length, 0)


TAP_ROWS = 320


def fused(
    block_input,
    reduce_weight,
    reduce_gain,
    reduce_bias,
    group_weight,
    group_gain,
    group_bias,
    expand_weight,
    expand_gain,
    expand_bias,
    out_grad,
):
    batches, members = lax.axis_size("batch"), lax.axis_size("group")
    channels, row_pixels = block_input.shape
    pixels = row_pixels // members
    count = row_pixels * batches
    local_mid = reduce_gain.shape[0]
    pack = jnp.concatenate([reduce_gain, reduce_bias, group_gain, group_bias, expand_gain, expand_bias]).reshape(-1, HALF)
    taps = group_weight.reshape(-1, 9, GW, GW).transpose(1, 2, 0, 3).reshape(9 * GW, HALF)
    taps = jnp.pad(taps, ((0, TAP_ROWS - 9 * GW), (0, 0)))
    masks = pixel_masks(pixels)
    x, grad_turned, reduce_full, expand_full, taps_full, packs = opening(
        block_input, out_grad, reduce_weight, expand_weight, taps, pack, batches, members
    )
    vectors = packs[:, :4].reshape(-1, 2, 4, HALF).transpose(0, 2, 1, 3).reshape(-1, 4, BLK)
    reduce_params, group_params = vectors[:, :2], vectors[:, 2:]
    expand_params = packs[:, 4:].reshape(-1, 2, BLK)

    def comm(collective_id, source=None, rows=None, into=None):
        return Comm(batches, members, collective_id, source, rows, into)

    first, second = 448, 1008
    reduced, reduce_sums, grad = reduce_product(x, reduce_full, comm(1, grad_turned, (0, first)))
    grouped, group_sums, grad = conv(
        reduced, reduce_sums, reduce_params, taps_full, masks, count, comm(2, grad_turned, (first, second - first), grad)
    )
    expanded, act, expand_sums, grad = expand_product(
        grouped, group_sums, group_params, expand_full, count, comm(3, grad_turned, (second, pixels - second), grad)
    )
    out, upstream, expand_stats = output(expanded, expand_sums, expand_params, x, grad, count, comm(4))
    first, second = 448, 1120
    back, group_up, group_stats, moved = expand_back(
        expanded,
        expand_sums,
        expand_params,
        upstream,
        expand_stats,
        expand_full,
        grouped,
        group_sums,
        group_params,
        count,
        comm(5, out, (0, first)),
    )
    reduce_up, taps_part, reduce_stats, moved = conv_back(
        reduced,
        reduce_sums,
        reduce_params,
        grouped,
        group_sums,
        group_params,
        group_up,
        group_stats,
        taps_full,
        masks,
        count,
        comm(6, out, (first, second - first), moved),
    )
    expand_part = weight_grad(back, act)
    inner, reduce_weight_grad, expand_weight_grad, taps_grad, moved = closing(
        reduced,
        reduce_sums,
        reduce_params,
        reduce_up,
        reduce_stats,
        x,
        upstream,
        reduce_full,
        expand_part,
        taps_part,
        out,
        moved,
        (second, pixels - second),
        count,
        batches,
        members,
    )
    block_output = turn_out(moved.reshape(row_pixels, channels), BF16)
    input_grad = turn_out(inner.reshape(row_pixels, channels), F32)
    taps_grad = taps_grad[: 9 * GW].reshape(9, GW, -1, GW).transpose(2, 0, 3, 1)
    return (
        block_output,
        input_grad,
        reduce_weight_grad,
        taps_grad.reshape(group_weight.shape),
        expand_weight_grad,
        own_part(reduce_stats, 1, local_mid),
        own_part(reduce_stats, 0, local_mid),
        own_part(group_stats, 1, local_mid),
        own_part(group_stats, 0, local_mid),
        own_part(expand_stats, 1, channels),
        own_part(expand_stats, 0, channels),
    )


def modular(
    block_input,
    reduce_weight,
    reduce_gain,
    reduce_bias,
    group_weight,
    group_gain,
    group_bias,
    expand_weight,
    expand_gain,
    expand_bias,
    out_grad,
):
    batches, members = lax.axis_size("batch"), lax.axis_size("group")
    channels, row_pixels = block_input.shape
    pixels = row_pixels // members
    count = row_pixels * batches
    mid_total = reduce_weight.shape[1]
    mids = mid_total // BLK
    blocks = channels * members // BLK
    me = lax.axis_index("group")

    def to_pixels(values):
        moved = lax.all_to_all(values.T.reshape(members, pixels, channels), "group", 0, 0)
        if channels == BLK:
            return moved
        share = BLK // channels
        moved = moved.reshape(blocks, share, pixels, channels).transpose(0, 2, 1, 3)
        return moved.reshape(blocks, pixels, BLK)

    def to_channels(values):
        if channels != BLK:
            share = BLK // channels
            values = values.reshape(blocks, pixels, share, channels).transpose(0, 2, 1, 3)
            values = values.reshape(members, pixels, channels)
        moved = lax.all_to_all(values, "group", 0, 0)
        return moved.reshape(row_pixels, channels).T

    def gather(values):
        return lax.all_gather(values, "group", axis=0, tiled=True)

    local_mid = reduce_gain.shape[0]
    pack = jnp.concatenate([reduce_gain, reduce_bias, group_gain, group_bias, expand_gain, expand_bias])
    packs = gather(pack[None])
    vectors, offset = [], 0
    for length in (local_mid, local_mid, local_mid, local_mid, channels, channels):
        vectors.append(packs[:, offset : offset + length].reshape(-1, BLK))
        offset += length
    reduce_params = jnp.stack(vectors[0:2], 1)
    group_params = jnp.stack(vectors[2:4], 1)
    expand_params = jnp.stack(vectors[4:6], 1)
    reduce_full = gather(reduce_weight).reshape(blocks, BLK, mid_total)
    expand_full = gather(expand_weight).reshape(blocks, BLK, mid_total)
    taps = gather(group_weight.reshape(group_weight.shape[0], 9, GW, GW))
    taps = taps.reshape(-1, HALF // GW, 9, GW, GW).transpose(0, 2, 3, 1, 4).reshape(-1, 9 * GW, HALF)
    taps = jnp.pad(taps, ((0, 0), (0, TAP_ROWS - 9 * GW), (0, 0)))
    masks = pixel_masks(pixels)

    x = to_pixels(block_input)
    grad = to_pixels(out_grad)

    reduced, reduce_sums = reduce_product(x, reduce_full, None)
    reduce_sums = exchange(reduce_sums, batches, members, 1)
    grouped, group_sums = conv(reduced, reduce_sums, reduce_params, taps, masks, count, None)
    group_sums = exchange(group_sums, batches, members, 1)
    expanded, act, expand_sums = expand_product(grouped, group_sums, group_params, expand_full, count, None)
    expand_sums = exchange(expand_sums, batches, members, 2)
    out, upstream, expand_stats = output(expanded, expand_sums, expand_params, x, grad, count, None)
    expand_stats = exchange(expand_stats, batches, members, 2)
    back, group_up, group_stats = expand_back(
        expanded, expand_sums, expand_params, upstream, expand_stats, expand_full, grouped, group_sums, group_params, count, None
    )
    expand_part = weight_grad(back, act)
    group_stats = exchange(group_stats, batches, members, 1)
    reduce_up, taps_part, reduce_stats = conv_back(
        reduced,
        reduce_sums,
        reduce_params,
        grouped,
        group_sums,
        group_params,
        group_up,
        group_stats,
        taps,
        masks,
        count,
        None,
    )
    reduce_stats = exchange(reduce_stats, batches, members, 1)
    inner, reduce_part = reduce_back(
        reduced, reduce_sums, reduce_params, reduce_up, reduce_stats, x, upstream, reduce_full, count
    )
    block_output = to_channels(out)
    input_grad = to_channels(inner).astype(F32)

    def shared_sum(part):
        rows = channels // batches
        part = part.reshape(members, batches, rows, mid_total).transpose(1, 0, 2, 3)
        part = lax.all_to_all(part, "batch", 0, 0).astype(F32).sum(0).astype(BF16)
        part = lax.all_to_all(part, "group", 0, 0).astype(F32).sum(0)
        return lax.all_gather(part, "batch", axis=0, tiled=True)

    expand_weight_grad = shared_sum(expand_part)
    reduce_weight_grad = shared_sum(reduce_part)
    taps_part = taps_part[:, : 9 * GW].reshape(-1, 9, GW, HALF // GW, GW).transpose(0, 3, 1, 4, 2)
    taps_part = taps_part.reshape(members, -1, 9, GW, GW)
    group_weight_grad = lax.all_to_all(taps_part, "group", 0, 0).astype(F32).sum(0)
    group_weight_grad = lax.psum(group_weight_grad, "batch").reshape(group_weight.shape)

    return (
        block_output,
        input_grad,
        reduce_weight_grad,
        group_weight_grad,
        expand_weight_grad,
        own_part(reduce_stats, 1, local_mid),
        own_part(reduce_stats, 0, local_mid),
        own_part(group_stats, 1, local_mid),
        own_part(group_stats, 0, local_mid),
        own_part(expand_stats, 1, channels),
        own_part(expand_stats, 0, channels),
    )


def local(*args):
    block_input = args[0]
    pixels = block_input.shape[1] // lax.axis_size("group")
    if block_input.shape[0] == BLK and pixels == 1568 and args[2].shape[0] == HALF and lax.axis_size("batch") == 4:
        return fused(*args)
    return modular(*args)


def solution(mesh):
    in_specs = (
        P("group", "batch"),
        P("group", None),
        P("group"),
        P("group"),
        P("group", None, None, None, None),
        P("group"),
        P("group"),
        P("group", None),
        P("group"),
        P("group"),
        P("group", "batch"),
    )
    out_specs = (
        P("group", "batch"),
        P("group", "batch"),
        P("group", None),
        P("group", None, None, None, None),
        P("group", None),
        P("group"),
        P("group"),
        P("group"),
        P("group"),
        P("group"),
        P("group"),
    )
    return jax.shard_map(local, mesh=mesh, in_specs=in_specs, out_specs=out_specs, check_vma=False)
```

```python
import functools

import jax
import jax.numpy as jnp
import numpy as np
from jax import lax
from jax.experimental import pallas as pl
from jax.experimental.pallas import tpu as pltpu
from jax.sharding import PartitionSpec as P

GW = 32
SIDE = 14
EPS = 1e-05
BLK = 256
HALF = 128
PAD = 16
F32 = jnp.float32
BF16 = jnp.bfloat16
MESH = pl.DeviceIdType.MESH
VMEM_LIMIT = 60 * 1024 * 1024


def silu_slope(values):
    sigma = jax.nn.sigmoid(values)
    return sigma * (1.0 + values * (1.0 - sigma))


def row_chunk(pixels):
    for size in (224, 208, 192, 176, 160, 144, 128, 112):
        if pixels % size == 0:
            return size
    return pixels


def over_rows(pixels, body):
    size = row_chunk(pixels)
    if size == pixels:
        body(0, size)
    else:

        @pl.loop(0, pixels // size)
        def _(step):
            body(pl.multiple_of(step * size, 16), size)


def coefficients(sums, params, count):
    center = sums[0:1] / count
    spread = sums[1:2] / count - center * center
    inverse = lax.rsqrt(spread + EPS)
    return center, inverse, params[0:1], params[1:2]


def standardize(values, coef):
    standard = (values - coef[0]) * coef[1]
    return standard, standard * coef[2] + coef[3]


def add_stats(ref, slot, first, second):
    ref[slot, 0:1] += jnp.sum(first, 0, keepdims=True)
    ref[slot, 1:2] += jnp.sum(second, 0, keepdims=True)


def clear_stats(ref):
    @pl.when(pl.program_id(0) == 0)
    def _():
        ref[...] = jnp.zeros_like(ref)


def dot(a, b, dims=((1,), (0,))):
    return lax.dot_general(a, b, (dims, ((), ())), preferred_element_type=F32)


def devices(batches, members):
    row, me = lax.axis_index("batch"), lax.axis_index("group")
    across = [(lax.rem(row + step, batches), me) for step in range(1, batches)]
    along = [(row, lax.rem(me + step, members)) for step in range(1, members)]
    return row, me, across, along


def greet(others):
    barrier = pltpu.get_barrier_semaphore()
    for device in others:
        pl.semaphore_signal(barrier, inc=1, device_id=device, device_id_type=MESH)
    pl.semaphore_wait(barrier, len(others))


def remote(source, target, send, recv, device):
    return pltpu.make_async_remote_copy(
        src_ref=source, dst_ref=target, send_sem=send, recv_sem=recv, device_id=device, device_id_type=MESH
    )


def each(copies, what):
    for copy in copies:
        getattr(copy, what)()


def spread(source, target, send, recv, others, beside):
    copies = [
        remote(source, target.at[step], send.at[step], recv.at[step], device) for step, device in enumerate(others)
    ]
    each(copies, "start")
    each(beside, "start")
    each(copies, "wait")


def total_stats(ref, across, along, first_ref, second_ref, mid_ref, send1, recv1, send2, recv2, beside=((), ())):
    mid_ref[0] = ref[...]
    spread(mid_ref.at[0], first_ref, send1, recv1, across, beside[0])
    total = mid_ref[0]
    for step in range(len(across)):
        total += first_ref[step]
    mid_ref[1] = total
    spread(mid_ref.at[1], second_ref, send2, recv2, along, beside[1])
    for step in range(len(along)):
        total += second_ref[step]
    ref[...] = total


def stats_scratch(dims, batches, members):
    return [
        pltpu.VMEM((batches - 1,) + dims, F32),
        pltpu.VMEM((members - 1,) + dims, F32),
        pltpu.VMEM((2,) + dims, F32),
        pltpu.SemaphoreType.DMA((batches - 1,)),
        pltpu.SemaphoreType.DMA((batches - 1,)),
        pltpu.SemaphoreType.DMA((members - 1,)),
        pltpu.SemaphoreType.DMA((members - 1,)),
    ]


class Comm:
    def __init__(self, batches, members, collective_id, source=None, low=0, sizes=(), into=None, stream=False):
        self.batches, self.members, self.collective_id = batches, members, collective_id
        self.source, self.low, self.sizes, self.into, self.stream = source, low, sizes, into, stream
        self.high = low + sum(sizes)


def piece_copies(source, target, low, size, me, along, send, recv, staged=False):
    rows = pl.ds(low, size)
    last = len(along)
    copies = [
        remote(
            source.at[step if staged else device[1], rows], target.at[me, rows], send.at[step], recv.at[step], device
        )
        for step, device in enumerate(along)
    ]
    return copies + [
        pltpu.make_async_copy(source.at[last if staged else me, rows], target.at[me, rows], send.at[last])
    ]


def call(kernel, grid, in_specs, out_specs, out_shape, scratch, flops, comm=None):
    if comm is None:
        return functools.partial(
            plain_call, kernel, grid, in_specs, out_specs, out_shape, scratch, flops, pltpu.CompilerParams(vmem_limit_bytes=VMEM_LIMIT)
        )
    n_in, n_out, n_scratch = len(in_specs), len(out_specs), len(scratch)
    stats = out_shape[-1].shape
    batches, members = comm.batches, comm.members

    sends = bool(comm.sizes)

    def wrapped(*refs):
        refs = list(refs)
        ins = refs[:n_in]
        del refs[:n_in]
        source = refs.pop(0) if sends and not comm.stream else None
        if comm.into is not None:
            refs.pop(0)
        outs = refs[:n_out]
        del refs[:n_out]
        target = refs.pop(0) if sends else None
        own = refs[:n_scratch]
        del refs[:n_scratch]
        stats_refs = refs[:7]
        del refs[:7]
        if comm.stream:
            source = refs.pop(0)
        row, me, across, along = devices(batches, members)
        step = pl.program_id(0)

        def copies(part):
            low = comm.low + sum(comm.sizes[:part])
            return piece_copies(
                source, target, low, comm.sizes[part], me, along, refs[0].at[part], refs[1].at[part], comm.stream
            )

        @pl.when(step == 0)
        def _():
            greet(across + along)
            if sends and not comm.stream:
                each(copies(0), "start")

        kernel(*ins, *outs, *own)
        if comm.stream:
            source[step] = outs[0][0, : comm.high]
            rows = pl.ds(0, comm.sizes[0])

            @pl.when(step < members - 1)
            def _():
                device = (row, lax.rem(me + 1 + step, members))
                remote(
                    source.at[step, rows], target.at[me, rows], refs[0].at[0, step], refs[1].at[0, step], device
                ).start()

            @pl.when(step == members - 1)
            def _():
                pltpu.make_async_copy(source.at[step, rows], target.at[me, rows], refs[0].at[0, step]).start()

        @pl.when(step == pl.num_programs(0) - 1)
        def _():
            total_stats(outs[-1], across, along, *stats_refs, beside=(copies(1), copies(2)) if sends else ((), ()))
            if sends:
                for part in range(3):
                    each(copies(part), "wait")

    scratch = list(scratch) + stats_scratch(stats, batches, members)
    in_specs, out_specs, out_shape = list(in_specs), list(out_specs), list(out_shape)
    extra, aliases = [], {}
    if sends:
        if comm.stream:
            dims, dtype = out_shape[0].shape, out_shape[0].dtype
            scratch.append(pltpu.VMEM((members, comm.high, dims[2]), dtype))
        else:
            dims, dtype = comm.source.shape, comm.source.dtype
            extra = [comm.source]
        if comm.into is not None:
            aliases = {len(in_specs) + len(extra): len(out_specs)}
            extra.append(comm.into)
        in_specs += [pl.BlockSpec(memory_space=pl.ANY)] * len(extra)
        out_specs.append(pl.BlockSpec(memory_space=pl.ANY))
        out_shape.append(shape(dims, dtype))
        scratch += [pltpu.SemaphoreType.DMA((3, members)), pltpu.SemaphoreType.DMA((3, members - 1))]
    params = pltpu.CompilerParams(
        vmem_limit_bytes=VMEM_LIMIT, collective_id=comm.collective_id, has_side_effects=True
    )
    inner = functools.partial(
        plain_call, wrapped, grid, in_specs, out_specs, out_shape, scratch, flops, params, aliases=aliases
    )
    return lambda *args: inner(*args, *extra)


def plain_call(kernel, grid, in_specs, out_specs, out_shape, scratch, flops, params, *args, aliases={}):
    return pl.pallas_call(
        kernel,
        grid=grid,
        in_specs=in_specs,
        out_specs=out_specs,
        out_shape=out_shape,
        scratch_shapes=scratch,
        input_output_aliases=aliases,
        compiler_params=params,
        cost_estimate=pl.CostEstimate(flops=flops, bytes_accessed=20_000_000, transcendentals=0),
    )(*args)


def shape(dims, dtype=F32):
    return jax.ShapeDtypeStruct(dims, dtype)


def block(*dims):
    return pl.BlockSpec((1,) + dims, lambda j: (j,) + (0,) * len(dims))


def turned_block(members, *dims):
    def index(j):
        return (lax.rem(lax.axis_index("group") + 1 + j, members),) + (0,) * len(dims)

    return pl.BlockSpec((1,) + dims, index)


def whole(*dims):
    return pl.BlockSpec(dims, lambda j: (0,) * len(dims))


def reduce_kernel(x_ref, w_ref, out_ref, sum_ref):
    clear_stats(sum_ref)
    slot = pl.program_id(0)

    def body(start, size):
        rows = pl.ds(start, size)
        total = dot(x_ref[0, rows], w_ref[0])
        for source in range(1, x_ref.shape[0]):
            total += dot(x_ref[source, rows], w_ref[source])
        out_ref[0, rows] = total
        add_stats(sum_ref, slot, total, total * total)

    over_rows(x_ref.shape[1], body)


def reduce_product(x, weight, comm):
    blocks, pixels, _ = x.shape
    mids = weight.shape[2] // BLK
    return call(
        reduce_kernel,
        (mids,),
        [whole(blocks, pixels, BLK), pl.BlockSpec((blocks, BLK, BLK), lambda j: (0, 0, j))],
        [block(pixels, BLK), whole(mids, 2, BLK)],
        [shape((mids, pixels, BLK)), shape((mids, 2, BLK))],
        [],
        2 * pixels * blocks * BLK * mids * BLK,
        comm,
    )(x, weight)


def same_group():
    return lax.broadcasted_iota(jnp.int32, (BLK, BLK), 0) // GW == lax.broadcasted_iota(jnp.int32, (BLK, BLK), 1) // GW


def spread_weight(compact_ref, dense_ref):
    own = same_group()
    for tap in range(9):
        rows = pl.ds(tap * GW, GW)
        compact = jnp.concatenate([compact_ref[0, rows], compact_ref[1, rows]], 1).astype(F32)
        tiled = jnp.concatenate([compact] * (BLK // GW), 0)
        dense_ref[tap] = jnp.where(own, tiled, 0.0).astype(BF16)


def twice(mask):
    return jnp.concatenate([mask, mask], 1)


def fill(stack_ref, mask_ref, rows_start, size, values):
    rows = pl.ds(rows_start, size)
    target = pl.ds(rows_start + PAD, size)
    for half in range(2):
        part = values[:, half * HALF : (half + 1) * HALF]
        stack_ref[1, half, target] = part
        stack_ref[0, half, target] = part * mask_ref[1, rows]
        stack_ref[2, half, target] = part * mask_ref[0, rows]


def clear_edges(stack_ref, pixels):
    edge = jnp.zeros(stack_ref.shape[:2] + (PAD, HALF), F32)
    stack_ref[:, :, 0:PAD] = edge
    stack_ref[:, :, PAD + pixels : PAD + pixels + PAD] = edge


def window(stack_ref, start, size, row_off, col_off):
    rows = pl.ds(start + (PAD + row_off * SIDE + col_off), size)
    return jnp.concatenate([stack_ref[col_off + 1, half, rows] for half in range(2)], 1).astype(BF16)


def conv_rows(stack_ref, mask_ref, dense_ref, start, size, flipped=False):
    rows = pl.ds(start, size)
    total = None
    for row_off in (-1, 0, 1):
        part = None
        for col_off in (-1, 0, 1):
            values = window(stack_ref, start, size, row_off, col_off)
            tap = (row_off + 1) * 3 + col_off + 1
            term = dot(values, dense_ref[8 - tap], ((1,), (1,))) if flipped else dot(values, dense_ref[tap])
            part = term if part is None else part + term
        if row_off:
            part = part * twice(mask_ref[2 if row_off < 0 else 3, rows])
        total = part if total is None else total + part
    return total


def conv_kernel(count, red_ref, sums_ref, prm_ref, weight_ref, mask_ref, out_ref, stat_ref, stack_ref, dense_ref):
    pixels = red_ref.shape[1]
    spread_weight(weight_ref, dense_ref)
    clear_edges(stack_ref, pixels)
    coef = coefficients(sums_ref[0], prm_ref[0], count)

    def enter(start, size):
        _, norm = standardize(red_ref[0, pl.ds(start, size)], coef)
        fill(stack_ref, mask_ref, start, size, (norm * jax.nn.sigmoid(norm)).astype(BF16).astype(F32))

    over_rows(pixels, enter)
    clear_stats(stat_ref)
    slot = pl.program_id(0)

    def body(start, size):
        total = conv_rows(stack_ref, mask_ref, dense_ref, start, size)
        out_ref[0, pl.ds(start, size)] = total
        add_stats(stat_ref, slot, total, total * total)

    over_rows(pixels, body)


def conv(reduced, sums, params, weight, masks, count, comm):
    mids, pixels, _ = reduced.shape
    return call(
        functools.partial(conv_kernel, count),
        (mids,),
        [
            block(pixels, BLK),
            block(2, BLK),
            block(2, BLK),
            pl.BlockSpec((2,) + weight.shape[1:], lambda j: (j, 0, 0)),
            whole(4, pixels, HALF),
        ],
        [block(pixels, BLK), whole(mids, 2, BLK)],
        [shape((mids, pixels, BLK)), shape((mids, 2, BLK))],
        [pltpu.VMEM((3, 2, pixels + 2 * PAD, HALF), F32), pltpu.VMEM((9, BLK, BLK), BF16)],
        2 * 9 * pixels * mids * BLK * BLK,
        comm,
    )(reduced, sums, params, weight, masks)


def conv_back_kernel(
    count,
    red_ref,
    sums_ref,
    prm_ref,
    grp_ref,
    gsums_ref,
    gprm_ref,
    up_ref,
    upsums_ref,
    weight_ref,
    mask_ref,
    *refs,
):
    *beside, out_ref, wgrad_ref, stat_ref, stack_ref, dense_ref, back_ref = refs
    if beside:
        left_ref, act_ref, epart_ref = beside
        for slot in range(left_ref.shape[0]):
            weight_grad_block(left_ref[slot], act_ref, epart_ref, slot)
    pixels = red_ref.shape[1]
    spread_weight(weight_ref, dense_ref)
    clear_edges(stack_ref, pixels)
    coef = coefficients(sums_ref[0], prm_ref[0], count)
    gcoef = coefficients(gsums_ref[0], gprm_ref[0], count)
    scale = gcoef[2] * gcoef[1]
    up_mean = upsums_ref[0, 0:1] / count
    up_lean = upsums_ref[0, 1:2] / count

    def back(start, size):
        rows = pl.ds(start, size)
        standard, _ = standardize(grp_ref[0, rows], gcoef)
        values = (scale * (up_ref[0, rows] - up_mean - standard * up_lean)).astype(BF16)
        back_ref[1, rows] = values
        values = values.astype(F32)
        back_ref[0, rows] = (values * twice(mask_ref[2, rows])).astype(BF16)
        back_ref[2, rows] = (values * twice(mask_ref[3, rows])).astype(BF16)
        fill(stack_ref, mask_ref, start, size, values)

    over_rows(pixels, back)
    clear_stats(stat_ref)
    slot = pl.program_id(0)

    def body(start, size):
        rows = pl.ds(start, size)
        standard, norm = standardize(red_ref[0, rows], coef)
        up = conv_rows(stack_ref, mask_ref, dense_ref, start, size, True) * silu_slope(norm)
        out_ref[0, rows] = up
        add_stats(stat_ref, slot, up, up * standard)

    over_rows(pixels, body)

    def enter(start, size):
        _, norm = standardize(red_ref[0, pl.ds(start, size)], coef)
        fill(stack_ref, mask_ref, start, size, (norm * jax.nn.sigmoid(norm)).astype(BF16).astype(F32))

    over_rows(pixels, enter)
    own = same_group()
    for tap in range(9):
        full = dot(back_ref[tap // 3], window(stack_ref, 0, pixels, tap // 3 - 1, tap % 3 - 1), ((0,), (0,)))
        full = jnp.where(own, full, 0.0)
        kept = full[0:GW]
        for group in range(1, BLK // GW):
            kept += full[group * GW : (group + 1) * GW]
        for half in range(2):
            wgrad_ref[half, tap * GW : (tap + 1) * GW] = kept[:, half * HALF : (half + 1) * HALF].astype(BF16)
    for half in range(2):
        wgrad_ref[half, 9 * GW :] = jnp.zeros((wgrad_ref.shape[1] - 9 * GW, HALF), BF16)


def conv_back(reduced, sums, params, grouped, gsums, gparams, up, upsums, weight, masks, count, comm, product=()):
    mids, pixels, _ = reduced.shape
    more_in, more_out, more_shape = [], [], []
    if product:
        left, right = product
        share = left.shape[0] // mids
        dims = (share, BLK, right.shape[1])
        more_in = [
            pl.BlockSpec((share, pixels, BLK), lambda j: (j, 0, 0)),
            pl.BlockSpec(right.shape, lambda j: (0, 0), pipeline_mode=pl.Buffered(1)),
        ]
        more_out = [pl.BlockSpec(dims, lambda j: (j, 0, 0))]
        more_shape = [shape((mids * share,) + dims[1:], BF16)]
    return call(
        functools.partial(conv_back_kernel, count),
        (mids,),
        [
            block(pixels, BLK),
            block(2, BLK),
            block(2, BLK),
            block(pixels, BLK),
            block(2, BLK),
            block(2, BLK),
            block(pixels, BLK),
            block(2, BLK),
            pl.BlockSpec((2,) + weight.shape[1:], lambda j: (j, 0, 0)),
            whole(4, pixels, HALF),
        ]
        + more_in,
        more_out
        + [block(pixels, BLK), pl.BlockSpec((2,) + weight.shape[1:], lambda j: (j, 0, 0)), whole(mids, 2, BLK)],
        more_shape + [shape((mids, pixels, BLK)), shape(weight.shape, BF16), shape((mids, 2, BLK))],
        [
            pltpu.VMEM((3, 2, pixels + 2 * PAD, HALF), F32),
            pltpu.VMEM((9, BLK, BLK), BF16),
            pltpu.VMEM((3, pixels, BLK), BF16),
        ],
        4 * 9 * pixels * mids * BLK * BLK,
        comm,
    )(reduced, sums, params, grouped, gsums, gparams, up, upsums, weight, masks, *product)


def expand_kernel(count, grp_ref, gsums_ref, gprm_ref, w_ref, out_ref, act_ref, sum_ref):
    mids, pixels, _ = grp_ref.shape

    @pl.when(pl.program_id(0) == 0)
    def _():
        for mid in range(mids):
            coef = coefficients(gsums_ref[mid], gprm_ref[mid], count)

            def body(start, size):
                rows = pl.ds(start, size)
                _, norm = standardize(grp_ref[mid, rows], coef)
                act_ref[rows, mid * BLK : (mid + 1) * BLK] = (norm * jax.nn.sigmoid(norm)).astype(BF16)

            over_rows(pixels, body)

    clear_stats(sum_ref)
    slot = pl.program_id(0)

    def product(start, size):
        rows = pl.ds(start, size)
        total = dot(act_ref[rows], w_ref[0], ((1,), (1,)))
        out_ref[0, rows] = total
        add_stats(sum_ref, slot, total, total * total)

    over_rows(pixels, product)


def expand_product(grouped, gsums, gparams, weight, count, comm):
    mids, pixels, _ = grouped.shape
    blocks = weight.shape[0]
    return call(
        functools.partial(expand_kernel, count),
        (blocks,),
        [
            whole(mids, pixels, BLK),
            whole(mids, 2, BLK),
            whole(mids, 2, BLK),
            block(BLK, mids * BLK),
        ],
        [block(pixels, BLK), whole(pixels, mids * BLK), whole(blocks, 2, BLK)],
        [shape((blocks, pixels, BLK)), shape((pixels, mids * BLK), BF16), shape((blocks, 2, BLK))],
        [],
        2 * pixels * blocks * BLK * mids * BLK,
        comm,
    )(grouped, gsums, gparams, weight)


def output_kernel(count, members, exp_ref, sums_ref, prm_ref, x_ref, grad_ref, out_ref, up_ref, stat_ref):
    coef = coefficients(sums_ref[0], prm_ref[0], count)
    clear_stats(stat_ref)
    slot = pl.program_id(0)
    if members:
        slot = lax.rem(lax.axis_index("group") + 1 + slot, members)

    def body(start, size):
        rows = pl.ds(start, size)
        standard, norm = standardize(exp_ref[0, rows], coef)
        summed = norm + x_ref[0, rows].astype(F32)
        sigma = jax.nn.sigmoid(summed)
        out_ref[0, rows] = (summed * sigma).astype(BF16)
        up = grad_ref[0, rows].astype(F32) * (sigma * (1.0 + summed * (1.0 - sigma)))
        up_ref[0, rows] = up
        add_stats(stat_ref, slot, up, up * standard)

    over_rows(exp_ref.shape[1], body)


def output(expanded, sums, params, x, grad, count, comm):
    blocks, pixels, _ = expanded.shape
    members = comm.members if comm else None
    one = functools.partial(turned_block, members) if comm else block
    return call(
        functools.partial(output_kernel, count, members),
        (blocks,),
        [one(pixels, BLK), one(2, BLK), one(2, BLK), one(pixels, BLK), one(pixels, BLK)],
        [one(pixels, BLK), one(pixels, BLK), whole(blocks, 2, BLK)],
        [shape((blocks, pixels, BLK), BF16), shape((blocks, pixels, BLK)), shape((blocks, 2, BLK))],
        [],
        20 * pixels * blocks * BLK,
        comm,
    )(expanded, sums, params, x, grad)


def expand_back_kernel(
    count,
    exp_ref,
    sums_ref,
    prm_ref,
    up_ref,
    upsums_ref,
    w_ref,
    grp_ref,
    gsums_ref,
    gprm_ref,
    back_ref,
    out_ref,
    stat_ref,
    keep_ref,
):
    blocks, pixels, _ = keep_ref.shape
    step = pl.program_id(0)
    clear_stats(stat_ref)

    @pl.when(step < blocks)
    def _():
        coef = coefficients(sums_ref[0], prm_ref[0], count)
        scale = coef[2] * coef[1]
        up_mean = upsums_ref[0, 0:1] / count
        up_lean = upsums_ref[0, 1:2] / count

        def back(start, size):
            rows = pl.ds(start, size)
            standard, _ = standardize(exp_ref[0, rows], coef)
            values = (scale * (up_ref[0, rows] - up_mean - standard * up_lean)).astype(BF16)
            back_ref[0, rows] = values
            keep_ref[step, rows] = values

        over_rows(pixels, back)

    @pl.when(step >= blocks)
    def _():
        coef = coefficients(gsums_ref[0], gprm_ref[0], count)

        def body(start, size):
            rows = pl.ds(start, size)
            total = dot(keep_ref[0, rows], w_ref[0])
            for source in range(1, blocks):
                total += dot(keep_ref[source, rows], w_ref[source])
            standard, norm = standardize(grp_ref[0, rows], coef)
            up = total * silu_slope(norm)
            out_ref[0, rows] = up
            add_stats(stat_ref, step - blocks, up, up * standard)

        over_rows(pixels, body)


def expand_back(expanded, sums, params, up, upsums, weight, grouped, gsums, gparams, count, comm):
    blocks, pixels, _ = expanded.shape
    mids = grouped.shape[0]

    def first(*dims):
        return pl.BlockSpec((1,) + dims, lambda j: (jnp.minimum(j, blocks - 1),) + (0,) * len(dims))

    def second(*dims):
        return pl.BlockSpec((1,) + dims, lambda j: (jnp.maximum(j - blocks, 0),) + (0,) * len(dims))

    return call(
        functools.partial(expand_back_kernel, count),
        (blocks + mids,),
        [
            first(pixels, BLK),
            first(2, BLK),
            first(2, BLK),
            first(pixels, BLK),
            first(2, BLK),
            pl.BlockSpec((blocks, BLK, BLK), lambda j: (0, 0, jnp.maximum(j - blocks, 0))),
            second(pixels, BLK),
            second(2, BLK),
            second(2, BLK),
        ],
        [first(pixels, BLK), second(pixels, BLK), whole(mids, 2, BLK)],
        [shape((blocks, pixels, BLK), BF16), shape((mids, pixels, BLK)), shape((mids, 2, BLK))],
        [pltpu.VMEM((blocks, pixels, BLK), BF16)],
        2 * pixels * blocks * BLK * mids * BLK,
        comm,
    )(expanded, sums, params, up, upsums, weight, grouped, gsums, gparams)


def weight_grad_kernel(left_ref, right_ref, out_ref):
    weight_grad_block(left_ref[0], right_ref, out_ref, 0)


def weight_grad(left, right):
    blocks, pixels, _ = left.shape
    width = right.shape[1]
    return call(
        weight_grad_kernel,
        (blocks,),
        [block(pixels, BLK), whole(pixels, width)],
        [block(BLK, width)],
        [shape((blocks, BLK, width), BF16)],
        [],
        2 * pixels * blocks * BLK * width,
    )(left, right)[0]


def first_back(count, red_ref, sums_ref, prm_ref, rup_ref, rupsums_ref, back_ref):
    mids, pixels, _ = red_ref.shape
    for mid in range(mids):
        coef = coefficients(sums_ref[mid], prm_ref[mid], count)
        scale = coef[2] * coef[1]
        up_mean = rupsums_ref[mid, 0:1] / count
        up_lean = rupsums_ref[mid, 1:2] / count

        def body(start, size):
            rows = pl.ds(start, size)
            standard, _ = standardize(red_ref[mid, rows], coef)
            values = scale * (rup_ref[mid, rows] - up_mean - standard * up_lean)
            back_ref[rows, mid * BLK : (mid + 1) * BLK] = values.astype(BF16)

        over_rows(pixels, body)


def weight_grad_block(left, right_ref, out_ref, slot):
    for first in range(0, right_ref.shape[1], BLK):
        columns = slice(first, first + BLK)
        out_ref[slot, :, columns] = dot(left, right_ref[:, columns], ((0,), (0,))).astype(BF16)


def reduce_back_kernel(count, red_ref, sums_ref, prm_ref, rup_ref, rupsums_ref, x_ref, up_ref, w_ref, grad_ref, wgrad_ref, back_ref):
    @pl.when(pl.program_id(0) == 0)
    def _():
        first_back(count, red_ref, sums_ref, prm_ref, rup_ref, rupsums_ref, back_ref)

    def product(start, size):
        rows = pl.ds(start, size)
        total = dot(back_ref[rows], w_ref[0], ((1,), (1,)))
        grad_ref[0, rows] = (up_ref[0, rows] + total).astype(BF16)

    over_rows(x_ref.shape[1], product)
    weight_grad_block(x_ref[0], back_ref, wgrad_ref, 0)


def reduce_back(reduced, sums, params, rup, rupsums, x, up, weight, count):
    mids, pixels, _ = reduced.shape
    blocks = x.shape[0]
    return call(
        functools.partial(reduce_back_kernel, count),
        (blocks,),
        [
            whole(mids, pixels, BLK),
            whole(mids, 2, BLK),
            whole(mids, 2, BLK),
            whole(mids, pixels, BLK),
            whole(mids, 2, BLK),
            block(pixels, BLK),
            block(pixels, BLK),
            block(BLK, mids * BLK),
        ],
        [block(pixels, BLK), block(BLK, mids * BLK)],
        [shape((blocks, pixels, BLK), BF16), shape((blocks, BLK, mids * BLK), BF16)],
        [pltpu.VMEM((pixels, mids * BLK), BF16)],
        4 * pixels * blocks * BLK * mids * BLK,
    )(reduced, sums, params, rup, rupsums, x, up, weight)


def exchange_kernel(batches, members, x_ref, out_ref, *scratch):
    row, me, across, along = devices(batches, members)
    greet(across + along)
    out_ref[...] = x_ref[...]
    total_stats(out_ref, across, along, *scratch)


def exchange(values, batches, members, collective_id):
    return pl.pallas_call(
        functools.partial(exchange_kernel, batches, members),
        in_specs=[pl.BlockSpec(memory_space=pltpu.VMEM)],
        out_specs=pl.BlockSpec(memory_space=pltpu.VMEM),
        out_shape=shape(values.shape),
        scratch_shapes=stats_scratch(values.shape, batches, members),
        compiler_params=pltpu.CompilerParams(collective_id=collective_id, has_side_effects=True),
    )(values)


def turn(source_ref, target_ref, slot, chunk):
    first = (49 * chunk) // 4

    @pl.loop(0, 13)
    def _(tile):
        columns = pl.ds(pl.multiple_of((first + tile) * HALF, HALF), HALF)
        rows = pl.ds(pl.multiple_of(tile * HALF, HALF), HALF)
        target_ref[slot, rows] = source_ref[:, columns].T


def turned(target_ref, slot, chunk, pixels):
    return target_ref.at[slot, pl.ds(pl.multiple_of(32 * (chunk % 4), 16), pixels)]


def opening_kernel(batches, members, *refs):
    x_ref, grad_ref, wr_ref, we_ref, wg_ref = refs[:5]
    vectors = refs[5:11]
    xp_ref, gradt_ref, wr_out, we_out, wg_out, prm_out = refs[11:17]
    xin, xturn, gin, gturn, prm_ref, load, own, xsend, xrecv, gsend, psend, precv = refs[17:29]
    zsend, zrecv, ysend, yrecv, fsend, frecv = refs[29:]
    row, me, across, along = devices(batches, members)
    pixels = xp_ref.shape[1]
    load_x = pltpu.make_async_copy(x_ref, xin, load.at[0])
    load_grad = pltpu.make_async_copy(grad_ref, gin, load.at[1])
    load_x.start()
    load_grad.start()
    weights = [(wr_ref, wr_out), (wg_ref, wg_out), (we_ref, we_out)]
    height, side = me // 2, me % 2
    levels = members // 2
    line = [(row, lax.rem(me + 2 * step, members)) for step in range(1, levels)]
    peer = (row, height * 2 + 1 - side)
    local_copies = []
    parts = []
    for index, (source, target) in enumerate(weights):
        size = source.shape[0] // batches
        part = pl.ds(pl.multiple_of(row * size, 16), size)
        parts.append(part)
        local_copies.append(pltpu.make_async_copy(source.at[part], target.at[height, side, part], own.at[index]))
    each(local_copies, "start")
    place = 0
    for vector in vectors:
        for low in range(0, vector.shape[0], HALF):
            prm_ref[place : place + 1] = vector[low : low + HALF].reshape(1, HALF)
            place += 1
    prm_own = pltpu.make_async_copy(prm_ref, prm_out.at[me], own.at[3])
    prm_own.start()
    greet(across + along)
    copies = [prm_own]
    first = []
    for index, (source, target) in enumerate(weights):
        for step, device in enumerate(line):
            first.append(
                remote(
                    source.at[parts[index]],
                    target.at[height, side, parts[index]],
                    zsend.at[index, step],
                    zrecv.at[index, step],
                    device,
                )
            )
    for step, device in enumerate(along):
        copy = remote(prm_ref, prm_out.at[me], psend.at[step], precv.at[step], device)
        copy.start()
        copies.append(copy)
    each(first, "start")
    load_x.wait()
    for step, device in enumerate(along):
        turn(xin, xturn, step, device[1])
        copy = remote(turned(xturn, step, device[1], pixels), xp_ref.at[me], xsend.at[step], xrecv.at[step], device)
        copy.start()
        copies.append(copy)
    last = members - 1
    turn(xin, xturn, last, me)
    copy = pltpu.make_async_copy(turned(xturn, last, me, pixels), xp_ref.at[me], xsend.at[last])
    copy.start()
    copies.append(copy)
    load_grad.wait()
    for member in range(members):
        turn(gin, gturn, member, member)
        copy = pltpu.make_async_copy(turned(gturn, member, member, pixels), gradt_ref.at[member], gsend.at[member])
        copy.start()
        copies.append(copy)
    each(local_copies, "wait")
    far, near = (lax.bitwise_xor(row, 2), me), (lax.bitwise_xor(row, 1), me)
    second, third = [], []
    for index, (_, target) in enumerate(weights):
        each(first[index * len(line) : (index + 1) * len(line)], "wait")
        held = target.at[:, side, parts[index]]
        second.append(remote(held, held, ysend.at[index], yrecv.at[index], peer))
        second[-1].start()
    for index, (_, target) in enumerate(weights):
        second[index].wait()
        held = target.at[:, :, parts[index]]
        third.append(remote(held, held, fsend.at[index, 0], frecv.at[index, 0], far))
        third[-1].start()
    for index, (source, target) in enumerate(weights):
        size = source.shape[0] // batches
        third[index].wait()
        for step, origin in enumerate((row, lax.bitwise_xor(row, 2))):
            held = target.at[:, :, pl.ds(pl.multiple_of(origin * size, 16), size)]
            copy = remote(held, held, fsend.at[index, 1 + step], frecv.at[index, 1 + step], near)
            copy.start()
            copies.append(copy)
    each(copies, "wait")


def opening(block_input, out_grad, reduce_weight, expand_weight, taps, vectors, batches, members):
    channels, row_pixels = block_input.shape
    pixels = row_pixels // members
    dma = pltpu.SemaphoreType.DMA
    other, across, levels = members - 1, batches - 1, members // 2
    padded = 13 * HALF
    lines = sum(vector.shape[0] for vector in vectors) // HALF
    weights = [reduce_weight, expand_weight, taps]
    x, grad, *gathered, params = pl.pallas_call(
        functools.partial(opening_kernel, batches, members),
        in_specs=[pl.BlockSpec(memory_space=pl.ANY)] * 5 + [pl.BlockSpec(memory_space=pltpu.VMEM)] * len(vectors),
        out_specs=[pl.BlockSpec(memory_space=pl.ANY)] * 6,
        out_shape=[shape((members, pixels, channels), BF16)] * 2
        + [shape((levels, 2) + weight.shape, BF16) for weight in weights]
        + [shape((members, lines, HALF))],
        scratch_shapes=[
            pltpu.VMEM((channels, row_pixels), BF16),
            pltpu.VMEM((members, padded, channels), BF16),
            pltpu.VMEM((channels, row_pixels), BF16),
            pltpu.VMEM((members, padded, channels), BF16),
            pltpu.VMEM((lines, HALF), F32),
            dma((2,)),
            dma((4,)),
            dma((members,)),
            dma((other,)),
            dma((members,)),
            dma((other,)),
            dma((other,)),
            dma((3, levels - 1)),
            dma((3, levels - 1)),
            dma((3,)),
            dma((3,)),
            dma((3, across)),
            dma((3, across)),
        ],
        compiler_params=pltpu.CompilerParams(vmem_limit_bytes=VMEM_LIMIT, collective_id=0, has_side_effects=True),
    )(block_input, out_grad, *weights, *vectors)
    gathered = [full.reshape((members,) + full.shape[2:]) for full in gathered]
    return x, grad, *gathered, params


class Reduce:
    def __init__(self, part, out, row, me, across, refs):
        self.part, self.out, self.row, self.across = part, out, row, across
        self.height, self.side = me // 2, me % 2
        self.first, self.held, self.pair, self.line, self.second, self.total = refs[:6]
        self.s1, self.r1, self.s2, self.r2, self.s3, self.r3, self.s4, self.r4 = refs[6:]
        self.levels = self.held.shape[0]
        self.size = self.total.shape[0]
        self.peer = (row, self.height * 2 + 1 - self.side)
        self.along = [(row, lax.rem(me + 2 * step, 2 * self.levels)) for step in range(1, self.levels)]

    def rows(self, row):
        return pl.ds(pl.multiple_of(row * self.size, 16), self.size)

    def over_batch(self):
        return [
            remote(
                self.part.at[:, self.rows(device[0])], self.first.at[step], self.s1.at[step], self.r1.at[step], device
            )
            for step, device in enumerate(self.across)
        ]

    def add_batch(self):
        @pl.loop(0, self.levels)
        def _(level):
            for side in range(2):
                total = self.part[2 * level + side, self.rows(self.row)].astype(F32)
                for step in range(len(self.across)):
                    total += self.first[step, 2 * level + side].astype(F32)
                self.held[level, side] = total.astype(BF16)

    def over_pair(self):
        return [remote(self.held.at[:, 1 - self.side], self.pair, self.s2.at[0], self.r2.at[0], self.peer)]

    def add_pair(self):
        @pl.loop(0, self.levels)
        def _(level):
            total = self.held[level, self.side].astype(F32) + self.pair[level].astype(F32)
            self.line[level] = total.astype(BF16)

    def over_line(self):
        return [
            remote(self.line.at[device[1] // 2], self.second.at[step], self.s3.at[step], self.r3.at[step], device)
            for step, device in enumerate(self.along)
        ]

    def add_line(self):
        total = self.line[self.height].astype(F32)
        for step in range(len(self.along)):
            total += self.second[step].astype(F32)
        self.total[...] = total

    def share(self):
        rows = self.rows(self.row)
        copies = [
            remote(self.total, self.out.at[rows], self.s4.at[step], self.r4.at[step], device)
            for step, device in enumerate(self.across)
        ]
        return copies + [pltpu.make_async_copy(self.total, self.out.at[rows], self.s4.at[len(self.across)])]


def reduce_scratch(dims, batches, members):
    rows, columns = dims[1] // batches, dims[2]
    levels = members // 2
    dma = pltpu.SemaphoreType.DMA
    return [
        pltpu.VMEM((batches - 1, members, rows, columns), BF16),
        pltpu.VMEM((levels, 2, rows, columns), BF16),
        pltpu.VMEM((levels, rows, columns), BF16),
        pltpu.VMEM((levels, rows, columns), BF16),
        pltpu.VMEM((levels - 1, rows, columns), BF16),
        pltpu.VMEM((rows, columns), F32),
        dma((batches - 1,)),
        dma((batches - 1,)),
        dma((1,)),
        dma((1,)),
        dma((levels - 1,)),
        dma((levels - 1,)),
        dma((batches,)),
        dma((batches - 1,)),
    ]


HELD_BACK = 2


def closing_kernel(count, batches, members, low, size, *refs):
    red_ref, sums_ref, prm_ref, rup_ref, rupsums_ref, x_ref, up_ref, w_ref, epart_ref, tpart_ref, src_ref, _ = refs[:12]
    recv_ref, rout_ref, eout_ref, tout_ref, dst_ref = refs[12:17]
    back_ref, grad_ref, wpart_ref, gsend, grecv, psend, precv = refs[17:24]
    row, me, across, along = devices(batches, members)
    step = pl.program_id(0)
    last = members - 1
    expand_sum = Reduce(epart_ref, eout_ref, row, me, across, refs[24:38])
    taps_sum = Reduce(tpart_ref, tout_ref, row, me, across, refs[38:52])
    reduce_sum = Reduce(wpart_ref, rout_ref, row, me, across, refs[52:66])
    parts = (expand_sum, taps_sum, reduce_sum)
    other = lax.rem(me + 1 + step, members)

    def pieces():
        return piece_copies(src_ref, dst_ref, low, size, me, along, psend, precv)

    def send(index):
        device = (row, lax.rem(me + 1 + index, members))
        return remote(grad_ref.at[index], recv_ref.at[me], gsend.at[index], grecv.at[index], device)

    @pl.when(step == 0)
    def _():
        greet(across + along)
        each(pieces(), "start")
        each(expand_sum.over_batch(), "start")
        each(taps_sum.over_batch(), "start")
        first_back(count, red_ref, sums_ref, prm_ref, rup_ref, rupsums_ref, back_ref)

    def product(start, size):
        part = pl.ds(start, size)
        total = dot(back_ref[part], w_ref[0], ((1,), (1,)))
        grad_ref[step, part] = (up_ref[0, part] + total).astype(BF16)

    over_rows(x_ref.shape[1], product)

    @pl.when(step < last - HELD_BACK)
    def _():
        send(step).start()

    weight_grad_block(x_ref[0], back_ref, wpart_ref, other)

    @pl.when(step == last)
    def _():
        own = pltpu.make_async_copy(grad_ref.at[last], recv_ref.at[me], gsend.at[last])
        own.start()
        each(reduce_sum.over_batch(), "start")
        for part in parts:
            each(part.over_batch(), "wait")
            part.add_batch()
            each(part.over_pair(), "start")
        for part in parts:
            each(part.over_pair(), "wait")
            part.add_pair()
            each(part.over_line(), "start")
        for index in range(last - HELD_BACK, last):
            send(index).start()
        for part in parts:
            each(part.over_line(), "wait")
            part.add_line()
            each(part.share(), "start")
        own.wait()
        each(pieces(), "wait")
        for index in range(last):
            send(index).wait()
        for part in parts:
            each(part.share(), "wait")


def closing(
    reduced, sums, params, rup, rupsums, x, up, weight, epart, tpart, source, into, low, size, count, batches, members
):
    mids, pixels, _ = reduced.shape
    blocks = x.shape[0]
    once = pl.Buffered(1)

    def keep(*dims):
        return pl.BlockSpec(dims, lambda j: (0,) * len(dims), pipeline_mode=once)

    turn_block = functools.partial(turned_block, members)
    anywhere = pl.BlockSpec(memory_space=pl.ANY)
    dma = pltpu.SemaphoreType.DMA
    wdims = (blocks, BLK, mids * BLK)
    scratch = [
        pltpu.VMEM((pixels, mids * BLK), BF16),
        pltpu.VMEM((blocks, pixels, BLK), BF16),
        pltpu.VMEM(wdims, BF16),
        dma((members,)),
        dma((members - 1,)),
        dma((members,)),
        dma((members - 1,)),
    ]
    for dims in (wdims, tpart.shape, wdims):
        scratch += reduce_scratch(dims, batches, members)
    return pl.pallas_call(
        functools.partial(closing_kernel, count, batches, members, low, size),
        grid=(blocks,),
        in_specs=[
            keep(mids, pixels, BLK),
            keep(mids, 2, BLK),
            keep(mids, 2, BLK),
            keep(mids, pixels, BLK),
            keep(mids, 2, BLK),
            turn_block(pixels, BLK),
            turn_block(pixels, BLK),
            turn_block(BLK, mids * BLK),
            keep(*wdims),
            keep(*tpart.shape),
            anywhere,
            anywhere,
        ],
        out_specs=[anywhere] * 5,
        out_shape=[
            shape((members, pixels, BLK), BF16),
            shape(wdims[1:]),
            shape(wdims[1:]),
            shape(tpart.shape[1:]),
            shape(source.shape, BF16),
        ],
        scratch_shapes=scratch,
        input_output_aliases={11: 4},
        compiler_params=pltpu.CompilerParams(vmem_limit_bytes=VMEM_LIMIT, collective_id=7, has_side_effects=True),
    )(reduced, sums, params, rup, rupsums, x, up, weight, epart, tpart, source, into)


def turn_out_kernel(in_ref, out_ref):
    for first in range(0, in_ref.shape[0], HALF):
        out_ref[:, first : first + HALF] = in_ref[first : first + HALF].astype(out_ref.dtype).T


def turn_out(values, dtype):
    rows, channels = values.shape
    size = next(part for part in (1792, 896, HALF) if rows % part == 0)
    return call(
        turn_out_kernel,
        (rows // size,),
        [pl.BlockSpec((size, channels), lambda j: (j, 0))],
        [pl.BlockSpec((channels, size), lambda j: (0, j))],
        [shape((channels, rows), dtype)],
        [],
        rows * channels,
    )(values)[0]


def pixel_masks(pixels):
    place = np.arange(pixels)
    tall, wide = (place // SIDE) % SIDE, place % SIDE
    masks = np.stack([wide != 0, wide != SIDE - 1, tall != 0, tall != SIDE - 1])
    return jnp.asarray(np.broadcast_to(masks[:, :, None], (4, pixels, HALF)).astype(np.float32))


def own_part(stats, which, length):
    return lax.dynamic_slice_in_dim(stats[:, which].reshape(-1), lax.axis_index("group") * length, length, 0)


TAP_ROWS = 320


def fused(
    block_input,
    reduce_weight,
    reduce_gain,
    reduce_bias,
    group_weight,
    group_gain,
    group_bias,
    expand_weight,
    expand_gain,
    expand_bias,
    out_grad,
):
    batches, members = lax.axis_size("batch"), lax.axis_size("group")
    channels, row_pixels = block_input.shape
    pixels = row_pixels // members
    count = row_pixels * batches
    local_mid = reduce_gain.shape[0]
    vectors = [reduce_gain, reduce_bias, group_gain, group_bias, expand_gain, expand_bias]
    taps = group_weight.reshape(-1, 9, GW, GW).transpose(1, 2, 0, 3).reshape(9 * GW, HALF)
    taps = jnp.pad(taps, ((0, TAP_ROWS - 9 * GW), (0, 0)))
    masks = pixel_masks(pixels)
    x, grad_turned, reduce_full, expand_full, taps_full, packs = opening(
        block_input, out_grad, reduce_weight, expand_weight, taps, vectors, batches, members
    )
    vectors = packs[:, :4].reshape(-1, 2, 4, HALF).transpose(0, 2, 1, 3).reshape(-1, 4, BLK)
    reduce_params, group_params = vectors[:, :2], vectors[:, 2:]
    expand_params = packs[:, 4:].reshape(-1, 2, BLK)

    comm = functools.partial(Comm, batches, members)
    beside = (64, 48)
    sends = comm(1, grad_turned, 0, (336,) + beside)
    reduced, reduce_sums, grad = reduce_product(x, reduce_full, sends)
    sends = comm(2, grad_turned, sends.high, (448,) + beside, grad)
    grouped, group_sums, grad = conv(reduced, reduce_sums, reduce_params, taps_full, masks, count, sends)
    sends = comm(3, grad_turned, sends.high, (pixels - sends.high - sum(beside),) + beside, grad)
    expanded, act, expand_sums, grad = expand_product(grouped, group_sums, group_params, expand_full, count, sends)
    sends = comm(4, None, 0, (224,) + beside, None, True)
    out, upstream, expand_stats, moved = output(expanded, expand_sums, expand_params, x, grad, count, sends)
    sends = comm(5, out, sends.high, (304,) + beside, moved)
    back, group_up, group_stats, moved = expand_back(
        expanded,
        expand_sums,
        expand_params,
        upstream,
        expand_stats,
        expand_full,
        grouped,
        group_sums,
        group_params,
        count,
        sends,
    )
    sends = comm(6, out, sends.high, (560,) + beside, moved)
    expand_part, reduce_up, taps_part, reduce_stats, moved = conv_back(
        reduced,
        reduce_sums,
        reduce_params,
        grouped,
        group_sums,
        group_params,
        group_up,
        group_stats,
        taps_full,
        masks,
        count,
        sends,
        (back, act),
    )
    inner, reduce_weight_grad, expand_weight_grad, taps_grad, moved = closing(
        reduced,
        reduce_sums,
        reduce_params,
        reduce_up,
        reduce_stats,
        x,
        upstream,
        reduce_full,
        expand_part,
        taps_part,
        out,
        moved,
        sends.high,
        pixels - sends.high,
        count,
        batches,
        members,
    )
    block_output = turn_out(moved.reshape(row_pixels, channels), BF16)
    input_grad = turn_out(inner.reshape(row_pixels, channels), F32)
    taps_grad = taps_grad[: 9 * GW].reshape(9, GW, -1, GW).transpose(2, 0, 3, 1)
    return (
        block_output,
        input_grad,
        reduce_weight_grad,
        taps_grad.reshape(group_weight.shape),
        expand_weight_grad,
        own_part(reduce_stats, 1, local_mid),
        own_part(reduce_stats, 0, local_mid),
        own_part(group_stats, 1, local_mid),
        own_part(group_stats, 0, local_mid),
        own_part(expand_stats, 1, channels),
        own_part(expand_stats, 0, channels),
    )


def modular(
    block_input,
    reduce_weight,
    reduce_gain,
    reduce_bias,
    group_weight,
    group_gain,
    group_bias,
    expand_weight,
    expand_gain,
    expand_bias,
    out_grad,
):
    batches, members = lax.axis_size("batch"), lax.axis_size("group")
    channels, row_pixels = block_input.shape
    pixels = row_pixels // members
    count = row_pixels * batches
    mid_total = reduce_weight.shape[1]
    mids = mid_total // BLK
    blocks = channels * members // BLK
    me = lax.axis_index("group")

    def to_pixels(values):
        moved = lax.all_to_all(values.T.reshape(members, pixels, channels), "group", 0, 0)
        if channels == BLK:
            return moved
        share = BLK // channels
        moved = moved.reshape(blocks, share, pixels, channels).transpose(0, 2, 1, 3)
        return moved.reshape(blocks, pixels, BLK)

    def to_channels(values):
        if channels != BLK:
            share = BLK // channels
            values = values.reshape(blocks, pixels, share, channels).transpose(0, 2, 1, 3)
            values = values.reshape(members, pixels, channels)
        moved = lax.all_to_all(values, "group", 0, 0)
        return moved.reshape(row_pixels, channels).T

    def gather(values):
        return lax.all_gather(values, "group", axis=0, tiled=True)

    local_mid = reduce_gain.shape[0]
    pack = jnp.concatenate([reduce_gain, reduce_bias, group_gain, group_bias, expand_gain, expand_bias])
    packs = gather(pack[None])
    vectors, offset = [], 0
    for length in (local_mid, local_mid, local_mid, local_mid, channels, channels):
        vectors.append(packs[:, offset : offset + length].reshape(-1, BLK))
        offset += length
    reduce_params = jnp.stack(vectors[0:2], 1)
    group_params = jnp.stack(vectors[2:4], 1)
    expand_params = jnp.stack(vectors[4:6], 1)
    reduce_full = gather(reduce_weight).reshape(blocks, BLK, mid_total)
    expand_full = gather(expand_weight).reshape(blocks, BLK, mid_total)
    taps = gather(group_weight.reshape(group_weight.shape[0], 9, GW, GW))
    taps = taps.reshape(-1, HALF // GW, 9, GW, GW).transpose(0, 2, 3, 1, 4).reshape(-1, 9 * GW, HALF)
    taps = jnp.pad(taps, ((0, 0), (0, TAP_ROWS - 9 * GW), (0, 0)))
    masks = pixel_masks(pixels)

    x = to_pixels(block_input)
    grad = to_pixels(out_grad)

    reduced, reduce_sums = reduce_product(x, reduce_full, None)
    reduce_sums = exchange(reduce_sums, batches, members, 1)
    grouped, group_sums = conv(reduced, reduce_sums, reduce_params, taps, masks, count, None)
    group_sums = exchange(group_sums, batches, members, 1)
    expanded, act, expand_sums = expand_product(grouped, group_sums, group_params, expand_full, count, None)
    expand_sums = exchange(expand_sums, batches, members, 2)
    out, upstream, expand_stats = output(expanded, expand_sums, expand_params, x, grad, count, None)
    expand_stats = exchange(expand_stats, batches, members, 2)
    back, group_up, group_stats = expand_back(
        expanded, expand_sums, expand_params, upstream, expand_stats, expand_full, grouped, group_sums, group_params, count, None
    )
    expand_part = weight_grad(back, act)
    group_stats = exchange(group_stats, batches, members, 1)
    reduce_up, taps_part, reduce_stats = conv_back(
        reduced,
        reduce_sums,
        reduce_params,
        grouped,
        group_sums,
        group_params,
        group_up,
        group_stats,
        taps,
        masks,
        count,
        None,
    )
    reduce_stats = exchange(reduce_stats, batches, members, 1)
    inner, reduce_part = reduce_back(
        reduced, reduce_sums, reduce_params, reduce_up, reduce_stats, x, upstream, reduce_full, count
    )
    block_output = to_channels(out)
    input_grad = to_channels(inner).astype(F32)

    def shared_sum(part):
        rows = channels // batches
        part = part.reshape(members, batches, rows, mid_total).transpose(1, 0, 2, 3)
        part = lax.all_to_all(part, "batch", 0, 0).astype(F32).sum(0).astype(BF16)
        part = lax.all_to_all(part, "group", 0, 0).astype(F32).sum(0)
        return lax.all_gather(part, "batch", axis=0, tiled=True)

    expand_weight_grad = shared_sum(expand_part)
    reduce_weight_grad = shared_sum(reduce_part)
    taps_part = taps_part[:, : 9 * GW].reshape(-1, 9, GW, HALF // GW, GW).transpose(0, 3, 1, 4, 2)
    taps_part = taps_part.reshape(members, -1, 9, GW, GW)
    group_weight_grad = lax.all_to_all(taps_part, "group", 0, 0).astype(F32).sum(0)
    group_weight_grad = lax.psum(group_weight_grad, "batch").reshape(group_weight.shape)

    return (
        block_output,
        input_grad,
        reduce_weight_grad,
        group_weight_grad,
        expand_weight_grad,
        own_part(reduce_stats, 1, local_mid),
        own_part(reduce_stats, 0, local_mid),
        own_part(group_stats, 1, local_mid),
        own_part(group_stats, 0, local_mid),
        own_part(expand_stats, 1, channels),
        own_part(expand_stats, 0, channels),
    )


def local(*args):
    block_input = args[0]
    pixels = block_input.shape[1] // lax.axis_size("group")
    if block_input.shape[0] == BLK and pixels == 1568 and args[2].shape[0] == HALF and lax.axis_size("group") == 8:
        return fused(*args)
    return modular(*args)


def solution(mesh):
    in_specs = (
        P("group", "batch"),
        P("group", None),
        P("group"),
        P("group"),
        P("group", None, None, None, None),
        P("group"),
        P("group"),
        P("group", None),
        P("group"),
        P("group"),
        P("group", "batch"),
    )
    out_specs = (
        P("group", "batch"),
        P("group", "batch"),
        P("group", None),
        P("group", None, None, None, None),
        P("group", None),
        P("group"),
        P("group"),
        P("group"),
        P("group"),
        P("group"),
        P("group"),
    )
    return jax.shard_map(local, mesh=mesh, in_specs=in_specs, out_specs=out_specs, check_vma=False)
```

```python
import functools

import jax
import jax.numpy as jnp
import numpy as np
from jax import lax
from jax.experimental import pallas as pl
from jax.experimental.pallas import tpu as pltpu
from jax.sharding import PartitionSpec as P

GW = 32
SIDE = 14
EPS = 1e-05
BLK = 256
HALF = 128
PAD = 16
F32 = jnp.float32
BF16 = jnp.bfloat16
MESH = pl.DeviceIdType.MESH
VMEM_LIMIT = 60 * 1024 * 1024


def silu_slope(values):
    sigma = jax.nn.sigmoid(values)
    return sigma * (1.0 + values * (1.0 - sigma))


def row_chunk(pixels):
    for size in (224, 208, 192, 176, 160, 144, 128, 112):
        if pixels % size == 0:
            return size
    return pixels


def over_rows(pixels, body):
    size = row_chunk(pixels)
    if size == pixels:
        body(0, size)
    else:

        @pl.loop(0, pixels // size)
        def _(step):
            body(pl.multiple_of(step * size, 16), size)


def coefficients(sums, params, count):
    center = sums[0:1] / count
    spread = sums[1:2] / count - center * center
    inverse = lax.rsqrt(spread + EPS)
    return center, inverse, params[0:1], params[1:2]


def standardize(values, coef):
    standard = (values - coef[0]) * coef[1]
    return standard, standard * coef[2] + coef[3]


def add_stats(ref, slot, first, second):
    ref[slot, 0:1] += jnp.sum(first, 0, keepdims=True)
    ref[slot, 1:2] += jnp.sum(second, 0, keepdims=True)


def clear_stats(ref):
    @pl.when(pl.program_id(0) == 0)
    def _():
        ref[...] = jnp.zeros_like(ref)


def dot(a, b, dims=((1,), (0,))):
    return lax.dot_general(a, b, (dims, ((), ())), preferred_element_type=F32)


def devices(batches, members):
    row, me = lax.axis_index("batch"), lax.axis_index("group")
    across = [(lax.rem(row + step, batches), me) for step in range(1, batches)]
    along = [(row, lax.rem(me + step, members)) for step in range(1, members)]
    return row, me, across, along


def greet(others):
    barrier = pltpu.get_barrier_semaphore()
    for device in others:
        pl.semaphore_signal(barrier, inc=1, device_id=device, device_id_type=MESH)
    pl.semaphore_wait(barrier, len(others))


def remote(source, target, send, recv, device):
    return pltpu.make_async_remote_copy(
        src_ref=source, dst_ref=target, send_sem=send, recv_sem=recv, device_id=device, device_id_type=MESH
    )


def each(copies, what):
    for copy in copies:
        getattr(copy, what)()


def spread(source, target, send, recv, others, beside):
    copies = [
        remote(source, target.at[step], send.at[step], recv.at[step], device) for step, device in enumerate(others)
    ]
    each(copies, "start")
    each(beside, "start")
    each(copies, "wait")


def total_stats(ref, across, along, first_ref, second_ref, mid_ref, send1, recv1, send2, recv2, beside=()):
    mid_ref[0] = ref[...]
    spread(mid_ref.at[0], second_ref, send2, recv2, along, beside)
    total = mid_ref[0]
    for step in range(len(along)):
        total += second_ref[step]
    mid_ref[1] = total
    spread(mid_ref.at[1], first_ref, send1, recv1, across, ())
    for step in range(len(across)):
        total += first_ref[step]
    ref[...] = total


def stats_scratch(dims, batches, members):
    return [
        pltpu.VMEM((batches - 1,) + dims, F32),
        pltpu.VMEM((members - 1,) + dims, F32),
        pltpu.VMEM((2,) + dims, F32),
        pltpu.SemaphoreType.DMA((batches - 1,)),
        pltpu.SemaphoreType.DMA((batches - 1,)),
        pltpu.SemaphoreType.DMA((members - 1,)),
        pltpu.SemaphoreType.DMA((members - 1,)),
    ]


class Comm:
    def __init__(self, batches, members, collective_id, source=None, low=0, sizes=(), into=None, stream=False):
        self.batches, self.members, self.collective_id = batches, members, collective_id
        self.source, self.low, self.sizes, self.into, self.stream = source, low, sizes, into, stream
        self.high = low + sum(sizes)


def piece_copies(source, target, low, size, me, along, send, recv, staged=False):
    rows = pl.ds(low, size)
    last = len(along)
    copies = [
        remote(
            source.at[step if staged else device[1], rows], target.at[me, rows], send.at[step], recv.at[step], device
        )
        for step, device in enumerate(along)
    ]
    return copies + [
        pltpu.make_async_copy(source.at[last if staged else me, rows], target.at[me, rows], send.at[last])
    ]


class Late:
    def __init__(self, dims, dtype=F32):
        self.dims, self.dtype = dims, dtype


def call(kernel, grid, in_specs, out_specs, out_shape, scratch, flops, comm=None):
    if comm is None:
        in_specs = [whole(*spec.dims) if isinstance(spec, Late) else spec for spec in in_specs]
        return functools.partial(
            plain_call, kernel, grid, in_specs, out_specs, out_shape, scratch, flops, pltpu.CompilerParams(vmem_limit_bytes=VMEM_LIMIT)
        )
    n_in, n_out, n_scratch = len(in_specs), len(out_specs), len(scratch)
    stats = out_shape[-1].shape
    batches, members = comm.batches, comm.members

    sends = bool(comm.sizes)
    late = [index for index, spec in enumerate(in_specs) if isinstance(spec, Late)]
    late_specs = [in_specs[index] for index in late]

    def wrapped(*refs):
        refs = list(refs)
        ins = refs[:n_in]
        del refs[:n_in]
        source = refs.pop(0) if sends and not comm.stream else None
        if comm.into is not None:
            refs.pop(0)
        outs = refs[:n_out]
        del refs[:n_out]
        target = refs.pop(0) if sends else None
        own = refs[:n_scratch]
        del refs[:n_scratch]
        stats_refs = refs[:7]
        del refs[:7]
        if comm.stream:
            source = refs.pop(0)
        loads = []
        if late:
            load_sem = refs.pop(0)
            for place, index in enumerate(late):
                held = refs.pop(0)
                loads.append(pltpu.make_async_copy(ins[index], held, load_sem.at[place]))
                ins[index] = held
        row, me, across, along = devices(batches, members)
        step = pl.program_id(0)

        def copies(part):
            low = comm.low + sum(comm.sizes[:part])
            return piece_copies(
                source, target, low, comm.sizes[part], me, along, refs[0].at[part], refs[1].at[part], comm.stream
            )

        @pl.when(step == 0)
        def _():
            greet(across + along)
            if sends and not comm.stream:
                each(copies(0), "start")
            each(loads, "start")
            each(loads, "wait")

        kernel(*ins, *outs, *own)
        if comm.stream:
            source[step] = outs[0][0, : comm.high]
            rows = pl.ds(0, comm.sizes[0])

            @pl.when(step < members - 1)
            def _():
                device = (row, lax.rem(me + 1 + step, members))
                remote(
                    source.at[step, rows], target.at[me, rows], refs[0].at[0, step], refs[1].at[0, step], device
                ).start()

            @pl.when(step == members - 1)
            def _():
                pltpu.make_async_copy(source.at[step, rows], target.at[me, rows], refs[0].at[0, step]).start()

        @pl.when(step == pl.num_programs(0) - 1)
        def _():
            total_stats(outs[-1], across, along, *stats_refs, beside=copies(1) if sends else ())
            if sends:
                for part in range(2):
                    each(copies(part), "wait")

    scratch = list(scratch) + stats_scratch(stats, batches, members)
    in_specs, out_specs, out_shape = list(in_specs), list(out_specs), list(out_shape)
    extra, aliases = [], {}
    if sends:
        if comm.stream:
            dims, dtype = out_shape[0].shape, out_shape[0].dtype
            scratch.append(pltpu.VMEM((members, comm.high, dims[2]), dtype))
        else:
            dims, dtype = comm.source.shape, comm.source.dtype
            extra = [comm.source]
        if comm.into is not None:
            aliases = {len(in_specs) + len(extra): len(out_specs)}
            extra.append(comm.into)
        in_specs = [pl.BlockSpec(memory_space=pl.ANY) if isinstance(spec, Late) else spec for spec in in_specs]
        in_specs += [pl.BlockSpec(memory_space=pl.ANY)] * len(extra)
        if late:
            scratch.append(pltpu.SemaphoreType.DMA((len(late),)))
            scratch += [pltpu.VMEM(spec.dims, spec.dtype) for spec in late_specs]
        out_specs.append(pl.BlockSpec(memory_space=pl.ANY))
        out_shape.append(shape(dims, dtype))
        scratch += [pltpu.SemaphoreType.DMA((2, members)), pltpu.SemaphoreType.DMA((2, members - 1))]
    params = pltpu.CompilerParams(
        vmem_limit_bytes=VMEM_LIMIT, collective_id=comm.collective_id, has_side_effects=True
    )
    inner = functools.partial(
        plain_call, wrapped, grid, in_specs, out_specs, out_shape, scratch, flops, params, aliases=aliases
    )
    return lambda *args: inner(*args, *extra)


def plain_call(kernel, grid, in_specs, out_specs, out_shape, scratch, flops, params, *args, aliases={}):
    return pl.pallas_call(
        kernel,
        grid=grid,
        in_specs=in_specs,
        out_specs=out_specs,
        out_shape=out_shape,
        scratch_shapes=scratch,
        input_output_aliases=aliases,
        compiler_params=params,
        cost_estimate=pl.CostEstimate(flops=flops, bytes_accessed=20_000_000, transcendentals=0),
    )(*args)


def shape(dims, dtype=F32):
    return jax.ShapeDtypeStruct(dims, dtype)


def block(*dims):
    return pl.BlockSpec((1,) + dims, lambda j: (j,) + (0,) * len(dims))


def turned_block(members, *dims):
    def index(j):
        return (lax.rem(lax.axis_index("group") + 1 + j, members),) + (0,) * len(dims)

    return pl.BlockSpec((1,) + dims, index)


def whole(*dims):
    return pl.BlockSpec(dims, lambda j: (0,) * len(dims))


def reduce_kernel(x_ref, w_ref, out_ref, sum_ref):
    clear_stats(sum_ref)
    slot = pl.program_id(0)

    def body(start, size):
        rows = pl.ds(start, size)
        total = dot(x_ref[0, rows], w_ref[0])
        for source in range(1, x_ref.shape[0]):
            total += dot(x_ref[source, rows], w_ref[source])
        out_ref[0, rows] = total
        add_stats(sum_ref, slot, total, total * total)

    over_rows(x_ref.shape[1], body)


def reduce_product(x, weight, comm):
    blocks, pixels, _ = x.shape
    mids = weight.shape[2] // BLK
    return call(
        reduce_kernel,
        (mids,),
        [Late((blocks, pixels, BLK), BF16), pl.BlockSpec((blocks, BLK, BLK), lambda j: (0, 0, j))],
        [block(pixels, BLK), whole(mids, 2, BLK)],
        [shape((mids, pixels, BLK)), shape((mids, 2, BLK))],
        [],
        2 * pixels * blocks * BLK * mids * BLK,
        comm,
    )(x, weight)


def same_group():
    return lax.broadcasted_iota(jnp.int32, (BLK, BLK), 0) // GW == lax.broadcasted_iota(jnp.int32, (BLK, BLK), 1) // GW


def spread_weight(compact_ref, dense_ref):
    own = same_group()
    for tap in range(9):
        rows = pl.ds(tap * GW, GW)
        compact = jnp.concatenate([compact_ref[0, rows], compact_ref[1, rows]], 1).astype(F32)
        tiled = jnp.concatenate([compact] * (BLK // GW), 0)
        dense_ref[tap] = jnp.where(own, tiled, 0.0).astype(BF16)


def twice(mask):
    return jnp.concatenate([mask, mask], 1)


def fill(stack_ref, mask_ref, rows_start, size, values):
    rows = pl.ds(rows_start, size)
    target = pl.ds(rows_start + PAD, size)
    for half in range(2):
        part = values[:, half * HALF : (half + 1) * HALF]
        stack_ref[1, half, target] = part
        stack_ref[0, half, target] = part * mask_ref[1, rows]
        stack_ref[2, half, target] = part * mask_ref[0, rows]


def clear_edges(stack_ref, pixels):
    edge = jnp.zeros(stack_ref.shape[:2] + (PAD, HALF), F32)
    stack_ref[:, :, 0:PAD] = edge
    stack_ref[:, :, PAD + pixels : PAD + pixels + PAD] = edge


def window(stack_ref, start, size, row_off, col_off):
    rows = pl.ds(start + (PAD + row_off * SIDE + col_off), size)
    return jnp.concatenate([stack_ref[col_off + 1, half, rows] for half in range(2)], 1).astype(BF16)


def conv_rows(stack_ref, mask_ref, dense_ref, start, size, flipped=False):
    rows = pl.ds(start, size)
    total = None
    for row_off in (-1, 0, 1):
        part = None
        for col_off in (-1, 0, 1):
            values = window(stack_ref, start, size, row_off, col_off)
            tap = (row_off + 1) * 3 + col_off + 1
            term = dot(values, dense_ref[8 - tap], ((1,), (1,))) if flipped else dot(values, dense_ref[tap])
            part = term if part is None else part + term
        if row_off:
            part = part * twice(mask_ref[2 if row_off < 0 else 3, rows])
        total = part if total is None else total + part
    return total


def conv_kernel(count, red_ref, sums_ref, prm_ref, weight_ref, mask_ref, out_ref, stat_ref, stack_ref, dense_ref):
    pixels = red_ref.shape[1]
    spread_weight(weight_ref, dense_ref)
    clear_edges(stack_ref, pixels)
    coef = coefficients(sums_ref[0], prm_ref[0], count)

    def enter(start, size):
        _, norm = standardize(red_ref[0, pl.ds(start, size)], coef)
        fill(stack_ref, mask_ref, start, size, (norm * jax.nn.sigmoid(norm)).astype(BF16).astype(F32))

    over_rows(pixels, enter)
    clear_stats(stat_ref)
    slot = pl.program_id(0)

    def body(start, size):
        total = conv_rows(stack_ref, mask_ref, dense_ref, start, size)
        out_ref[0, pl.ds(start, size)] = total
        add_stats(stat_ref, slot, total, total * total)

    over_rows(pixels, body)


def conv(reduced, sums, params, weight, masks, count, comm):
    mids, pixels, _ = reduced.shape
    return call(
        functools.partial(conv_kernel, count),
        (mids,),
        [
            block(pixels, BLK),
            block(2, BLK),
            block(2, BLK),
            pl.BlockSpec((2,) + weight.shape[1:], lambda j: (j, 0, 0)),
            Late((4, pixels, HALF)),
        ],
        [block(pixels, BLK), whole(mids, 2, BLK)],
        [shape((mids, pixels, BLK)), shape((mids, 2, BLK))],
        [pltpu.VMEM((3, 2, pixels + 2 * PAD, HALF), F32), pltpu.VMEM((9, BLK, BLK), BF16)],
        2 * 9 * pixels * mids * BLK * BLK,
        comm,
    )(reduced, sums, params, weight, masks)


def conv_back_kernel(
    count,
    red_ref,
    sums_ref,
    prm_ref,
    grp_ref,
    gsums_ref,
    gprm_ref,
    up_ref,
    upsums_ref,
    weight_ref,
    mask_ref,
    *refs,
):
    out_ref, wgrad_ref, stat_ref, stack_ref, dense_ref, back_ref = refs
    pixels = red_ref.shape[1]
    spread_weight(weight_ref, dense_ref)
    clear_edges(stack_ref, pixels)
    coef = coefficients(sums_ref[0], prm_ref[0], count)
    gcoef = coefficients(gsums_ref[0], gprm_ref[0], count)
    scale = gcoef[2] * gcoef[1]
    up_mean = upsums_ref[0, 0:1] / count
    up_lean = upsums_ref[0, 1:2] / count

    def back(start, size):
        rows = pl.ds(start, size)
        standard, _ = standardize(grp_ref[0, rows], gcoef)
        values = (scale * (up_ref[0, rows] - up_mean - standard * up_lean)).astype(BF16)
        back_ref[1, rows] = values
        values = values.astype(F32)
        back_ref[0, rows] = (values * twice(mask_ref[2, rows])).astype(BF16)
        back_ref[2, rows] = (values * twice(mask_ref[3, rows])).astype(BF16)
        fill(stack_ref, mask_ref, start, size, values)

    over_rows(pixels, back)
    clear_stats(stat_ref)
    slot = pl.program_id(0)

    def body(start, size):
        rows = pl.ds(start, size)
        standard, norm = standardize(red_ref[0, rows], coef)
        up = conv_rows(stack_ref, mask_ref, dense_ref, start, size, True) * silu_slope(norm)
        out_ref[0, rows] = up
        add_stats(stat_ref, slot, up, up * standard)

    over_rows(pixels, body)

    def enter(start, size):
        _, norm = standardize(red_ref[0, pl.ds(start, size)], coef)
        fill(stack_ref, mask_ref, start, size, (norm * jax.nn.sigmoid(norm)).astype(BF16).astype(F32))

    over_rows(pixels, enter)
    own = same_group()
    for tap in range(9):
        full = dot(back_ref[tap // 3], window(stack_ref, 0, pixels, tap // 3 - 1, tap % 3 - 1), ((0,), (0,)))
        full = jnp.where(own, full, 0.0)
        kept = full[0:GW]
        for group in range(1, BLK // GW):
            kept += full[group * GW : (group + 1) * GW]
        for half in range(2):
            wgrad_ref[half, tap * GW : (tap + 1) * GW] = kept[:, half * HALF : (half + 1) * HALF].astype(BF16)
    for half in range(2):
        wgrad_ref[half, 9 * GW :] = jnp.zeros((wgrad_ref.shape[1] - 9 * GW, HALF), BF16)


def conv_back(reduced, sums, params, grouped, gsums, gparams, up, upsums, weight, masks, count, comm):
    mids, pixels, _ = reduced.shape
    return call(
        functools.partial(conv_back_kernel, count),
        (mids,),
        [
            block(pixels, BLK),
            block(2, BLK),
            block(2, BLK),
            block(pixels, BLK),
            block(2, BLK),
            block(2, BLK),
            block(pixels, BLK),
            block(2, BLK),
            pl.BlockSpec((2,) + weight.shape[1:], lambda j: (j, 0, 0)),
            Late((4, pixels, HALF)),
        ],
        [block(pixels, BLK), pl.BlockSpec((2,) + weight.shape[1:], lambda j: (j, 0, 0)), whole(mids, 2, BLK)],
        [shape((mids, pixels, BLK)), shape(weight.shape, BF16), shape((mids, 2, BLK))],
        [
            pltpu.VMEM((3, 2, pixels + 2 * PAD, HALF), F32),
            pltpu.VMEM((9, BLK, BLK), BF16),
            pltpu.VMEM((3, pixels, BLK), BF16),
        ],
        4 * 9 * pixels * mids * BLK * BLK,
        comm,
    )(reduced, sums, params, grouped, gsums, gparams, up, upsums, weight, masks)


def expand_kernel(count, grp_ref, gsums_ref, gprm_ref, w_ref, out_ref, act_ref, sum_ref):
    mids, pixels, _ = grp_ref.shape

    @pl.when(pl.program_id(0) == 0)
    def _():
        for mid in range(mids):
            coef = coefficients(gsums_ref[mid], gprm_ref[mid], count)

            def body(start, size):
                rows = pl.ds(start, size)
                _, norm = standardize(grp_ref[mid, rows], coef)
                act_ref[rows, mid * BLK : (mid + 1) * BLK] = (norm * jax.nn.sigmoid(norm)).astype(BF16)

            over_rows(pixels, body)

    clear_stats(sum_ref)
    slot = pl.program_id(0)

    def product(start, size):
        rows = pl.ds(start, size)
        total = dot(act_ref[rows], w_ref[0], ((1,), (1,)))
        out_ref[0, rows] = total
        add_stats(sum_ref, slot, total, total * total)

    over_rows(pixels, product)


def expand_product(grouped, gsums, gparams, weight, count, comm):
    mids, pixels, _ = grouped.shape
    blocks = weight.shape[0]
    return call(
        functools.partial(expand_kernel, count),
        (blocks,),
        [
            Late((mids, pixels, BLK)),
            whole(mids, 2, BLK),
            whole(mids, 2, BLK),
            block(BLK, mids * BLK),
        ],
        [block(pixels, BLK), whole(pixels, mids * BLK), whole(blocks, 2, BLK)],
        [shape((blocks, pixels, BLK)), shape((pixels, mids * BLK), BF16), shape((blocks, 2, BLK))],
        [],
        2 * pixels * blocks * BLK * mids * BLK,
        comm,
    )(grouped, gsums, gparams, weight)


def output_kernel(count, members, exp_ref, sums_ref, prm_ref, x_ref, grad_ref, out_ref, up_ref, stat_ref):
    coef = coefficients(sums_ref[0], prm_ref[0], count)
    clear_stats(stat_ref)
    slot = pl.program_id(0)
    if members:
        slot = lax.rem(lax.axis_index("group") + 1 + slot, members)

    def body(start, size):
        rows = pl.ds(start, size)
        standard, norm = standardize(exp_ref[0, rows], coef)
        summed = norm + x_ref[0, rows].astype(F32)
        sigma = jax.nn.sigmoid(summed)
        out_ref[0, rows] = (summed * sigma).astype(BF16)
        up = grad_ref[0, rows].astype(F32) * (sigma * (1.0 + summed * (1.0 - sigma)))
        up_ref[0, rows] = up
        add_stats(stat_ref, slot, up, up * standard)

    over_rows(exp_ref.shape[1], body)


def output(expanded, sums, params, x, grad, count, comm):
    blocks, pixels, _ = expanded.shape
    members = comm.members if comm else None
    one = functools.partial(turned_block, members) if comm else block
    return call(
        functools.partial(output_kernel, count, members),
        (blocks,),
        [one(pixels, BLK), one(2, BLK), one(2, BLK), one(pixels, BLK), one(pixels, BLK)],
        [one(pixels, BLK), one(pixels, BLK), whole(blocks, 2, BLK)],
        [shape((blocks, pixels, BLK), BF16), shape((blocks, pixels, BLK)), shape((blocks, 2, BLK))],
        [],
        20 * pixels * blocks * BLK,
        comm,
    )(expanded, sums, params, x, grad)


def expand_back_kernel(
    count,
    exp_ref,
    sums_ref,
    prm_ref,
    up_ref,
    upsums_ref,
    w_ref,
    grp_ref,
    gsums_ref,
    gprm_ref,
    act_ref,
    wgrad_ref,
    out_ref,
    stat_ref,
    keep_ref,
):
    blocks, pixels, _ = keep_ref.shape
    step = pl.program_id(0)
    clear_stats(stat_ref)

    @pl.when(step < blocks)
    def _():
        coef = coefficients(sums_ref[0], prm_ref[0], count)
        scale = coef[2] * coef[1]
        up_mean = upsums_ref[0, 0:1] / count
        up_lean = upsums_ref[0, 1:2] / count

        def back(start, size):
            rows = pl.ds(start, size)
            standard, _ = standardize(exp_ref[0, rows], coef)
            values = (scale * (up_ref[0, rows] - up_mean - standard * up_lean)).astype(BF16)
            keep_ref[step, rows] = values

        over_rows(pixels, back)
        weight_grad_block(keep_ref[step], act_ref, wgrad_ref, 0)

    @pl.when(step >= blocks)
    def _():
        coef = coefficients(gsums_ref[0], gprm_ref[0], count)

        def body(start, size):
            rows = pl.ds(start, size)
            total = dot(keep_ref[0, rows], w_ref[0])
            for source in range(1, blocks):
                total += dot(keep_ref[source, rows], w_ref[source])
            standard, norm = standardize(grp_ref[0, rows], coef)
            up = total * silu_slope(norm)
            out_ref[0, rows] = up
            add_stats(stat_ref, step - blocks, up, up * standard)

        over_rows(pixels, body)


def expand_back(expanded, sums, params, up, upsums, weight, grouped, gsums, gparams, act, count, comm):
    blocks, pixels, _ = expanded.shape
    mids = grouped.shape[0]

    def first(*dims):
        return pl.BlockSpec((1,) + dims, lambda j: (jnp.minimum(j, blocks - 1),) + (0,) * len(dims))

    def second(*dims):
        return pl.BlockSpec((1,) + dims, lambda j: (jnp.maximum(j - blocks, 0),) + (0,) * len(dims))

    return call(
        functools.partial(expand_back_kernel, count),
        (blocks + mids,),
        [
            first(pixels, BLK),
            first(2, BLK),
            first(2, BLK),
            first(pixels, BLK),
            first(2, BLK),
            pl.BlockSpec((blocks, BLK, BLK), lambda j: (0, 0, jnp.maximum(j - blocks, 0))),
            second(pixels, BLK),
            second(2, BLK),
            second(2, BLK),
            Late((pixels, mids * BLK), BF16),
        ],
        [first(BLK, mids * BLK), second(pixels, BLK), whole(mids, 2, BLK)],
        [shape((blocks, BLK, mids * BLK), BF16), shape((mids, pixels, BLK)), shape((mids, 2, BLK))],
        [pltpu.VMEM((blocks, pixels, BLK), BF16)],
        4 * pixels * blocks * BLK * mids * BLK,
        comm,
    )(expanded, sums, params, up, upsums, weight, grouped, gsums, gparams, act)


def first_back(count, red_ref, sums_ref, prm_ref, rup_ref, rupsums_ref, back_ref, loads=()):
    mids, pixels, _ = red_ref.shape
    for mid in range(mids):
        for load in loads[2 * mid : 2 * mid + 2]:
            load.wait()
        coef = coefficients(sums_ref[mid], prm_ref[mid], count)
        scale = coef[2] * coef[1]
        up_mean = rupsums_ref[mid, 0:1] / count
        up_lean = rupsums_ref[mid, 1:2] / count

        def body(start, size):
            rows = pl.ds(start, size)
            standard, _ = standardize(red_ref[mid, rows], coef)
            values = scale * (rup_ref[mid, rows] - up_mean - standard * up_lean)
            back_ref[rows, mid * BLK : (mid + 1) * BLK] = values.astype(BF16)

        over_rows(pixels, body)


def weight_grad_block(left, right_ref, out_ref, slot):
    for first in range(0, right_ref.shape[1], BLK):
        columns = slice(first, first + BLK)
        out_ref[slot, :, columns] = dot(left, right_ref[:, columns], ((0,), (0,))).astype(BF16)


def reduce_back_kernel(count, red_ref, sums_ref, prm_ref, rup_ref, rupsums_ref, x_ref, up_ref, w_ref, grad_ref, wgrad_ref, back_ref):
    @pl.when(pl.program_id(0) == 0)
    def _():
        first_back(count, red_ref, sums_ref, prm_ref, rup_ref, rupsums_ref, back_ref)

    def product(start, size):
        rows = pl.ds(start, size)
        total = dot(back_ref[rows], w_ref[0], ((1,), (1,)))
        grad_ref[0, rows] = (up_ref[0, rows] + total).astype(BF16)

    over_rows(x_ref.shape[1], product)
    weight_grad_block(x_ref[0], back_ref, wgrad_ref, 0)


def reduce_back(reduced, sums, params, rup, rupsums, x, up, weight, count):
    mids, pixels, _ = reduced.shape
    blocks = x.shape[0]
    return call(
        functools.partial(reduce_back_kernel, count),
        (blocks,),
        [
            whole(mids, pixels, BLK),
            whole(mids, 2, BLK),
            whole(mids, 2, BLK),
            whole(mids, pixels, BLK),
            whole(mids, 2, BLK),
            block(pixels, BLK),
            block(pixels, BLK),
            block(BLK, mids * BLK),
        ],
        [block(pixels, BLK), block(BLK, mids * BLK)],
        [shape((blocks, pixels, BLK), BF16), shape((blocks, BLK, mids * BLK), BF16)],
        [pltpu.VMEM((pixels, mids * BLK), BF16)],
        4 * pixels * blocks * BLK * mids * BLK,
    )(reduced, sums, params, rup, rupsums, x, up, weight)


def exchange_kernel(batches, members, x_ref, out_ref, *scratch):
    row, me, across, along = devices(batches, members)
    greet(across + along)
    out_ref[...] = x_ref[...]
    total_stats(out_ref, across, along, *scratch)


def exchange(values, batches, members, collective_id):
    return pl.pallas_call(
        functools.partial(exchange_kernel, batches, members),
        in_specs=[pl.BlockSpec(memory_space=pltpu.VMEM)],
        out_specs=pl.BlockSpec(memory_space=pltpu.VMEM),
        out_shape=shape(values.shape),
        scratch_shapes=stats_scratch(values.shape, batches, members),
        compiler_params=pltpu.CompilerParams(collective_id=collective_id, has_side_effects=True),
    )(values)


def turn(source_ref, target_ref, slot, chunk):
    first = (49 * chunk) // 4

    @pl.loop(0, 13)
    def _(tile):
        columns = pl.ds(pl.multiple_of((first + tile) * HALF, HALF), HALF)
        rows = pl.ds(pl.multiple_of(tile * HALF, HALF), HALF)
        target_ref[slot, rows] = source_ref[:, columns].T


def turned(target_ref, slot, chunk, pixels):
    return target_ref.at[slot, pl.ds(pl.multiple_of(32 * (chunk % 4), 16), pixels)]


def opening_kernel(batches, members, *refs):
    x_ref, grad_ref, wr_ref, we_ref, wg_ref = refs[:5]
    vectors = refs[5:11]
    xp_ref, gradt_ref, wr_out, we_out, wg_out, prm_out = refs[11:17]
    xin, xturn, gin, gturn, prm_ref, load, own, xsend, xrecv, gsend, psend, precv = refs[17:29]
    zsend, zrecv, ysend, yrecv, fsend, frecv = refs[29:]
    row, me, across, along = devices(batches, members)
    pixels = xp_ref.shape[1]
    load_x = pltpu.make_async_copy(x_ref, xin, load.at[0])
    load_grad = pltpu.make_async_copy(grad_ref, gin, load.at[1])
    load_x.start()
    load_grad.start()
    weights = [(wr_ref, wr_out), (wg_ref, wg_out), (we_ref, we_out)]
    height, side = me // 2, me % 2
    levels = members // 2
    line = [(row, lax.rem(me + 2 * step, members)) for step in range(1, levels)]
    peer = (row, height * 2 + 1 - side)
    local_copies = []
    parts = []
    for index, (source, target) in enumerate(weights):
        size = source.shape[0] // batches
        part = pl.ds(pl.multiple_of(row * size, 16), size)
        parts.append(part)
        local_copies.append(pltpu.make_async_copy(source.at[part], target.at[height, side, part], own.at[index]))
    each(local_copies, "start")
    place = 0
    for vector in vectors:
        for low in range(0, vector.shape[0], HALF):
            prm_ref[place : place + 1] = vector[low : low + HALF].reshape(1, HALF)
            place += 1
    prm_own = pltpu.make_async_copy(prm_ref, prm_out.at[me], own.at[3])
    prm_own.start()
    greet(across + along)
    copies = [prm_own]
    first = []
    for index, (source, target) in enumerate(weights):
        for step, device in enumerate(line):
            first.append(
                remote(
                    source.at[parts[index]],
                    target.at[height, side, parts[index]],
                    zsend.at[index, step],
                    zrecv.at[index, step],
                    device,
                )
            )
    for step, device in enumerate(along):
        copy = remote(prm_ref, prm_out.at[me], psend.at[step], precv.at[step], device)
        copy.start()
        copies.append(copy)
    each(first, "start")
    load_x.wait()
    for step, device in enumerate(along):
        turn(xin, xturn, step, device[1])
        copy = remote(turned(xturn, step, device[1], pixels), xp_ref.at[me], xsend.at[step], xrecv.at[step], device)
        copy.start()
        copies.append(copy)
    last = members - 1
    turn(xin, xturn, last, me)
    copy = pltpu.make_async_copy(turned(xturn, last, me, pixels), xp_ref.at[me], xsend.at[last])
    copy.start()
    copies.append(copy)
    load_grad.wait()
    for member in range(members):
        turn(gin, gturn, member, member)
        copy = pltpu.make_async_copy(turned(gturn, member, member, pixels), gradt_ref.at[member], gsend.at[member])
        copy.start()
        copies.append(copy)
    each(local_copies, "wait")
    far, near = (lax.bitwise_xor(row, 2), me), (lax.bitwise_xor(row, 1), me)
    second, third = [], []
    for index, (_, target) in enumerate(weights):
        each(first[index * len(line) : (index + 1) * len(line)], "wait")
        held = target.at[:, side, parts[index]]
        second.append(remote(held, held, ysend.at[index], yrecv.at[index], peer))
        second[-1].start()
    for index, (_, target) in enumerate(weights):
        second[index].wait()
        held = target.at[:, :, parts[index]]
        third.append(remote(held, held, fsend.at[index, 0], frecv.at[index, 0], far))
        third[-1].start()
    for index, (source, target) in enumerate(weights):
        size = source.shape[0] // batches
        third[index].wait()
        for step, origin in enumerate((row, lax.bitwise_xor(row, 2))):
            held = target.at[:, :, pl.ds(pl.multiple_of(origin * size, 16), size)]
            copy = remote(held, held, fsend.at[index, 1 + step], frecv.at[index, 1 + step], near)
            copy.start()
            copies.append(copy)
    each(copies, "wait")


def opening(block_input, out_grad, reduce_weight, expand_weight, taps, vectors, batches, members):
    channels, row_pixels = block_input.shape
    pixels = row_pixels // members
    dma = pltpu.SemaphoreType.DMA
    other, across, levels = members - 1, batches - 1, members // 2
    padded = 13 * HALF
    lines = sum(vector.shape[0] for vector in vectors) // HALF
    weights = [reduce_weight, expand_weight, taps]
    x, grad, *gathered, params = pl.pallas_call(
        functools.partial(opening_kernel, batches, members),
        in_specs=[pl.BlockSpec(memory_space=pl.ANY)] * 5 + [pl.BlockSpec(memory_space=pltpu.VMEM)] * len(vectors),
        out_specs=[pl.BlockSpec(memory_space=pl.ANY)] * 6,
        out_shape=[shape((members, pixels, channels), BF16)] * 2
        + [shape((levels, 2) + weight.shape, BF16) for weight in weights]
        + [shape((members, lines, HALF))],
        scratch_shapes=[
            pltpu.VMEM((channels, row_pixels), BF16),
            pltpu.VMEM((members, padded, channels), BF16),
            pltpu.VMEM((channels, row_pixels), BF16),
            pltpu.VMEM((members, padded, channels), BF16),
            pltpu.VMEM((lines, HALF), F32),
            dma((2,)),
            dma((4,)),
            dma((members,)),
            dma((other,)),
            dma((members,)),
            dma((other,)),
            dma((other,)),
            dma((3, levels - 1)),
            dma((3, levels - 1)),
            dma((3,)),
            dma((3,)),
            dma((3, across)),
            dma((3, across)),
        ],
        compiler_params=pltpu.CompilerParams(vmem_limit_bytes=VMEM_LIMIT, collective_id=0, has_side_effects=True),
    )(block_input, out_grad, *weights, *vectors)
    gathered = [full.reshape((members,) + full.shape[2:]) for full in gathered]
    return x, grad, *gathered, params


class Reduce:
    def __init__(self, part, out, row, me, refs, source=None):
        self.part, self.out, self.row = part, out, row
        self.source = part if source is None else source
        self.height, self.side = me // 2, me % 2
        self.place, self.core = row // 2, row % 2
        self.fresh, self.chip, self.cross, self.held, self.pair, self.line, self.second, self.total = refs[:8]
        self.send, self.recv = refs[8:]
        self.levels = self.held.shape[0]
        self.size = self.total.shape[0]
        self.near = (self.place * 2 + 1 - self.core, me)
        self.far = ((1 - self.place) * 2 + self.core, me)
        self.peer = (row, self.height * 2 + 1 - self.side)
        self.along = [(row, lax.rem(me + 2 * step, 2 * self.levels)) for step in range(1, self.levels)]

    def rows(self, row):
        return pl.ds(pl.multiple_of(row * self.size, 16), self.size)

    def copy(self, source, target, index, device):
        return remote(source, target, self.send.at[index], self.recv.at[index], device)

    def over_cores(self):
        return [
            self.copy(self.source.at[:, self.rows(2 * place + 1 - self.core)], self.fresh.at[place], place, self.near)
            for place in range(2)
        ]

    def add_cores(self):
        @pl.loop(0, 2 * self.levels)
        def _(member):
            for place in range(2):
                total = self.part[member, self.rows(2 * place + self.core)].astype(F32)
                self.chip[place, member] = (total + self.fresh[place, member].astype(F32)).astype(BF16)

    def over_x(self):
        return [self.copy(self.chip.at[1 - self.place], self.cross, 2, self.far)]

    def add_x(self):
        @pl.loop(0, self.levels)
        def _(level):
            for side in range(2):
                member = 2 * level + side
                total = self.chip[self.place, member].astype(F32) + self.cross[member].astype(F32)
                self.held[level, side] = total.astype(BF16)

    def over_pair(self):
        return [self.copy(self.held.at[:, 1 - self.side], self.pair, 3, self.peer)]

    def add_pair(self):
        @pl.loop(0, self.levels)
        def _(level):
            total = self.held[level, self.side].astype(F32) + self.pair[level].astype(F32)
            self.line[level] = total.astype(BF16)

    def over_line(self):
        return [
            self.copy(self.line.at[device[1] // 2], self.second.at[step], 4 + step, device)
            for step, device in enumerate(self.along)
        ]

    def add_line(self):
        total = self.line[self.height].astype(F32)
        for step in range(len(self.along)):
            total += self.second[step].astype(F32)
        self.total[...] = total

    def keep(self):
        return [pltpu.make_async_copy(self.total, self.out.at[self.rows(self.row)], self.send.at[10])]

    def share_x(self):
        return [self.copy(self.total, self.out.at[self.rows(self.row)], 7, self.far)]

    def share_cores(self):
        own = self.copy(self.total, self.out.at[self.rows(self.row)], 8, self.near)
        rows = self.rows((1 - self.place) * 2 + self.core)
        return [own, self.copy(self.out.at[rows], self.out.at[rows], 9, self.near)]


def reduce_scratch(dims, batches, members):
    rows, columns = dims[1] // batches, dims[2]
    levels = members // 2
    return [
        pltpu.VMEM((2, members, rows, columns), BF16),
        pltpu.VMEM((2, members, rows, columns), BF16),
        pltpu.VMEM((members, rows, columns), BF16),
        pltpu.VMEM((levels, 2, rows, columns), BF16),
        pltpu.VMEM((levels, rows, columns), BF16),
        pltpu.VMEM((levels, rows, columns), BF16),
        pltpu.VMEM((levels - 1, rows, columns), BF16),
        pltpu.VMEM((rows, columns), F32),
        pltpu.SemaphoreType.DMA((11,)),
        pltpu.SemaphoreType.DMA((10,)),
    ]


HELD_BACK = 2
EARLY = 3


def closing_steps(step, members):
    late = jnp.maximum(step - members, EARLY)
    return jnp.where(step < EARLY, step, late), jnp.clip(step - EARLY, 0, members - 1)


def closing_kernel(count, batches, members, low, size, *refs):
    red_ref, sums_ref, prm_ref, rup_ref, rupsums_ref, x_ref, up_ref, w_ref, epart_ref, tpart_ref, src_ref, _ = refs[:12]
    recv_ref, rout_ref, eout_ref, tout_ref, dst_ref = refs[12:17]
    back_ref, grad_ref, wpart_ref, gsend, grecv, psend, precv = refs[17:24]
    red_held, rup_held, epart_held, load_sem = refs[54:]
    row, me, across, along = devices(batches, members)
    step = pl.program_id(0)
    last = members - 1
    expand_sum = Reduce(epart_held, eout_ref, row, me, refs[24:34], epart_ref)
    taps_sum = Reduce(tpart_ref, tout_ref, row, me, refs[34:44])
    reduce_sum = Reduce(wpart_ref, rout_ref, row, me, refs[44:54])
    parts = (expand_sum, taps_sum, reduce_sum)
    grad_step, weight_step = closing_steps(step, members)

    def pieces():
        return piece_copies(src_ref, dst_ref, low, size, me, along, psend, precv)

    def send(index):
        device = (row, lax.rem(me + 1 + index, members))
        return remote(grad_ref.at[index], recv_ref.at[me], gsend.at[index], grecv.at[index], device)

    mids = red_held.shape[0]
    load_part = pltpu.make_async_copy(epart_ref, epart_held, load_sem.at[2 * mids])

    @pl.when(step == 0)
    def _():
        greet(across + along)
        each(pieces(), "start")
        loads = []
        for mid in range(mids):
            for which, (source, held) in enumerate(((red_ref, red_held), (rup_ref, rup_held))):
                loads.append(pltpu.make_async_copy(source.at[mid], held.at[mid], load_sem.at[2 * mid + which]))
        each(loads, "start")
        load_part.start()
        each(expand_sum.over_cores(), "start")
        each(taps_sum.over_cores(), "start")
        first_back(count, red_held, sums_ref, prm_ref, rup_held, rupsums_ref, back_ref, loads)

    weight_turn = (step >= EARLY) & (step < EARLY + members)

    @pl.when(weight_turn)
    def _():
        weight_grad_block(x_ref[0], back_ref, wpart_ref, lax.rem(me + 1 + weight_step, members))

    @pl.when(jnp.logical_not(weight_turn))
    def _():
        def product(start, size):
            part = pl.ds(start, size)
            total = dot(back_ref[part], w_ref[0], ((1,), (1,)))
            grad_ref[grad_step, part] = (up_ref[0, part] + total).astype(BF16)

        over_rows(x_ref.shape[1], product)

        @pl.when(grad_step < last - HELD_BACK)
        def _():
            send(grad_step).start()

    @pl.when(step == EARLY)
    def _():
        load_part.wait()
        for part in parts[:2]:
            each(part.over_cores(), "wait")
            part.add_cores()
            each(part.over_x(), "start")

    @pl.when(step == EARLY + members - 1)
    def _():
        each(reduce_sum.over_cores(), "start")
        for part in parts[:2]:
            each(part.over_x(), "wait")
            part.add_x()
            each(part.over_pair(), "start")

    @pl.when(step == EARLY + members)
    def _():
        each(reduce_sum.over_cores(), "wait")
        reduce_sum.add_cores()
        each(reduce_sum.over_x(), "start")

    @pl.when(step == 2 * members - 1)
    def _():
        own = pltpu.make_async_copy(grad_ref.at[last], recv_ref.at[me], gsend.at[last])
        own.start()
        for part in parts[:2]:
            each(part.over_pair(), "wait")
            part.add_pair()
            each(part.over_line(), "start")
        each(reduce_sum.over_x(), "wait")
        reduce_sum.add_x()
        each(reduce_sum.over_pair(), "start")
        each(reduce_sum.over_pair(), "wait")
        reduce_sum.add_pair()
        each(reduce_sum.over_line(), "start")
        for index in range(last - HELD_BACK, last):
            send(index).start()
        for part in parts:
            each(part.over_line(), "wait")
            part.add_line()
            each(part.share_x() + part.keep(), "start")
        for part in parts:
            each(part.share_x(), "wait")
            each(part.share_cores(), "start")
        own.wait()
        each(pieces(), "wait")
        for index in range(last):
            send(index).wait()
        for part in parts:
            each(part.share_cores() + part.keep(), "wait")


def closing(
    reduced, sums, params, rup, rupsums, x, up, weight, epart, tpart, source, into, low, size, count, batches, members
):
    mids, pixels, _ = reduced.shape
    blocks = x.shape[0]
    once = pl.Buffered(1)

    def keep(*dims):
        return pl.BlockSpec(dims, lambda j: (0,) * len(dims), pipeline_mode=once)

    def turn_block(which, *dims):
        def index(j):
            return (lax.rem(lax.axis_index("group") + 1 + closing_steps(j, members)[which], members),) + (0,) * len(dims)

        return pl.BlockSpec((1,) + dims, index)

    anywhere = pl.BlockSpec(memory_space=pl.ANY)
    dma = pltpu.SemaphoreType.DMA
    wdims = (blocks, BLK, mids * BLK)
    scratch = [
        pltpu.VMEM((pixels, mids * BLK), BF16),
        pltpu.VMEM((blocks, pixels, BLK), BF16),
        pltpu.VMEM(wdims, BF16),
        dma((members,)),
        dma((members - 1,)),
        dma((members,)),
        dma((members - 1,)),
    ]
    for dims in (wdims, tpart.shape, wdims):
        scratch += reduce_scratch(dims, batches, members)
    scratch += [
        pltpu.VMEM((mids, pixels, BLK), F32),
        pltpu.VMEM((mids, pixels, BLK), F32),
        pltpu.VMEM(wdims, BF16),
        dma((2 * mids + 1,)),
    ]
    return pl.pallas_call(
        functools.partial(closing_kernel, count, batches, members, low, size),
        grid=(2 * blocks,),
        in_specs=[
            anywhere,
            keep(mids, 2, BLK),
            keep(mids, 2, BLK),
            anywhere,
            keep(mids, 2, BLK),
            turn_block(1, pixels, BLK),
            turn_block(0, pixels, BLK),
            turn_block(0, BLK, mids * BLK),
            anywhere,
            keep(*tpart.shape),
            anywhere,
            anywhere,
        ],
        out_specs=[anywhere] * 5,
        out_shape=[
            shape((members, pixels, BLK), BF16),
            shape(wdims[1:]),
            shape(wdims[1:]),
            shape(tpart.shape[1:]),
            shape(source.shape, BF16),
        ],
        scratch_shapes=scratch,
        input_output_aliases={11: 4},
        compiler_params=pltpu.CompilerParams(vmem_limit_bytes=VMEM_LIMIT, collective_id=7, has_side_effects=True),
    )(reduced, sums, params, rup, rupsums, x, up, weight, epart, tpart, source, into)


def turn_out_kernel(first_ref, second_ref, first_out, second_out):
    own = lax.broadcasted_iota(jnp.int32, (BLK, BLK), 0) == lax.broadcasted_iota(jnp.int32, (BLK, BLK), 1)
    identity = jnp.where(own, 1.0, 0.0).astype(BF16)
    half = pl.num_programs(0) // 2

    def turn_part(in_ref, out_ref):
        for low in range(0, in_ref.shape[0], HALF):
            part = dot(identity, in_ref[low : low + HALF], ((1,), (1,)))
            out_ref[:, low : low + HALF] = part.astype(out_ref.dtype)

    @pl.when(pl.program_id(0) < half)
    def _():
        turn_part(first_ref, first_out)

    @pl.when(pl.program_id(0) >= half)
    def _():
        turn_part(second_ref, second_out)


def turn_out(first, second):
    rows, channels = first.shape
    parts = 2
    size = rows // parts

    def early(j):
        return jnp.minimum(j, parts - 1)

    def late(j):
        return jnp.maximum(j - parts, 0)

    return call(
        turn_out_kernel,
        (2 * parts,),
        [
            pl.BlockSpec((size, channels), lambda j: (early(j), 0)),
            pl.BlockSpec((size, channels), lambda j: (late(j), 0)),
        ],
        [
            pl.BlockSpec((channels, size), lambda j: (0, early(j))),
            pl.BlockSpec((channels, size), lambda j: (0, late(j))),
        ],
        [shape((channels, rows)), shape((channels, rows), BF16)],
        [],
        4 * rows * channels * BLK,
    )(first, second)


def own_kernel(reduce_ref, group_ref, expand_ref, *outs):
    me = lax.axis_index("group")
    half = pl.ds(pl.multiple_of((me % 2) * HALF, HALF), HALF)
    for index, stats_ref in enumerate((reduce_ref, group_ref)):
        for which in range(2):
            outs[2 * index + 1 - which][...] = stats_ref[me // 2, which : which + 1, half]
    for which in range(2):
        outs[5 - which][...] = expand_ref[me, which : which + 1]


def own_parts(reduce_stats, group_stats, expand_stats):
    sizes = (HALF,) * 4 + (BLK,) * 2
    outs = pl.pallas_call(own_kernel, out_shape=[shape((1, size)) for size in sizes])(
        reduce_stats, group_stats, expand_stats
    )
    return tuple(out.reshape(-1) for out in outs)


def pixel_masks(pixels):
    place = np.arange(pixels)
    tall, wide = (place // SIDE) % SIDE, place % SIDE
    masks = np.stack([wide != 0, wide != SIDE - 1, tall != 0, tall != SIDE - 1])
    return jnp.asarray(np.broadcast_to(masks[:, :, None], (4, pixels, HALF)).astype(np.float32))


def own_part(stats, which, length):
    return lax.dynamic_slice_in_dim(stats[:, which].reshape(-1), lax.axis_index("group") * length, length, 0)


TAP_ROWS = 320


def fused(
    block_input,
    reduce_weight,
    reduce_gain,
    reduce_bias,
    group_weight,
    group_gain,
    group_bias,
    expand_weight,
    expand_gain,
    expand_bias,
    out_grad,
):
    batches, members = lax.axis_size("batch"), lax.axis_size("group")
    channels, row_pixels = block_input.shape
    pixels = row_pixels // members
    count = row_pixels * batches
    vectors = [reduce_gain, reduce_bias, group_gain, group_bias, expand_gain, expand_bias]
    taps = group_weight.reshape(-1, 9, GW, GW).transpose(1, 2, 0, 3).reshape(9 * GW, HALF)
    taps = jnp.pad(taps, ((0, TAP_ROWS - 9 * GW), (0, 0)))
    masks = pixel_masks(pixels)
    x, grad_turned, reduce_full, expand_full, taps_full, packs = opening(
        block_input, out_grad, reduce_weight, expand_weight, taps, vectors, batches, members
    )
    vectors = packs[:, :4].reshape(-1, 2, 4, HALF).transpose(0, 2, 1, 3).reshape(-1, 4, BLK)
    reduce_params, group_params = vectors[:, :2], vectors[:, 2:]
    expand_params = packs[:, 4:].reshape(-1, 2, BLK)

    comm = functools.partial(Comm, batches, members)
    sends = comm(1, grad_turned, 0, (208, 240))
    reduced, reduce_sums, grad = reduce_product(x, reduce_full, sends)
    sends = comm(2, grad_turned, sends.high, (336, 224), grad)
    grouped, group_sums, grad = conv(reduced, reduce_sums, reduce_params, taps_full, masks, count, sends)
    sends = comm(3, grad_turned, sends.high, (pixels - sends.high - 224, 224), grad)
    expanded, act, expand_sums, grad = expand_product(grouped, group_sums, group_params, expand_full, count, sends)
    sends = comm(4, None, 0, (224, 112), None, True)
    out, upstream, expand_stats, moved = output(expanded, expand_sums, expand_params, x, grad, count, sends)
    sends = comm(5, out, sends.high, (384, 96), moved)
    expand_part, group_up, group_stats, moved = expand_back(
        expanded,
        expand_sums,
        expand_params,
        upstream,
        expand_stats,
        expand_full,
        grouped,
        group_sums,
        group_params,
        act,
        count,
        sends,
    )
    sends = comm(6, out, sends.high, (496, 112), moved)
    reduce_up, taps_part, reduce_stats, moved = conv_back(
        reduced,
        reduce_sums,
        reduce_params,
        grouped,
        group_sums,
        group_params,
        group_up,
        group_stats,
        taps_full,
        masks,
        count,
        sends,
    )
    inner, reduce_weight_grad, expand_weight_grad, taps_grad, moved = closing(
        reduced,
        reduce_sums,
        reduce_params,
        reduce_up,
        reduce_stats,
        x,
        upstream,
        reduce_full,
        expand_part,
        taps_part,
        out,
        moved,
        sends.high,
        pixels - sends.high,
        count,
        batches,
        members,
    )
    input_grad, block_output = turn_out(inner.reshape(row_pixels, channels), moved.reshape(row_pixels, channels))
    taps_grad = taps_grad[: 9 * GW].reshape(9, GW, -1, GW).transpose(2, 0, 3, 1)
    return (
        block_output,
        input_grad,
        reduce_weight_grad,
        taps_grad.reshape(group_weight.shape),
        expand_weight_grad,
    ) + own_parts(reduce_stats, group_stats, expand_stats)


def modular(
    block_input,
    reduce_weight,
    reduce_gain,
    reduce_bias,
    group_weight,
    group_gain,
    group_bias,
    expand_weight,
    expand_gain,
    expand_bias,
    out_grad,
):
    batches, members = lax.axis_size("batch"), lax.axis_size("group")
    channels, row_pixels = block_input.shape
    pixels = row_pixels // members
    count = row_pixels * batches
    mid_total = reduce_weight.shape[1]
    mids = mid_total // BLK
    blocks = channels * members // BLK
    me = lax.axis_index("group")

    def to_pixels(values):
        moved = lax.all_to_all(values.T.reshape(members, pixels, channels), "group", 0, 0)
        if channels == BLK:
            return moved
        share = BLK // channels
        moved = moved.reshape(blocks, share, pixels, channels).transpose(0, 2, 1, 3)
        return moved.reshape(blocks, pixels, BLK)

    def to_channels(values):
        if channels != BLK:
            share = BLK // channels
            values = values.reshape(blocks, pixels, share, channels).transpose(0, 2, 1, 3)
            values = values.reshape(members, pixels, channels)
        moved = lax.all_to_all(values, "group", 0, 0)
        return moved.reshape(row_pixels, channels).T

    def gather(values):
        return lax.all_gather(values, "group", axis=0, tiled=True)

    local_mid = reduce_gain.shape[0]
    pack = jnp.concatenate([reduce_gain, reduce_bias, group_gain, group_bias, expand_gain, expand_bias])
    packs = gather(pack[None])
    vectors, offset = [], 0
    for length in (local_mid, local_mid, local_mid, local_mid, channels, channels):
        vectors.append(packs[:, offset : offset + length].reshape(-1, BLK))
        offset += length
    reduce_params = jnp.stack(vectors[0:2], 1)
    group_params = jnp.stack(vectors[2:4], 1)
    expand_params = jnp.stack(vectors[4:6], 1)
    reduce_full = gather(reduce_weight).reshape(blocks, BLK, mid_total)
    expand_full = gather(expand_weight).reshape(blocks, BLK, mid_total)
    taps = gather(group_weight.reshape(group_weight.shape[0], 9, GW, GW))
    taps = taps.reshape(-1, HALF // GW, 9, GW, GW).transpose(0, 2, 3, 1, 4).reshape(-1, 9 * GW, HALF)
    taps = jnp.pad(taps, ((0, 0), (0, TAP_ROWS - 9 * GW), (0, 0)))
    masks = pixel_masks(pixels)

    x = to_pixels(block_input)
    grad = to_pixels(out_grad)

    reduced, reduce_sums = reduce_product(x, reduce_full, None)
    reduce_sums = exchange(reduce_sums, batches, members, 1)
    grouped, group_sums = conv(reduced, reduce_sums, reduce_params, taps, masks, count, None)
    group_sums = exchange(group_sums, batches, members, 1)
    expanded, act, expand_sums = expand_product(grouped, group_sums, group_params, expand_full, count, None)
    expand_sums = exchange(expand_sums, batches, members, 2)
    out, upstream, expand_stats = output(expanded, expand_sums, expand_params, x, grad, count, None)
    expand_stats = exchange(expand_stats, batches, members, 2)
    expand_part, group_up, group_stats = expand_back(
        expanded, expand_sums, expand_params, upstream, expand_stats, expand_full, grouped, group_sums, group_params, act, count, None
    )
    group_stats = exchange(group_stats, batches, members, 1)
    reduce_up, taps_part, reduce_stats = conv_back(
        reduced,
        reduce_sums,
        reduce_params,
        grouped,
        group_sums,
        group_params,
        group_up,
        group_stats,
        taps,
        masks,
        count,
        None,
    )
    reduce_stats = exchange(reduce_stats, batches, members, 1)
    inner, reduce_part = reduce_back(
        reduced, reduce_sums, reduce_params, reduce_up, reduce_stats, x, upstream, reduce_full, count
    )
    block_output = to_channels(out)
    input_grad = to_channels(inner).astype(F32)

    def shared_sum(part):
        rows = channels // batches
        part = part.reshape(members, batches, rows, mid_total).transpose(1, 0, 2, 3)
        part = lax.all_to_all(part, "batch", 0, 0).astype(F32).sum(0).astype(BF16)
        part = lax.all_to_all(part, "group", 0, 0).astype(F32).sum(0)
        return lax.all_gather(part, "batch", axis=0, tiled=True)

    expand_weight_grad = shared_sum(expand_part)
    reduce_weight_grad = shared_sum(reduce_part)
    taps_part = taps_part[:, : 9 * GW].reshape(-1, 9, GW, HALF // GW, GW).transpose(0, 3, 1, 4, 2)
    taps_part = taps_part.reshape(members, -1, 9, GW, GW)
    group_weight_grad = lax.all_to_all(taps_part, "group", 0, 0).astype(F32).sum(0)
    group_weight_grad = lax.psum(group_weight_grad, "batch").reshape(group_weight.shape)

    return (
        block_output,
        input_grad,
        reduce_weight_grad,
        group_weight_grad,
        expand_weight_grad,
        own_part(reduce_stats, 1, local_mid),
        own_part(reduce_stats, 0, local_mid),
        own_part(group_stats, 1, local_mid),
        own_part(group_stats, 0, local_mid),
        own_part(expand_stats, 1, channels),
        own_part(expand_stats, 0, channels),
    )


def local(*args):
    block_input = args[0]
    pixels = block_input.shape[1] // lax.axis_size("group")
    if block_input.shape[0] == BLK and pixels == 1568 and args[2].shape[0] == HALF and lax.axis_size("group") == 8:
        return fused(*args)
    return modular(*args)


def solution(mesh):
    in_specs = (
        P("group", "batch"),
        P("group", None),
        P("group"),
        P("group"),
        P("group", None, None, None, None),
        P("group"),
        P("group"),
        P("group", None),
        P("group"),
        P("group"),
        P("group", "batch"),
    )
    out_specs = (
        P("group", "batch"),
        P("group", "batch"),
        P("group", None),
        P("group", None, None, None, None),
        P("group", None),
        P("group"),
        P("group"),
        P("group"),
        P("group"),
        P("group"),
        P("group"),
    )
    return jax.shard_map(local, mesh=mesh, in_specs=in_specs, out_specs=out_specs, check_vma=False)
```

```python
import functools

import jax
import jax.numpy as jnp
import numpy as np
from jax import lax
from jax.experimental import pallas as pl
from jax.experimental.pallas import tpu as pltpu
from jax.sharding import PartitionSpec as P

GW = 32
SIDE = 14
EPS = 1e-05
BLK = 256
HALF = 128
PAD = 16
F32 = jnp.float32
BF16 = jnp.bfloat16
MESH = pl.DeviceIdType.MESH
VMEM_LIMIT = 60 * 1024 * 1024


def silu_slope(values):
    sigma = jax.nn.sigmoid(values)
    return sigma * (1.0 + values * (1.0 - sigma))


def row_chunk(pixels):
    for size in (224, 208, 192, 176, 160, 144, 128, 112):
        if pixels % size == 0:
            return size
    return pixels


def over_rows(pixels, body):
    size = row_chunk(pixels)
    if size == pixels:
        body(0, size)
    else:

        @pl.loop(0, pixels // size)
        def _(step):
            body(pl.multiple_of(step * size, 16), size)


def coefficients(sums, params, count):
    center = sums[0:1] / count
    spread = sums[1:2] / count - center * center
    inverse = lax.rsqrt(spread + EPS)
    return center, inverse, params[0:1], params[1:2]


def standardize(values, coef):
    standard = (values - coef[0]) * coef[1]
    return standard, standard * coef[2] + coef[3]


def add_stats(ref, slot, first, second):
    ref[slot, 0:1] += jnp.sum(first, 0, keepdims=True)
    ref[slot, 1:2] += jnp.sum(second, 0, keepdims=True)


PHASE_START = [0]


def grid_step():
    return pl.program_id(0) - PHASE_START[-1]


def in_phase(start, steps, body):
    step = pl.program_id(0)

    @pl.when((step >= start) & (step < start + steps))
    def _():
        PHASE_START.append(start)
        try:
            body()
        finally:
            PHASE_START.pop()


def phase_block(start, steps, *dims):
    return pl.BlockSpec((1,) + dims, lambda j: (jnp.clip(j - start, 0, steps - 1),) + (0,) * len(dims))


def clear_stats(ref):
    @pl.when(grid_step() == 0)
    def _():
        ref[...] = jnp.zeros_like(ref)


def dot(a, b, dims=((1,), (0,))):
    return lax.dot_general(a, b, (dims, ((), ())), preferred_element_type=F32)


def devices(batches, members):
    row, me = lax.axis_index("batch"), lax.axis_index("group")
    across = [(lax.rem(row + step, batches), me) for step in range(1, batches)]
    along = [(row, lax.rem(me + step, members)) for step in range(1, members)]
    return row, me, across, along


def greet(others):
    barrier = pltpu.get_barrier_semaphore()
    for device in others:
        pl.semaphore_signal(barrier, inc=1, device_id=device, device_id_type=MESH)
    pl.semaphore_wait(barrier, len(others))


def remote(source, target, send, recv, device):
    return pltpu.make_async_remote_copy(
        src_ref=source, dst_ref=target, send_sem=send, recv_sem=recv, device_id=device, device_id_type=MESH
    )


def each(copies, what):
    for copy in copies:
        getattr(copy, what)()


def spread(source, target, send, recv, others, beside):
    copies = [
        remote(source, target.at[step], send.at[step], recv.at[step], device) for step, device in enumerate(others)
    ]
    each(copies, "start")
    each(beside, "start")
    each(copies, "wait")


def total_stats(ref, across, along, first_ref, second_ref, mid_ref, send1, recv1, send2, recv2, beside=()):
    mid_ref[0] = ref[...]
    spread(mid_ref.at[0], second_ref, send2, recv2, along, beside)
    total = mid_ref[0]
    for step in range(len(along)):
        total += second_ref[step]
    mid_ref[1] = total
    spread(mid_ref.at[1], first_ref, send1, recv1, across, ())
    for step in range(len(across)):
        total += first_ref[step]
    ref[...] = total


def stats_scratch(dims, batches, members):
    return [
        pltpu.VMEM((batches - 1,) + dims, F32),
        pltpu.VMEM((members - 1,) + dims, F32),
        pltpu.VMEM((2,) + dims, F32),
        pltpu.SemaphoreType.DMA((batches - 1,)),
        pltpu.SemaphoreType.DMA((batches - 1,)),
        pltpu.SemaphoreType.DMA((members - 1,)),
        pltpu.SemaphoreType.DMA((members - 1,)),
    ]


class Comm:
    def __init__(self, batches, members, collective_id, source=None, low=0, sizes=(), into=None, stream=False):
        self.batches, self.members, self.collective_id = batches, members, collective_id
        self.source, self.low, self.sizes, self.into, self.stream = source, low, sizes, into, stream
        self.high = low + sum(sizes)


def piece_copies(source, target, low, size, me, along, send, recv, staged=False):
    rows = pl.ds(low, size)
    last = len(along)
    copies = [
        remote(
            source.at[step if staged else device[1], rows], target.at[me, rows], send.at[step], recv.at[step], device
        )
        for step, device in enumerate(along)
    ]
    return copies + [
        pltpu.make_async_copy(source.at[last if staged else me, rows], target.at[me, rows], send.at[last])
    ]


class Late:
    def __init__(self, dims, dtype=F32):
        self.dims, self.dtype = dims, dtype


def call(kernel, grid, in_specs, out_specs, out_shape, scratch, flops, comm=None):
    if comm is None:
        in_specs = [whole(*spec.dims) if isinstance(spec, Late) else spec for spec in in_specs]
        return functools.partial(
            plain_call, kernel, grid, in_specs, out_specs, out_shape, scratch, flops, pltpu.CompilerParams(vmem_limit_bytes=VMEM_LIMIT)
        )
    n_in, n_out, n_scratch = len(in_specs), len(out_specs), len(scratch)
    stats = out_shape[-1].shape
    batches, members = comm.batches, comm.members

    sends = bool(comm.sizes)
    late = [index for index, spec in enumerate(in_specs) if isinstance(spec, Late)]
    late_specs = [in_specs[index] for index in late]

    def wrapped(*refs):
        refs = list(refs)
        ins = refs[:n_in]
        del refs[:n_in]
        source = refs.pop(0) if sends and not comm.stream else None
        if comm.into is not None:
            refs.pop(0)
        outs = refs[:n_out]
        del refs[:n_out]
        target = refs.pop(0) if sends else None
        own = refs[:n_scratch]
        del refs[:n_scratch]
        stats_refs = refs[:7]
        del refs[:7]
        if comm.stream:
            source = refs.pop(0)
        loads = []
        if late:
            load_sem = refs.pop(0)
            for place, index in enumerate(late):
                held = refs.pop(0)
                loads.append(pltpu.make_async_copy(ins[index], held, load_sem.at[place]))
                ins[index] = held
        row, me, across, along = devices(batches, members)
        step = pl.program_id(0)

        def copies(part):
            low = comm.low + sum(comm.sizes[:part])
            return piece_copies(
                source, target, low, comm.sizes[part], me, along, refs[0].at[part], refs[1].at[part], comm.stream
            )

        @pl.when(step == 0)
        def _():
            greet(across + along)
            if sends and not comm.stream:
                each(copies(0), "start")
            each(loads, "start")
            each(loads, "wait")

        kernel(*ins, *outs, *own)
        if comm.stream:
            source[step] = outs[0][0, : comm.high]
            rows = pl.ds(0, comm.sizes[0])

            @pl.when(step < members - 1)
            def _():
                device = (row, lax.rem(me + 1 + step, members))
                remote(
                    source.at[step, rows], target.at[me, rows], refs[0].at[0, step], refs[1].at[0, step], device
                ).start()

            @pl.when(step == members - 1)
            def _():
                pltpu.make_async_copy(source.at[step, rows], target.at[me, rows], refs[0].at[0, step]).start()

        @pl.when(step == pl.num_programs(0) - 1)
        def _():
            total_stats(outs[-1], across, along, *stats_refs, beside=copies(1) if sends else ())
            if sends:
                for part in range(2):
                    each(copies(part), "wait")

    scratch = list(scratch) + stats_scratch(stats, batches, members)
    in_specs, out_specs, out_shape = list(in_specs), list(out_specs), list(out_shape)
    extra, aliases = [], {}
    if sends:
        if comm.stream:
            dims, dtype = out_shape[0].shape, out_shape[0].dtype
            scratch.append(pltpu.VMEM((members, comm.high, dims[2]), dtype))
        else:
            dims, dtype = comm.source.shape, comm.source.dtype
            extra = [comm.source]
        if comm.into is not None:
            aliases = {len(in_specs) + len(extra): len(out_specs)}
            extra.append(comm.into)
        in_specs = [pl.BlockSpec(memory_space=pl.ANY) if isinstance(spec, Late) else spec for spec in in_specs]
        in_specs += [pl.BlockSpec(memory_space=pl.ANY)] * len(extra)
        if late:
            scratch.append(pltpu.SemaphoreType.DMA((len(late),)))
            scratch += [pltpu.VMEM(spec.dims, spec.dtype) for spec in late_specs]
        out_specs.append(pl.BlockSpec(memory_space=pl.ANY))
        out_shape.append(shape(dims, dtype))
        scratch += [pltpu.SemaphoreType.DMA((2, members)), pltpu.SemaphoreType.DMA((2, members - 1))]
    params = pltpu.CompilerParams(
        vmem_limit_bytes=VMEM_LIMIT, collective_id=comm.collective_id, has_side_effects=True
    )
    inner = functools.partial(
        plain_call, wrapped, grid, in_specs, out_specs, out_shape, scratch, flops, params, aliases=aliases
    )
    return lambda *args: inner(*args, *extra)


def plain_call(kernel, grid, in_specs, out_specs, out_shape, scratch, flops, params, *args, aliases={}):
    return pl.pallas_call(
        kernel,
        grid=grid,
        in_specs=in_specs,
        out_specs=out_specs,
        out_shape=out_shape,
        scratch_shapes=scratch,
        input_output_aliases=aliases,
        compiler_params=params,
        cost_estimate=pl.CostEstimate(flops=flops, bytes_accessed=20_000_000, transcendentals=0),
    )(*args)


def shape(dims, dtype=F32):
    return jax.ShapeDtypeStruct(dims, dtype)


def block(*dims):
    return pl.BlockSpec((1,) + dims, lambda j: (j,) + (0,) * len(dims))


def turned_block(members, *dims):
    def index(j):
        return (lax.rem(lax.axis_index("group") + 1 + j, members),) + (0,) * len(dims)

    return pl.BlockSpec((1,) + dims, index)


def whole(*dims):
    return pl.BlockSpec(dims, lambda j: (0,) * len(dims))


def reduce_kernel(x_ref, w_ref, out_ref, sum_ref):
    clear_stats(sum_ref)
    slot = grid_step()

    def body(start, size):
        rows = pl.ds(start, size)
        total = dot(x_ref[0, rows], w_ref[0])
        for source in range(1, x_ref.shape[0]):
            total += dot(x_ref[source, rows], w_ref[source])
        out_ref[0, rows] = total
        add_stats(sum_ref, slot, total, total * total)

    over_rows(x_ref.shape[1], body)


def reduce_product(x, weight, comm):
    blocks, pixels, _ = x.shape
    mids = weight.shape[2] // BLK
    return call(
        reduce_kernel,
        (mids,),
        [Late((blocks, pixels, BLK), BF16), pl.BlockSpec((blocks, BLK, BLK), lambda j: (0, 0, j))],
        [block(pixels, BLK), whole(mids, 2, BLK)],
        [shape((mids, pixels, BLK)), shape((mids, 2, BLK))],
        [],
        2 * pixels * blocks * BLK * mids * BLK,
        comm,
    )(x, weight)


def same_group():
    return lax.broadcasted_iota(jnp.int32, (BLK, BLK), 0) // GW == lax.broadcasted_iota(jnp.int32, (BLK, BLK), 1) // GW


def spread_weight(compact_ref, dense_ref):
    own = same_group()
    for tap in range(9):
        rows = pl.ds(tap * GW, GW)
        compact = jnp.concatenate([compact_ref[0, rows], compact_ref[1, rows]], 1).astype(F32)
        tiled = jnp.concatenate([compact] * (BLK // GW), 0)
        dense_ref[tap] = jnp.where(own, tiled, 0.0).astype(BF16)


def twice(mask):
    return jnp.concatenate([mask, mask], 1)


def fill(stack_ref, mask_ref, rows_start, size, values):
    rows = pl.ds(rows_start, size)
    target = pl.ds(rows_start + PAD, size)
    for half in range(2):
        part = values[:, half * HALF : (half + 1) * HALF]
        stack_ref[1, half, target] = part
        stack_ref[0, half, target] = part * mask_ref[1, rows]
        stack_ref[2, half, target] = part * mask_ref[0, rows]


def clear_edges(stack_ref, pixels):
    edge = jnp.zeros(stack_ref.shape[:2] + (PAD, HALF), F32)
    stack_ref[:, :, 0:PAD] = edge
    stack_ref[:, :, PAD + pixels : PAD + pixels + PAD] = edge


def window(stack_ref, start, size, row_off, col_off):
    rows = pl.ds(start + (PAD + row_off * SIDE + col_off), size)
    return jnp.concatenate([stack_ref[col_off + 1, half, rows] for half in range(2)], 1).astype(BF16)


def conv_rows(stack_ref, mask_ref, dense_ref, start, size, flipped=False):
    rows = pl.ds(start, size)
    total = None
    for row_off in (-1, 0, 1):
        part = None
        for col_off in (-1, 0, 1):
            values = window(stack_ref, start, size, row_off, col_off)
            tap = (row_off + 1) * 3 + col_off + 1
            term = dot(values, dense_ref[8 - tap], ((1,), (1,))) if flipped else dot(values, dense_ref[tap])
            part = term if part is None else part + term
        if row_off:
            part = part * twice(mask_ref[2 if row_off < 0 else 3, rows])
        total = part if total is None else total + part
    return total


def conv_kernel(count, red_ref, sums_ref, prm_ref, weight_ref, mask_ref, out_ref, stat_ref, stack_ref, dense_ref):
    pixels = red_ref.shape[1]
    spread_weight(weight_ref, dense_ref)
    clear_edges(stack_ref, pixels)
    coef = coefficients(sums_ref[0], prm_ref[0], count)

    def enter(start, size):
        _, norm = standardize(red_ref[0, pl.ds(start, size)], coef)
        fill(stack_ref, mask_ref, start, size, (norm * jax.nn.sigmoid(norm)).astype(BF16).astype(F32))

    over_rows(pixels, enter)
    clear_stats(stat_ref)
    slot = grid_step()

    def body(start, size):
        total = conv_rows(stack_ref, mask_ref, dense_ref, start, size)
        out_ref[0, pl.ds(start, size)] = total
        add_stats(stat_ref, slot, total, total * total)

    over_rows(pixels, body)


def conv(reduced, sums, params, weight, masks, count, comm):
    mids, pixels, _ = reduced.shape
    return call(
        functools.partial(conv_kernel, count),
        (mids,),
        [
            block(pixels, BLK),
            block(2, BLK),
            block(2, BLK),
            pl.BlockSpec((2,) + weight.shape[1:], lambda j: (j, 0, 0)),
            Late((4, pixels, HALF)),
        ],
        [block(pixels, BLK), whole(mids, 2, BLK)],
        [shape((mids, pixels, BLK)), shape((mids, 2, BLK))],
        [pltpu.VMEM((3, 2, pixels + 2 * PAD, HALF), F32), pltpu.VMEM((9, BLK, BLK), BF16)],
        2 * 9 * pixels * mids * BLK * BLK,
        comm,
    )(reduced, sums, params, weight, masks)


def conv_back_kernel(
    count,
    red_ref,
    sums_ref,
    prm_ref,
    grp_ref,
    gsums_ref,
    gprm_ref,
    up_ref,
    upsums_ref,
    weight_ref,
    mask_ref,
    *refs,
):
    out_ref, wgrad_ref, stat_ref, stack_ref, dense_ref, back_ref = refs
    pixels = red_ref.shape[1]
    spread_weight(weight_ref, dense_ref)
    clear_edges(stack_ref, pixels)
    coef = coefficients(sums_ref[0], prm_ref[0], count)
    gcoef = coefficients(gsums_ref[0], gprm_ref[0], count)
    scale = gcoef[2] * gcoef[1]
    up_mean = upsums_ref[0, 0:1] / count
    up_lean = upsums_ref[0, 1:2] / count

    def back(start, size):
        rows = pl.ds(start, size)
        standard, _ = standardize(grp_ref[0, rows], gcoef)
        values = (scale * (up_ref[0, rows] - up_mean - standard * up_lean)).astype(BF16)
        back_ref[1, rows] = values
        values = values.astype(F32)
        back_ref[0, rows] = (values * twice(mask_ref[2, rows])).astype(BF16)
        back_ref[2, rows] = (values * twice(mask_ref[3, rows])).astype(BF16)
        fill(stack_ref, mask_ref, start, size, values)

    over_rows(pixels, back)
    clear_stats(stat_ref)
    slot = grid_step()

    def body(start, size):
        rows = pl.ds(start, size)
        standard, norm = standardize(red_ref[0, rows], coef)
        up = conv_rows(stack_ref, mask_ref, dense_ref, start, size, True) * silu_slope(norm)
        out_ref[0, rows] = up
        add_stats(stat_ref, slot, up, up * standard)

    over_rows(pixels, body)

    def enter(start, size):
        _, norm = standardize(red_ref[0, pl.ds(start, size)], coef)
        fill(stack_ref, mask_ref, start, size, (norm * jax.nn.sigmoid(norm)).astype(BF16).astype(F32))

    over_rows(pixels, enter)
    own = same_group()
    for tap in range(9):
        full = dot(back_ref[tap // 3], window(stack_ref, 0, pixels, tap // 3 - 1, tap % 3 - 1), ((0,), (0,)))
        full = jnp.where(own, full, 0.0)
        kept = full[0:GW]
        for group in range(1, BLK // GW):
            kept += full[group * GW : (group + 1) * GW]
        for half in range(2):
            wgrad_ref[half, tap * GW : (tap + 1) * GW] = kept[:, half * HALF : (half + 1) * HALF].astype(BF16)
    for half in range(2):
        wgrad_ref[half, 9 * GW :] = jnp.zeros((wgrad_ref.shape[1] - 9 * GW, HALF), BF16)


def conv_back(reduced, sums, params, grouped, gsums, gparams, up, upsums, weight, masks, count, comm):
    mids, pixels, _ = reduced.shape
    return call(
        functools.partial(conv_back_kernel, count),
        (mids,),
        [
            block(pixels, BLK),
            block(2, BLK),
            block(2, BLK),
            block(pixels, BLK),
            block(2, BLK),
            block(2, BLK),
            block(pixels, BLK),
            block(2, BLK),
            pl.BlockSpec((2,) + weight.shape[1:], lambda j: (j, 0, 0)),
            Late((4, pixels, HALF)),
        ],
        [block(pixels, BLK), pl.BlockSpec((2,) + weight.shape[1:], lambda j: (j, 0, 0)), whole(mids, 2, BLK)],
        [shape((mids, pixels, BLK)), shape(weight.shape, BF16), shape((mids, 2, BLK))],
        [
            pltpu.VMEM((3, 2, pixels + 2 * PAD, HALF), F32),
            pltpu.VMEM((9, BLK, BLK), BF16),
            pltpu.VMEM((3, pixels, BLK), BF16),
        ],
        4 * 9 * pixels * mids * BLK * BLK,
        comm,
    )(reduced, sums, params, grouped, gsums, gparams, up, upsums, weight, masks)


def expand_kernel(count, grp_ref, gsums_ref, gprm_ref, w_ref, out_ref, act_ref, sum_ref):
    mids, pixels, _ = grp_ref.shape

    @pl.when(grid_step() == 0)
    def _():
        for mid in range(mids):
            coef = coefficients(gsums_ref[mid], gprm_ref[mid], count)

            def body(start, size):
                rows = pl.ds(start, size)
                _, norm = standardize(grp_ref[mid, rows], coef)
                act_ref[rows, mid * BLK : (mid + 1) * BLK] = (norm * jax.nn.sigmoid(norm)).astype(BF16)

            over_rows(pixels, body)

    clear_stats(sum_ref)
    slot = grid_step()

    def product(start, size):
        rows = pl.ds(start, size)
        total = dot(act_ref[rows], w_ref[0], ((1,), (1,)))
        out_ref[0, rows] = total
        add_stats(sum_ref, slot, total, total * total)

    over_rows(pixels, product)


def expand_product(grouped, gsums, gparams, weight, count, comm):
    mids, pixels, _ = grouped.shape
    blocks = weight.shape[0]
    return call(
        functools.partial(expand_kernel, count),
        (blocks,),
        [
            Late((mids, pixels, BLK)),
            whole(mids, 2, BLK),
            whole(mids, 2, BLK),
            block(BLK, mids * BLK),
        ],
        [block(pixels, BLK), whole(pixels, mids * BLK), whole(blocks, 2, BLK)],
        [shape((blocks, pixels, BLK)), shape((pixels, mids * BLK), BF16), shape((blocks, 2, BLK))],
        [],
        2 * pixels * blocks * BLK * mids * BLK,
        comm,
    )(grouped, gsums, gparams, weight)


def output_kernel(count, members, exp_ref, sums_ref, prm_ref, x_ref, grad_ref, out_ref, up_ref, stat_ref):
    coef = coefficients(sums_ref[0], prm_ref[0], count)
    clear_stats(stat_ref)
    slot = grid_step()
    if members:
        slot = lax.rem(lax.axis_index("group") + 1 + slot, members)

    def body(start, size):
        rows = pl.ds(start, size)
        standard, norm = standardize(exp_ref[0, rows], coef)
        summed = norm + x_ref[0, rows].astype(F32)
        sigma = jax.nn.sigmoid(summed)
        out_ref[0, rows] = (summed * sigma).astype(BF16)
        up = grad_ref[0, rows].astype(F32) * (sigma * (1.0 + summed * (1.0 - sigma)))
        up_ref[0, rows] = up
        add_stats(stat_ref, slot, up, up * standard)

    over_rows(exp_ref.shape[1], body)


def output(expanded, sums, params, x, grad, count, comm):
    blocks, pixels, _ = expanded.shape
    members = comm.members if comm else None
    one = functools.partial(turned_block, members) if comm else block
    return call(
        functools.partial(output_kernel, count, members),
        (blocks,),
        [one(pixels, BLK), one(2, BLK), one(2, BLK), one(pixels, BLK), one(pixels, BLK)],
        [one(pixels, BLK), one(pixels, BLK), whole(blocks, 2, BLK)],
        [shape((blocks, pixels, BLK), BF16), shape((blocks, pixels, BLK)), shape((blocks, 2, BLK))],
        [],
        20 * pixels * blocks * BLK,
        comm,
    )(expanded, sums, params, x, grad)


def expand_back_kernel(
    count,
    exp_ref,
    sums_ref,
    prm_ref,
    up_ref,
    upsums_ref,
    w_ref,
    grp_ref,
    gsums_ref,
    gprm_ref,
    act_ref,
    wgrad_ref,
    out_ref,
    stat_ref,
    keep_ref,
):
    blocks, pixels, _ = keep_ref.shape
    step = grid_step()
    clear_stats(stat_ref)

    @pl.when(step < blocks)
    def _():
        coef = coefficients(sums_ref[0], prm_ref[0], count)
        scale = coef[2] * coef[1]
        up_mean = upsums_ref[0, 0:1] / count
        up_lean = upsums_ref[0, 1:2] / count

        def back(start, size):
            rows = pl.ds(start, size)
            standard, _ = standardize(exp_ref[0, rows], coef)
            values = (scale * (up_ref[0, rows] - up_mean - standard * up_lean)).astype(BF16)
            keep_ref[step, rows] = values

        over_rows(pixels, back)
        weight_grad_block(keep_ref[step], act_ref, wgrad_ref, 0)

    @pl.when(step >= blocks)
    def _():
        coef = coefficients(gsums_ref[0], gprm_ref[0], count)

        def body(start, size):
            rows = pl.ds(start, size)
            total = dot(keep_ref[0, rows], w_ref[0])
            for source in range(1, blocks):
                total += dot(keep_ref[source, rows], w_ref[source])
            standard, norm = standardize(grp_ref[0, rows], coef)
            up = total * silu_slope(norm)
            out_ref[0, rows] = up
            add_stats(stat_ref, step - blocks, up, up * standard)

        over_rows(pixels, body)


def expand_back(expanded, sums, params, up, upsums, weight, grouped, gsums, gparams, act, count, comm):
    blocks, pixels, _ = expanded.shape
    mids = grouped.shape[0]

    def first(*dims):
        return pl.BlockSpec((1,) + dims, lambda j: (jnp.minimum(j, blocks - 1),) + (0,) * len(dims))

    def second(*dims):
        return pl.BlockSpec((1,) + dims, lambda j: (jnp.maximum(j - blocks, 0),) + (0,) * len(dims))

    return call(
        functools.partial(expand_back_kernel, count),
        (blocks + mids,),
        [
            first(pixels, BLK),
            first(2, BLK),
            first(2, BLK),
            first(pixels, BLK),
            first(2, BLK),
            pl.BlockSpec((blocks, BLK, BLK), lambda j: (0, 0, jnp.maximum(j - blocks, 0))),
            second(pixels, BLK),
            second(2, BLK),
            second(2, BLK),
            Late((pixels, mids * BLK), BF16),
        ],
        [first(BLK, mids * BLK), second(pixels, BLK), whole(mids, 2, BLK)],
        [shape((blocks, BLK, mids * BLK), BF16), shape((mids, pixels, BLK)), shape((mids, 2, BLK))],
        [pltpu.VMEM((blocks, pixels, BLK), BF16)],
        4 * pixels * blocks * BLK * mids * BLK,
        comm,
    )(expanded, sums, params, up, upsums, weight, grouped, gsums, gparams, act)


def first_back(count, red_ref, sums_ref, prm_ref, rup_ref, rupsums_ref, back_ref, loads=()):
    mids, pixels, _ = red_ref.shape
    for mid in range(mids):
        for load in loads[2 * mid : 2 * mid + 2]:
            load.wait()
        coef = coefficients(sums_ref[mid], prm_ref[mid], count)
        scale = coef[2] * coef[1]
        up_mean = rupsums_ref[mid, 0:1] / count
        up_lean = rupsums_ref[mid, 1:2] / count

        def body(start, size):
            rows = pl.ds(start, size)
            standard, _ = standardize(red_ref[mid, rows], coef)
            values = scale * (rup_ref[mid, rows] - up_mean - standard * up_lean)
            back_ref[rows, mid * BLK : (mid + 1) * BLK] = values.astype(BF16)

        over_rows(pixels, body)


def weight_grad_block(left, right_ref, out_ref, slot):
    for first in range(0, right_ref.shape[1], BLK):
        columns = slice(first, first + BLK)
        out_ref[slot, :, columns] = dot(left, right_ref[:, columns], ((0,), (0,))).astype(BF16)


def reduce_back_kernel(count, red_ref, sums_ref, prm_ref, rup_ref, rupsums_ref, x_ref, up_ref, w_ref, grad_ref, wgrad_ref, back_ref):
    @pl.when(pl.program_id(0) == 0)
    def _():
        first_back(count, red_ref, sums_ref, prm_ref, rup_ref, rupsums_ref, back_ref)

    def product(start, size):
        rows = pl.ds(start, size)
        total = dot(back_ref[rows], w_ref[0], ((1,), (1,)))
        grad_ref[0, rows] = (up_ref[0, rows] + total).astype(BF16)

    over_rows(x_ref.shape[1], product)
    weight_grad_block(x_ref[0], back_ref, wgrad_ref, 0)


def reduce_back(reduced, sums, params, rup, rupsums, x, up, weight, count):
    mids, pixels, _ = reduced.shape
    blocks = x.shape[0]
    return call(
        functools.partial(reduce_back_kernel, count),
        (blocks,),
        [
            whole(mids, pixels, BLK),
            whole(mids, 2, BLK),
            whole(mids, 2, BLK),
            whole(mids, pixels, BLK),
            whole(mids, 2, BLK),
            block(pixels, BLK),
            block(pixels, BLK),
            block(BLK, mids * BLK),
        ],
        [block(pixels, BLK), block(BLK, mids * BLK)],
        [shape((blocks, pixels, BLK), BF16), shape((blocks, BLK, mids * BLK), BF16)],
        [pltpu.VMEM((pixels, mids * BLK), BF16)],
        4 * pixels * blocks * BLK * mids * BLK,
    )(reduced, sums, params, rup, rupsums, x, up, weight)


def exchange_kernel(batches, members, x_ref, out_ref, *scratch):
    row, me, across, along = devices(batches, members)
    greet(across + along)
    out_ref[...] = x_ref[...]
    total_stats(out_ref, across, along, *scratch)


def exchange(values, batches, members, collective_id):
    return pl.pallas_call(
        functools.partial(exchange_kernel, batches, members),
        in_specs=[pl.BlockSpec(memory_space=pltpu.VMEM)],
        out_specs=pl.BlockSpec(memory_space=pltpu.VMEM),
        out_shape=shape(values.shape),
        scratch_shapes=stats_scratch(values.shape, batches, members),
        compiler_params=pltpu.CompilerParams(collective_id=collective_id, has_side_effects=True),
    )(values)


class Sends:
    def __init__(self, source, target, low, sizes, me, along, send, recv):
        self.parts = []
        for part, size in enumerate(sizes):
            self.parts.append(
                functools.partial(
                    piece_copies, source, target, low, size, me, along, send.at[part], recv.at[part]
                )
            )
            low += size

    def start(self, part):
        each(self.parts[part](), "start")

    def wait(self):
        for part in self.parts:
            each(part(), "wait")


def at_step(step, body):
    pl.when(pl.program_id(0) == step)(body)


def forward_kernel(count, batches, members, sizes, *refs):
    x_any, wr_ref, prm_ref, taps_ref, masks_any, gprm_ref, we_ref, src_ref = refs[:8]
    red_any, grp_any, act_any, exp_ref, sums_ref, gsums_ref, esums_ref, dst_ref = refs[8:16]
    x_held, masks, red, grp, act, stack, dense, psend, precv, load, keep = refs[16:27]
    stats = [refs[27 + 7 * index : 34 + 7 * index] for index in range(3)]
    row, me, across, along = devices(batches, members)
    mids, blocks = red.shape[0], x_held.shape[0]
    second, third, end = mids, 2 * mids, 2 * mids + blocks
    sends = Sends(src_ref, dst_ref, 0, sizes, me, along, psend, precv)
    loads = [pltpu.make_async_copy(x_any, x_held, load.at[0]), pltpu.make_async_copy(masks_any, masks, load.at[1])]
    kept = [
        pltpu.make_async_copy(held, out, keep.at[index])
        for index, (held, out) in enumerate(((red, red_any), (grp, grp_any), (act, act_any)))
    ]

    def begin():
        greet(across + along)
        sends.start(0)
        each(loads, "start")
        each(loads, "wait")

    at_step(0, begin)

    def product():
        reduce_kernel(x_held, wr_ref, red.at[pl.ds(grid_step(), 1)], sums_ref)

    in_phase(0, mids, product)

    def exchange_first():
        kept[0].start()
        total_stats(sums_ref, across, along, *stats[0], beside=sends.parts[1]())
        sends.start(2)

    at_step(second - 1, exchange_first)

    def conv_phase():
        own = pl.ds(grid_step(), 1)
        conv_kernel(
            count, red.at[own], sums_ref.at[own], prm_ref, taps_ref, masks, grp.at[own], gsums_ref, stack, dense
        )

    in_phase(second, mids, conv_phase)

    def exchange_second():
        kept[1].start()
        total_stats(gsums_ref, across, along, *stats[1], beside=sends.parts[3]())
        sends.start(4)

    at_step(third - 1, exchange_second)
    in_phase(third, blocks, lambda: expand_kernel(count, grp, gsums_ref, gprm_ref, we_ref, exp_ref, act, esums_ref))

    def finish():
        kept[2].start()
        total_stats(esums_ref, across, along, *stats[2], beside=sends.parts[5]())
        each(kept, "wait")
        sends.wait()

    at_step(end - 1, finish)


def forward(x, reduce_full, reduce_params, taps, masks, group_params, expand_full, source, sizes, count, batches, members):
    blocks, pixels, _ = x.shape
    mid_total = reduce_full.shape[2]
    mids = mid_total // BLK
    anywhere = pl.BlockSpec(memory_space=pl.ANY)
    dma = pltpu.SemaphoreType.DMA
    mid_dims, sum_dims = (mids, pixels, BLK), (mids, 2, BLK)
    scratch = [
        pltpu.VMEM(x.shape, BF16),
        pltpu.VMEM(masks.shape, F32),
        pltpu.VMEM(mid_dims, F32),
        pltpu.VMEM(mid_dims, F32),
        pltpu.VMEM((pixels, mid_total), BF16),
        pltpu.VMEM((3, 2, pixels + 2 * PAD, HALF), F32),
        pltpu.VMEM((9, BLK, BLK), BF16),
        dma((len(sizes), members)),
        dma((len(sizes), members - 1)),
        dma((2,)),
        dma((3,)),
    ]
    for dims in (sum_dims, sum_dims, (blocks, 2, BLK)):
        scratch += stats_scratch(dims, batches, members)
    return pl.pallas_call(
        functools.partial(forward_kernel, count, batches, members, sizes),
        grid=(2 * mids + blocks,),
        in_specs=[
            anywhere,
            pl.BlockSpec((blocks, BLK, BLK), lambda j: (0, 0, jnp.minimum(j, mids - 1))),
            phase_block(mids, mids, 2, BLK),
            pl.BlockSpec((2,) + taps.shape[1:], lambda j: (jnp.clip(j - mids, 0, mids - 1), 0, 0)),
            anywhere,
            whole(*sum_dims),
            phase_block(2 * mids, blocks, BLK, mid_total),
            anywhere,
        ],
        out_specs=[
            anywhere,
            anywhere,
            anywhere,
            phase_block(2 * mids, blocks, pixels, BLK),
            whole(*sum_dims),
            whole(*sum_dims),
            whole(blocks, 2, BLK),
            anywhere,
        ],
        out_shape=[
            shape(mid_dims),
            shape(mid_dims),
            shape((pixels, mid_total), BF16),
            shape(x.shape),
            shape(sum_dims),
            shape(sum_dims),
            shape((blocks, 2, BLK)),
            shape(source.shape, BF16),
        ],
        scratch_shapes=scratch,
        compiler_params=pltpu.CompilerParams(vmem_limit_bytes=VMEM_LIMIT, collective_id=1, has_side_effects=True),
    )(x, reduce_full, reduce_params, taps, masks, group_params, expand_full, source)


def backward_kernel(count, batches, members, low, sizes, *refs):
    exp_ref, esums_ref, eprm_ref, up_ref, upsums_ref, we_ref, grp_ref, gsums_ref, gprm_ref = refs[:9]
    red_ref, sums_ref, prm_ref, taps_ref, act_any, masks_any, src_ref, _ = refs[9:17]
    epart_ref, rup_ref, tpart_ref, gstats_ref, rstats_ref, dst_ref = refs[17:23]
    keep, gup, act, masks, stack, dense, back, psend, precv, load = refs[23:33]
    stats = [refs[33 + 7 * index : 40 + 7 * index] for index in range(2)]
    row, me, across, along = devices(batches, members)
    blocks, mids = keep.shape[0], gup.shape[0]
    middle, second, end = blocks, blocks + mids, blocks + 2 * mids
    sends = Sends(src_ref, dst_ref, low, sizes, me, along, psend, precv)
    loads = [pltpu.make_async_copy(act_any, act, load.at[0]), pltpu.make_async_copy(masks_any, masks, load.at[1])]

    def begin():
        greet(across + along)
        sends.start(0)
        each(loads, "start")
        each(loads, "wait")

    at_step(0, begin)

    def expand_phase():
        place = jnp.clip(grid_step() - middle, 0, mids - 1)
        expand_back_kernel(
            count,
            exp_ref,
            esums_ref,
            eprm_ref,
            up_ref,
            upsums_ref,
            we_ref,
            grp_ref,
            gsums_ref,
            gprm_ref,
            act,
            epart_ref,
            gup.at[pl.ds(place, 1)],
            gstats_ref,
            keep,
        )

    in_phase(0, second, expand_phase)

    def exchange_first():
        total_stats(gstats_ref, across, along, *stats[0], beside=sends.parts[1]())
        sends.start(2)

    at_step(second - 1, exchange_first)

    def conv_phase():
        own = pl.ds(grid_step(), 1)
        conv_back_kernel(
            count,
            red_ref,
            sums_ref,
            prm_ref,
            grp_ref,
            gsums_ref,
            gprm_ref,
            gup.at[own],
            gstats_ref.at[own],
            taps_ref,
            masks,
            rup_ref,
            tpart_ref,
            rstats_ref,
            stack,
            dense,
            back,
        )

    in_phase(second, mids, conv_phase)

    def finish():
        total_stats(rstats_ref, across, along, *stats[1], beside=sends.parts[3]())
        sends.wait()

    at_step(end - 1, finish)


def backward(
    expanded,
    esums,
    eparams,
    up,
    upsums,
    expand_full,
    grouped,
    gsums,
    gparams,
    reduced,
    sums,
    params,
    taps,
    act,
    masks,
    source,
    into,
    low,
    sizes,
    count,
    batches,
    members,
):
    blocks, pixels, _ = expanded.shape
    mids = grouped.shape[0]
    mid_total = mids * BLK
    anywhere = pl.BlockSpec(memory_space=pl.ANY)
    dma = pltpu.SemaphoreType.DMA
    second = blocks + mids

    def both(*dims):
        def index(j):
            return (jnp.where(j < second, jnp.maximum(j - blocks, 0), j - second),) + (0,) * len(dims)

        return pl.BlockSpec((1,) + dims, index)

    first = functools.partial(phase_block, 0, blocks)
    last = functools.partial(phase_block, second, mids)
    pairs = pl.BlockSpec((2,) + taps.shape[1:], lambda j: (jnp.clip(j - second, 0, mids - 1), 0, 0))
    scratch = [
        pltpu.VMEM((blocks, pixels, BLK), BF16),
        pltpu.VMEM((mids, pixels, BLK), F32),
        pltpu.VMEM((pixels, mid_total), BF16),
        pltpu.VMEM(masks.shape, F32),
        pltpu.VMEM((3, 2, pixels + 2 * PAD, HALF), F32),
        pltpu.VMEM((9, BLK, BLK), BF16),
        pltpu.VMEM((3, pixels, BLK), BF16),
        dma((len(sizes), members)),
        dma((len(sizes), members - 1)),
        dma((2,)),
    ]
    for _ in range(2):
        scratch += stats_scratch((mids, 2, BLK), batches, members)
    return pl.pallas_call(
        functools.partial(backward_kernel, count, batches, members, low, sizes),
        grid=(second + mids,),
        in_specs=[
            first(pixels, BLK),
            first(2, BLK),
            first(2, BLK),
            first(pixels, BLK),
            first(2, BLK),
            pl.BlockSpec((blocks, BLK, BLK), lambda j: (0, 0, jnp.clip(j - blocks, 0, mids - 1))),
            both(pixels, BLK),
            both(2, BLK),
            both(2, BLK),
            last(pixels, BLK),
            last(2, BLK),
            last(2, BLK),
            pairs,
            anywhere,
            anywhere,
            anywhere,
            anywhere,
        ],
        out_specs=[
            first(BLK, mid_total),
            last(pixels, BLK),
            pairs,
            whole(mids, 2, BLK),
            whole(mids, 2, BLK),
            anywhere,
        ],
        out_shape=[
            shape((blocks, BLK, mid_total), BF16),
            shape((mids, pixels, BLK)),
            shape(taps.shape, BF16),
            shape((mids, 2, BLK)),
            shape((mids, 2, BLK)),
            shape(source.shape, BF16),
        ],
        scratch_shapes=scratch,
        input_output_aliases={16: 5},
        compiler_params=pltpu.CompilerParams(vmem_limit_bytes=VMEM_LIMIT, collective_id=5, has_side_effects=True),
    )(
        expanded,
        esums,
        eparams,
        up,
        upsums,
        expand_full,
        grouped,
        gsums,
        gparams,
        reduced,
        sums,
        params,
        taps,
        act,
        masks,
        source,
        into,
    )


def turn(source_ref, target_ref, slot, chunk):
    first = (49 * chunk) // 4

    @pl.loop(0, 13)
    def _(tile):
        columns = pl.ds(pl.multiple_of((first + tile) * HALF, HALF), HALF)
        rows = pl.ds(pl.multiple_of(tile * HALF, HALF), HALF)
        target_ref[slot, rows] = source_ref[:, columns].T


def turned(target_ref, slot, chunk, pixels):
    return target_ref.at[slot, pl.ds(pl.multiple_of(32 * (chunk % 4), 16), pixels)]


def opening_kernel(batches, members, *refs):
    x_ref, grad_ref, wr_ref, we_ref, wg_ref = refs[:5]
    vectors = refs[5:11]
    xp_ref, gradt_ref, wr_out, we_out, wg_out, prm_out = refs[11:17]
    xin, xturn, gin, gturn, prm_ref, load, own, xsend, xrecv, gsend, psend, precv = refs[17:29]
    zsend, zrecv, ysend, yrecv, fsend, frecv = refs[29:]
    row, me, across, along = devices(batches, members)
    pixels = xp_ref.shape[1]
    load_x = pltpu.make_async_copy(x_ref, xin, load.at[0])
    load_grad = pltpu.make_async_copy(grad_ref, gin, load.at[1])
    load_x.start()
    load_grad.start()
    weights = [(wr_ref, wr_out), (wg_ref, wg_out), (we_ref, we_out)]
    height, side = me // 2, me % 2
    levels = members // 2
    line = [(row, lax.rem(me + 2 * step, members)) for step in range(1, levels)]
    peer = (row, height * 2 + 1 - side)
    local_copies = []
    parts = []
    for index, (source, target) in enumerate(weights):
        size = source.shape[0] // batches
        part = pl.ds(pl.multiple_of(row * size, 16), size)
        parts.append(part)
        local_copies.append(pltpu.make_async_copy(source.at[part], target.at[height, side, part], own.at[index]))
    each(local_copies, "start")
    place = 0
    for vector in vectors:
        for low in range(0, vector.shape[0], HALF):
            prm_ref[place : place + 1] = vector[low : low + HALF].reshape(1, HALF)
            place += 1
    prm_own = pltpu.make_async_copy(prm_ref, prm_out.at[me], own.at[3])
    prm_own.start()
    greet(across + along)
    copies = [prm_own]
    first = []
    for index, (source, target) in enumerate(weights):
        for step, device in enumerate(line):
            first.append(
                remote(
                    source.at[parts[index]],
                    target.at[height, side, parts[index]],
                    zsend.at[index, step],
                    zrecv.at[index, step],
                    device,
                )
            )
    for step, device in enumerate(along):
        copy = remote(prm_ref, prm_out.at[me], psend.at[step], precv.at[step], device)
        copy.start()
        copies.append(copy)
    each(first, "start")
    load_x.wait()
    for step, device in enumerate(along):
        turn(xin, xturn, step, device[1])
        copy = remote(turned(xturn, step, device[1], pixels), xp_ref.at[me], xsend.at[step], xrecv.at[step], device)
        copy.start()
        copies.append(copy)
    last = members - 1
    turn(xin, xturn, last, me)
    copy = pltpu.make_async_copy(turned(xturn, last, me, pixels), xp_ref.at[me], xsend.at[last])
    copy.start()
    copies.append(copy)
    load_grad.wait()
    for member in range(members):
        turn(gin, gturn, member, member)
        copy = pltpu.make_async_copy(turned(gturn, member, member, pixels), gradt_ref.at[member], gsend.at[member])
        copy.start()
        copies.append(copy)
    each(local_copies, "wait")
    far, near = (lax.bitwise_xor(row, 2), me), (lax.bitwise_xor(row, 1), me)
    second, third = [], []
    for index, (_, target) in enumerate(weights):
        each(first[index * len(line) : (index + 1) * len(line)], "wait")
        held = target.at[:, side, parts[index]]
        second.append(remote(held, held, ysend.at[index], yrecv.at[index], peer))
        second[-1].start()
    for index, (_, target) in enumerate(weights):
        second[index].wait()
        held = target.at[:, :, parts[index]]
        third.append(remote(held, held, fsend.at[index, 0], frecv.at[index, 0], far))
        third[-1].start()
    for index, (source, target) in enumerate(weights):
        size = source.shape[0] // batches
        third[index].wait()
        for step, origin in enumerate((row, lax.bitwise_xor(row, 2))):
            held = target.at[:, :, pl.ds(pl.multiple_of(origin * size, 16), size)]
            copy = remote(held, held, fsend.at[index, 1 + step], frecv.at[index, 1 + step], near)
            copy.start()
            copies.append(copy)
    each(copies, "wait")


def opening(block_input, out_grad, reduce_weight, expand_weight, taps, vectors, batches, members):
    channels, row_pixels = block_input.shape
    pixels = row_pixels // members
    dma = pltpu.SemaphoreType.DMA
    other, across, levels = members - 1, batches - 1, members // 2
    padded = 13 * HALF
    lines = sum(vector.shape[0] for vector in vectors) // HALF
    weights = [reduce_weight, expand_weight, taps]
    x, grad, *gathered, params = pl.pallas_call(
        functools.partial(opening_kernel, batches, members),
        in_specs=[pl.BlockSpec(memory_space=pl.ANY)] * 5 + [pl.BlockSpec(memory_space=pltpu.VMEM)] * len(vectors),
        out_specs=[pl.BlockSpec(memory_space=pl.ANY)] * 6,
        out_shape=[shape((members, pixels, channels), BF16)] * 2
        + [shape((levels, 2) + weight.shape, BF16) for weight in weights]
        + [shape((members, lines, HALF))],
        scratch_shapes=[
            pltpu.VMEM((channels, row_pixels), BF16),
            pltpu.VMEM((members, padded, channels), BF16),
            pltpu.VMEM((channels, row_pixels), BF16),
            pltpu.VMEM((members, padded, channels), BF16),
            pltpu.VMEM((lines, HALF), F32),
            dma((2,)),
            dma((4,)),
            dma((members,)),
            dma((other,)),
            dma((members,)),
            dma((other,)),
            dma((other,)),
            dma((3, levels - 1)),
            dma((3, levels - 1)),
            dma((3,)),
            dma((3,)),
            dma((3, across)),
            dma((3, across)),
        ],
        compiler_params=pltpu.CompilerParams(vmem_limit_bytes=VMEM_LIMIT, collective_id=0, has_side_effects=True),
    )(block_input, out_grad, *weights, *vectors)
    gathered = [full.reshape((members,) + full.shape[2:]) for full in gathered]
    return x, grad, *gathered, params


class Reduce:
    def __init__(self, part, out, row, me, refs, source=None):
        self.part, self.out, self.row = part, out, row
        self.source = part if source is None else source
        self.height, self.side = me // 2, me % 2
        self.place, self.core = row // 2, row % 2
        self.fresh, self.chip, self.cross, self.held, self.pair, self.line, self.second, self.total = refs[:8]
        self.send, self.recv = refs[8:]
        self.levels = self.held.shape[0]
        self.size = self.total.shape[0]
        self.near = (self.place * 2 + 1 - self.core, me)
        self.far = ((1 - self.place) * 2 + self.core, me)
        self.peer = (row, self.height * 2 + 1 - self.side)
        self.along = [(row, lax.rem(me + 2 * step, 2 * self.levels)) for step in range(1, self.levels)]

    def rows(self, row):
        return pl.ds(pl.multiple_of(row * self.size, 16), self.size)

    def copy(self, source, target, index, device):
        return remote(source, target, self.send.at[index], self.recv.at[index], device)

    def over_cores(self):
        return [
            self.copy(self.source.at[:, self.rows(2 * place + 1 - self.core)], self.fresh.at[place], place, self.near)
            for place in range(2)
        ]

    def add_cores(self):
        @pl.loop(0, 2 * self.levels)
        def _(member):
            for place in range(2):
                total = self.part[member, self.rows(2 * place + self.core)].astype(F32)
                self.chip[place, member] = (total + self.fresh[place, member].astype(F32)).astype(BF16)

    def over_x(self):
        return [self.copy(self.chip.at[1 - self.place], self.cross, 2, self.far)]

    def add_x(self):
        @pl.loop(0, self.levels)
        def _(level):
            for side in range(2):
                member = 2 * level + side
                total = self.chip[self.place, member].astype(F32) + self.cross[member].astype(F32)
                self.held[level, side] = total.astype(BF16)

    def over_pair(self):
        return [self.copy(self.held.at[:, 1 - self.side], self.pair, 3, self.peer)]

    def add_pair(self):
        @pl.loop(0, self.levels)
        def _(level):
            total = self.held[level, self.side].astype(F32) + self.pair[level].astype(F32)
            self.line[level] = total.astype(BF16)

    def over_line(self):
        return [
            self.copy(self.line.at[device[1] // 2], self.second.at[step], 4 + step, device)
            for step, device in enumerate(self.along)
        ]

    def add_line(self):
        total = self.line[self.height].astype(F32)
        for step in range(len(self.along)):
            total += self.second[step].astype(F32)
        self.total[...] = total

    def keep(self):
        return [pltpu.make_async_copy(self.total, self.out.at[self.rows(self.row)], self.send.at[10])]

    def share_x(self):
        return [self.copy(self.total, self.out.at[self.rows(self.row)], 7, self.far)]

    def share_cores(self):
        own = self.copy(self.total, self.out.at[self.rows(self.row)], 8, self.near)
        rows = self.rows((1 - self.place) * 2 + self.core)
        return [own, self.copy(self.out.at[rows], self.out.at[rows], 9, self.near)]


def reduce_scratch(dims, batches, members):
    rows, columns = dims[1] // batches, dims[2]
    levels = members // 2
    return [
        pltpu.VMEM((2, members, rows, columns), BF16),
        pltpu.VMEM((2, members, rows, columns), BF16),
        pltpu.VMEM((members, rows, columns), BF16),
        pltpu.VMEM((levels, 2, rows, columns), BF16),
        pltpu.VMEM((levels, rows, columns), BF16),
        pltpu.VMEM((levels, rows, columns), BF16),
        pltpu.VMEM((levels - 1, rows, columns), BF16),
        pltpu.VMEM((rows, columns), F32),
        pltpu.SemaphoreType.DMA((11,)),
        pltpu.SemaphoreType.DMA((10,)),
    ]


HELD_BACK = 2
EARLY = 3


def closing_steps(step, members):
    late = jnp.maximum(step - members, EARLY)
    return jnp.where(step < EARLY, step, late), jnp.clip(step - EARLY, 0, members - 1)


def closing_kernel(count, batches, members, low, size, *refs):
    red_ref, sums_ref, prm_ref, rup_ref, rupsums_ref, x_ref, up_ref, w_ref, epart_ref, tpart_ref, src_ref, _ = refs[:12]
    recv_ref, rout_ref, eout_ref, tout_ref, dst_ref = refs[12:17]
    back_ref, grad_ref, wpart_ref, gsend, grecv, psend, precv = refs[17:24]
    red_held, rup_held, epart_held, load_sem = refs[54:]
    row, me, across, along = devices(batches, members)
    step = pl.program_id(0)
    last = members - 1
    expand_sum = Reduce(epart_held, eout_ref, row, me, refs[24:34], epart_ref)
    taps_sum = Reduce(tpart_ref, tout_ref, row, me, refs[34:44])
    reduce_sum = Reduce(wpart_ref, rout_ref, row, me, refs[44:54])
    parts = (expand_sum, taps_sum, reduce_sum)
    grad_step, weight_step = closing_steps(step, members)

    def pieces():
        return piece_copies(src_ref, dst_ref, low, size, me, along, psend, precv)

    def send(index):
        device = (row, lax.rem(me + 1 + index, members))
        return remote(grad_ref.at[index], recv_ref.at[me], gsend.at[index], grecv.at[index], device)

    mids = red_held.shape[0]
    load_part = pltpu.make_async_copy(epart_ref, epart_held, load_sem.at[2 * mids])

    @pl.when(step == 0)
    def _():
        greet(across + along)
        each(pieces(), "start")
        loads = []
        for mid in range(mids):
            for which, (source, held) in enumerate(((red_ref, red_held), (rup_ref, rup_held))):
                loads.append(pltpu.make_async_copy(source.at[mid], held.at[mid], load_sem.at[2 * mid + which]))
        each(loads, "start")
        load_part.start()
        each(expand_sum.over_cores(), "start")
        each(taps_sum.over_cores(), "start")
        first_back(count, red_held, sums_ref, prm_ref, rup_held, rupsums_ref, back_ref, loads)

    weight_turn = (step >= EARLY) & (step < EARLY + members)

    @pl.when(weight_turn)
    def _():
        weight_grad_block(x_ref[0], back_ref, wpart_ref, lax.rem(me + 1 + weight_step, members))

    @pl.when(jnp.logical_not(weight_turn))
    def _():
        def product(start, size):
            part = pl.ds(start, size)
            total = dot(back_ref[part], w_ref[0], ((1,), (1,)))
            grad_ref[grad_step, part] = (up_ref[0, part] + total).astype(BF16)

        over_rows(x_ref.shape[1], product)

        @pl.when(grad_step < last - HELD_BACK)
        def _():
            send(grad_step).start()

    @pl.when(step == EARLY)
    def _():
        load_part.wait()
        for part in parts[:2]:
            each(part.over_cores(), "wait")
            part.add_cores()
            each(part.over_x(), "start")

    @pl.when(step == EARLY + members - 1)
    def _():
        each(reduce_sum.over_cores(), "start")
        for part in parts[:2]:
            each(part.over_x(), "wait")
            part.add_x()
            each(part.over_pair(), "start")

    @pl.when(step == EARLY + members)
    def _():
        each(reduce_sum.over_cores(), "wait")
        reduce_sum.add_cores()
        each(reduce_sum.over_x(), "start")

    @pl.when(step == 2 * members - 1)
    def _():
        own = pltpu.make_async_copy(grad_ref.at[last], recv_ref.at[me], gsend.at[last])
        own.start()
        for part in parts[:2]:
            each(part.over_pair(), "wait")
            part.add_pair()
            each(part.over_line(), "start")
        each(reduce_sum.over_x(), "wait")
        reduce_sum.add_x()
        each(reduce_sum.over_pair(), "start")
        each(reduce_sum.over_pair(), "wait")
        reduce_sum.add_pair()
        each(reduce_sum.over_line(), "start")
        for index in range(last - HELD_BACK, last):
            send(index).start()
        for part in parts:
            each(part.over_line(), "wait")
            part.add_line()
            each(part.share_x() + part.keep(), "start")
        for part in parts:
            each(part.share_x(), "wait")
            each(part.share_cores(), "start")
        own.wait()
        each(pieces(), "wait")
        for index in range(last):
            send(index).wait()
        for part in parts:
            each(part.share_cores() + part.keep(), "wait")


def closing(
    reduced, sums, params, rup, rupsums, x, up, weight, epart, tpart, source, into, low, size, count, batches, members
):
    mids, pixels, _ = reduced.shape
    blocks = x.shape[0]
    once = pl.Buffered(1)

    def keep(*dims):
        return pl.BlockSpec(dims, lambda j: (0,) * len(dims), pipeline_mode=once)

    def turn_block(which, *dims):
        def index(j):
            return (lax.rem(lax.axis_index("group") + 1 + closing_steps(j, members)[which], members),) + (0,) * len(dims)

        return pl.BlockSpec((1,) + dims, index)

    anywhere = pl.BlockSpec(memory_space=pl.ANY)
    dma = pltpu.SemaphoreType.DMA
    wdims = (blocks, BLK, mids * BLK)
    scratch = [
        pltpu.VMEM((pixels, mids * BLK), BF16),
        pltpu.VMEM((blocks, pixels, BLK), BF16),
        pltpu.VMEM(wdims, BF16),
        dma((members,)),
        dma((members - 1,)),
        dma((members,)),
        dma((members - 1,)),
    ]
    for dims in (wdims, tpart.shape, wdims):
        scratch += reduce_scratch(dims, batches, members)
    scratch += [
        pltpu.VMEM((mids, pixels, BLK), F32),
        pltpu.VMEM((mids, pixels, BLK), F32),
        pltpu.VMEM(wdims, BF16),
        dma((2 * mids + 1,)),
    ]
    return pl.pallas_call(
        functools.partial(closing_kernel, count, batches, members, low, size),
        grid=(2 * blocks,),
        in_specs=[
            anywhere,
            keep(mids, 2, BLK),
            keep(mids, 2, BLK),
            anywhere,
            keep(mids, 2, BLK),
            turn_block(1, pixels, BLK),
            turn_block(0, pixels, BLK),
            turn_block(0, BLK, mids * BLK),
            anywhere,
            keep(*tpart.shape),
            anywhere,
            anywhere,
        ],
        out_specs=[anywhere] * 5,
        out_shape=[
            shape((members, pixels, BLK), BF16),
            shape(wdims[1:]),
            shape(wdims[1:]),
            shape(tpart.shape[1:]),
            shape(source.shape, BF16),
        ],
        scratch_shapes=scratch,
        input_output_aliases={11: 4},
        compiler_params=pltpu.CompilerParams(vmem_limit_bytes=VMEM_LIMIT, collective_id=7, has_side_effects=True),
    )(reduced, sums, params, rup, rupsums, x, up, weight, epart, tpart, source, into)


def turn_out_kernel(first_ref, second_ref, first_out, second_out):
    own = lax.broadcasted_iota(jnp.int32, (BLK, BLK), 0) == lax.broadcasted_iota(jnp.int32, (BLK, BLK), 1)
    identity = jnp.where(own, 1.0, 0.0).astype(BF16)
    half = pl.num_programs(0) // 2

    def turn_part(in_ref, out_ref):
        for low in range(0, in_ref.shape[0], HALF):
            part = dot(identity, in_ref[low : low + HALF], ((1,), (1,)))
            out_ref[:, low : low + HALF] = part.astype(out_ref.dtype)

    @pl.when(pl.program_id(0) < half)
    def _():
        turn_part(first_ref, first_out)

    @pl.when(pl.program_id(0) >= half)
    def _():
        turn_part(second_ref, second_out)


def turn_out(first, second):
    rows, channels = first.shape
    parts = 2
    size = rows // parts

    def early(j):
        return jnp.minimum(j, parts - 1)

    def late(j):
        return jnp.maximum(j - parts, 0)

    return call(
        turn_out_kernel,
        (2 * parts,),
        [
            pl.BlockSpec((size, channels), lambda j: (early(j), 0)),
            pl.BlockSpec((size, channels), lambda j: (late(j), 0)),
        ],
        [
            pl.BlockSpec((channels, size), lambda j: (0, early(j))),
            pl.BlockSpec((channels, size), lambda j: (0, late(j))),
        ],
        [shape((channels, rows)), shape((channels, rows), BF16)],
        [],
        4 * rows * channels * BLK,
    )(first, second)


def own_kernel(reduce_ref, group_ref, expand_ref, *outs):
    me = lax.axis_index("group")
    half = pl.ds(pl.multiple_of((me % 2) * HALF, HALF), HALF)
    for index, stats_ref in enumerate((reduce_ref, group_ref)):
        for which in range(2):
            outs[2 * index + 1 - which][...] = stats_ref[me // 2, which : which + 1, half]
    for which in range(2):
        outs[5 - which][...] = expand_ref[me, which : which + 1]


def own_parts(reduce_stats, group_stats, expand_stats):
    sizes = (HALF,) * 4 + (BLK,) * 2
    outs = pl.pallas_call(own_kernel, out_shape=[shape((1, size)) for size in sizes])(
        reduce_stats, group_stats, expand_stats
    )
    return tuple(out.reshape(-1) for out in outs)


def pixel_masks(pixels):
    place = np.arange(pixels)
    tall, wide = (place // SIDE) % SIDE, place % SIDE
    masks = np.stack([wide != 0, wide != SIDE - 1, tall != 0, tall != SIDE - 1])
    return jnp.asarray(np.broadcast_to(masks[:, :, None], (4, pixels, HALF)).astype(np.float32))


def own_part(stats, which, length):
    return lax.dynamic_slice_in_dim(stats[:, which].reshape(-1), lax.axis_index("group") * length, length, 0)


TAP_ROWS = 320


def fused(
    block_input,
    reduce_weight,
    reduce_gain,
    reduce_bias,
    group_weight,
    group_gain,
    group_bias,
    expand_weight,
    expand_gain,
    expand_bias,
    out_grad,
):
    batches, members = lax.axis_size("batch"), lax.axis_size("group")
    channels, row_pixels = block_input.shape
    pixels = row_pixels // members
    count = row_pixels * batches
    vectors = [reduce_gain, reduce_bias, group_gain, group_bias, expand_gain, expand_bias]
    taps = group_weight.reshape(-1, 9, GW, GW).transpose(1, 2, 0, 3).reshape(9 * GW, HALF)
    taps = jnp.pad(taps, ((0, TAP_ROWS - 9 * GW), (0, 0)))
    masks = pixel_masks(pixels)
    x, grad_turned, reduce_full, expand_full, taps_full, packs = opening(
        block_input, out_grad, reduce_weight, expand_weight, taps, vectors, batches, members
    )
    vectors = packs[:, :4].reshape(-1, 2, 4, HALF).transpose(0, 2, 1, 3).reshape(-1, 4, BLK)
    reduce_params, group_params = vectors[:, :2], vectors[:, 2:]
    expand_params = packs[:, 4:].reshape(-1, 2, BLK)

    sizes = (208, 240, 304, 240, 304)
    reduced, grouped, act, expanded, reduce_sums, group_sums, expand_sums, grad = forward(
        x,
        reduce_full,
        reduce_params,
        taps_full,
        masks,
        group_params,
        expand_full,
        grad_turned,
        sizes + (pixels - sum(sizes),),
        count,
        batches,
        members,
    )
    sends = Comm(batches, members, 4, None, 0, (176, 64), None, True)
    out, upstream, expand_stats, moved = output(expanded, expand_sums, expand_params, x, grad, count, sends)
    sizes = (480, 144, 448, 112)
    expand_part, reduce_up, taps_part, group_stats, reduce_stats, moved = backward(
        expanded,
        expand_sums,
        expand_params,
        upstream,
        expand_stats,
        expand_full,
        grouped,
        group_sums,
        group_params,
        reduced,
        reduce_sums,
        reduce_params,
        taps_full,
        act,
        masks,
        out,
        moved,
        sends.high,
        sizes,
        count,
        batches,
        members,
    )
    high = sends.high + sum(sizes)
    inner, reduce_weight_grad, expand_weight_grad, taps_grad, moved = closing(
        reduced,
        reduce_sums,
        reduce_params,
        reduce_up,
        reduce_stats,
        x,
        upstream,
        reduce_full,
        expand_part,
        taps_part,
        out,
        moved,
        high,
        pixels - high,
        count,
        batches,
        members,
    )
    input_grad, block_output = turn_out(inner.reshape(row_pixels, channels), moved.reshape(row_pixels, channels))
    taps_grad = taps_grad[: 9 * GW].reshape(9, GW, -1, GW).transpose(2, 0, 3, 1)
    return (
        block_output,
        input_grad,
        reduce_weight_grad,
        taps_grad.reshape(group_weight.shape),
        expand_weight_grad,
    ) + own_parts(reduce_stats, group_stats, expand_stats)


def modular(
    block_input,
    reduce_weight,
    reduce_gain,
    reduce_bias,
    group_weight,
    group_gain,
    group_bias,
    expand_weight,
    expand_gain,
    expand_bias,
    out_grad,
):
    batches, members = lax.axis_size("batch"), lax.axis_size("group")
    channels, row_pixels = block_input.shape
    pixels = row_pixels // members
    count = row_pixels * batches
    mid_total = reduce_weight.shape[1]
    mids = mid_total // BLK
    blocks = channels * members // BLK
    me = lax.axis_index("group")

    def to_pixels(values):
        moved = lax.all_to_all(values.T.reshape(members, pixels, channels), "group", 0, 0)
        if channels == BLK:
            return moved
        share = BLK // channels
        moved = moved.reshape(blocks, share, pixels, channels).transpose(0, 2, 1, 3)
        return moved.reshape(blocks, pixels, BLK)

    def to_channels(values):
        if channels != BLK:
            share = BLK // channels
            values = values.reshape(blocks, pixels, share, channels).transpose(0, 2, 1, 3)
            values = values.reshape(members, pixels, channels)
        moved = lax.all_to_all(values, "group", 0, 0)
        return moved.reshape(row_pixels, channels).T

    def gather(values):
        return lax.all_gather(values, "group", axis=0, tiled=True)

    local_mid = reduce_gain.shape[0]
    pack = jnp.concatenate([reduce_gain, reduce_bias, group_gain, group_bias, expand_gain, expand_bias])
    packs = gather(pack[None])
    vectors, offset = [], 0
    for length in (local_mid, local_mid, local_mid, local_mid, channels, channels):
        vectors.append(packs[:, offset : offset + length].reshape(-1, BLK))
        offset += length
    reduce_params = jnp.stack(vectors[0:2], 1)
    group_params = jnp.stack(vectors[2:4], 1)
    expand_params = jnp.stack(vectors[4:6], 1)
    reduce_full = gather(reduce_weight).reshape(blocks, BLK, mid_total)
    expand_full = gather(expand_weight).reshape(blocks, BLK, mid_total)
    taps = gather(group_weight.reshape(group_weight.shape[0], 9, GW, GW))
    taps = taps.reshape(-1, HALF // GW, 9, GW, GW).transpose(0, 2, 3, 1, 4).reshape(-1, 9 * GW, HALF)
    taps = jnp.pad(taps, ((0, 0), (0, TAP_ROWS - 9 * GW), (0, 0)))
    masks = pixel_masks(pixels)

    x = to_pixels(block_input)
    grad = to_pixels(out_grad)

    reduced, reduce_sums = reduce_product(x, reduce_full, None)
    reduce_sums = exchange(reduce_sums, batches, members, 1)
    grouped, group_sums = conv(reduced, reduce_sums, reduce_params, taps, masks, count, None)
    group_sums = exchange(group_sums, batches, members, 1)
    expanded, act, expand_sums = expand_product(grouped, group_sums, group_params, expand_full, count, None)
    expand_sums = exchange(expand_sums, batches, members, 2)
    out, upstream, expand_stats = output(expanded, expand_sums, expand_params, x, grad, count, None)
    expand_stats = exchange(expand_stats, batches, members, 2)
    expand_part, group_up, group_stats = expand_back(
        expanded, expand_sums, expand_params, upstream, expand_stats, expand_full, grouped, group_sums, group_params, act, count, None
    )
    group_stats = exchange(group_stats, batches, members, 1)
    reduce_up, taps_part, reduce_stats = conv_back(
        reduced,
        reduce_sums,
        reduce_params,
        grouped,
        group_sums,
        group_params,
        group_up,
        group_stats,
        taps,
        masks,
        count,
        None,
    )
    reduce_stats = exchange(reduce_stats, batches, members, 1)
    inner, reduce_part = reduce_back(
        reduced, reduce_sums, reduce_params, reduce_up, reduce_stats, x, upstream, reduce_full, count
    )
    block_output = to_channels(out)
    input_grad = to_channels(inner).astype(F32)

    def shared_sum(part):
        rows = channels // batches
        part = part.reshape(members, batches, rows, mid_total).transpose(1, 0, 2, 3)
        part = lax.all_to_all(part, "batch", 0, 0).astype(F32).sum(0).astype(BF16)
        part = lax.all_to_all(part, "group", 0, 0).astype(F32).sum(0)
        return lax.all_gather(part, "batch", axis=0, tiled=True)

    expand_weight_grad = shared_sum(expand_part)
    reduce_weight_grad = shared_sum(reduce_part)
    taps_part = taps_part[:, : 9 * GW].reshape(-1, 9, GW, HALF // GW, GW).transpose(0, 3, 1, 4, 2)
    taps_part = taps_part.reshape(members, -1, 9, GW, GW)
    group_weight_grad = lax.all_to_all(taps_part, "group", 0, 0).astype(F32).sum(0)
    group_weight_grad = lax.psum(group_weight_grad, "batch").reshape(group_weight.shape)

    return (
        block_output,
        input_grad,
        reduce_weight_grad,
        group_weight_grad,
        expand_weight_grad,
        own_part(reduce_stats, 1, local_mid),
        own_part(reduce_stats, 0, local_mid),
        own_part(group_stats, 1, local_mid),
        own_part(group_stats, 0, local_mid),
        own_part(expand_stats, 1, channels),
        own_part(expand_stats, 0, channels),
    )


def local(*args):
    block_input = args[0]
    pixels = block_input.shape[1] // lax.axis_size("group")
    if block_input.shape[0] == BLK and pixels == 1568 and args[2].shape[0] == HALF and lax.axis_size("group") == 8:
        return fused(*args)
    return modular(*args)


def solution(mesh):
    in_specs = (
        P("group", "batch"),
        P("group", None),
        P("group"),
        P("group"),
        P("group", None, None, None, None),
        P("group"),
        P("group"),
        P("group", None),
        P("group"),
        P("group"),
        P("group", "batch"),
    )
    out_specs = (
        P("group", "batch"),
        P("group", "batch"),
        P("group", None),
        P("group", None, None, None, None),
        P("group", None),
        P("group"),
        P("group"),
        P("group"),
        P("group"),
        P("group"),
        P("group"),
    )
    return jax.shard_map(local, mesh=mesh, in_specs=in_specs, out_specs=out_specs, check_vma=False)
```

```python
import functools

import jax
import jax.numpy as jnp
import numpy as np
from jax import lax
from jax.experimental import pallas as pl
from jax.experimental.pallas import tpu as pltpu
from jax.sharding import PartitionSpec as P

GW = 32
SIDE = 14
EPS = 1e-05
BLK = 256
HALF = 128
PAD = 16
F32 = jnp.float32
BF16 = jnp.bfloat16
MESH = pl.DeviceIdType.MESH
VMEM_LIMIT = 60 * 1024 * 1024


def silu_slope(values):
    sigma = jax.nn.sigmoid(values)
    return sigma * (1.0 + values * (1.0 - sigma))


def row_chunk(pixels):
    for size in (224, 208, 192, 176, 160, 144, 128, 112):
        if pixels % size == 0:
            return size
    return pixels


def over_rows(pixels, body):
    size = row_chunk(pixels)
    if size == pixels:
        body(0, size)
    else:

        @pl.loop(0, pixels // size)
        def _(step):
            body(pl.multiple_of(step * size, 16), size)


def coefficients(sums, params, count):
    center = sums[0:1] / count
    spread = sums[1:2] / count - center * center
    inverse = lax.rsqrt(spread + EPS)
    return center, inverse, params[0:1], params[1:2]


def standardize(values, coef):
    standard = (values - coef[0]) * coef[1]
    return standard, standard * coef[2] + coef[3]


def add_stats(ref, slot, first, second):
    ref[slot, 0:1] += jnp.sum(first, 0, keepdims=True)
    ref[slot, 1:2] += jnp.sum(second, 0, keepdims=True)


PHASE_START = [0]


def grid_step():
    return pl.program_id(0) - PHASE_START[-1]


def in_phase(start, steps, body):
    step = pl.program_id(0)

    @pl.when((step >= start) & (step < start + steps))
    def _():
        PHASE_START.append(start)
        try:
            body()
        finally:
            PHASE_START.pop()


def phase_block(start, steps, *dims):
    return pl.BlockSpec((1,) + dims, lambda j: (jnp.clip(j - start, 0, steps - 1),) + (0,) * len(dims))


def clear_stats(ref):
    @pl.when(grid_step() == 0)
    def _():
        ref[...] = jnp.zeros_like(ref)


def dot(a, b, dims=((1,), (0,))):
    return lax.dot_general(a, b, (dims, ((), ())), preferred_element_type=F32)


def devices(batches, members):
    row, me = lax.axis_index("batch"), lax.axis_index("group")
    across = [(lax.rem(row + step, batches), me) for step in range(1, batches)]
    along = [(row, lax.rem(me + step, members)) for step in range(1, members)]
    return row, me, across, along


def greet(others):
    barrier = pltpu.get_barrier_semaphore()
    for device in others:
        pl.semaphore_signal(barrier, inc=1, device_id=device, device_id_type=MESH)
    pl.semaphore_wait(barrier, len(others))


def remote(source, target, send, recv, device):
    return pltpu.make_async_remote_copy(
        src_ref=source, dst_ref=target, send_sem=send, recv_sem=recv, device_id=device, device_id_type=MESH
    )


def each(copies, what):
    for copy in copies:
        getattr(copy, what)()


def spread(source, target, send, recv, others, beside):
    copies = [
        remote(source, target.at[step], send.at[step], recv.at[step], device) for step, device in enumerate(others)
    ]
    each(copies, "start")
    each(beside, "start")
    each(copies, "wait")


def total_stats(ref, across, along, first_ref, second_ref, mid_ref, send1, recv1, send2, recv2, beside=()):
    mid_ref[0] = ref[...]
    spread(mid_ref.at[0], second_ref, send2, recv2, along, beside)
    total = mid_ref[0]
    for step in range(len(along)):
        total += second_ref[step]
    mid_ref[1] = total
    spread(mid_ref.at[1], first_ref, send1, recv1, across, ())
    for step in range(len(across)):
        total += first_ref[step]
    ref[...] = total


def stats_scratch(dims, batches, members):
    return [
        pltpu.VMEM((batches - 1,) + dims, F32),
        pltpu.VMEM((members - 1,) + dims, F32),
        pltpu.VMEM((2,) + dims, F32),
        pltpu.SemaphoreType.DMA((batches - 1,)),
        pltpu.SemaphoreType.DMA((batches - 1,)),
        pltpu.SemaphoreType.DMA((members - 1,)),
        pltpu.SemaphoreType.DMA((members - 1,)),
    ]


class Comm:
    def __init__(self, batches, members, collective_id, source=None, low=0, sizes=(), into=None, stream=False):
        self.batches, self.members, self.collective_id = batches, members, collective_id
        self.source, self.low, self.sizes, self.into, self.stream = source, low, sizes, into, stream
        self.high = low + sum(sizes)


def piece_copies(source, target, low, size, me, along, send, recv, staged=False):
    rows = pl.ds(low, size)
    last = len(along)
    copies = [
        remote(
            source.at[step if staged else device[1], rows], target.at[me, rows], send.at[step], recv.at[step], device
        )
        for step, device in enumerate(along)
    ]
    return copies + [
        pltpu.make_async_copy(source.at[last if staged else me, rows], target.at[me, rows], send.at[last])
    ]


class Late:
    def __init__(self, dims, dtype=F32):
        self.dims, self.dtype = dims, dtype


def call(kernel, grid, in_specs, out_specs, out_shape, scratch, flops, comm=None):
    if comm is None:
        in_specs = [whole(*spec.dims) if isinstance(spec, Late) else spec for spec in in_specs]
        return functools.partial(
            plain_call, kernel, grid, in_specs, out_specs, out_shape, scratch, flops, pltpu.CompilerParams(vmem_limit_bytes=VMEM_LIMIT)
        )
    n_in, n_out, n_scratch = len(in_specs), len(out_specs), len(scratch)
    stats = out_shape[-1].shape
    batches, members = comm.batches, comm.members

    sends = bool(comm.sizes)
    late = [index for index, spec in enumerate(in_specs) if isinstance(spec, Late)]
    late_specs = [in_specs[index] for index in late]

    def wrapped(*refs):
        refs = list(refs)
        ins = refs[:n_in]
        del refs[:n_in]
        source = refs.pop(0) if sends and not comm.stream else None
        if comm.into is not None:
            refs.pop(0)
        outs = refs[:n_out]
        del refs[:n_out]
        target = refs.pop(0) if sends else None
        own = refs[:n_scratch]
        del refs[:n_scratch]
        stats_refs = refs[:7]
        del refs[:7]
        if comm.stream:
            source = refs.pop(0)
        loads = []
        if late:
            load_sem = refs.pop(0)
            for place, index in enumerate(late):
                held = refs.pop(0)
                loads.append(pltpu.make_async_copy(ins[index], held, load_sem.at[place]))
                ins[index] = held
        row, me, across, along = devices(batches, members)
        step = pl.program_id(0)

        def copies(part):
            low = comm.low + sum(comm.sizes[:part])
            return piece_copies(
                source, target, low, comm.sizes[part], me, along, refs[0].at[part], refs[1].at[part], comm.stream
            )

        @pl.when(step == 0)
        def _():
            greet(across + along)
            if sends and not comm.stream:
                each(copies(0), "start")
            each(loads, "start")
            each(loads, "wait")

        kernel(*ins, *outs, *own)
        if comm.stream:
            source[step] = outs[0][0, : comm.high]
            rows = pl.ds(0, comm.sizes[0])

            @pl.when(step < members - 1)
            def _():
                device = (row, lax.rem(me + 1 + step, members))
                remote(
                    source.at[step, rows], target.at[me, rows], refs[0].at[0, step], refs[1].at[0, step], device
                ).start()

            @pl.when(step == members - 1)
            def _():
                pltpu.make_async_copy(source.at[step, rows], target.at[me, rows], refs[0].at[0, step]).start()

        @pl.when(step == pl.num_programs(0) - 1)
        def _():
            total_stats(outs[-1], across, along, *stats_refs, beside=copies(1) if sends else ())
            if sends:
                for part in range(2):
                    each(copies(part), "wait")

    scratch = list(scratch) + stats_scratch(stats, batches, members)
    in_specs, out_specs, out_shape = list(in_specs), list(out_specs), list(out_shape)
    extra, aliases = [], {}
    if sends:
        if comm.stream:
            dims, dtype = out_shape[0].shape, out_shape[0].dtype
            scratch.append(pltpu.VMEM((members, comm.high, dims[2]), dtype))
        else:
            dims, dtype = comm.source.shape, comm.source.dtype
            extra = [comm.source]
        if comm.into is not None:
            aliases = {len(in_specs) + len(extra): len(out_specs)}
            extra.append(comm.into)
        in_specs = [pl.BlockSpec(memory_space=pl.ANY) if isinstance(spec, Late) else spec for spec in in_specs]
        in_specs += [pl.BlockSpec(memory_space=pl.ANY)] * len(extra)
        if late:
            scratch.append(pltpu.SemaphoreType.DMA((len(late),)))
            scratch += [pltpu.VMEM(spec.dims, spec.dtype) for spec in late_specs]
        out_specs.append(pl.BlockSpec(memory_space=pl.ANY))
        out_shape.append(shape(dims, dtype))
        scratch += [pltpu.SemaphoreType.DMA((2, members)), pltpu.SemaphoreType.DMA((2, members - 1))]
    params = pltpu.CompilerParams(
        vmem_limit_bytes=VMEM_LIMIT, collective_id=comm.collective_id, has_side_effects=True
    )
    inner = functools.partial(
        plain_call, wrapped, grid, in_specs, out_specs, out_shape, scratch, flops, params, aliases=aliases
    )
    return lambda *args: inner(*args, *extra)


def plain_call(kernel, grid, in_specs, out_specs, out_shape, scratch, flops, params, *args, aliases={}):
    return pl.pallas_call(
        kernel,
        grid=grid,
        in_specs=in_specs,
        out_specs=out_specs,
        out_shape=out_shape,
        scratch_shapes=scratch,
        input_output_aliases=aliases,
        compiler_params=params,
        cost_estimate=pl.CostEstimate(flops=flops, bytes_accessed=20_000_000, transcendentals=0),
    )(*args)


def shape(dims, dtype=F32):
    return jax.ShapeDtypeStruct(dims, dtype)


def block(*dims):
    return pl.BlockSpec((1,) + dims, lambda j: (j,) + (0,) * len(dims))


def turned_block(members, *dims):
    def index(j):
        return (lax.rem(lax.axis_index("group") + 1 + j, members),) + (0,) * len(dims)

    return pl.BlockSpec((1,) + dims, index)


def whole(*dims):
    return pl.BlockSpec(dims, lambda j: (0,) * len(dims))


def reduce_kernel(x_ref, w_ref, out_ref, sum_ref):
    clear_stats(sum_ref)
    slot = grid_step()

    def body(start, size):
        rows = pl.ds(start, size)
        total = dot(x_ref[0, rows], w_ref[0])
        for source in range(1, x_ref.shape[0]):
            total += dot(x_ref[source, rows], w_ref[source])
        out_ref[0, rows] = total
        add_stats(sum_ref, slot, total, total * total)

    over_rows(x_ref.shape[1], body)


def reduce_product(x, weight, comm):
    blocks, pixels, _ = x.shape
    mids = weight.shape[2] // BLK
    return call(
        reduce_kernel,
        (mids,),
        [Late((blocks, pixels, BLK), BF16), pl.BlockSpec((blocks, BLK, BLK), lambda j: (0, 0, j))],
        [block(pixels, BLK), whole(mids, 2, BLK)],
        [shape((mids, pixels, BLK)), shape((mids, 2, BLK))],
        [],
        2 * pixels * blocks * BLK * mids * BLK,
        comm,
    )(x, weight)


def same_group():
    return lax.broadcasted_iota(jnp.int32, (BLK, BLK), 0) // GW == lax.broadcasted_iota(jnp.int32, (BLK, BLK), 1) // GW


def spread_weight(compact_ref, dense_ref):
    own = same_group()
    for tap in range(9):
        rows = pl.ds(tap * GW, GW)
        compact = jnp.concatenate([compact_ref[0, rows], compact_ref[1, rows]], 1).astype(F32)
        tiled = jnp.concatenate([compact] * (BLK // GW), 0)
        dense_ref[tap] = jnp.where(own, tiled, 0.0).astype(BF16)


def twice(mask):
    return jnp.concatenate([mask, mask], 1)


def fill(stack_ref, mask_ref, rows_start, size, values):
    rows = pl.ds(rows_start, size)
    target = pl.ds(rows_start + PAD, size)
    for half in range(2):
        part = values[:, half * HALF : (half + 1) * HALF]
        stack_ref[1, half, target] = part
        stack_ref[0, half, target] = part * mask_ref[1, rows]
        stack_ref[2, half, target] = part * mask_ref[0, rows]


def clear_edges(stack_ref, pixels):
    edge = jnp.zeros(stack_ref.shape[:2] + (PAD, HALF), F32)
    stack_ref[:, :, 0:PAD] = edge
    stack_ref[:, :, PAD + pixels : PAD + pixels + PAD] = edge


def window(stack_ref, start, size, row_off, col_off):
    rows = pl.ds(start + (PAD + row_off * SIDE + col_off), size)
    return jnp.concatenate([stack_ref[col_off + 1, half, rows] for half in range(2)], 1).astype(BF16)


def conv_rows(stack_ref, mask_ref, dense_ref, start, size, flipped=False):
    rows = pl.ds(start, size)
    total = None
    for row_off in (-1, 0, 1):
        part = None
        for col_off in (-1, 0, 1):
            values = window(stack_ref, start, size, row_off, col_off)
            tap = (row_off + 1) * 3 + col_off + 1
            term = dot(values, dense_ref[8 - tap], ((1,), (1,))) if flipped else dot(values, dense_ref[tap])
            part = term if part is None else part + term
        if row_off:
            part = part * twice(mask_ref[2 if row_off < 0 else 3, rows])
        total = part if total is None else total + part
    return total


def conv_kernel(count, red_ref, sums_ref, prm_ref, weight_ref, mask_ref, out_ref, stat_ref, stack_ref, dense_ref):
    pixels = red_ref.shape[1]
    spread_weight(weight_ref, dense_ref)
    clear_edges(stack_ref, pixels)
    coef = coefficients(sums_ref[0], prm_ref[0], count)

    def enter(start, size):
        _, norm = standardize(red_ref[0, pl.ds(start, size)], coef)
        fill(stack_ref, mask_ref, start, size, (norm * jax.nn.sigmoid(norm)).astype(BF16).astype(F32))

    over_rows(pixels, enter)
    clear_stats(stat_ref)
    slot = grid_step()

    def body(start, size):
        total = conv_rows(stack_ref, mask_ref, dense_ref, start, size)
        out_ref[0, pl.ds(start, size)] = total
        add_stats(stat_ref, slot, total, total * total)

    over_rows(pixels, body)


def conv(reduced, sums, params, weight, masks, count, comm):
    mids, pixels, _ = reduced.shape
    return call(
        functools.partial(conv_kernel, count),
        (mids,),
        [
            block(pixels, BLK),
            block(2, BLK),
            block(2, BLK),
            pl.BlockSpec((2,) + weight.shape[1:], lambda j: (j, 0, 0)),
            Late((4, pixels, HALF)),
        ],
        [block(pixels, BLK), whole(mids, 2, BLK)],
        [shape((mids, pixels, BLK)), shape((mids, 2, BLK))],
        [pltpu.VMEM((3, 2, pixels + 2 * PAD, HALF), F32), pltpu.VMEM((9, BLK, BLK), BF16)],
        2 * 9 * pixels * mids * BLK * BLK,
        comm,
    )(reduced, sums, params, weight, masks)


def conv_back_kernel(
    count,
    red_ref,
    sums_ref,
    prm_ref,
    grp_ref,
    gsums_ref,
    gprm_ref,
    up_ref,
    upsums_ref,
    weight_ref,
    mask_ref,
    *refs,
):
    out_ref, wgrad_ref, stat_ref, stack_ref, dense_ref, back_ref = refs
    pixels = red_ref.shape[1]
    spread_weight(weight_ref, dense_ref)
    clear_edges(stack_ref, pixels)
    coef = coefficients(sums_ref[0], prm_ref[0], count)
    gcoef = coefficients(gsums_ref[0], gprm_ref[0], count)
    scale = gcoef[2] * gcoef[1]
    up_mean = upsums_ref[0, 0:1] / count
    up_lean = upsums_ref[0, 1:2] / count

    def back(start, size):
        rows = pl.ds(start, size)
        standard, _ = standardize(grp_ref[0, rows], gcoef)
        values = (scale * (up_ref[0, rows] - up_mean - standard * up_lean)).astype(BF16)
        back_ref[1, rows] = values
        values = values.astype(F32)
        back_ref[0, rows] = (values * twice(mask_ref[2, rows])).astype(BF16)
        back_ref[2, rows] = (values * twice(mask_ref[3, rows])).astype(BF16)
        fill(stack_ref, mask_ref, start, size, values)

    over_rows(pixels, back)
    clear_stats(stat_ref)
    slot = grid_step()

    def body(start, size):
        rows = pl.ds(start, size)
        standard, norm = standardize(red_ref[0, rows], coef)
        up = conv_rows(stack_ref, mask_ref, dense_ref, start, size, True) * silu_slope(norm)
        out_ref[0, rows] = up
        add_stats(stat_ref, slot, up, up * standard)

    over_rows(pixels, body)

    def enter(start, size):
        _, norm = standardize(red_ref[0, pl.ds(start, size)], coef)
        fill(stack_ref, mask_ref, start, size, (norm * jax.nn.sigmoid(norm)).astype(BF16).astype(F32))

    over_rows(pixels, enter)
    own = same_group()
    for tap in range(9):
        full = dot(back_ref[tap // 3], window(stack_ref, 0, pixels, tap // 3 - 1, tap % 3 - 1), ((0,), (0,)))
        full = jnp.where(own, full, 0.0)
        kept = full[0:GW]
        for group in range(1, BLK // GW):
            kept += full[group * GW : (group + 1) * GW]
        for half in range(2):
            wgrad_ref[half, tap * GW : (tap + 1) * GW] = kept[:, half * HALF : (half + 1) * HALF].astype(BF16)
    for half in range(2):
        wgrad_ref[half, 9 * GW :] = jnp.zeros((wgrad_ref.shape[1] - 9 * GW, HALF), BF16)


def conv_back(reduced, sums, params, grouped, gsums, gparams, up, upsums, weight, masks, count, comm):
    mids, pixels, _ = reduced.shape
    return call(
        functools.partial(conv_back_kernel, count),
        (mids,),
        [
            block(pixels, BLK),
            block(2, BLK),
            block(2, BLK),
            block(pixels, BLK),
            block(2, BLK),
            block(2, BLK),
            block(pixels, BLK),
            block(2, BLK),
            pl.BlockSpec((2,) + weight.shape[1:], lambda j: (j, 0, 0)),
            Late((4, pixels, HALF)),
        ],
        [block(pixels, BLK), pl.BlockSpec((2,) + weight.shape[1:], lambda j: (j, 0, 0)), whole(mids, 2, BLK)],
        [shape((mids, pixels, BLK)), shape(weight.shape, BF16), shape((mids, 2, BLK))],
        [
            pltpu.VMEM((3, 2, pixels + 2 * PAD, HALF), F32),
            pltpu.VMEM((9, BLK, BLK), BF16),
            pltpu.VMEM((3, pixels, BLK), BF16),
        ],
        4 * 9 * pixels * mids * BLK * BLK,
        comm,
    )(reduced, sums, params, grouped, gsums, gparams, up, upsums, weight, masks)


def expand_kernel(count, grp_ref, gsums_ref, gprm_ref, w_ref, out_ref, act_ref, sum_ref):
    mids, pixels, _ = grp_ref.shape

    @pl.when(grid_step() == 0)
    def _():
        for mid in range(mids):
            coef = coefficients(gsums_ref[mid], gprm_ref[mid], count)

            def body(start, size):
                rows = pl.ds(start, size)
                _, norm = standardize(grp_ref[mid, rows], coef)
                act_ref[rows, mid * BLK : (mid + 1) * BLK] = (norm * jax.nn.sigmoid(norm)).astype(BF16)

            over_rows(pixels, body)

    clear_stats(sum_ref)
    slot = grid_step()

    def product(start, size):
        rows = pl.ds(start, size)
        total = dot(act_ref[rows], w_ref[0], ((1,), (1,)))
        out_ref[0, rows] = total
        add_stats(sum_ref, slot, total, total * total)

    over_rows(pixels, product)


def expand_product(grouped, gsums, gparams, weight, count, comm):
    mids, pixels, _ = grouped.shape
    blocks = weight.shape[0]
    return call(
        functools.partial(expand_kernel, count),
        (blocks,),
        [
            Late((mids, pixels, BLK)),
            whole(mids, 2, BLK),
            whole(mids, 2, BLK),
            block(BLK, mids * BLK),
        ],
        [block(pixels, BLK), whole(pixels, mids * BLK), whole(blocks, 2, BLK)],
        [shape((blocks, pixels, BLK)), shape((pixels, mids * BLK), BF16), shape((blocks, 2, BLK))],
        [],
        2 * pixels * blocks * BLK * mids * BLK,
        comm,
    )(grouped, gsums, gparams, weight)


def output_kernel(count, members, exp_ref, sums_ref, prm_ref, x_ref, grad_ref, out_ref, up_ref, stat_ref):
    coef = coefficients(sums_ref[0], prm_ref[0], count)
    clear_stats(stat_ref)
    slot = grid_step()
    if members:
        slot = lax.rem(lax.axis_index("group") + 1 + slot, members)

    def body(start, size):
        rows = pl.ds(start, size)
        standard, norm = standardize(exp_ref[0, rows], coef)
        summed = norm + x_ref[0, rows].astype(F32)
        sigma = jax.nn.sigmoid(summed)
        out_ref[0, rows] = (summed * sigma).astype(BF16)
        up = grad_ref[0, rows].astype(F32) * (sigma * (1.0 + summed * (1.0 - sigma)))
        up_ref[0, rows] = up
        add_stats(stat_ref, slot, up, up * standard)

    over_rows(exp_ref.shape[1], body)


def output(expanded, sums, params, x, grad, count, comm):
    blocks, pixels, _ = expanded.shape
    members = comm.members if comm else None
    one = functools.partial(turned_block, members) if comm else block
    return call(
        functools.partial(output_kernel, count, members),
        (blocks,),
        [one(pixels, BLK), one(2, BLK), one(2, BLK), one(pixels, BLK), one(pixels, BLK)],
        [one(pixels, BLK), one(pixels, BLK), whole(blocks, 2, BLK)],
        [shape((blocks, pixels, BLK), BF16), shape((blocks, pixels, BLK)), shape((blocks, 2, BLK))],
        [],
        20 * pixels * blocks * BLK,
        comm,
    )(expanded, sums, params, x, grad)


def expand_back_kernel(
    count,
    exp_ref,
    sums_ref,
    prm_ref,
    up_ref,
    upsums_ref,
    w_ref,
    grp_ref,
    gsums_ref,
    gprm_ref,
    act_ref,
    wgrad_ref,
    out_ref,
    stat_ref,
    keep_ref,
):
    blocks, pixels, _ = keep_ref.shape
    step = grid_step()
    clear_stats(stat_ref)

    @pl.when(step < blocks)
    def _():
        coef = coefficients(sums_ref[0], prm_ref[0], count)
        scale = coef[2] * coef[1]
        up_mean = upsums_ref[0, 0:1] / count
        up_lean = upsums_ref[0, 1:2] / count

        def back(start, size):
            rows = pl.ds(start, size)
            standard, _ = standardize(exp_ref[0, rows], coef)
            values = (scale * (up_ref[0, rows] - up_mean - standard * up_lean)).astype(BF16)
            keep_ref[step, rows] = values

        over_rows(pixels, back)
        weight_grad_block(keep_ref[step], act_ref, wgrad_ref, 0)

    @pl.when(step >= blocks)
    def _():
        coef = coefficients(gsums_ref[0], gprm_ref[0], count)

        def body(start, size):
            rows = pl.ds(start, size)
            total = dot(keep_ref[0, rows], w_ref[0])
            for source in range(1, blocks):
                total += dot(keep_ref[source, rows], w_ref[source])
            standard, norm = standardize(grp_ref[0, rows], coef)
            up = total * silu_slope(norm)
            out_ref[0, rows] = up
            add_stats(stat_ref, step - blocks, up, up * standard)

        over_rows(pixels, body)


def expand_back(expanded, sums, params, up, upsums, weight, grouped, gsums, gparams, act, count, comm):
    blocks, pixels, _ = expanded.shape
    mids = grouped.shape[0]

    def first(*dims):
        return pl.BlockSpec((1,) + dims, lambda j: (jnp.minimum(j, blocks - 1),) + (0,) * len(dims))

    def second(*dims):
        return pl.BlockSpec((1,) + dims, lambda j: (jnp.maximum(j - blocks, 0),) + (0,) * len(dims))

    return call(
        functools.partial(expand_back_kernel, count),
        (blocks + mids,),
        [
            first(pixels, BLK),
            first(2, BLK),
            first(2, BLK),
            first(pixels, BLK),
            first(2, BLK),
            pl.BlockSpec((blocks, BLK, BLK), lambda j: (0, 0, jnp.maximum(j - blocks, 0))),
            second(pixels, BLK),
            second(2, BLK),
            second(2, BLK),
            Late((pixels, mids * BLK), BF16),
        ],
        [first(BLK, mids * BLK), second(pixels, BLK), whole(mids, 2, BLK)],
        [shape((blocks, BLK, mids * BLK), BF16), shape((mids, pixels, BLK)), shape((mids, 2, BLK))],
        [pltpu.VMEM((blocks, pixels, BLK), BF16)],
        4 * pixels * blocks * BLK * mids * BLK,
        comm,
    )(expanded, sums, params, up, upsums, weight, grouped, gsums, gparams, act)


def first_back(count, red_ref, sums_ref, prm_ref, rup_ref, rupsums_ref, back_ref, loads=()):
    mids, pixels, _ = red_ref.shape
    for mid in range(mids):
        for load in loads[2 * mid : 2 * mid + 2]:
            load.wait()
        coef = coefficients(sums_ref[mid], prm_ref[mid], count)
        scale = coef[2] * coef[1]
        up_mean = rupsums_ref[mid, 0:1] / count
        up_lean = rupsums_ref[mid, 1:2] / count

        def body(start, size):
            rows = pl.ds(start, size)
            standard, _ = standardize(red_ref[mid, rows], coef)
            values = scale * (rup_ref[mid, rows] - up_mean - standard * up_lean)
            back_ref[rows, mid * BLK : (mid + 1) * BLK] = values.astype(BF16)

        over_rows(pixels, body)


def weight_grad_block(left, right_ref, out_ref, slot):
    for first in range(0, right_ref.shape[1], BLK):
        columns = slice(first, first + BLK)
        out_ref[slot, :, columns] = dot(left, right_ref[:, columns], ((0,), (0,))).astype(BF16)


def reduce_back_kernel(count, red_ref, sums_ref, prm_ref, rup_ref, rupsums_ref, x_ref, up_ref, w_ref, grad_ref, wgrad_ref, back_ref):
    @pl.when(pl.program_id(0) == 0)
    def _():
        first_back(count, red_ref, sums_ref, prm_ref, rup_ref, rupsums_ref, back_ref)

    def product(start, size):
        rows = pl.ds(start, size)
        total = dot(back_ref[rows], w_ref[0], ((1,), (1,)))
        grad_ref[0, rows] = (up_ref[0, rows] + total).astype(BF16)

    over_rows(x_ref.shape[1], product)
    weight_grad_block(x_ref[0], back_ref, wgrad_ref, 0)


def reduce_back(reduced, sums, params, rup, rupsums, x, up, weight, count):
    mids, pixels, _ = reduced.shape
    blocks = x.shape[0]
    return call(
        functools.partial(reduce_back_kernel, count),
        (blocks,),
        [
            whole(mids, pixels, BLK),
            whole(mids, 2, BLK),
            whole(mids, 2, BLK),
            whole(mids, pixels, BLK),
            whole(mids, 2, BLK),
            block(pixels, BLK),
            block(pixels, BLK),
            block(BLK, mids * BLK),
        ],
        [block(pixels, BLK), block(BLK, mids * BLK)],
        [shape((blocks, pixels, BLK), BF16), shape((blocks, BLK, mids * BLK), BF16)],
        [pltpu.VMEM((pixels, mids * BLK), BF16)],
        4 * pixels * blocks * BLK * mids * BLK,
    )(reduced, sums, params, rup, rupsums, x, up, weight)


def exchange_kernel(batches, members, x_ref, out_ref, *scratch):
    row, me, across, along = devices(batches, members)
    greet(across + along)
    out_ref[...] = x_ref[...]
    total_stats(out_ref, across, along, *scratch)


def exchange(values, batches, members, collective_id):
    return pl.pallas_call(
        functools.partial(exchange_kernel, batches, members),
        in_specs=[pl.BlockSpec(memory_space=pltpu.VMEM)],
        out_specs=pl.BlockSpec(memory_space=pltpu.VMEM),
        out_shape=shape(values.shape),
        scratch_shapes=stats_scratch(values.shape, batches, members),
        compiler_params=pltpu.CompilerParams(collective_id=collective_id, has_side_effects=True),
    )(values)


class Sends:
    def __init__(self, source, target, low, sizes, me, along, send, recv):
        self.parts = []
        for part, size in enumerate(sizes):
            self.parts.append(
                functools.partial(
                    piece_copies, source, target, low, size, me, along, send.at[part], recv.at[part]
                )
            )
            low += size

    def start(self, part):
        each(self.parts[part](), "start")

    def wait(self):
        for part in self.parts:
            each(part(), "wait")


def at_step(step, body):
    pl.when(pl.program_id(0) == step)(body)


def forward_kernel(count, batches, members, sizes, *refs):
    x_any, wr_ref, prm_ref, taps_ref, masks_any, gprm_ref, we_ref, src_ref = refs[:8]
    red_any, grp_any, act_any, exp_ref, sums_ref, gsums_ref, esums_ref, dst_ref = refs[8:16]
    x_held, masks, red, grp, act, stack, dense, psend, precv, load, keep = refs[16:27]
    stats = [refs[27 + 7 * index : 34 + 7 * index] for index in range(3)]
    row, me, across, along = devices(batches, members)
    mids, blocks = red.shape[0], x_held.shape[0]
    second, third, end = mids, 2 * mids, 2 * mids + blocks
    sends = Sends(src_ref, dst_ref, 0, sizes, me, along, psend, precv)
    loads = [pltpu.make_async_copy(x_any, x_held, load.at[0]), pltpu.make_async_copy(masks_any, masks, load.at[1])]
    kept = [
        pltpu.make_async_copy(held, out, keep.at[index])
        for index, (held, out) in enumerate(((red, red_any), (grp, grp_any), (act, act_any)))
    ]

    def begin():
        greet(across + along)
        sends.start(0)
        each(loads, "start")
        each(loads, "wait")

    at_step(0, begin)

    def product():
        reduce_kernel(x_held, wr_ref, red.at[pl.ds(grid_step(), 1)], sums_ref)

    in_phase(0, mids, product)

    def exchange_first():
        kept[0].start()
        total_stats(sums_ref, across, along, *stats[0], beside=sends.parts[1]())
        sends.start(2)

    at_step(second - 1, exchange_first)

    def conv_phase():
        own = pl.ds(grid_step(), 1)
        conv_kernel(
            count, red.at[own], sums_ref.at[own], prm_ref, taps_ref, masks, grp.at[own], gsums_ref, stack, dense
        )

    in_phase(second, mids, conv_phase)

    def exchange_second():
        kept[1].start()
        total_stats(gsums_ref, across, along, *stats[1], beside=sends.parts[3]())
        sends.start(4)

    at_step(third - 1, exchange_second)
    in_phase(third, blocks, lambda: expand_kernel(count, grp, gsums_ref, gprm_ref, we_ref, exp_ref, act, esums_ref))

    def finish():
        kept[2].start()
        total_stats(esums_ref, across, along, *stats[2], beside=sends.parts[5]())
        each(kept, "wait")
        sends.wait()

    at_step(end - 1, finish)


def forward(x, reduce_full, reduce_params, taps, masks, group_params, expand_full, source, sizes, count, batches, members):
    blocks, pixels, _ = x.shape
    mid_total = reduce_full.shape[2]
    mids = mid_total // BLK
    anywhere = pl.BlockSpec(memory_space=pl.ANY)
    dma = pltpu.SemaphoreType.DMA
    mid_dims, sum_dims = (mids, pixels, BLK), (mids, 2, BLK)
    scratch = [
        pltpu.VMEM(x.shape, BF16),
        pltpu.VMEM(masks.shape, F32),
        pltpu.VMEM(mid_dims, F32),
        pltpu.VMEM(mid_dims, F32),
        pltpu.VMEM((pixels, mid_total), BF16),
        pltpu.VMEM((3, 2, pixels + 2 * PAD, HALF), F32),
        pltpu.VMEM((9, BLK, BLK), BF16),
        dma((len(sizes), members)),
        dma((len(sizes), members - 1)),
        dma((2,)),
        dma((3,)),
    ]
    for dims in (sum_dims, sum_dims, (blocks, 2, BLK)):
        scratch += stats_scratch(dims, batches, members)
    return pl.pallas_call(
        functools.partial(forward_kernel, count, batches, members, sizes),
        grid=(2 * mids + blocks,),
        in_specs=[
            anywhere,
            pl.BlockSpec((blocks, BLK, BLK), lambda j: (0, 0, jnp.minimum(j, mids - 1))),
            phase_block(mids, mids, 2, BLK),
            pl.BlockSpec((2,) + taps.shape[1:], lambda j: (jnp.clip(j - mids, 0, mids - 1), 0, 0)),
            anywhere,
            whole(*sum_dims),
            phase_block(2 * mids, blocks, BLK, mid_total),
            anywhere,
        ],
        out_specs=[
            anywhere,
            anywhere,
            anywhere,
            phase_block(2 * mids, blocks, pixels, BLK),
            whole(*sum_dims),
            whole(*sum_dims),
            whole(blocks, 2, BLK),
            anywhere,
        ],
        out_shape=[
            shape(mid_dims),
            shape(mid_dims),
            shape((pixels, mid_total), BF16),
            shape(x.shape),
            shape(sum_dims),
            shape(sum_dims),
            shape((blocks, 2, BLK)),
            shape(source.shape, BF16),
        ],
        scratch_shapes=scratch,
        compiler_params=pltpu.CompilerParams(vmem_limit_bytes=VMEM_LIMIT, collective_id=1, has_side_effects=True),
    )(x, reduce_full, reduce_params, taps, masks, group_params, expand_full, source)


def backward_kernel(count, batches, members, low, sizes, *refs):
    exp_ref, esums_ref, eprm_ref, up_ref, upsums_ref, we_ref, grp_ref, gsums_ref, gprm_ref = refs[:9]
    red_ref, sums_ref, prm_ref, taps_ref, act_any, masks_any, src_ref, _ = refs[9:17]
    epart_ref, rup_ref, tpart_ref, gstats_ref, rstats_ref, dst_ref = refs[17:23]
    keep, gup, act, masks, stack, dense, back, psend, precv, load = refs[23:33]
    stats = [refs[33 + 7 * index : 40 + 7 * index] for index in range(2)]
    row, me, across, along = devices(batches, members)
    blocks, mids = keep.shape[0], gup.shape[0]
    middle, second, end = blocks, blocks + mids, blocks + 2 * mids
    sends = Sends(src_ref, dst_ref, low, sizes, me, along, psend, precv)
    loads = [pltpu.make_async_copy(act_any, act, load.at[0]), pltpu.make_async_copy(masks_any, masks, load.at[1])]

    def begin():
        greet(across + along)
        sends.start(0)
        each(loads, "start")
        each(loads, "wait")

    at_step(0, begin)

    def expand_phase():
        place = jnp.clip(grid_step() - middle, 0, mids - 1)
        expand_back_kernel(
            count,
            exp_ref,
            esums_ref,
            eprm_ref,
            up_ref,
            upsums_ref,
            we_ref,
            grp_ref,
            gsums_ref,
            gprm_ref,
            act,
            epart_ref,
            gup.at[pl.ds(place, 1)],
            gstats_ref,
            keep,
        )

    in_phase(0, second, expand_phase)

    def exchange_first():
        total_stats(gstats_ref, across, along, *stats[0], beside=sends.parts[1]())
        sends.start(2)

    at_step(second - 1, exchange_first)

    def conv_phase():
        own = pl.ds(grid_step(), 1)
        conv_back_kernel(
            count,
            red_ref,
            sums_ref,
            prm_ref,
            grp_ref,
            gsums_ref,
            gprm_ref,
            gup.at[own],
            gstats_ref.at[own],
            taps_ref,
            masks,
            rup_ref,
            tpart_ref,
            rstats_ref,
            stack,
            dense,
            back,
        )

    in_phase(second, mids, conv_phase)

    def finish():
        total_stats(rstats_ref, across, along, *stats[1], beside=sends.parts[3]())
        sends.wait()

    at_step(end - 1, finish)


def backward(
    expanded,
    esums,
    eparams,
    up,
    upsums,
    expand_full,
    grouped,
    gsums,
    gparams,
    reduced,
    sums,
    params,
    taps,
    act,
    masks,
    source,
    into,
    low,
    sizes,
    count,
    batches,
    members,
):
    blocks, pixels, _ = expanded.shape
    mids = grouped.shape[0]
    mid_total = mids * BLK
    anywhere = pl.BlockSpec(memory_space=pl.ANY)
    dma = pltpu.SemaphoreType.DMA
    second = blocks + mids

    def both(*dims):
        def index(j):
            return (jnp.where(j < second, jnp.maximum(j - blocks, 0), j - second),) + (0,) * len(dims)

        return pl.BlockSpec((1,) + dims, index)

    first = functools.partial(phase_block, 0, blocks)
    last = functools.partial(phase_block, second, mids)
    pairs = pl.BlockSpec((2,) + taps.shape[1:], lambda j: (jnp.clip(j - second, 0, mids - 1), 0, 0))
    scratch = [
        pltpu.VMEM((blocks, pixels, BLK), BF16),
        pltpu.VMEM((mids, pixels, BLK), F32),
        pltpu.VMEM((pixels, mid_total), BF16),
        pltpu.VMEM(masks.shape, F32),
        pltpu.VMEM((3, 2, pixels + 2 * PAD, HALF), F32),
        pltpu.VMEM((9, BLK, BLK), BF16),
        pltpu.VMEM((3, pixels, BLK), BF16),
        dma((len(sizes), members)),
        dma((len(sizes), members - 1)),
        dma((2,)),
    ]
    for _ in range(2):
        scratch += stats_scratch((mids, 2, BLK), batches, members)
    return pl.pallas_call(
        functools.partial(backward_kernel, count, batches, members, low, sizes),
        grid=(second + mids,),
        in_specs=[
            first(pixels, BLK),
            first(2, BLK),
            first(2, BLK),
            first(pixels, BLK),
            first(2, BLK),
            pl.BlockSpec((blocks, BLK, BLK), lambda j: (0, 0, jnp.clip(j - blocks, 0, mids - 1))),
            both(pixels, BLK),
            both(2, BLK),
            both(2, BLK),
            last(pixels, BLK),
            last(2, BLK),
            last(2, BLK),
            pairs,
            anywhere,
            anywhere,
            anywhere,
            anywhere,
        ],
        out_specs=[
            first(BLK, mid_total),
            last(pixels, BLK),
            pairs,
            whole(mids, 2, BLK),
            whole(mids, 2, BLK),
            anywhere,
        ],
        out_shape=[
            shape((blocks, BLK, mid_total), BF16),
            shape((mids, pixels, BLK)),
            shape(taps.shape, BF16),
            shape((mids, 2, BLK)),
            shape((mids, 2, BLK)),
            shape(source.shape, BF16),
        ],
        scratch_shapes=scratch,
        input_output_aliases={16: 5},
        compiler_params=pltpu.CompilerParams(vmem_limit_bytes=VMEM_LIMIT, collective_id=5, has_side_effects=True),
    )(
        expanded,
        esums,
        eparams,
        up,
        upsums,
        expand_full,
        grouped,
        gsums,
        gparams,
        reduced,
        sums,
        params,
        taps,
        act,
        masks,
        source,
        into,
    )


def turn(source_ref, target_ref, slot, chunk):
    first = (49 * chunk) // 4

    @pl.loop(0, 13)
    def _(tile):
        columns = pl.ds(pl.multiple_of((first + tile) * HALF, HALF), HALF)
        rows = pl.ds(pl.multiple_of(tile * HALF, HALF), HALF)
        target_ref[slot, rows] = source_ref[:, columns].T


def turned(target_ref, slot, chunk, pixels):
    return target_ref.at[slot, pl.ds(pl.multiple_of(32 * (chunk % 4), 16), pixels)]


def opening_kernel(batches, members, *refs):
    x_ref, grad_ref, wr_ref, we_ref, wg_ref = refs[:5]
    vectors = refs[5:11]
    xp_ref, gradt_ref, wr_out, we_out, wg_out, prm_out = refs[11:17]
    xin, xturn, gin, gturn, prm_ref, load, own, xsend, xrecv, gsend, psend, precv = refs[17:29]
    zsend, zrecv, ysend, yrecv, fsend, frecv = refs[29:]
    row, me, across, along = devices(batches, members)
    pixels = xp_ref.shape[1]
    load_x = pltpu.make_async_copy(x_ref, xin, load.at[0])
    load_grad = pltpu.make_async_copy(grad_ref, gin, load.at[1])
    load_x.start()
    load_grad.start()
    weights = [(wr_ref, wr_out), (wg_ref, wg_out), (we_ref, we_out)]
    height, side = me // 2, me % 2
    levels = members // 2
    line = [(row, lax.rem(me + 2 * step, members)) for step in range(1, levels)]
    peer = (row, height * 2 + 1 - side)
    local_copies = []
    parts = []
    for index, (source, target) in enumerate(weights):
        size = source.shape[0] // batches
        part = pl.ds(pl.multiple_of(row * size, 16), size)
        parts.append(part)
        local_copies.append(pltpu.make_async_copy(source.at[part], target.at[height, side, part], own.at[index]))
    each(local_copies, "start")
    place = 0
    for vector in vectors:
        for low in range(0, vector.shape[0], HALF):
            prm_ref[place : place + 1] = vector[low : low + HALF].reshape(1, HALF)
            place += 1
    prm_own = pltpu.make_async_copy(prm_ref, prm_out.at[me], own.at[3])
    prm_own.start()
    greet(across + along)
    copies = [prm_own]
    first = []
    for index, (source, target) in enumerate(weights):
        for step, device in enumerate(line):
            first.append(
                remote(
                    source.at[parts[index]],
                    target.at[height, side, parts[index]],
                    zsend.at[index, step],
                    zrecv.at[index, step],
                    device,
                )
            )
    for step, device in enumerate(along):
        copy = remote(prm_ref, prm_out.at[me], psend.at[step], precv.at[step], device)
        copy.start()
        copies.append(copy)
    each(first, "start")
    load_x.wait()
    for step, device in enumerate(along):
        turn(xin, xturn, step, device[1])
        copy = remote(turned(xturn, step, device[1], pixels), xp_ref.at[me], xsend.at[step], xrecv.at[step], device)
        copy.start()
        copies.append(copy)
    last = members - 1
    turn(xin, xturn, last, me)
    copy = pltpu.make_async_copy(turned(xturn, last, me, pixels), xp_ref.at[me], xsend.at[last])
    copy.start()
    copies.append(copy)
    load_grad.wait()
    for member in range(members):
        turn(gin, gturn, member, member)
        copy = pltpu.make_async_copy(turned(gturn, member, member, pixels), gradt_ref.at[member], gsend.at[member])
        copy.start()
        copies.append(copy)
    each(local_copies, "wait")
    far, near = (lax.bitwise_xor(row, 2), me), (lax.bitwise_xor(row, 1), me)
    second, third = [], []
    for index, (_, target) in enumerate(weights):
        each(first[index * len(line) : (index + 1) * len(line)], "wait")
        held = target.at[:, side, parts[index]]
        second.append(remote(held, held, ysend.at[index], yrecv.at[index], peer))
        second[-1].start()
    for index, (_, target) in enumerate(weights):
        second[index].wait()
        held = target.at[:, :, parts[index]]
        third.append(remote(held, held, fsend.at[index, 0], frecv.at[index, 0], far))
        third[-1].start()
    for index, (source, target) in enumerate(weights):
        size = source.shape[0] // batches
        third[index].wait()
        for step, origin in enumerate((row, lax.bitwise_xor(row, 2))):
            held = target.at[:, :, pl.ds(pl.multiple_of(origin * size, 16), size)]
            copy = remote(held, held, fsend.at[index, 1 + step], frecv.at[index, 1 + step], near)
            copy.start()
            copies.append(copy)
    each(copies, "wait")


def opening(block_input, out_grad, reduce_weight, expand_weight, taps, vectors, batches, members):
    channels, row_pixels = block_input.shape
    pixels = row_pixels // members
    dma = pltpu.SemaphoreType.DMA
    other, across, levels = members - 1, batches - 1, members // 2
    padded = 13 * HALF
    lines = sum(vector.shape[0] for vector in vectors) // HALF
    weights = [reduce_weight, expand_weight, taps]
    x, grad, *gathered, params = pl.pallas_call(
        functools.partial(opening_kernel, batches, members),
        in_specs=[pl.BlockSpec(memory_space=pl.ANY)] * 5 + [pl.BlockSpec(memory_space=pltpu.VMEM)] * len(vectors),
        out_specs=[pl.BlockSpec(memory_space=pl.ANY)] * 6,
        out_shape=[shape((members, pixels, channels), BF16)] * 2
        + [shape((levels, 2) + weight.shape, BF16) for weight in weights]
        + [shape((members, lines, HALF))],
        scratch_shapes=[
            pltpu.VMEM((channels, row_pixels), BF16),
            pltpu.VMEM((members, padded, channels), BF16),
            pltpu.VMEM((channels, row_pixels), BF16),
            pltpu.VMEM((members, padded, channels), BF16),
            pltpu.VMEM((lines, HALF), F32),
            dma((2,)),
            dma((4,)),
            dma((members,)),
            dma((other,)),
            dma((members,)),
            dma((other,)),
            dma((other,)),
            dma((3, levels - 1)),
            dma((3, levels - 1)),
            dma((3,)),
            dma((3,)),
            dma((3, across)),
            dma((3, across)),
        ],
        compiler_params=pltpu.CompilerParams(vmem_limit_bytes=VMEM_LIMIT, collective_id=0, has_side_effects=True),
    )(block_input, out_grad, *weights, *vectors)
    gathered = [full.reshape((members,) + full.shape[2:]) for full in gathered]
    return x, grad, *gathered, params


class Reduce:
    def __init__(self, part, out, row, me, refs, source=None):
        self.part, self.out, self.row = part, out, row
        self.source = part if source is None else source
        self.height, self.side = me // 2, me % 2
        self.place, self.core = row // 2, row % 2
        self.fresh, self.chip, self.cross, self.held, self.pair, self.line, self.second, self.total = refs[:8]
        self.send, self.recv = refs[8:]
        self.levels = self.held.shape[0]
        self.size = self.total.shape[0]
        self.near = (self.place * 2 + 1 - self.core, me)
        self.far = ((1 - self.place) * 2 + self.core, me)
        self.peer = (row, self.height * 2 + 1 - self.side)
        self.along = [(row, lax.rem(me + 2 * step, 2 * self.levels)) for step in range(1, self.levels)]

    def rows(self, row):
        return pl.ds(pl.multiple_of(row * self.size, 16), self.size)

    def copy(self, source, target, index, device):
        return remote(source, target, self.send.at[index], self.recv.at[index], device)

    def over_cores(self):
        return [
            self.copy(self.source.at[:, self.rows(2 * place + 1 - self.core)], self.fresh.at[place], place, self.near)
            for place in range(2)
        ]

    def add_cores(self):
        @pl.loop(0, 2 * self.levels)
        def _(member):
            for place in range(2):
                total = self.part[member, self.rows(2 * place + self.core)].astype(F32)
                self.chip[place, member] = (total + self.fresh[place, member].astype(F32)).astype(BF16)

    def over_x(self):
        return [self.copy(self.chip.at[1 - self.place], self.cross, 2, self.far)]

    def add_x(self):
        @pl.loop(0, self.levels)
        def _(level):
            for side in range(2):
                member = 2 * level + side
                total = self.chip[self.place, member].astype(F32) + self.cross[member].astype(F32)
                self.held[level, side] = total.astype(BF16)

    def over_pair(self):
        return [self.copy(self.held.at[:, 1 - self.side], self.pair, 3, self.peer)]

    def add_pair(self):
        @pl.loop(0, self.levels)
        def _(level):
            total = self.held[level, self.side].astype(F32) + self.pair[level].astype(F32)
            self.line[level] = total.astype(BF16)

    def over_line(self):
        return [
            self.copy(self.line.at[device[1] // 2], self.second.at[step], 4 + step, device)
            for step, device in enumerate(self.along)
        ]

    def add_line(self):
        total = self.line[self.height].astype(F32)
        for step in range(len(self.along)):
            total += self.second[step].astype(F32)
        self.total[...] = total

    def keep(self):
        return [pltpu.make_async_copy(self.total, self.out.at[self.rows(self.row)], self.send.at[10])]

    def share_x(self):
        return [self.copy(self.total, self.out.at[self.rows(self.row)], 7, self.far)]

    def share_cores(self):
        own = self.copy(self.total, self.out.at[self.rows(self.row)], 8, self.near)
        rows = self.rows((1 - self.place) * 2 + self.core)
        return [own, self.copy(self.out.at[rows], self.out.at[rows], 9, self.near)]


def reduce_scratch(dims, batches, members):
    rows, columns = dims[1] // batches, dims[2]
    levels = members // 2
    return [
        pltpu.VMEM((2, members, rows, columns), BF16),
        pltpu.VMEM((2, members, rows, columns), BF16),
        pltpu.VMEM((members, rows, columns), BF16),
        pltpu.VMEM((levels, 2, rows, columns), BF16),
        pltpu.VMEM((levels, rows, columns), BF16),
        pltpu.VMEM((levels, rows, columns), BF16),
        pltpu.VMEM((levels - 1, rows, columns), BF16),
        pltpu.VMEM((rows, columns), F32),
        pltpu.SemaphoreType.DMA((11,)),
        pltpu.SemaphoreType.DMA((10,)),
    ]


HELD_BACK = 4
EARLY = 3


def closing_steps(step, members):
    late = jnp.maximum(step - members, EARLY)
    return jnp.where(step < EARLY, step, late), jnp.clip(step - EARLY, 0, members - 1)


def closing_kernel(count, batches, members, low, size, *refs):
    red_ref, sums_ref, prm_ref, rup_ref, rupsums_ref, x_ref, up_ref, w_ref, epart_ref, tpart_ref, src_ref, _ = refs[:12]
    recv_ref, rout_ref, eout_ref, tout_ref, dst_ref = refs[12:17]
    back_ref, grad_ref, wpart_ref, gsend, grecv, psend, precv = refs[17:24]
    red_held, rup_held, epart_held, load_sem = refs[54:]
    row, me, across, along = devices(batches, members)
    step = pl.program_id(0)
    last = members - 1
    expand_sum = Reduce(epart_held, eout_ref, row, me, refs[24:34], epart_ref)
    taps_sum = Reduce(tpart_ref, tout_ref, row, me, refs[34:44])
    reduce_sum = Reduce(wpart_ref, rout_ref, row, me, refs[44:54])
    parts = (expand_sum, taps_sum, reduce_sum)
    grad_step, weight_step = closing_steps(step, members)

    def pieces():
        return piece_copies(src_ref, dst_ref, low, size, me, along, psend, precv)

    def send(index):
        device = (row, lax.rem(me + 1 + index, members))
        return remote(grad_ref.at[index], recv_ref.at[me], gsend.at[index], grecv.at[index], device)

    mids = red_held.shape[0]
    load_part = pltpu.make_async_copy(epart_ref, epart_held, load_sem.at[2 * mids])

    @pl.when(step == 0)
    def _():
        greet(across + along)
        each(pieces(), "start")
        loads = []
        for mid in range(mids):
            for which, (source, held) in enumerate(((red_ref, red_held), (rup_ref, rup_held))):
                loads.append(pltpu.make_async_copy(source.at[mid], held.at[mid], load_sem.at[2 * mid + which]))
        each(loads, "start")
        load_part.start()
        each(expand_sum.over_cores(), "start")
        each(taps_sum.over_cores(), "start")
        first_back(count, red_held, sums_ref, prm_ref, rup_held, rupsums_ref, back_ref, loads)

    weight_turn = (step >= EARLY) & (step < EARLY + members)

    @pl.when(weight_turn)
    def _():
        weight_grad_block(x_ref[0], back_ref, wpart_ref, lax.rem(me + 1 + weight_step, members))

    @pl.when(jnp.logical_not(weight_turn))
    def _():
        def product(start, size):
            part = pl.ds(start, size)
            total = dot(back_ref[part], w_ref[0], ((1,), (1,)))
            grad_ref[grad_step, part] = (up_ref[0, part] + total).astype(BF16)

        over_rows(x_ref.shape[1], product)

        @pl.when(grad_step < last - HELD_BACK)
        def _():
            send(grad_step).start()

    @pl.when(step == EARLY)
    def _():
        load_part.wait()
        for part in parts[:2]:
            each(part.over_cores(), "wait")
            part.add_cores()
            each(part.over_x(), "start")

    @pl.when(step == EARLY + members - 1)
    def _():
        each(reduce_sum.over_cores(), "start")
        for part in parts[:2]:
            each(part.over_x(), "wait")
            part.add_x()
            each(part.over_pair(), "start")

    @pl.when(step == EARLY + members)
    def _():
        each(reduce_sum.over_cores(), "wait")
        reduce_sum.add_cores()
        each(reduce_sum.over_x(), "start")

    @pl.when(step == 2 * members - 1)
    def _():
        own = pltpu.make_async_copy(grad_ref.at[last], recv_ref.at[me], gsend.at[last])
        own.start()
        send(last - HELD_BACK).start()
        for part in parts[:2]:
            each(part.over_pair(), "wait")
            part.add_pair()
            each(part.over_line(), "start")
        each(reduce_sum.over_x(), "wait")
        reduce_sum.add_x()
        each(reduce_sum.over_pair(), "start")
        each(reduce_sum.over_pair(), "wait")
        reduce_sum.add_pair()
        each(reduce_sum.over_line(), "start")
        for index in range(last - HELD_BACK + 1, last):
            send(index).start()
        for part in parts:
            each(part.over_line(), "wait")
            part.add_line()
            each(part.share_x() + part.keep(), "start")
        for part in parts:
            each(part.share_x(), "wait")
            each(part.share_cores(), "start")
        own.wait()
        each(pieces(), "wait")
        for index in range(last):
            send(index).wait()
        for part in parts:
            each(part.share_cores() + part.keep(), "wait")


def closing(
    reduced, sums, params, rup, rupsums, x, up, weight, epart, tpart, source, into, low, size, count, batches, members
):
    mids, pixels, _ = reduced.shape
    blocks = x.shape[0]
    once = pl.Buffered(1)

    def keep(*dims):
        return pl.BlockSpec(dims, lambda j: (0,) * len(dims), pipeline_mode=once)

    def turn_block(which, *dims):
        def index(j):
            return (lax.rem(lax.axis_index("group") + 1 + closing_steps(j, members)[which], members),) + (0,) * len(dims)

        return pl.BlockSpec((1,) + dims, index)

    anywhere = pl.BlockSpec(memory_space=pl.ANY)
    dma = pltpu.SemaphoreType.DMA
    wdims = (blocks, BLK, mids * BLK)
    scratch = [
        pltpu.VMEM((pixels, mids * BLK), BF16),
        pltpu.VMEM((blocks, pixels, BLK), BF16),
        pltpu.VMEM(wdims, BF16),
        dma((members,)),
        dma((members - 1,)),
        dma((members,)),
        dma((members - 1,)),
    ]
    for dims in (wdims, tpart.shape, wdims):
        scratch += reduce_scratch(dims, batches, members)
    scratch += [
        pltpu.VMEM((mids, pixels, BLK), F32),
        pltpu.VMEM((mids, pixels, BLK), F32),
        pltpu.VMEM(wdims, BF16),
        dma((2 * mids + 1,)),
    ]
    return pl.pallas_call(
        functools.partial(closing_kernel, count, batches, members, low, size),
        grid=(2 * blocks,),
        in_specs=[
            anywhere,
            keep(mids, 2, BLK),
            keep(mids, 2, BLK),
            anywhere,
            keep(mids, 2, BLK),
            turn_block(1, pixels, BLK),
            turn_block(0, pixels, BLK),
            turn_block(0, BLK, mids * BLK),
            anywhere,
            keep(*tpart.shape),
            anywhere,
            anywhere,
        ],
        out_specs=[anywhere] * 5,
        out_shape=[
            shape((members, pixels, BLK), BF16),
            shape(wdims[1:]),
            shape(wdims[1:]),
            shape(tpart.shape[1:]),
            shape(source.shape, BF16),
        ],
        scratch_shapes=scratch,
        input_output_aliases={11: 4},
        compiler_params=pltpu.CompilerParams(vmem_limit_bytes=VMEM_LIMIT, collective_id=7, has_side_effects=True),
    )(reduced, sums, params, rup, rupsums, x, up, weight, epart, tpart, source, into)


def own_parts(reduce_ref, group_ref, expand_ref, outs):
    me = lax.axis_index("group")
    half = pl.ds(pl.multiple_of((me % 2) * HALF, HALF), HALF)
    for index, stats_ref in enumerate((reduce_ref, group_ref)):
        for which in range(2):
            outs[2 * index + 1 - which][...] = stats_ref[me // 2, which : which + 1, half]
    for which in range(2):
        outs[5 - which][...] = expand_ref[me, which : which + 1]


def turn_out_kernel(first_ref, second_ref, reduce_ref, group_ref, expand_ref, first_out, second_out, *outs):
    own = lax.broadcasted_iota(jnp.int32, (BLK, BLK), 0) == lax.broadcasted_iota(jnp.int32, (BLK, BLK), 1)
    identity = jnp.where(own, 1.0, 0.0).astype(BF16)
    half = pl.num_programs(0) // 2

    @pl.when(pl.program_id(0) == 0)
    def _():
        own_parts(reduce_ref, group_ref, expand_ref, outs)

    def turn_part(in_ref, out_ref):
        for low in range(0, in_ref.shape[0], HALF):
            part = dot(identity, in_ref[low : low + HALF], ((1,), (1,)))
            out_ref[:, low : low + HALF] = part.astype(out_ref.dtype)

    @pl.when(pl.program_id(0) < half)
    def _():
        turn_part(first_ref, first_out)

    @pl.when(pl.program_id(0) >= half)
    def _():
        turn_part(second_ref, second_out)


def turn_out(first, second, stats):
    sizes = (HALF,) * 4 + (BLK,) * 2
    rows, channels = first.shape
    parts = 2
    size = rows // parts

    def early(j):
        return jnp.minimum(j, parts - 1)

    def late(j):
        return jnp.maximum(j - parts, 0)

    return call(
        turn_out_kernel,
        (2 * parts,),
        [
            pl.BlockSpec((size, channels), lambda j: (early(j), 0)),
            pl.BlockSpec((size, channels), lambda j: (late(j), 0)),
        ]
        + [whole(*part.shape) for part in stats],
        [
            pl.BlockSpec((channels, size), lambda j: (0, early(j))),
            pl.BlockSpec((channels, size), lambda j: (0, late(j))),
        ]
        + [whole(1, width) for width in sizes],
        [shape((channels, rows)), shape((channels, rows), BF16)] + [shape((1, width)) for width in sizes],
        [],
        4 * rows * channels * BLK,
    )(first, second, *stats)


def pixel_masks(pixels):
    place = np.arange(pixels)
    tall, wide = (place // SIDE) % SIDE, place % SIDE
    masks = np.stack([wide != 0, wide != SIDE - 1, tall != 0, tall != SIDE - 1])
    return jnp.asarray(np.broadcast_to(masks[:, :, None], (4, pixels, HALF)).astype(np.float32))


def own_part(stats, which, length):
    return lax.dynamic_slice_in_dim(stats[:, which].reshape(-1), lax.axis_index("group") * length, length, 0)


TAP_ROWS = 320


def fused(
    block_input,
    reduce_weight,
    reduce_gain,
    reduce_bias,
    group_weight,
    group_gain,
    group_bias,
    expand_weight,
    expand_gain,
    expand_bias,
    out_grad,
):
    batches, members = lax.axis_size("batch"), lax.axis_size("group")
    channels, row_pixels = block_input.shape
    pixels = row_pixels // members
    count = row_pixels * batches
    vectors = [reduce_gain, reduce_bias, group_gain, group_bias, expand_gain, expand_bias]
    taps = group_weight.reshape(-1, 9, GW, GW).transpose(1, 2, 0, 3).reshape(9 * GW, HALF)
    taps = jnp.pad(taps, ((0, TAP_ROWS - 9 * GW), (0, 0)))
    masks = pixel_masks(pixels)
    x, grad_turned, reduce_full, expand_full, taps_full, packs = opening(
        block_input, out_grad, reduce_weight, expand_weight, taps, vectors, batches, members
    )
    vectors = packs[:, :4].reshape(-1, 2, 4, HALF).transpose(0, 2, 1, 3).reshape(-1, 4, BLK)
    reduce_params, group_params = vectors[:, :2], vectors[:, 2:]
    expand_params = packs[:, 4:].reshape(-1, 2, BLK)

    sizes = (208, 240, 304, 240, 304)
    reduced, grouped, act, expanded, reduce_sums, group_sums, expand_sums, grad = forward(
        x,
        reduce_full,
        reduce_params,
        taps_full,
        masks,
        group_params,
        expand_full,
        grad_turned,
        sizes + (pixels - sum(sizes),),
        count,
        batches,
        members,
    )
    sends = Comm(batches, members, 4, None, 0, (208, 112), None, True)
    out, upstream, expand_stats, moved = output(expanded, expand_sums, expand_params, x, grad, count, sends)
    sizes = (416, 144, 432, 112)
    expand_part, reduce_up, taps_part, group_stats, reduce_stats, moved = backward(
        expanded,
        expand_sums,
        expand_params,
        upstream,
        expand_stats,
        expand_full,
        grouped,
        group_sums,
        group_params,
        reduced,
        reduce_sums,
        reduce_params,
        taps_full,
        act,
        masks,
        out,
        moved,
        sends.high,
        sizes,
        count,
        batches,
        members,
    )
    high = sends.high + sum(sizes)
    inner, reduce_weight_grad, expand_weight_grad, taps_grad, moved = closing(
        reduced,
        reduce_sums,
        reduce_params,
        reduce_up,
        reduce_stats,
        x,
        upstream,
        reduce_full,
        expand_part,
        taps_part,
        out,
        moved,
        high,
        pixels - high,
        count,
        batches,
        members,
    )
    input_grad, block_output, *sums = turn_out(
        inner.reshape(row_pixels, channels),
        moved.reshape(row_pixels, channels),
        (reduce_stats, group_stats, expand_stats),
    )
    taps_grad = taps_grad[: 9 * GW].reshape(9, GW, -1, GW).transpose(2, 0, 3, 1)
    return (
        block_output,
        input_grad,
        reduce_weight_grad,
        taps_grad.reshape(group_weight.shape),
        expand_weight_grad,
    ) + tuple(part.reshape(-1) for part in sums)


def modular(
    block_input,
    reduce_weight,
    reduce_gain,
    reduce_bias,
    group_weight,
    group_gain,
    group_bias,
    expand_weight,
    expand_gain,
    expand_bias,
    out_grad,
):
    batches, members = lax.axis_size("batch"), lax.axis_size("group")
    channels, row_pixels = block_input.shape
    pixels = row_pixels // members
    count = row_pixels * batches
    mid_total = reduce_weight.shape[1]
    mids = mid_total // BLK
    blocks = channels * members // BLK
    me = lax.axis_index("group")

    def to_pixels(values):
        moved = lax.all_to_all(values.T.reshape(members, pixels, channels), "group", 0, 0)
        if channels == BLK:
            return moved
        share = BLK // channels
        moved = moved.reshape(blocks, share, pixels, channels).transpose(0, 2, 1, 3)
        return moved.reshape(blocks, pixels, BLK)

    def to_channels(values):
        if channels != BLK:
            share = BLK // channels
            values = values.reshape(blocks, pixels, share, channels).transpose(0, 2, 1, 3)
            values = values.reshape(members, pixels, channels)
        moved = lax.all_to_all(values, "group", 0, 0)
        return moved.reshape(row_pixels, channels).T

    def gather(values):
        return lax.all_gather(values, "group", axis=0, tiled=True)

    local_mid = reduce_gain.shape[0]
    pack = jnp.concatenate([reduce_gain, reduce_bias, group_gain, group_bias, expand_gain, expand_bias])
    packs = gather(pack[None])
    vectors, offset = [], 0
    for length in (local_mid, local_mid, local_mid, local_mid, channels, channels):
        vectors.append(packs[:, offset : offset + length].reshape(-1, BLK))
        offset += length
    reduce_params = jnp.stack(vectors[0:2], 1)
    group_params = jnp.stack(vectors[2:4], 1)
    expand_params = jnp.stack(vectors[4:6], 1)
    reduce_full = gather(reduce_weight).reshape(blocks, BLK, mid_total)
    expand_full = gather(expand_weight).reshape(blocks, BLK, mid_total)
    taps = gather(group_weight.reshape(group_weight.shape[0], 9, GW, GW))
    taps = taps.reshape(-1, HALF // GW, 9, GW, GW).transpose(0, 2, 3, 1, 4).reshape(-1, 9 * GW, HALF)
    taps = jnp.pad(taps, ((0, 0), (0, TAP_ROWS - 9 * GW), (0, 0)))
    masks = pixel_masks(pixels)

    x = to_pixels(block_input)
    grad = to_pixels(out_grad)

    reduced, reduce_sums = reduce_product(x, reduce_full, None)
    reduce_sums = exchange(reduce_sums, batches, members, 1)
    grouped, group_sums = conv(reduced, reduce_sums, reduce_params, taps, masks, count, None)
    group_sums = exchange(group_sums, batches, members, 1)
    expanded, act, expand_sums = expand_product(grouped, group_sums, group_params, expand_full, count, None)
    expand_sums = exchange(expand_sums, batches, members, 2)
    out, upstream, expand_stats = output(expanded, expand_sums, expand_params, x, grad, count, None)
    expand_stats = exchange(expand_stats, batches, members, 2)
    expand_part, group_up, group_stats = expand_back(
        expanded, expand_sums, expand_params, upstream, expand_stats, expand_full, grouped, group_sums, group_params, act, count, None
    )
    group_stats = exchange(group_stats, batches, members, 1)
    reduce_up, taps_part, reduce_stats = conv_back(
        reduced,
        reduce_sums,
        reduce_params,
        grouped,
        group_sums,
        group_params,
        group_up,
        group_stats,
        taps,
        masks,
        count,
        None,
    )
    reduce_stats = exchange(reduce_stats, batches, members, 1)
    inner, reduce_part = reduce_back(
        reduced, reduce_sums, reduce_params, reduce_up, reduce_stats, x, upstream, reduce_full, count
    )
    block_output = to_channels(out)
    input_grad = to_channels(inner).astype(F32)

    def shared_sum(part):
        rows = channels // batches
        part = part.reshape(members, batches, rows, mid_total).transpose(1, 0, 2, 3)
        part = lax.all_to_all(part, "batch", 0, 0).astype(F32).sum(0).astype(BF16)
        part = lax.all_to_all(part, "group", 0, 0).astype(F32).sum(0)
        return lax.all_gather(part, "batch", axis=0, tiled=True)

    expand_weight_grad = shared_sum(expand_part)
    reduce_weight_grad = shared_sum(reduce_part)
    taps_part = taps_part[:, : 9 * GW].reshape(-1, 9, GW, HALF // GW, GW).transpose(0, 3, 1, 4, 2)
    taps_part = taps_part.reshape(members, -1, 9, GW, GW)
    group_weight_grad = lax.all_to_all(taps_part, "group", 0, 0).astype(F32).sum(0)
    group_weight_grad = lax.psum(group_weight_grad, "batch").reshape(group_weight.shape)

    return (
        block_output,
        input_grad,
        reduce_weight_grad,
        group_weight_grad,
        expand_weight_grad,
        own_part(reduce_stats, 1, local_mid),
        own_part(reduce_stats, 0, local_mid),
        own_part(group_stats, 1, local_mid),
        own_part(group_stats, 0, local_mid),
        own_part(expand_stats, 1, channels),
        own_part(expand_stats, 0, channels),
    )


def local(*args):
    block_input = args[0]
    pixels = block_input.shape[1] // lax.axis_size("group")
    if block_input.shape[0] == BLK and pixels == 1568 and args[2].shape[0] == HALF and lax.axis_size("group") == 8:
        return fused(*args)
    return modular(*args)


def solution(mesh):
    in_specs = (
        P("group", "batch"),
        P("group", None),
        P("group"),
        P("group"),
        P("group", None, None, None, None),
        P("group"),
        P("group"),
        P("group", None),
        P("group"),
        P("group"),
        P("group", "batch"),
    )
    out_specs = (
        P("group", "batch"),
        P("group", "batch"),
        P("group", None),
        P("group", None, None, None, None),
        P("group", None),
        P("group"),
        P("group"),
        P("group"),
        P("group"),
        P("group"),
        P("group"),
    )
    return jax.shard_map(local, mesh=mesh, in_specs=in_specs, out_specs=out_specs, check_vma=False)
```

```python
import functools

import jax
import jax.numpy as jnp
import numpy as np
from jax import lax
from jax.experimental import pallas as pl
from jax.experimental.pallas import tpu as pltpu
from jax.sharding import PartitionSpec as P

GW = 32
SIDE = 14
EPS = 1e-05
BLK = 256
HALF = 128
PAD = 16
F32 = jnp.float32
BF16 = jnp.bfloat16
MESH = pl.DeviceIdType.MESH
VMEM_LIMIT = 60 * 1024 * 1024


def silu_slope(values):
    sigma = jax.nn.sigmoid(values)
    return sigma * (1.0 + values * (1.0 - sigma))


def row_chunk(pixels):
    for size in (224, 208, 192, 176, 160, 144, 128, 112):
        if pixels % size == 0:
            return size
    return pixels


def over_rows(pixels, body):
    size = row_chunk(pixels)
    if size == pixels:
        body(0, size)
    else:

        @pl.loop(0, pixels // size)
        def _(step):
            body(pl.multiple_of(step * size, 16), size)


def coefficients(sums, params, count):
    center = sums[0:1] / count
    spread = sums[1:2] / count - center * center
    inverse = lax.rsqrt(spread + EPS)
    return center, inverse, params[0:1], params[1:2]


def standardize(values, coef):
    standard = (values - coef[0]) * coef[1]
    return standard, standard * coef[2] + coef[3]


def add_stats(ref, slot, first, second):
    ref[slot, 0:1] += jnp.sum(first, 0, keepdims=True)
    ref[slot, 1:2] += jnp.sum(second, 0, keepdims=True)


PHASE_START = [0]


def grid_step():
    return pl.program_id(0) - PHASE_START[-1]


def in_phase(start, steps, body):
    step = pl.program_id(0)

    @pl.when((step >= start) & (step < start + steps))
    def _():
        PHASE_START.append(start)
        try:
            body()
        finally:
            PHASE_START.pop()


def phase_block(start, steps, *dims):
    return pl.BlockSpec((1,) + dims, lambda j: (jnp.clip(j - start, 0, steps - 1),) + (0,) * len(dims))


def clear_stats(ref):
    @pl.when(grid_step() == 0)
    def _():
        ref[...] = jnp.zeros_like(ref)


def dot(a, b, dims=((1,), (0,))):
    return lax.dot_general(a, b, (dims, ((), ())), preferred_element_type=F32)


def devices(batches, members):
    row, me = lax.axis_index("batch"), lax.axis_index("group")
    across = [(lax.rem(row + step, batches), me) for step in range(1, batches)]
    along = [(row, lax.rem(me + step, members)) for step in range(1, members)]
    return row, me, across, along


def greet(others):
    barrier = pltpu.get_barrier_semaphore()
    for device in others:
        pl.semaphore_signal(barrier, inc=1, device_id=device, device_id_type=MESH)
    pl.semaphore_wait(barrier, len(others))


def remote(source, target, send, recv, device):
    return pltpu.make_async_remote_copy(
        src_ref=source, dst_ref=target, send_sem=send, recv_sem=recv, device_id=device, device_id_type=MESH
    )


def each(copies, what):
    for copy in copies:
        getattr(copy, what)()


def spread(source, target, send, recv, others, beside):
    copies = [
        remote(source, target.at[step], send.at[step], recv.at[step], device) for step, device in enumerate(others)
    ]
    each(copies, "start")
    each(beside, "start")
    each(copies, "wait")


def total_stats(ref, across, along, first_ref, second_ref, mid_ref, send1, recv1, send2, recv2, beside=()):
    mid_ref[0] = ref[...]
    spread(mid_ref.at[0], second_ref, send2, recv2, along, beside)
    total = mid_ref[0]
    for step in range(len(along)):
        total += second_ref[step]
    mid_ref[1] = total
    spread(mid_ref.at[1], first_ref, send1, recv1, across, ())
    for step in range(len(across)):
        total += first_ref[step]
    ref[...] = total


def stats_scratch(dims, batches, members):
    return [
        pltpu.VMEM((batches - 1,) + dims, F32),
        pltpu.VMEM((members - 1,) + dims, F32),
        pltpu.VMEM((2,) + dims, F32),
        pltpu.SemaphoreType.DMA((batches - 1,)),
        pltpu.SemaphoreType.DMA((batches - 1,)),
        pltpu.SemaphoreType.DMA((members - 1,)),
        pltpu.SemaphoreType.DMA((members - 1,)),
    ]


class Comm:
    def __init__(self, batches, members, collective_id, source=None, low=0, sizes=(), into=None, stream=False):
        self.batches, self.members, self.collective_id = batches, members, collective_id
        self.source, self.low, self.sizes, self.into, self.stream = source, low, sizes, into, stream
        self.high = low + sum(sizes)


def piece_copies(source, target, low, size, me, along, send, recv, staged=False):
    rows = pl.ds(low, size)
    last = len(along)
    copies = [
        remote(
            source.at[step if staged else device[1], rows], target.at[me, rows], send.at[step], recv.at[step], device
        )
        for step, device in enumerate(along)
    ]
    return copies + [
        pltpu.make_async_copy(source.at[last if staged else me, rows], target.at[me, rows], send.at[last])
    ]


class Late:
    def __init__(self, dims, dtype=F32):
        self.dims, self.dtype = dims, dtype


def call(kernel, grid, in_specs, out_specs, out_shape, scratch, flops, comm=None):
    if comm is None:
        in_specs = [whole(*spec.dims) if isinstance(spec, Late) else spec for spec in in_specs]
        return functools.partial(
            plain_call, kernel, grid, in_specs, out_specs, out_shape, scratch, flops, pltpu.CompilerParams(vmem_limit_bytes=VMEM_LIMIT)
        )
    n_in, n_out, n_scratch = len(in_specs), len(out_specs), len(scratch)
    stats = out_shape[-1].shape
    batches, members = comm.batches, comm.members

    sends = bool(comm.sizes)
    late = [index for index, spec in enumerate(in_specs) if isinstance(spec, Late)]
    late_specs = [in_specs[index] for index in late]

    def wrapped(*refs):
        refs = list(refs)
        ins = refs[:n_in]
        del refs[:n_in]
        source = refs.pop(0) if sends and not comm.stream else None
        if comm.into is not None:
            refs.pop(0)
        outs = refs[:n_out]
        del refs[:n_out]
        target = refs.pop(0) if sends else None
        own = refs[:n_scratch]
        del refs[:n_scratch]
        stats_refs = refs[:7]
        del refs[:7]
        if comm.stream:
            source = refs.pop(0)
        loads = []
        if late:
            load_sem = refs.pop(0)
            for place, index in enumerate(late):
                held = refs.pop(0)
                loads.append(pltpu.make_async_copy(ins[index], held, load_sem.at[place]))
                ins[index] = held
        row, me, across, along = devices(batches, members)
        step = pl.program_id(0)

        def copies(part):
            low = comm.low + sum(comm.sizes[:part])
            return piece_copies(
                source, target, low, comm.sizes[part], me, along, refs[0].at[part], refs[1].at[part], comm.stream
            )

        @pl.when(step == 0)
        def _():
            greet(across + along)
            if sends and not comm.stream:
                each(copies(0), "start")
            each(loads, "start")
            each(loads, "wait")

        kernel(*ins, *outs, *own)
        if comm.stream:
            source[step] = outs[0][0, : comm.high]
            rows = pl.ds(0, comm.sizes[0])

            @pl.when(step < members - 1)
            def _():
                device = (row, lax.rem(me + 1 + step, members))
                remote(
                    source.at[step, rows], target.at[me, rows], refs[0].at[0, step], refs[1].at[0, step], device
                ).start()

            @pl.when(step == members - 1)
            def _():
                pltpu.make_async_copy(source.at[step, rows], target.at[me, rows], refs[0].at[0, step]).start()

        @pl.when(step == pl.num_programs(0) - 1)
        def _():
            total_stats(outs[-1], across, along, *stats_refs, beside=copies(1) if sends else ())
            if sends:
                for part in range(2):
                    each(copies(part), "wait")

    scratch = list(scratch) + stats_scratch(stats, batches, members)
    in_specs, out_specs, out_shape = list(in_specs), list(out_specs), list(out_shape)
    extra, aliases = [], {}
    if sends:
        if comm.stream:
            dims, dtype = out_shape[0].shape, out_shape[0].dtype
            scratch.append(pltpu.VMEM((members, comm.high, dims[2]), dtype))
        else:
            dims, dtype = comm.source.shape, comm.source.dtype
            extra = [comm.source]
        if comm.into is not None:
            aliases = {len(in_specs) + len(extra): len(out_specs)}
            extra.append(comm.into)
        in_specs = [pl.BlockSpec(memory_space=pl.ANY) if isinstance(spec, Late) else spec for spec in in_specs]
        in_specs += [pl.BlockSpec(memory_space=pl.ANY)] * len(extra)
        if late:
            scratch.append(pltpu.SemaphoreType.DMA((len(late),)))
            scratch += [pltpu.VMEM(spec.dims, spec.dtype) for spec in late_specs]
        out_specs.append(pl.BlockSpec(memory_space=pl.ANY))
        out_shape.append(shape(dims, dtype))
        scratch += [pltpu.SemaphoreType.DMA((2, members)), pltpu.SemaphoreType.DMA((2, members - 1))]
    params = pltpu.CompilerParams(
        vmem_limit_bytes=VMEM_LIMIT, collective_id=comm.collective_id, has_side_effects=True
    )
    inner = functools.partial(
        plain_call, wrapped, grid, in_specs, out_specs, out_shape, scratch, flops, params, aliases=aliases
    )
    return lambda *args: inner(*args, *extra)


def plain_call(kernel, grid, in_specs, out_specs, out_shape, scratch, flops, params, *args, aliases={}):
    return pl.pallas_call(
        kernel,
        grid=grid,
        in_specs=in_specs,
        out_specs=out_specs,
        out_shape=out_shape,
        scratch_shapes=scratch,
        input_output_aliases=aliases,
        compiler_params=params,
        cost_estimate=pl.CostEstimate(flops=flops, bytes_accessed=20_000_000, transcendentals=0),
    )(*args)


def shape(dims, dtype=F32):
    return jax.ShapeDtypeStruct(dims, dtype)


def block(*dims):
    return pl.BlockSpec((1,) + dims, lambda j: (j,) + (0,) * len(dims))


def turned_block(members, *dims):
    def index(j):
        return (lax.rem(lax.axis_index("group") + 1 + j, members),) + (0,) * len(dims)

    return pl.BlockSpec((1,) + dims, index)


def whole(*dims):
    return pl.BlockSpec(dims, lambda j: (0,) * len(dims))


def reduce_kernel(x_ref, w_ref, out_ref, sum_ref):
    clear_stats(sum_ref)
    slot = grid_step()

    def body(start, size):
        rows = pl.ds(start, size)
        total = dot(x_ref[0, rows], w_ref[0])
        for source in range(1, x_ref.shape[0]):
            total += dot(x_ref[source, rows], w_ref[source])
        out_ref[0, rows] = total
        add_stats(sum_ref, slot, total, total * total)

    over_rows(x_ref.shape[1], body)


def reduce_product(x, weight, comm):
    blocks, pixels, _ = x.shape
    mids = weight.shape[2] // BLK
    return call(
        reduce_kernel,
        (mids,),
        [Late((blocks, pixels, BLK), BF16), pl.BlockSpec((blocks, BLK, BLK), lambda j: (0, 0, j))],
        [block(pixels, BLK), whole(mids, 2, BLK)],
        [shape((mids, pixels, BLK)), shape((mids, 2, BLK))],
        [],
        2 * pixels * blocks * BLK * mids * BLK,
        comm,
    )(x, weight)


def same_group():
    return lax.broadcasted_iota(jnp.int32, (BLK, BLK), 0) // GW == lax.broadcasted_iota(jnp.int32, (BLK, BLK), 1) // GW


def spread_weight(compact_ref, dense_ref):
    own = same_group()
    for tap in range(9):
        rows = pl.ds(tap * GW, GW)
        compact = jnp.concatenate([compact_ref[0, rows], compact_ref[1, rows]], 1).astype(F32)
        tiled = jnp.concatenate([compact] * (BLK // GW), 0)
        dense_ref[tap] = jnp.where(own, tiled, 0.0).astype(BF16)


def twice(mask):
    return jnp.concatenate([mask, mask], 1)


def fill(stack_ref, mask_ref, rows_start, size, values):
    rows = pl.ds(rows_start, size)
    target = pl.ds(rows_start + PAD, size)
    for half in range(2):
        part = values[:, half * HALF : (half + 1) * HALF]
        stack_ref[1, half, target] = part
        stack_ref[0, half, target] = part * mask_ref[1, rows]
        stack_ref[2, half, target] = part * mask_ref[0, rows]


def clear_edges(stack_ref, pixels):
    edge = jnp.zeros(stack_ref.shape[:2] + (PAD, HALF), F32)
    stack_ref[:, :, 0:PAD] = edge
    stack_ref[:, :, PAD + pixels : PAD + pixels + PAD] = edge


def window(stack_ref, start, size, row_off, col_off):
    rows = pl.ds(start + (PAD + row_off * SIDE + col_off), size)
    return jnp.concatenate([stack_ref[col_off + 1, half, rows] for half in range(2)], 1).astype(BF16)


def conv_rows(stack_ref, mask_ref, dense_ref, start, size, flipped=False):
    rows = pl.ds(start, size)
    total = None
    for row_off in (-1, 0, 1):
        part = None
        for col_off in (-1, 0, 1):
            values = window(stack_ref, start, size, row_off, col_off)
            tap = (row_off + 1) * 3 + col_off + 1
            term = dot(values, dense_ref[8 - tap], ((1,), (1,))) if flipped else dot(values, dense_ref[tap])
            part = term if part is None else part + term
        if row_off:
            part = part * twice(mask_ref[2 if row_off < 0 else 3, rows])
        total = part if total is None else total + part
    return total


def conv_kernel(count, red_ref, sums_ref, prm_ref, weight_ref, mask_ref, out_ref, stat_ref, stack_ref, dense_ref):
    pixels = red_ref.shape[1]
    spread_weight(weight_ref, dense_ref)
    clear_edges(stack_ref, pixels)
    coef = coefficients(sums_ref[0], prm_ref[0], count)

    def enter(start, size):
        _, norm = standardize(red_ref[0, pl.ds(start, size)], coef)
        fill(stack_ref, mask_ref, start, size, (norm * jax.nn.sigmoid(norm)).astype(BF16).astype(F32))

    over_rows(pixels, enter)
    clear_stats(stat_ref)
    slot = grid_step()

    def body(start, size):
        total = conv_rows(stack_ref, mask_ref, dense_ref, start, size)
        out_ref[0, pl.ds(start, size)] = total
        add_stats(stat_ref, slot, total, total * total)

    over_rows(pixels, body)


def conv(reduced, sums, params, weight, masks, count, comm):
    mids, pixels, _ = reduced.shape
    return call(
        functools.partial(conv_kernel, count),
        (mids,),
        [
            block(pixels, BLK),
            block(2, BLK),
            block(2, BLK),
            pl.BlockSpec((2,) + weight.shape[1:], lambda j: (j, 0, 0)),
            Late((4, pixels, HALF)),
        ],
        [block(pixels, BLK), whole(mids, 2, BLK)],
        [shape((mids, pixels, BLK)), shape((mids, 2, BLK))],
        [pltpu.VMEM((3, 2, pixels + 2 * PAD, HALF), F32), pltpu.VMEM((9, BLK, BLK), BF16)],
        2 * 9 * pixels * mids * BLK * BLK,
        comm,
    )(reduced, sums, params, weight, masks)


def conv_back_kernel(
    count,
    red_ref,
    sums_ref,
    prm_ref,
    grp_ref,
    gsums_ref,
    gprm_ref,
    up_ref,
    upsums_ref,
    weight_ref,
    mask_ref,
    *refs,
):
    out_ref, wgrad_ref, stat_ref, stack_ref, dense_ref, back_ref = refs
    pixels = red_ref.shape[1]
    spread_weight(weight_ref, dense_ref)
    clear_edges(stack_ref, pixels)
    coef = coefficients(sums_ref[0], prm_ref[0], count)
    gcoef = coefficients(gsums_ref[0], gprm_ref[0], count)
    scale = gcoef[2] * gcoef[1]
    up_mean = upsums_ref[0, 0:1] / count
    up_lean = upsums_ref[0, 1:2] / count

    def back(start, size):
        rows = pl.ds(start, size)
        standard, _ = standardize(grp_ref[0, rows], gcoef)
        values = (scale * (up_ref[0, rows] - up_mean - standard * up_lean)).astype(BF16)
        back_ref[1, rows] = values
        values = values.astype(F32)
        back_ref[0, rows] = (values * twice(mask_ref[2, rows])).astype(BF16)
        back_ref[2, rows] = (values * twice(mask_ref[3, rows])).astype(BF16)
        fill(stack_ref, mask_ref, start, size, values)

    over_rows(pixels, back)
    clear_stats(stat_ref)
    slot = grid_step()

    def body(start, size):
        rows = pl.ds(start, size)
        standard, norm = standardize(red_ref[0, rows], coef)
        up = conv_rows(stack_ref, mask_ref, dense_ref, start, size, True) * silu_slope(norm)
        out_ref[0, rows] = up
        add_stats(stat_ref, slot, up, up * standard)

    over_rows(pixels, body)

    def enter(start, size):
        _, norm = standardize(red_ref[0, pl.ds(start, size)], coef)
        fill(stack_ref, mask_ref, start, size, (norm * jax.nn.sigmoid(norm)).astype(BF16).astype(F32))

    over_rows(pixels, enter)
    own = same_group()
    for tap in range(9):
        full = dot(back_ref[tap // 3], window(stack_ref, 0, pixels, tap // 3 - 1, tap % 3 - 1), ((0,), (0,)))
        full = jnp.where(own, full, 0.0)
        kept = full[0:GW]
        for group in range(1, BLK // GW):
            kept += full[group * GW : (group + 1) * GW]
        for half in range(2):
            wgrad_ref[half, tap * GW : (tap + 1) * GW] = kept[:, half * HALF : (half + 1) * HALF].astype(BF16)
    for half in range(2):
        wgrad_ref[half, 9 * GW :] = jnp.zeros((wgrad_ref.shape[1] - 9 * GW, HALF), BF16)


def conv_back(reduced, sums, params, grouped, gsums, gparams, up, upsums, weight, masks, count, comm):
    mids, pixels, _ = reduced.shape
    return call(
        functools.partial(conv_back_kernel, count),
        (mids,),
        [
            block(pixels, BLK),
            block(2, BLK),
            block(2, BLK),
            block(pixels, BLK),
            block(2, BLK),
            block(2, BLK),
            block(pixels, BLK),
            block(2, BLK),
            pl.BlockSpec((2,) + weight.shape[1:], lambda j: (j, 0, 0)),
            Late((4, pixels, HALF)),
        ],
        [block(pixels, BLK), pl.BlockSpec((2,) + weight.shape[1:], lambda j: (j, 0, 0)), whole(mids, 2, BLK)],
        [shape((mids, pixels, BLK)), shape(weight.shape, BF16), shape((mids, 2, BLK))],
        [
            pltpu.VMEM((3, 2, pixels + 2 * PAD, HALF), F32),
            pltpu.VMEM((9, BLK, BLK), BF16),
            pltpu.VMEM((3, pixels, BLK), BF16),
        ],
        4 * 9 * pixels * mids * BLK * BLK,
        comm,
    )(reduced, sums, params, grouped, gsums, gparams, up, upsums, weight, masks)


def expand_kernel(count, grp_ref, gsums_ref, gprm_ref, w_ref, out_ref, act_ref, sum_ref):
    mids, pixels, _ = grp_ref.shape

    @pl.when(grid_step() == 0)
    def _():
        for mid in range(mids):
            coef = coefficients(gsums_ref[mid], gprm_ref[mid], count)

            def body(start, size):
                rows = pl.ds(start, size)
                _, norm = standardize(grp_ref[mid, rows], coef)
                act_ref[rows, mid * BLK : (mid + 1) * BLK] = (norm * jax.nn.sigmoid(norm)).astype(BF16)

            over_rows(pixels, body)

    clear_stats(sum_ref)
    slot = grid_step()

    def product(start, size):
        rows = pl.ds(start, size)
        total = dot(act_ref[rows], w_ref[0], ((1,), (1,)))
        out_ref[0, rows] = total
        add_stats(sum_ref, slot, total, total * total)

    over_rows(pixels, product)


def expand_product(grouped, gsums, gparams, weight, count, comm):
    mids, pixels, _ = grouped.shape
    blocks = weight.shape[0]
    return call(
        functools.partial(expand_kernel, count),
        (blocks,),
        [
            Late((mids, pixels, BLK)),
            whole(mids, 2, BLK),
            whole(mids, 2, BLK),
            block(BLK, mids * BLK),
        ],
        [block(pixels, BLK), whole(pixels, mids * BLK), whole(blocks, 2, BLK)],
        [shape((blocks, pixels, BLK)), shape((pixels, mids * BLK), BF16), shape((blocks, 2, BLK))],
        [],
        2 * pixels * blocks * BLK * mids * BLK,
        comm,
    )(grouped, gsums, gparams, weight)


def output_kernel(count, members, exp_ref, sums_ref, prm_ref, x_ref, grad_ref, out_ref, up_ref, stat_ref):
    coef = coefficients(sums_ref[0], prm_ref[0], count)
    clear_stats(stat_ref)
    slot = grid_step()
    if members:
        slot = lax.rem(lax.axis_index("group") + 1 + slot, members)

    def body(start, size):
        rows = pl.ds(start, size)
        standard, norm = standardize(exp_ref[0, rows], coef)
        summed = norm + x_ref[0, rows].astype(F32)
        sigma = jax.nn.sigmoid(summed)
        out_ref[0, rows] = (summed * sigma).astype(BF16)
        up = grad_ref[0, rows].astype(F32) * (sigma * (1.0 + summed * (1.0 - sigma)))
        up_ref[0, rows] = up
        add_stats(stat_ref, slot, up, up * standard)

    over_rows(exp_ref.shape[1], body)


def output(expanded, sums, params, x, grad, count, comm):
    blocks, pixels, _ = expanded.shape
    members = comm.members if comm else None
    one = functools.partial(turned_block, members) if comm else block
    return call(
        functools.partial(output_kernel, count, members),
        (blocks,),
        [one(pixels, BLK), one(2, BLK), one(2, BLK), one(pixels, BLK), one(pixels, BLK)],
        [one(pixels, BLK), one(pixels, BLK), whole(blocks, 2, BLK)],
        [shape((blocks, pixels, BLK), BF16), shape((blocks, pixels, BLK)), shape((blocks, 2, BLK))],
        [],
        20 * pixels * blocks * BLK,
        comm,
    )(expanded, sums, params, x, grad)


def expand_back_kernel(
    count,
    exp_ref,
    sums_ref,
    prm_ref,
    up_ref,
    upsums_ref,
    w_ref,
    grp_ref,
    gsums_ref,
    gprm_ref,
    act_ref,
    wgrad_ref,
    out_ref,
    stat_ref,
    keep_ref,
):
    blocks, pixels, _ = keep_ref.shape
    step = grid_step()
    clear_stats(stat_ref)

    @pl.when(step < blocks)
    def _():
        coef = coefficients(sums_ref[0], prm_ref[0], count)
        scale = coef[2] * coef[1]
        up_mean = upsums_ref[0, 0:1] / count
        up_lean = upsums_ref[0, 1:2] / count

        def back(start, size):
            rows = pl.ds(start, size)
            standard, _ = standardize(exp_ref[0, rows], coef)
            values = (scale * (up_ref[0, rows] - up_mean - standard * up_lean)).astype(BF16)
            keep_ref[step, rows] = values

        over_rows(pixels, back)
        weight_grad_block(keep_ref[step], act_ref, wgrad_ref, 0)

    @pl.when(step >= blocks)
    def _():
        coef = coefficients(gsums_ref[0], gprm_ref[0], count)

        def body(start, size):
            rows = pl.ds(start, size)
            total = dot(keep_ref[0, rows], w_ref[0])
            for source in range(1, blocks):
                total += dot(keep_ref[source, rows], w_ref[source])
            standard, norm = standardize(grp_ref[0, rows], coef)
            up = total * silu_slope(norm)
            out_ref[0, rows] = up
            add_stats(stat_ref, step - blocks, up, up * standard)

        over_rows(pixels, body)


def expand_back(expanded, sums, params, up, upsums, weight, grouped, gsums, gparams, act, count, comm):
    blocks, pixels, _ = expanded.shape
    mids = grouped.shape[0]

    def first(*dims):
        return pl.BlockSpec((1,) + dims, lambda j: (jnp.minimum(j, blocks - 1),) + (0,) * len(dims))

    def second(*dims):
        return pl.BlockSpec((1,) + dims, lambda j: (jnp.maximum(j - blocks, 0),) + (0,) * len(dims))

    return call(
        functools.partial(expand_back_kernel, count),
        (blocks + mids,),
        [
            first(pixels, BLK),
            first(2, BLK),
            first(2, BLK),
            first(pixels, BLK),
            first(2, BLK),
            pl.BlockSpec((blocks, BLK, BLK), lambda j: (0, 0, jnp.maximum(j - blocks, 0))),
            second(pixels, BLK),
            second(2, BLK),
            second(2, BLK),
            Late((pixels, mids * BLK), BF16),
        ],
        [first(BLK, mids * BLK), second(pixels, BLK), whole(mids, 2, BLK)],
        [shape((blocks, BLK, mids * BLK), BF16), shape((mids, pixels, BLK)), shape((mids, 2, BLK))],
        [pltpu.VMEM((blocks, pixels, BLK), BF16)],
        4 * pixels * blocks * BLK * mids * BLK,
        comm,
    )(expanded, sums, params, up, upsums, weight, grouped, gsums, gparams, act)


def first_back(count, red_ref, sums_ref, prm_ref, rup_ref, rupsums_ref, back_ref, loads=()):
    mids, pixels, _ = red_ref.shape
    for mid in range(mids):
        for load in loads[2 * mid : 2 * mid + 2]:
            load.wait()
        coef = coefficients(sums_ref[mid], prm_ref[mid], count)
        scale = coef[2] * coef[1]
        up_mean = rupsums_ref[mid, 0:1] / count
        up_lean = rupsums_ref[mid, 1:2] / count

        def body(start, size):
            rows = pl.ds(start, size)
            standard, _ = standardize(red_ref[mid, rows], coef)
            values = scale * (rup_ref[mid, rows] - up_mean - standard * up_lean)
            back_ref[rows, mid * BLK : (mid + 1) * BLK] = values.astype(BF16)

        over_rows(pixels, body)


def weight_grad_block(left, right_ref, out_ref, slot):
    for first in range(0, right_ref.shape[1], BLK):
        columns = slice(first, first + BLK)
        out_ref[slot, :, columns] = dot(left, right_ref[:, columns], ((0,), (0,))).astype(BF16)


def reduce_back_kernel(count, red_ref, sums_ref, prm_ref, rup_ref, rupsums_ref, x_ref, up_ref, w_ref, grad_ref, wgrad_ref, back_ref):
    @pl.when(pl.program_id(0) == 0)
    def _():
        first_back(count, red_ref, sums_ref, prm_ref, rup_ref, rupsums_ref, back_ref)

    def product(start, size):
        rows = pl.ds(start, size)
        total = dot(back_ref[rows], w_ref[0], ((1,), (1,)))
        grad_ref[0, rows] = (up_ref[0, rows] + total).astype(BF16)

    over_rows(x_ref.shape[1], product)
    weight_grad_block(x_ref[0], back_ref, wgrad_ref, 0)


def reduce_back(reduced, sums, params, rup, rupsums, x, up, weight, count):
    mids, pixels, _ = reduced.shape
    blocks = x.shape[0]
    return call(
        functools.partial(reduce_back_kernel, count),
        (blocks,),
        [
            whole(mids, pixels, BLK),
            whole(mids, 2, BLK),
            whole(mids, 2, BLK),
            whole(mids, pixels, BLK),
            whole(mids, 2, BLK),
            block(pixels, BLK),
            block(pixels, BLK),
            block(BLK, mids * BLK),
        ],
        [block(pixels, BLK), block(BLK, mids * BLK)],
        [shape((blocks, pixels, BLK), BF16), shape((blocks, BLK, mids * BLK), BF16)],
        [pltpu.VMEM((pixels, mids * BLK), BF16)],
        4 * pixels * blocks * BLK * mids * BLK,
    )(reduced, sums, params, rup, rupsums, x, up, weight)


def exchange_kernel(batches, members, x_ref, out_ref, *scratch):
    row, me, across, along = devices(batches, members)
    greet(across + along)
    out_ref[...] = x_ref[...]
    total_stats(out_ref, across, along, *scratch)


def exchange(values, batches, members, collective_id):
    return pl.pallas_call(
        functools.partial(exchange_kernel, batches, members),
        in_specs=[pl.BlockSpec(memory_space=pltpu.VMEM)],
        out_specs=pl.BlockSpec(memory_space=pltpu.VMEM),
        out_shape=shape(values.shape),
        scratch_shapes=stats_scratch(values.shape, batches, members),
        compiler_params=pltpu.CompilerParams(collective_id=collective_id, has_side_effects=True),
    )(values)


class Sends:
    def __init__(self, source, target, low, sizes, me, along, send, recv):
        self.parts = []
        for part, size in enumerate(sizes):
            self.parts.append(
                functools.partial(
                    piece_copies, source, target, low, size, me, along, send.at[part], recv.at[part]
                )
            )
            low += size

    def start(self, part):
        each(self.parts[part](), "start")

    def wait(self):
        for part in self.parts:
            each(part(), "wait")


def at_step(step, body):
    pl.when(pl.program_id(0) == step)(body)


def forward_kernel(count, batches, members, sizes, *refs):
    x_any, wr_ref, prm_ref, taps_ref, masks_any, gprm_ref, we_ref, src_ref = refs[:8]
    red_any, grp_any, act_any, exp_ref, sums_ref, gsums_ref, esums_ref, dst_ref = refs[8:16]
    x_held, masks, red, grp, act, stack, dense, psend, precv, load, keep = refs[16:27]
    stats = [refs[27 + 7 * index : 34 + 7 * index] for index in range(3)]
    row, me, across, along = devices(batches, members)
    mids, blocks = red.shape[0], x_held.shape[0]
    second, third, end = mids, 2 * mids, 2 * mids + blocks
    sends = Sends(src_ref, dst_ref, 0, sizes, me, along, psend, precv)
    loads = [pltpu.make_async_copy(x_any, x_held, load.at[0]), pltpu.make_async_copy(masks_any, masks, load.at[1])]
    kept = [
        pltpu.make_async_copy(held, out, keep.at[index])
        for index, (held, out) in enumerate(((red, red_any), (grp, grp_any), (act, act_any)))
    ]

    def begin():
        greet(across + along)
        sends.start(0)
        each(loads, "start")
        each(loads, "wait")

    at_step(0, begin)

    def product():
        reduce_kernel(x_held, wr_ref, red.at[pl.ds(grid_step(), 1)], sums_ref)

    in_phase(0, mids, product)

    def exchange_first():
        kept[0].start()
        total_stats(sums_ref, across, along, *stats[0], beside=sends.parts[1]())
        sends.start(2)

    at_step(second - 1, exchange_first)

    def conv_phase():
        own = pl.ds(grid_step(), 1)
        conv_kernel(
            count, red.at[own], sums_ref.at[own], prm_ref, taps_ref, masks, grp.at[own], gsums_ref, stack, dense
        )

    in_phase(second, mids, conv_phase)

    def exchange_second():
        kept[1].start()
        total_stats(gsums_ref, across, along, *stats[1], beside=sends.parts[3]())
        sends.start(4)

    at_step(third - 1, exchange_second)
    in_phase(third, blocks, lambda: expand_kernel(count, grp, gsums_ref, gprm_ref, we_ref, exp_ref, act, esums_ref))

    def finish():
        kept[2].start()
        total_stats(esums_ref, across, along, *stats[2], beside=sends.parts[5]())
        each(kept, "wait")
        sends.wait()

    at_step(end - 1, finish)


def forward(x, reduce_full, reduce_params, taps, masks, group_params, expand_full, source, sizes, count, batches, members):
    blocks, pixels, _ = x.shape
    mid_total = reduce_full.shape[2]
    mids = mid_total // BLK
    anywhere = pl.BlockSpec(memory_space=pl.ANY)
    dma = pltpu.SemaphoreType.DMA
    mid_dims, sum_dims = (mids, pixels, BLK), (mids, 2, BLK)
    scratch = [
        pltpu.VMEM(x.shape, BF16),
        pltpu.VMEM(masks.shape, F32),
        pltpu.VMEM(mid_dims, F32),
        pltpu.VMEM(mid_dims, F32),
        pltpu.VMEM((pixels, mid_total), BF16),
        pltpu.VMEM((3, 2, pixels + 2 * PAD, HALF), F32),
        pltpu.VMEM((9, BLK, BLK), BF16),
        dma((len(sizes), members)),
        dma((len(sizes), members - 1)),
        dma((2,)),
        dma((3,)),
    ]
    for dims in (sum_dims, sum_dims, (blocks, 2, BLK)):
        scratch += stats_scratch(dims, batches, members)
    return pl.pallas_call(
        functools.partial(forward_kernel, count, batches, members, sizes),
        grid=(2 * mids + blocks,),
        in_specs=[
            anywhere,
            pl.BlockSpec((blocks, BLK, BLK), lambda j: (0, 0, jnp.minimum(j, mids - 1))),
            phase_block(mids, mids, 2, BLK),
            pl.BlockSpec((2,) + taps.shape[1:], lambda j: (jnp.clip(j - mids, 0, mids - 1), 0, 0)),
            anywhere,
            whole(*sum_dims),
            phase_block(2 * mids, blocks, BLK, mid_total),
            anywhere,
        ],
        out_specs=[
            anywhere,
            anywhere,
            anywhere,
            phase_block(2 * mids, blocks, pixels, BLK),
            whole(*sum_dims),
            whole(*sum_dims),
            whole(blocks, 2, BLK),
            anywhere,
        ],
        out_shape=[
            shape(mid_dims),
            shape(mid_dims),
            shape((pixels, mid_total), BF16),
            shape(x.shape),
            shape(sum_dims),
            shape(sum_dims),
            shape((blocks, 2, BLK)),
            shape(source.shape, BF16),
        ],
        scratch_shapes=scratch,
        compiler_params=pltpu.CompilerParams(vmem_limit_bytes=VMEM_LIMIT, collective_id=1, has_side_effects=True),
    )(x, reduce_full, reduce_params, taps, masks, group_params, expand_full, source)


def backward_kernel(count, batches, members, low, sizes, *refs):
    exp_ref, esums_ref, eprm_ref, up_ref, upsums_ref, we_ref, grp_ref, gsums_ref, gprm_ref = refs[:9]
    red_ref, sums_ref, prm_ref, taps_ref, act_any, masks_any, src_ref, _ = refs[9:17]
    epart_ref, rup_ref, tpart_ref, gstats_ref, rstats_ref, dst_ref = refs[17:23]
    keep, gup, act, masks, stack, dense, back, psend, precv, load = refs[23:33]
    stats = [refs[33 + 7 * index : 40 + 7 * index] for index in range(2)]
    row, me, across, along = devices(batches, members)
    blocks, mids = keep.shape[0], gup.shape[0]
    middle, second, end = blocks, blocks + mids, blocks + 2 * mids
    sends = Sends(src_ref, dst_ref, low, sizes, me, along, psend, precv)
    loads = [pltpu.make_async_copy(act_any, act, load.at[0]), pltpu.make_async_copy(masks_any, masks, load.at[1])]

    def begin():
        greet(across + along)
        sends.start(0)
        each(loads, "start")
        each(loads, "wait")

    at_step(0, begin)

    def expand_phase():
        place = jnp.clip(grid_step() - middle, 0, mids - 1)
        expand_back_kernel(
            count,
            exp_ref,
            esums_ref,
            eprm_ref,
            up_ref,
            upsums_ref,
            we_ref,
            grp_ref,
            gsums_ref,
            gprm_ref,
            act,
            epart_ref,
            gup.at[pl.ds(place, 1)],
            gstats_ref,
            keep,
        )

    in_phase(0, second, expand_phase)

    def exchange_first():
        total_stats(gstats_ref, across, along, *stats[0], beside=sends.parts[1]())
        sends.start(2)

    at_step(second - 1, exchange_first)

    def conv_phase():
        own = pl.ds(grid_step(), 1)
        conv_back_kernel(
            count,
            red_ref,
            sums_ref,
            prm_ref,
            grp_ref,
            gsums_ref,
            gprm_ref,
            gup.at[own],
            gstats_ref.at[own],
            taps_ref,
            masks,
            rup_ref,
            tpart_ref,
            rstats_ref,
            stack,
            dense,
            back,
        )

    in_phase(second, mids, conv_phase)

    def finish():
        total_stats(rstats_ref, across, along, *stats[1], beside=sends.parts[3]())
        sends.wait()

    at_step(end - 1, finish)


def backward(
    expanded,
    esums,
    eparams,
    up,
    upsums,
    expand_full,
    grouped,
    gsums,
    gparams,
    reduced,
    sums,
    params,
    taps,
    act,
    masks,
    source,
    into,
    low,
    sizes,
    count,
    batches,
    members,
):
    blocks, pixels, _ = expanded.shape
    mids = grouped.shape[0]
    mid_total = mids * BLK
    anywhere = pl.BlockSpec(memory_space=pl.ANY)
    dma = pltpu.SemaphoreType.DMA
    second = blocks + mids

    def both(*dims):
        def index(j):
            return (jnp.where(j < second, jnp.maximum(j - blocks, 0), j - second),) + (0,) * len(dims)

        return pl.BlockSpec((1,) + dims, index)

    first = functools.partial(phase_block, 0, blocks)
    last = functools.partial(phase_block, second, mids)
    pairs = pl.BlockSpec((2,) + taps.shape[1:], lambda j: (jnp.clip(j - second, 0, mids - 1), 0, 0))
    scratch = [
        pltpu.VMEM((blocks, pixels, BLK), BF16),
        pltpu.VMEM((mids, pixels, BLK), F32),
        pltpu.VMEM((pixels, mid_total), BF16),
        pltpu.VMEM(masks.shape, F32),
        pltpu.VMEM((3, 2, pixels + 2 * PAD, HALF), F32),
        pltpu.VMEM((9, BLK, BLK), BF16),
        pltpu.VMEM((3, pixels, BLK), BF16),
        dma((len(sizes), members)),
        dma((len(sizes), members - 1)),
        dma((2,)),
    ]
    for _ in range(2):
        scratch += stats_scratch((mids, 2, BLK), batches, members)
    return pl.pallas_call(
        functools.partial(backward_kernel, count, batches, members, low, sizes),
        grid=(second + mids,),
        in_specs=[
            first(pixels, BLK),
            first(2, BLK),
            first(2, BLK),
            first(pixels, BLK),
            first(2, BLK),
            pl.BlockSpec((blocks, BLK, BLK), lambda j: (0, 0, jnp.clip(j - blocks, 0, mids - 1))),
            both(pixels, BLK),
            both(2, BLK),
            both(2, BLK),
            last(pixels, BLK),
            last(2, BLK),
            last(2, BLK),
            pairs,
            anywhere,
            anywhere,
            anywhere,
            anywhere,
        ],
        out_specs=[
            first(BLK, mid_total),
            last(pixels, BLK),
            pairs,
            whole(mids, 2, BLK),
            whole(mids, 2, BLK),
            anywhere,
        ],
        out_shape=[
            shape((blocks, BLK, mid_total), BF16),
            shape((mids, pixels, BLK)),
            shape(taps.shape, BF16),
            shape((mids, 2, BLK)),
            shape((mids, 2, BLK)),
            shape(source.shape, BF16),
        ],
        scratch_shapes=scratch,
        input_output_aliases={16: 5},
        compiler_params=pltpu.CompilerParams(vmem_limit_bytes=VMEM_LIMIT, collective_id=5, has_side_effects=True),
    )(
        expanded,
        esums,
        eparams,
        up,
        upsums,
        expand_full,
        grouped,
        gsums,
        gparams,
        reduced,
        sums,
        params,
        taps,
        act,
        masks,
        source,
        into,
    )


def turn(source_ref, target_ref, slot, chunk):
    first = (49 * chunk) // 4

    @pl.loop(0, 13)
    def _(tile):
        columns = pl.ds(pl.multiple_of((first + tile) * HALF, HALF), HALF)
        rows = pl.ds(pl.multiple_of(tile * HALF, HALF), HALF)
        target_ref[slot, rows] = source_ref[:, columns].T


def turned(target_ref, slot, chunk, pixels):
    return target_ref.at[slot, pl.ds(pl.multiple_of(32 * (chunk % 4), 16), pixels)]


def opening_kernel(batches, members, *refs):
    x_ref, grad_ref, wr_ref, we_ref, wg_ref = refs[:5]
    vectors = refs[5:11]
    xp_ref, gradt_ref, wr_out, we_out, wg_out, prm_out = refs[11:17]
    xin, xturn, gin, gturn, prm_ref, load, own, xsend, xrecv, gsend, psend, precv = refs[17:29]
    zsend, zrecv, ysend, yrecv, fsend, frecv = refs[29:]
    row, me, across, along = devices(batches, members)
    pixels = xp_ref.shape[1]
    load_x = pltpu.make_async_copy(x_ref, xin, load.at[0])
    load_grad = pltpu.make_async_copy(grad_ref, gin, load.at[1])
    load_x.start()
    load_grad.start()
    weights = [(wr_ref, wr_out), (wg_ref, wg_out), (we_ref, we_out)]
    height, side = me // 2, me % 2
    levels = members // 2
    line = [(row, lax.rem(me + 2 * step, members)) for step in range(1, levels)]
    peer = (row, height * 2 + 1 - side)
    local_copies = []
    parts = []
    for index, (source, target) in enumerate(weights):
        size = source.shape[0] // batches
        part = pl.ds(pl.multiple_of(row * size, 16), size)
        parts.append(part)
        local_copies.append(pltpu.make_async_copy(source.at[part], target.at[height, side, part], own.at[index]))
    each(local_copies, "start")
    place = 0
    for vector in vectors:
        for low in range(0, vector.shape[0], HALF):
            prm_ref[place : place + 1] = vector[low : low + HALF].reshape(1, HALF)
            place += 1
    prm_own = pltpu.make_async_copy(prm_ref, prm_out.at[me], own.at[3])
    prm_own.start()
    greet(across + along)
    copies = [prm_own]
    first = []
    for index, (source, target) in enumerate(weights):
        for step, device in enumerate(line):
            first.append(
                remote(
                    source.at[parts[index]],
                    target.at[height, side, parts[index]],
                    zsend.at[index, step],
                    zrecv.at[index, step],
                    device,
                )
            )
    for step, device in enumerate(along):
        copy = remote(prm_ref, prm_out.at[me], psend.at[step], precv.at[step], device)
        copy.start()
        copies.append(copy)
    each(first, "start")
    load_x.wait()
    for step, device in enumerate(along):
        turn(xin, xturn, step, device[1])
        copy = remote(turned(xturn, step, device[1], pixels), xp_ref.at[me], xsend.at[step], xrecv.at[step], device)
        copy.start()
        copies.append(copy)
    last = members - 1
    turn(xin, xturn, last, me)
    copy = pltpu.make_async_copy(turned(xturn, last, me, pixels), xp_ref.at[me], xsend.at[last])
    copy.start()
    copies.append(copy)
    load_grad.wait()
    for member in range(members):
        turn(gin, gturn, member, member)
        copy = pltpu.make_async_copy(turned(gturn, member, member, pixels), gradt_ref.at[member], gsend.at[member])
        copy.start()
        copies.append(copy)
    each(local_copies, "wait")
    far, near = (lax.bitwise_xor(row, 2), me), (lax.bitwise_xor(row, 1), me)
    second, third = [], []
    for index, (_, target) in enumerate(weights):
        each(first[index * len(line) : (index + 1) * len(line)], "wait")
        held = target.at[:, side, parts[index]]
        second.append(remote(held, held, ysend.at[index], yrecv.at[index], peer))
        second[-1].start()
    for index, (_, target) in enumerate(weights):
        second[index].wait()
        held = target.at[:, :, parts[index]]
        third.append(remote(held, held, fsend.at[index, 0], frecv.at[index, 0], far))
        third[-1].start()
    for index, (source, target) in enumerate(weights):
        size = source.shape[0] // batches
        third[index].wait()
        for step, origin in enumerate((row, lax.bitwise_xor(row, 2))):
            held = target.at[:, :, pl.ds(pl.multiple_of(origin * size, 16), size)]
            copy = remote(held, held, fsend.at[index, 1 + step], frecv.at[index, 1 + step], near)
            copy.start()
            copies.append(copy)
    each(copies, "wait")


def opening(block_input, out_grad, reduce_weight, expand_weight, taps, vectors, batches, members):
    channels, row_pixels = block_input.shape
    pixels = row_pixels // members
    dma = pltpu.SemaphoreType.DMA
    other, across, levels = members - 1, batches - 1, members // 2
    padded = 13 * HALF
    lines = sum(vector.shape[0] for vector in vectors) // HALF
    weights = [reduce_weight, expand_weight, taps]
    x, grad, *gathered, params = pl.pallas_call(
        functools.partial(opening_kernel, batches, members),
        in_specs=[pl.BlockSpec(memory_space=pl.ANY)] * 5 + [pl.BlockSpec(memory_space=pltpu.VMEM)] * len(vectors),
        out_specs=[pl.BlockSpec(memory_space=pl.ANY)] * 6,
        out_shape=[shape((members, pixels, channels), BF16)] * 2
        + [shape((levels, 2) + weight.shape, BF16) for weight in weights]
        + [shape((members, lines, HALF))],
        scratch_shapes=[
            pltpu.VMEM((channels, row_pixels), BF16),
            pltpu.VMEM((members, padded, channels), BF16),
            pltpu.VMEM((channels, row_pixels), BF16),
            pltpu.VMEM((members, padded, channels), BF16),
            pltpu.VMEM((lines, HALF), F32),
            dma((2,)),
            dma((4,)),
            dma((members,)),
            dma((other,)),
            dma((members,)),
            dma((other,)),
            dma((other,)),
            dma((3, levels - 1)),
            dma((3, levels - 1)),
            dma((3,)),
            dma((3,)),
            dma((3, across)),
            dma((3, across)),
        ],
        compiler_params=pltpu.CompilerParams(vmem_limit_bytes=VMEM_LIMIT, collective_id=0, has_side_effects=True),
    )(block_input, out_grad, *weights, *vectors)
    gathered = [full.reshape((members,) + full.shape[2:]) for full in gathered]
    return x, grad, *gathered, params


class Reduce:
    def __init__(self, part, out, row, me, refs, source=None):
        self.part, self.out, self.row = part, out, row
        self.source = part if source is None else source
        self.height, self.side = me // 2, me % 2
        self.place, self.core = row // 2, row % 2
        self.fresh, self.chip, self.cross, self.held, self.pair, self.line, self.second, self.total = refs[:8]
        self.send, self.recv = refs[8:]
        self.levels = self.held.shape[0]
        self.size = self.total.shape[0]
        self.near = (self.place * 2 + 1 - self.core, me)
        self.far = ((1 - self.place) * 2 + self.core, me)
        self.peer = (row, self.height * 2 + 1 - self.side)
        self.along = [(row, lax.rem(me + 2 * step, 2 * self.levels)) for step in range(1, self.levels)]

    def rows(self, row):
        return pl.ds(pl.multiple_of(row * self.size, 16), self.size)

    def copy(self, source, target, index, device):
        return remote(source, target, self.send.at[index], self.recv.at[index], device)

    def over_cores(self):
        return [
            self.copy(self.source.at[:, self.rows(2 * place + 1 - self.core)], self.fresh.at[place], place, self.near)
            for place in range(2)
        ]

    def add_cores(self):
        @pl.loop(0, 2 * self.levels)
        def _(member):
            for place in range(2):
                total = self.part[member, self.rows(2 * place + self.core)].astype(F32)
                self.chip[place, member] = (total + self.fresh[place, member].astype(F32)).astype(BF16)

    def over_x(self):
        return [self.copy(self.chip.at[1 - self.place], self.cross, 2, self.far)]

    def add_x(self):
        @pl.loop(0, self.levels)
        def _(level):
            for side in range(2):
                member = 2 * level + side
                total = self.chip[self.place, member].astype(F32) + self.cross[member].astype(F32)
                self.held[level, side] = total.astype(BF16)

    def over_pair(self):
        return [self.copy(self.held.at[:, 1 - self.side], self.pair, 3, self.peer)]

    def add_pair(self):
        @pl.loop(0, self.levels)
        def _(level):
            total = self.held[level, self.side].astype(F32) + self.pair[level].astype(F32)
            self.line[level] = total.astype(BF16)

    def over_line(self):
        return [
            self.copy(self.line.at[device[1] // 2], self.second.at[step], 4 + step, device)
            for step, device in enumerate(self.along)
        ]

    def add_line(self):
        total = self.line[self.height].astype(F32)
        for step in range(len(self.along)):
            total += self.second[step].astype(F32)
        self.total[...] = total

    def keep(self):
        return [pltpu.make_async_copy(self.total, self.out.at[self.rows(self.row)], self.send.at[10])]

    def share_x(self):
        return [self.copy(self.total, self.out.at[self.rows(self.row)], 7, self.far)]

    def share_cores(self):
        own = self.copy(self.total, self.out.at[self.rows(self.row)], 8, self.near)
        rows = self.rows((1 - self.place) * 2 + self.core)
        return [own, self.copy(self.out.at[rows], self.out.at[rows], 9, self.near)]


def reduce_scratch(dims, batches, members):
    rows, columns = dims[1] // batches, dims[2]
    levels = members // 2
    return [
        pltpu.VMEM((2, members, rows, columns), BF16),
        pltpu.VMEM((2, members, rows, columns), BF16),
        pltpu.VMEM((members, rows, columns), BF16),
        pltpu.VMEM((levels, 2, rows, columns), BF16),
        pltpu.VMEM((levels, rows, columns), BF16),
        pltpu.VMEM((levels, rows, columns), BF16),
        pltpu.VMEM((levels - 1, rows, columns), BF16),
        pltpu.VMEM((rows, columns), F32),
        pltpu.SemaphoreType.DMA((11,)),
        pltpu.SemaphoreType.DMA((10,)),
    ]


HELD_BACK = 4
EARLY = 3


def closing_steps(step, members):
    late = jnp.maximum(step - members, EARLY)
    return jnp.where(step < EARLY, step, late), jnp.clip(step - EARLY, 0, members - 1)


def closing_kernel(count, batches, members, low, size, *refs):
    red_ref, sums_ref, prm_ref, rup_ref, rupsums_ref, x_ref, up_ref, w_ref, epart_ref, tpart_ref, src_ref, _ = refs[:12]
    recv_ref, rout_ref, eout_ref, tout_ref, dst_ref = refs[12:17]
    back_ref, grad_ref, wpart_ref, gsend, grecv, psend, precv = refs[17:24]
    red_held, rup_held, epart_held, load_sem = refs[54:]
    row, me, across, along = devices(batches, members)
    step = pl.program_id(0)
    last = members - 1
    expand_sum = Reduce(epart_held, eout_ref, row, me, refs[24:34], epart_ref)
    taps_sum = Reduce(tpart_ref, tout_ref, row, me, refs[34:44])
    reduce_sum = Reduce(wpart_ref, rout_ref, row, me, refs[44:54])
    parts = (expand_sum, taps_sum, reduce_sum)
    grad_step, weight_step = closing_steps(step, members)

    def pieces():
        return piece_copies(src_ref, dst_ref, low, size, me, along, psend, precv)

    def send(index):
        device = (row, lax.rem(me + 1 + index, members))
        return remote(grad_ref.at[index], recv_ref.at[me], gsend.at[index], grecv.at[index], device)

    mids = red_held.shape[0]
    load_part = pltpu.make_async_copy(epart_ref, epart_held, load_sem.at[2 * mids])

    @pl.when(step == 0)
    def _():
        greet(across + along)
        each(pieces(), "start")
        loads = []
        for mid in range(mids):
            for which, (source, held) in enumerate(((red_ref, red_held), (rup_ref, rup_held))):
                loads.append(pltpu.make_async_copy(source.at[mid], held.at[mid], load_sem.at[2 * mid + which]))
        each(loads, "start")
        load_part.start()
        each(expand_sum.over_cores(), "start")
        each(taps_sum.over_cores(), "start")
        first_back(count, red_held, sums_ref, prm_ref, rup_held, rupsums_ref, back_ref, loads)

    weight_turn = (step >= EARLY) & (step < EARLY + members)

    @pl.when(weight_turn)
    def _():
        weight_grad_block(x_ref[0], back_ref, wpart_ref, lax.rem(me + 1 + weight_step, members))

    @pl.when(jnp.logical_not(weight_turn))
    def _():
        def product(start, size):
            part = pl.ds(start, size)
            total = dot(back_ref[part], w_ref[0], ((1,), (1,)))
            grad_ref[grad_step, part] = (up_ref[0, part] + total).astype(BF16)

        over_rows(x_ref.shape[1], product)

        @pl.when(grad_step < last - HELD_BACK)
        def _():
            send(grad_step).start()

    @pl.when(step == EARLY)
    def _():
        load_part.wait()
        for part in parts[:2]:
            each(part.over_cores(), "wait")
            part.add_cores()
            each(part.over_x(), "start")

    @pl.when(step == EARLY + members - 1)
    def _():
        each(reduce_sum.over_cores(), "start")
        for part in parts[:2]:
            each(part.over_x(), "wait")
            part.add_x()
            each(part.over_pair(), "start")

    @pl.when(step == EARLY + members)
    def _():
        each(reduce_sum.over_cores(), "wait")
        reduce_sum.add_cores()
        each(reduce_sum.over_x(), "start")

    @pl.when(step == 2 * members - 1)
    def _():
        own = pltpu.make_async_copy(grad_ref.at[last], recv_ref.at[me], gsend.at[last])
        own.start()
        send(last - HELD_BACK).start()
        for part in parts[:2]:
            each(part.over_pair(), "wait")
            part.add_pair()
            each(part.over_line(), "start")
        each(reduce_sum.over_x(), "wait")
        reduce_sum.add_x()
        each(reduce_sum.over_pair(), "start")
        each(reduce_sum.over_pair(), "wait")
        reduce_sum.add_pair()
        each(reduce_sum.over_line(), "start")
        for index in range(last - HELD_BACK + 1, last):
            send(index).start()
        for part in parts:
            each(part.over_line(), "wait")
            part.add_line()
            each(part.share_x() + part.keep(), "start")
        for part in parts:
            each(part.share_x(), "wait")
            each(part.share_cores(), "start")
        own.wait()
        each(pieces(), "wait")
        for index in range(last):
            send(index).wait()
        for part in parts:
            each(part.share_cores() + part.keep(), "wait")


def closing(
    reduced, sums, params, rup, rupsums, x, up, weight, epart, tpart, source, into, low, size, count, batches, members
):
    mids, pixels, _ = reduced.shape
    blocks = x.shape[0]
    once = pl.Buffered(1)

    def keep(*dims):
        return pl.BlockSpec(dims, lambda j: (0,) * len(dims), pipeline_mode=once)

    def turn_block(which, *dims):
        def index(j):
            return (lax.rem(lax.axis_index("group") + 1 + closing_steps(j, members)[which], members),) + (0,) * len(dims)

        return pl.BlockSpec((1,) + dims, index)

    anywhere = pl.BlockSpec(memory_space=pl.ANY)
    dma = pltpu.SemaphoreType.DMA
    wdims = (blocks, BLK, mids * BLK)
    scratch = [
        pltpu.VMEM((pixels, mids * BLK), BF16),
        pltpu.VMEM((blocks, pixels, BLK), BF16),
        pltpu.VMEM(wdims, BF16),
        dma((members,)),
        dma((members - 1,)),
        dma((members,)),
        dma((members - 1,)),
    ]
    for dims in (wdims, tpart.shape, wdims):
        scratch += reduce_scratch(dims, batches, members)
    scratch += [
        pltpu.VMEM((mids, pixels, BLK), F32),
        pltpu.VMEM((mids, pixels, BLK), F32),
        pltpu.VMEM(wdims, BF16),
        dma((2 * mids + 1,)),
    ]
    return pl.pallas_call(
        functools.partial(closing_kernel, count, batches, members, low, size),
        grid=(2 * blocks,),
        in_specs=[
            anywhere,
            keep(mids, 2, BLK),
            keep(mids, 2, BLK),
            anywhere,
            keep(mids, 2, BLK),
            turn_block(1, pixels, BLK),
            turn_block(0, pixels, BLK),
            turn_block(0, BLK, mids * BLK),
            anywhere,
            keep(*tpart.shape),
            anywhere,
            anywhere,
        ],
        out_specs=[anywhere] * 5,
        out_shape=[
            shape((members, pixels, BLK), BF16),
            shape(wdims[1:]),
            shape(wdims[1:]),
            shape(tpart.shape[1:]),
            shape(source.shape, BF16),
        ],
        scratch_shapes=scratch,
        input_output_aliases={11: 4},
        compiler_params=pltpu.CompilerParams(vmem_limit_bytes=VMEM_LIMIT, collective_id=7, has_side_effects=True),
    )(reduced, sums, params, rup, rupsums, x, up, weight, epart, tpart, source, into)


def own_parts(reduce_ref, group_ref, expand_ref, outs):
    me = lax.axis_index("group")
    half = pl.ds(pl.multiple_of((me % 2) * HALF, HALF), HALF)
    for index, stats_ref in enumerate((reduce_ref, group_ref)):
        for which in range(2):
            outs[2 * index + 1 - which][...] = stats_ref[me // 2, which : which + 1, half]
    for which in range(2):
        outs[5 - which][...] = expand_ref[me, which : which + 1]


def turn_out_kernel(first_ref, second_ref, reduce_ref, group_ref, expand_ref, first_out, second_out, *outs):
    own = lax.broadcasted_iota(jnp.int32, (BLK, BLK), 0) == lax.broadcasted_iota(jnp.int32, (BLK, BLK), 1)
    identity = jnp.where(own, 1.0, 0.0).astype(BF16)
    half = pl.num_programs(0) // 2

    @pl.when(pl.program_id(0) == 0)
    def _():
        own_parts(reduce_ref, group_ref, expand_ref, outs)

    def turn_part(in_ref, out_ref):
        for low in range(0, in_ref.shape[0], HALF):
            part = dot(identity, in_ref[low : low + HALF], ((1,), (1,)))
            out_ref[:, low : low + HALF] = part.astype(out_ref.dtype)

    @pl.when(pl.program_id(0) < half)
    def _():
        turn_part(first_ref, first_out)

    @pl.when(pl.program_id(0) >= half)
    def _():
        turn_part(second_ref, second_out)


def turn_out(first, second, stats):
    sizes = (HALF,) * 4 + (BLK,) * 2
    rows, channels = first.shape
    parts = 2
    size = rows // parts

    def early(j):
        return jnp.minimum(j, parts - 1)

    def late(j):
        return jnp.maximum(j - parts, 0)

    return call(
        turn_out_kernel,
        (2 * parts,),
        [
            pl.BlockSpec((size, channels), lambda j: (early(j), 0)),
            pl.BlockSpec((size, channels), lambda j: (late(j), 0)),
        ]
        + [whole(*part.shape) for part in stats],
        [
            pl.BlockSpec((channels, size), lambda j: (0, early(j))),
            pl.BlockSpec((channels, size), lambda j: (0, late(j))),
        ]
        + [whole(1, width) for width in sizes],
        [shape((channels, rows)), shape((channels, rows), BF16)] + [shape((1, width)) for width in sizes],
        [],
        4 * rows * channels * BLK,
    )(first, second, *stats)


def pixel_masks(pixels):
    place = np.arange(pixels)
    tall, wide = (place // SIDE) % SIDE, place % SIDE
    masks = np.stack([wide != 0, wide != SIDE - 1, tall != 0, tall != SIDE - 1])
    return jnp.asarray(np.broadcast_to(masks[:, :, None], (4, pixels, HALF)).astype(np.float32))


def own_part(stats, which, length):
    return lax.dynamic_slice_in_dim(stats[:, which].reshape(-1), lax.axis_index("group") * length, length, 0)


TAP_ROWS = 320


def fused(
    block_input,
    reduce_weight,
    reduce_gain,
    reduce_bias,
    group_weight,
    group_gain,
    group_bias,
    expand_weight,
    expand_gain,
    expand_bias,
    out_grad,
):
    batches, members = lax.axis_size("batch"), lax.axis_size("group")
    channels, row_pixels = block_input.shape
    pixels = row_pixels // members
    count = row_pixels * batches
    vectors = [reduce_gain, reduce_bias, group_gain, group_bias, expand_gain, expand_bias]
    taps = group_weight.reshape(-1, 9, GW, GW).transpose(1, 2, 0, 3).reshape(9 * GW, HALF)
    taps = jnp.pad(taps, ((0, TAP_ROWS - 9 * GW), (0, 0)))
    masks = pixel_masks(pixels)
    x, grad_turned, reduce_full, expand_full, taps_full, packs = opening(
        block_input, out_grad, reduce_weight, expand_weight, taps, vectors, batches, members
    )
    vectors = packs[:, :4].reshape(-1, 2, 4, HALF).transpose(0, 2, 1, 3).reshape(-1, 4, BLK)
    reduce_params, group_params = vectors[:, :2], vectors[:, 2:]
    expand_params = packs[:, 4:].reshape(-1, 2, BLK)

    sizes = (256, 240, 336, 240, 304)
    reduced, grouped, act, expanded, reduce_sums, group_sums, expand_sums, grad = forward(
        x,
        reduce_full,
        reduce_params,
        taps_full,
        masks,
        group_params,
        expand_full,
        grad_turned,
        sizes + (pixels - sum(sizes),),
        count,
        batches,
        members,
    )
    sends = Comm(batches, members, 4, None, 0, (208, 112), None, True)
    out, upstream, expand_stats, moved = output(expanded, expand_sums, expand_params, x, grad, count, sends)
    sizes = (416, 144, 432, 112)
    expand_part, reduce_up, taps_part, group_stats, reduce_stats, moved = backward(
        expanded,
        expand_sums,
        expand_params,
        upstream,
        expand_stats,
        expand_full,
        grouped,
        group_sums,
        group_params,
        reduced,
        reduce_sums,
        reduce_params,
        taps_full,
        act,
        masks,
        out,
        moved,
        sends.high,
        sizes,
        count,
        batches,
        members,
    )
    high = sends.high + sum(sizes)
    inner, reduce_weight_grad, expand_weight_grad, taps_grad, moved = closing(
        reduced,
        reduce_sums,
        reduce_params,
        reduce_up,
        reduce_stats,
        x,
        upstream,
        reduce_full,
        expand_part,
        taps_part,
        out,
        moved,
        high,
        pixels - high,
        count,
        batches,
        members,
    )
    input_grad, block_output, *sums = turn_out(
        inner.reshape(row_pixels, channels),
        moved.reshape(row_pixels, channels),
        (reduce_stats, group_stats, expand_stats),
    )
    taps_grad = taps_grad[: 9 * GW].reshape(9, GW, -1, GW).transpose(2, 0, 3, 1)
    return (
        block_output,
        input_grad,
        reduce_weight_grad,
        taps_grad.reshape(group_weight.shape),
        expand_weight_grad,
    ) + tuple(part.reshape(-1) for part in sums)


def modular(
    block_input,
    reduce_weight,
    reduce_gain,
    reduce_bias,
    group_weight,
    group_gain,
    group_bias,
    expand_weight,
    expand_gain,
    expand_bias,
    out_grad,
):
    batches, members = lax.axis_size("batch"), lax.axis_size("group")
    channels, row_pixels = block_input.shape
    pixels = row_pixels // members
    count = row_pixels * batches
    mid_total = reduce_weight.shape[1]
    mids = mid_total // BLK
    blocks = channels * members // BLK
    me = lax.axis_index("group")

    def to_pixels(values):
        moved = lax.all_to_all(values.T.reshape(members, pixels, channels), "group", 0, 0)
        if channels == BLK:
            return moved
        share = BLK // channels
        moved = moved.reshape(blocks, share, pixels, channels).transpose(0, 2, 1, 3)
        return moved.reshape(blocks, pixels, BLK)

    def to_channels(values):
        if channels != BLK:
            share = BLK // channels
            values = values.reshape(blocks, pixels, share, channels).transpose(0, 2, 1, 3)
            values = values.reshape(members, pixels, channels)
        moved = lax.all_to_all(values, "group", 0, 0)
        return moved.reshape(row_pixels, channels).T

    def gather(values):
        return lax.all_gather(values, "group", axis=0, tiled=True)

    local_mid = reduce_gain.shape[0]
    pack = jnp.concatenate([reduce_gain, reduce_bias, group_gain, group_bias, expand_gain, expand_bias])
    packs = gather(pack[None])
    vectors, offset = [], 0
    for length in (local_mid, local_mid, local_mid, local_mid, channels, channels):
        vectors.append(packs[:, offset : offset + length].reshape(-1, BLK))
        offset += length
    reduce_params = jnp.stack(vectors[0:2], 1)
    group_params = jnp.stack(vectors[2:4], 1)
    expand_params = jnp.stack(vectors[4:6], 1)
    reduce_full = gather(reduce_weight).reshape(blocks, BLK, mid_total)
    expand_full = gather(expand_weight).reshape(blocks, BLK, mid_total)
    taps = gather(group_weight.reshape(group_weight.shape[0], 9, GW, GW))
    taps = taps.reshape(-1, HALF // GW, 9, GW, GW).transpose(0, 2, 3, 1, 4).reshape(-1, 9 * GW, HALF)
    taps = jnp.pad(taps, ((0, 0), (0, TAP_ROWS - 9 * GW), (0, 0)))
    masks = pixel_masks(pixels)

    x = to_pixels(block_input)
    grad = to_pixels(out_grad)

    reduced, reduce_sums = reduce_product(x, reduce_full, None)
    reduce_sums = exchange(reduce_sums, batches, members, 1)
    grouped, group_sums = conv(reduced, reduce_sums, reduce_params, taps, masks, count, None)
    group_sums = exchange(group_sums, batches, members, 1)
    expanded, act, expand_sums = expand_product(grouped, group_sums, group_params, expand_full, count, None)
    expand_sums = exchange(expand_sums, batches, members, 2)
    out, upstream, expand_stats = output(expanded, expand_sums, expand_params, x, grad, count, None)
    expand_stats = exchange(expand_stats, batches, members, 2)
    expand_part, group_up, group_stats = expand_back(
        expanded, expand_sums, expand_params, upstream, expand_stats, expand_full, grouped, group_sums, group_params, act, count, None
    )
    group_stats = exchange(group_stats, batches, members, 1)
    reduce_up, taps_part, reduce_stats = conv_back(
        reduced,
        reduce_sums,
        reduce_params,
        grouped,
        group_sums,
        group_params,
        group_up,
        group_stats,
        taps,
        masks,
        count,
        None,
    )
    reduce_stats = exchange(reduce_stats, batches, members, 1)
    inner, reduce_part = reduce_back(
        reduced, reduce_sums, reduce_params, reduce_up, reduce_stats, x, upstream, reduce_full, count
    )
    block_output = to_channels(out)
    input_grad = to_channels(inner).astype(F32)

    def shared_sum(part):
        rows = channels // batches
        part = part.reshape(members, batches, rows, mid_total).transpose(1, 0, 2, 3)
        part = lax.all_to_all(part, "batch", 0, 0).astype(F32).sum(0).astype(BF16)
        part = lax.all_to_all(part, "group", 0, 0).astype(F32).sum(0)
        return lax.all_gather(part, "batch", axis=0, tiled=True)

    expand_weight_grad = shared_sum(expand_part)
    reduce_weight_grad = shared_sum(reduce_part)
    taps_part = taps_part[:, : 9 * GW].reshape(-1, 9, GW, HALF // GW, GW).transpose(0, 3, 1, 4, 2)
    taps_part = taps_part.reshape(members, -1, 9, GW, GW)
    group_weight_grad = lax.all_to_all(taps_part, "group", 0, 0).astype(F32).sum(0)
    group_weight_grad = lax.psum(group_weight_grad, "batch").reshape(group_weight.shape)

    return (
        block_output,
        input_grad,
        reduce_weight_grad,
        group_weight_grad,
        expand_weight_grad,
        own_part(reduce_stats, 1, local_mid),
        own_part(reduce_stats, 0, local_mid),
        own_part(group_stats, 1, local_mid),
        own_part(group_stats, 0, local_mid),
        own_part(expand_stats, 1, channels),
        own_part(expand_stats, 0, channels),
    )


def local(*args):
    block_input = args[0]
    pixels = block_input.shape[1] // lax.axis_size("group")
    if block_input.shape[0] == BLK and pixels == 1568 and args[2].shape[0] == HALF and lax.axis_size("group") == 8:
        return fused(*args)
    return modular(*args)


def solution(mesh):
    in_specs = (
        P("group", "batch"),
        P("group", None),
        P("group"),
        P("group"),
        P("group", None, None, None, None),
        P("group"),
        P("group"),
        P("group", None),
        P("group"),
        P("group"),
        P("group", "batch"),
    )
    out_specs = (
        P("group", "batch"),
        P("group", "batch"),
        P("group", None),
        P("group", None, None, None, None),
        P("group", None),
        P("group"),
        P("group"),
        P("group"),
        P("group"),
        P("group"),
        P("group"),
    )
    return jax.shard_map(local, mesh=mesh, in_specs=in_specs, out_specs=out_specs, check_vma=False)
```
